128 devices in a mesh: seq: 64 (over z, y_hi, x, core), tp: 2 (over y_lo).
Axes of the slice: x: 4, y: 4 (y_hi: 2, y_lo: 2; y = y_hi * 2 + y_lo), z: 4, core: 2. Of those that a mesh axis runs over, the one named last changes fastest.
Arguments:
- hidden_in: float32 [8192, 1536], P(('seq', 'tp')), as said below
- cotangent: float32 [8192, 1536], P(('seq', 'tp')), may hold values from -6 to 6
- needle_mask: int32 [8192], P(('seq', 'tp')), may hold values 0 or 1
- attn_gain: float32 [1536], replicated, as said below
- lambdas: float32 [4, 12, 64], replicated, may hold values from -0.625 to 0.625
- subln_gain: float32 [128], replicated, may hold values from 0.1 to 1.9
- ffn_gain: float32 [1536], replicated, may hold values from 0.1 to 1.9
- weight_query: bfloat16 [1536, 1536], P(None, 'tp'), as said below
- weight_key: bfloat16 [1536, 1536], P(None, 'tp'), as said below
- weight_value: bfloat16 [1536, 1536], P(None, 'tp'), may hold values from -0.15625 to 0.15625
- weight_out: bfloat16 [1536, 1536], P(None, 'tp'), may hold values from -0.75 to 0.75
- weight_gate: bfloat16 [1536, 4096], P(None, 'tp'), may hold values from -0.15625 to 0.15625
- weight_up: bfloat16 [1536, 4096], P(None, 'tp'), may hold values from -0.15625 to 0.15625
- weight_down: bfloat16 [1536, 4096], P(None, 'tp'), may hold values from -0.09375 to 0.09375
Outputs:
- output: float32 [8192, 1536], P(('seq', 'tp'))
- grad_input: float32 [8192, 1536], P(('seq', 'tp'))
- grad_query: float32 [1536, 1536], P('seq', 'tp')
- grad_key: float32 [1536, 1536], P('seq', 'tp')
- grad_value: float32 [1536, 1536], P('seq', 'tp')
- grad_out_proj: float32 [1536, 1536], P('seq', 'tp')
- grad_gate: float32 [1536, 4096], P('seq', 'tp')
- grad_up: float32 [1536, 4096], P('seq', 'tp')
- grad_down: float32 [1536, 4096], P('seq', 'tp')
- grad_attn_gain: float32 [1536], replicated
- grad_lambdas: float32 [4, 12, 64], replicated
- grad_subln_gain: float32 [128], replicated
- grad_ffn_gain: float32 [1536], replicated
The draws below stay inside these ranges and needn't reach their ends.
Inputs may be any that keep to these rules, and one draw needn't show every extreme that they name: `hidden_in`: entries of order one, independent. `attn_gain`: entries about 1, each within 0.1 to 1.9. `weight_query`: independent entries of deviation about 1 / sqrt(1536). `weight_key`: independent entries of deviation about 1 / sqrt(1536).
All inputs are finite; a program needn't handle non-finite values. No bound on the sum of `needle_mask` on one device may be relied on, other than what follows from the above.
Results may differ from the reference program's by a relative error of at most 0.017.
Values may be sent and summed in bfloat16 or wider, within the bound.
A program may use at most 256 MiB of HBM per device.

```python
import math
import jax
import jax.numpy as jnp
from jax import lax

D = 1536
H = 12
HD = 64
FF = 4096
VD = 128
SEQ = 8192


def draw_hidden_in(key, part):
    key = jax.random.fold_in(key, 11)
    return jnp.clip(jax.random.normal(key, (SEQ, D), jnp.float32), -6.0, 6.0)


def draw_attn_gain(key, part):
    key = jax.random.fold_in(key, 12)
    return 1.0 + jnp.clip(0.18 * jax.random.normal(key, (D,), jnp.float32), -0.9, 0.9)


def projection(key):
    values = jnp.clip(jax.random.normal(key, (D, H * VD), jnp.float32), -6.0, 6.0)
    return (values * D ** (-0.5)).astype(jnp.bfloat16)


def draw_weight_query(key, part):
    key = jax.random.fold_in(key, 13)
    return projection(key)


def draw_weight_key(key, part):
    key = jax.random.fold_in(key, 14)
    return projection(key)


def set_ends(drawn, rng, low, high):
    extent = drawn.shape
    index_at = [jax.random.randint(jax.random.fold_in(rng, axis), (), 0, extent[axis]) for axis in range(len(extent))]
    drawn = drawn.at[tuple(index_at)].set(low)
    longest = extent.index(max(extent))
    index_at[longest] = (index_at[longest] + 1) % extent[longest]
    return drawn.at[tuple(index_at)].set(high)


def level_of(rng, dims, split, low, largest):
    def one(dim, blocks):
        heights = jax.random.uniform(jax.random.fold_in(jax.random.fold_in(rng, 6), dim), (blocks,), jnp.float32, low / len(split), largest / len(split))
        return jnp.repeat(jnp.exp(heights), dims[dim] // blocks).reshape((-1,) + (1,) * (len(dims) - dim - 1))

    gain = one(*split[0])
    for cut in split[1:]:
        gain = gain * one(*cut)
    return gain


def centred(stream_key, extent, deviation, bound, pieces=(), kind=jnp.bfloat16):
    array = deviation * jax.random.normal(stream_key, extent, jnp.float32)
    if pieces:
        array = array * level_of(stream_key, extent, pieces, -0.22, 0.18)
    return jnp.clip(array, -bound, bound).astype(kind)


def setup_inputs(seed: int = 0) -> dict:
    seeds = jax.random.split(jax.random.key(seed), 15)
    hidden_in = draw_hidden_in(jax.random.fold_in(seeds[14], 71), 0)
    cotangent = centred(seeds[1], (SEQ, D), 1.0, 6.0, ((0, 128),), jnp.float32)
    needle_mask = set_ends((jax.random.randint(seeds[2], (SEQ,), 0, 4) < 3).astype(jnp.int32), jax.random.fold_in(seeds[2], 1), 0, 1)
    attn_gain = draw_attn_gain(jax.random.fold_in(seeds[14], 71), 0)
    lambdas = centred(seeds[4], (4, H, HD), 0.1, 0.625, (), jnp.float32)
    subln_gain = jnp.clip(1.0 + 0.18 * jax.random.normal(seeds[5], (VD,), jnp.float32), 0.1, 1.9)
    ffn_gain = jnp.clip(1.0 + 0.18 * jax.random.normal(seeds[6], (D,), jnp.float32), 0.1, 1.9)
    weight_query = draw_weight_query(jax.random.fold_in(seeds[14], 71), 0)
    weight_key = draw_weight_key(jax.random.fold_in(seeds[14], 71), 0)
    weight_value = centred(seeds[9], (D, H * VD), D ** -0.5, 0.15625, ((1, 2),))
    weight_out = centred(seeds[10], (D, H * VD), (max(H * VD // 21, 1)) ** -0.5, 0.75, ((1, 2),))
    weight_gate = centred(seeds[11], (D, FF), D ** -0.5, 0.15625, ((1, 2),))
    weight_up = centred(seeds[12], (D, FF), D ** -0.5, 0.15625, ((1, 2),))
    weight_down = centred(seeds[13], (D, FF), FF ** -0.5, 0.09375, ((1, 2),))
    return {"hidden_in": hidden_in, "cotangent": cotangent, "needle_mask": needle_mask, "attn_gain": attn_gain, "lambdas": lambdas, "subln_gain": subln_gain, "ffn_gain": ffn_gain, "weight_query": weight_query, "weight_key": weight_key, "weight_value": weight_value, "weight_out": weight_out, "weight_gate": weight_gate, "weight_up": weight_up, "weight_down": weight_down}


@jax.custom_vjp
def low(v):
    return lax.optimization_barrier(v.astype(jnp.bfloat16)).astype(jnp.float32)

@jax.custom_vjp
def low_back(v):
    return v

def low_keep(v):
    return (low(v), None)

def low_pass(kept, grad):
    return (grad,)

def back_keep(v):
    return (v, None)

def back_low(kept, grad):
    return (low(grad),)
low.defvjp(low_keep, low_pass)
low_back.defvjp(back_keep, back_low)
highest = lax.Precision.HIGHEST
eps = 1e-06
lambda_init = 0.8 - 0.6 * math.exp(-3.6)

def matmul(left, right):
    return jnp.dot(left, right, preferred_element_type=jnp.float32, precision=highest)

def rms_scale(values):
    return lax.rsqrt(lax.optimization_barrier(jnp.mean(values * values, axis=-1, keepdims=True)) + eps)

def lambda_values(lambdas):
    first = jnp.exp(lax.optimization_barrier(jnp.sum(lambdas[0] * lambdas[1], axis=-1)))
    second = jnp.exp(lax.optimization_barrier(jnp.sum(lambdas[2] * lambdas[3], axis=-1)))
    return first - second + lambda_init

def attend_block(query_block, start, keys, values, lambda_value):
    half = keys.shape[-1] // 2
    query_pos = start + jnp.arange(query_block.shape[0], dtype=jnp.int32)
    key_pos = jnp.arange(keys.shape[0], dtype=jnp.int32)
    visible = (key_pos[None, :] <= query_pos[:, None])[None]
    parts = []
    for offset in (0, half):
        score = jnp.einsum('qhd,khd->hqk', query_block[..., offset:offset + half], keys[..., offset:offset + half], precision=highest) * half ** (-0.5)
        score = low_back(score)
        score = jnp.where(visible, score, -jnp.inf)
        probability = low(jax.nn.softmax(score, axis=-1))
        parts.append(jnp.einsum('hqk,khd->qhd', probability, values, precision=highest))
    return low_back(parts[0] - lambda_value[None, :, None] * parts[1])

def forward(hidden_in, attn_gain, lambdas, subln_gain, ffn_gain, weight_query, weight_key, weight_value, weight_out, weight_gate, weight_up, weight_down):
    length = hidden_in.shape[0]
    heads = lambdas.shape[1]
    width = weight_query.shape[1]
    head_width = width // heads
    normed = low(hidden_in * rms_scale(hidden_in) * attn_gain)
    query = low(low_back(matmul(normed, weight_query))).reshape(length, heads, head_width)
    keys = low(low_back(matmul(normed, weight_key))).reshape(length, heads, head_width)
    values = low(low_back(matmul(normed, weight_value))).reshape(length, heads, head_width)
    lambda_value = lambda_values(lambdas)
    block = math.gcd(length, 512)
    blocks = query.reshape(length // block, block, heads, head_width)
    starts = jnp.arange(length // block, dtype=jnp.int32) * block
    attend = jax.checkpoint(attend_block)
    differ = lax.map(lambda item: attend(item[0], item[1], keys, values, lambda_value), (blocks, starts)).reshape(length, heads, head_width)
    heads_normed = differ * rms_scale(differ) * subln_gain * (1.0 - lambda_init)
    mixed = low(heads_normed.reshape(length, width))
    resid = hidden_in + low_back(matmul(mixed, weight_out.T))
    ffn_normed = low(resid * rms_scale(resid) * ffn_gain)
    gate = low_back(matmul(ffn_normed, weight_gate))
    up_values = low_back(matmul(ffn_normed, weight_up))
    hidden = low(jax.nn.silu(gate) * up_values)
    return resid + low_back(matmul(hidden, weight_down.T))

def reference(hidden_in, cotangent, needle_mask, attn_gain, lambdas, subln_gain, ffn_gain, weight_query, weight_key, weight_value, weight_out, weight_gate, weight_up, weight_down):
    inputs = (hidden_in, attn_gain, lambdas, subln_gain, ffn_gain, weight_query.astype(jnp.float32), weight_key.astype(jnp.float32), weight_value.astype(jnp.float32), weight_out.astype(jnp.float32), weight_gate.astype(jnp.float32), weight_up.astype(jnp.float32), weight_down.astype(jnp.float32))
    output, pullback = jax.vjp(forward, *inputs)
    grads = pullback(cotangent * needle_mask.astype(jnp.float32)[:, None])
    return (output, grads[0], grads[5], grads[6], grads[7], grads[8], grads[9], grads[10], grads[11], grads[1], grads[2], grads[3], grads[4])
```

```python
import math

import jax
import jax.numpy as jnp
from jax import lax
from jax.experimental import pallas as pl
from jax.experimental.pallas import tpu as pltpu
from jax.sharding import PartitionSpec as P

MESH = pl.DeviceIdType.MESH
BF = jnp.bfloat16
F32 = jnp.float32
EPS = 1e-06
LAMBDA_INIT = 0.8 - 0.6 * math.exp(-3.6)
OUT_SCALE = 1.0 - LAMBDA_INIT
D = 1536
CHIPS = 32
SERVED = 30
PER_HEAD = 5
ROWS = 64
BLOCK = 256
TILE = 128
SLOTS = 7
KB = 512
LOG2E = 1.4426950408889634
SCORE = 0.125 * LOG2E
VMEM_LIMIT = 60 * 2**20


def place():
    s = lax.axis_index("seq")
    return s // 2, s % 2, lax.axis_index("tp")


def owner_of(tile):
    step = (tile - 4) // 10
    pos = (tile - 4) % 10
    slot = jnp.where(step % 2 == 0, pos, 9 - pos)
    early = tile < 4
    return jnp.where(early, tile, slot), jnp.where(early, 0, step + 1)


def tile_of(slot, r):
    if r == 0:
        return slot
    return 4 + 10 * (r - 1) + (slot if (r - 1) % 2 == 0 else 9 - slot)


def matmul(a, b):
    return jnp.dot(a, b, preferred_element_type=F32)


def matmul_t(a, b):
    return lax.dot_general(a, b, (((1,), (1,)), ((), ())), preferred_element_type=F32)


def rms_scale(values, axis=-1):
    return lax.rsqrt(jnp.mean(values * values, axis=axis, keepdims=True) + EPS)


def norm_back(grad_normed, gain, rms, hat, axis=-1):
    scaled = grad_normed * gain
    return rms * (scaled - hat * jnp.mean(scaled * hat, axis=axis, keepdims=True))


def greet_all(chip, core, t):
    barrier = pltpu.get_barrier_semaphore()
    s = 2 * chip + core

    def greet(o, carry):
        pl.semaphore_signal(
            barrier, inc=1, device_id=(lax.rem(s + o, 2 * CHIPS), t), device_id_type=MESH
        )
        return carry

    lax.fori_loop(1, 2 * CHIPS, greet, 0)
    pl.semaphore_signal(barrier, inc=1, device_id=(s, 1 - t), device_id_type=MESH)
    pl.semaphore_wait(barrier, 2 * CHIPS)


def remote(src, dst, send_sem, recv_sem, s, t):
    return pltpu.make_async_remote_copy(
        src_ref=src,
        dst_ref=dst,
        send_sem=send_sem,
        recv_sem=recv_sem,
        device_id=(s, t),
        device_id_type=MESH,
    )


def rows_at(ref, start, count):
    return ref.at[pl.ds(pl.multiple_of(start, ROWS), count)]


class QuadGather:
    def __init__(self, buf, send, recv, chip, core, t):
        self.buf, self.send, self.recv = buf, send, recv
        self.chip, self.core, self.t = chip, core, t
        mine = core * 128 + t * ROWS
        self.mine = mine
        self.near = core * 128 + (1 - t) * ROWS
        sib = (2 * chip + 1 - core, t)
        self.to_near = self.copy(mine, 0, (2 * chip + core, 1 - t))
        self.to_sib = self.copy(mine, 1, sib)
        self.forward = self.copy(self.near, 2, sib)

    def copy(self, row, k, target):
        view = rows_at(self.buf, row, ROWS)
        return remote(view, view, self.send.at[k], self.recv.at[k], *target)

    def start(self):
        self.to_near.start()
        self.to_sib.start()

    def finish(self):
        self.to_near.wait_recv()
        self.forward.start()
        self.to_sib.wait_recv()
        self.forward.wait_recv()

    def drain(self):
        self.to_near.wait_send()
        self.to_sib.wait_send()
        self.forward.wait_send()


GATHER_SEMS = [pltpu.SemaphoreType.DMA((3,)), pltpu.SemaphoreType.DMA((3,))]
CW = 512
NC = D // CW


class QuadReduce:
    def __init__(self, part, dsend, drecv, ysend, yrecv, ds, dr, ys, yr, chip, core, t):
        self.part, self.dsend, self.drecv = part, dsend, drecv
        self.ysend, self.yrecv = ysend, yrecv
        self.core, self.t = core, t
        self.d = [
            remote(dsend.at[k], drecv.at[k], ds.at[k], dr.at[k], 2 * chip + 1 - core, t)
            for k in range(NC)
        ]
        self.y = [
            remote(ysend.at[k], yrecv.at[k], ys.at[k], yr.at[k], 2 * chip + core, 1 - t)
            for k in range(NC)
        ]

    def rows(self, start, count, k):
        return self.part[pl.ds(pl.multiple_of(start, ROWS), count), k * CW : (k + 1) * CW]

    def put(self, k, value):
        self.part[:, k * CW : (k + 1) * CW] = value
        self.dsend[k] = self.rows((1 - self.core) * 128, 128, k).astype(BF)
        self.d[k].start()

    def middle(self, k):
        self.d[k].wait_recv()
        near = (1 - self.t) * ROWS
        far = self.rows(self.core * 128 + near, ROWS, k)
        got = self.drecv[k, pl.ds(pl.multiple_of(near, ROWS), ROWS), :]
        self.ysend[k] = (far + got.astype(F32)).astype(BF)
        self.y[k].start()

    def result(self, k):
        mine = self.t * ROWS
        own = self.rows(self.core * 128 + mine, ROWS, k)
        got = self.drecv[k, pl.ds(pl.multiple_of(mine, ROWS), ROWS), :].astype(F32)
        self.y[k].wait_recv()
        return own + got + self.yrecv[k].astype(F32)

    def run(self, term):
        for k in range(NC):
            self.put(k, term(k))
            if k:
                self.middle(k - 1)
        self.middle(NC - 1)

    def drain(self):
        for k in range(NC):
            self.d[k].wait_send()
            self.y[k].wait_send()


REDUCE_SCRATCH = [
    pltpu.VMEM((BLOCK, D), F32),
    pltpu.VMEM((NC, 128, CW), BF),
    pltpu.VMEM((NC, 128, CW), BF),
    pltpu.VMEM((NC, ROWS, CW), BF),
    pltpu.VMEM((NC, ROWS, CW), BF),
] + [pltpu.SemaphoreType.DMA((NC,))] * 4


def tile_sends(tiles, land, send, recv, chip, core, t, start):
    s = 2 * chip + core
    for j in range(3):
        for u in range(2):
            slot, index = owner_of(2 * chip + u)
            target = (core * 3 + j) * 10 + slot
            k = j * 2 + u

            if start:

                @pl.when(target == s)
                def _():
                    pltpu.make_async_copy(tiles.at[j, u], land.at[index], recv.at[index]).start()

            @pl.when(target != s)
            def _():
                cp = remote(tiles.at[j, u], land.at[index], send.at[k], recv.at[index], target, t)
                if start:
                    cp.start()
                else:
                    cp.wait_send()


def tile_waits(tiles, land, send, recv, chip, core, t):
    slot = (2 * chip + core) % 10
    for r in range(SLOTS):
        here = chip < SERVED
        if r == 0:
            here = jnp.logical_and(here, slot < 4)

        @pl.when(here)
        def _():
            pltpu.make_async_copy(tiles.at[0, 0], land.at[r], recv.at[r]).wait()


def home_sends(tiles, land, send, recv, chip, core, t, start):
    s = 2 * chip + core
    slot = s % 10
    head = chip // PER_HEAD
    for r in range(SLOTS):
        here = chip < SERVED
        if r == 0:
            here = jnp.logical_and(here, slot < 4)
        tile = tile_of(slot, r)
        target = (tile // 2) * 2 + head // 3
        j, u = head % 3, tile % 2

        if start:

            @pl.when(jnp.logical_and(here, target == s))
            def _():
                pltpu.make_async_copy(tiles.at[r], land.at[j, u], recv.at[j, u]).start()

        @pl.when(jnp.logical_and(here, target != s))
        def _():
            cp = remote(tiles.at[r], land.at[j, u], send.at[r], recv.at[j, u], target, t)
            if start:
                cp.start()
            else:
                cp.wait_send()


def home_waits(tiles, land, recv):
    for j in range(3):
        for u in range(2):
            pltpu.make_async_copy(tiles.at[0], land.at[j, u], recv.at[j, u]).wait()


def weight_load(ref, buf, sem, core, width):
    return pltpu.make_async_copy(
        ref.at[:, pl.ds(pl.multiple_of(core * width, 128), width)], buf, sem
    )


def project_kernel(
    x_ref, gain_ref, wq_ref, wk_ref, wv_ref,
    normed_ref, q_ref, kv_ref,
    nbuf, wbuf, kvsrc, qsrc, wsem, nsend, nrecv, kvsend, kvrecv, fsend, qsend, qrecv, osem,
):
    chip, core, t = place()
    s = 2 * chip + core
    loads = [
        weight_load(ref, wbuf.at[k], wsem.at[k], core, 384)
        for k, ref in enumerate((wk_ref, wv_ref, wq_ref))
    ]
    for load in loads:
        load.start()
    x = x_ref[...]
    normed = (x * rms_scale(x) * gain_ref[...]).astype(BF)
    quad = QuadGather(nbuf, nsend, nrecv, chip, core, t)
    nbuf[pl.ds(pl.multiple_of(quad.mine, ROWS), ROWS), :] = normed
    greet_all(chip, core, t)
    quad.start()
    quad.finish()
    out = pltpu.make_async_copy(nbuf, normed_ref, osem)
    out.start()
    for k in range(2):
        loads[k].wait()
        value = matmul(nbuf[...], wbuf[k]).astype(BF)
        for j in range(3):
            kvsrc[j, :, k * 128 : (k + 1) * 128] = value[:, j * 128 : (j + 1) * 128]

    def kv_sends(start):
        for j in range(3):
            for p in range(PER_HEAD):
                w = (core * 3 + j) * PER_HEAD + p
                target = 2 * w + chip % 2

                if start:

                    @pl.when(target == s)
                    def _():
                        pltpu.make_async_copy(kvsrc.at[j], kv_ref.at[chip], kvrecv.at[chip]).start()

                @pl.when(target != s)
                def _():
                    cp = remote(
                        kvsrc.at[j], kv_ref.at[chip], kvsend.at[j * PER_HEAD + p],
                        kvrecv.at[chip], target, t,
                    )
                    if start:
                        cp.start()
                    else:
                        cp.wait_send()

    kv_sends(True)
    loads[2].wait()
    value = matmul(nbuf[...], wbuf[2]).astype(BF)
    for j in range(3):
        for u in range(2):
            qsrc[j, u] = value[u * 128 : (u + 1) * 128, j * 128 : (j + 1) * 128]
    tile_sends(qsrc, q_ref, qsend, qrecv, chip, core, t, True)

    @pl.when(chip < SERVED)
    def _():
        def forward(o):
            source = lax.rem((chip // 2 + o) * 2 + core, CHIPS)
            view = kv_ref.at[source]
            return source, remote(view, view, fsend.at[o], kvrecv.at[source], s + 1 - 2 * core, t)

        def take(o, carry):
            source, cp = forward(o)
            pltpu.make_async_copy(kvsrc.at[0], kv_ref.at[source], kvrecv.at[source]).wait()
            cp.start()
            return carry

        lax.fori_loop(0, CHIPS // 2, take, 0)

        def finish(o, carry):
            source = 2 * o + 1 - core
            pltpu.make_async_copy(kvsrc.at[0], kv_ref.at[source], kvrecv.at[source]).wait()
            forward(o)[1].wait_send()
            return carry

        lax.fori_loop(0, CHIPS // 2, finish, 0)

    tile_waits(qsrc, q_ref, qsend, qrecv, chip, core, t)
    kv_sends(False)
    tile_sends(qsrc, q_ref, qsend, qrecv, chip, core, t, False)
    quad.drain()
    out.wait()


VM = pl.BlockSpec(memory_space=pltpu.VMEM)
SM = pl.BlockSpec(memory_space=pltpu.SMEM)
ANY = pl.BlockSpec(memory_space=pl.ANY)


def shape(dims, dtype):
    return jax.ShapeDtypeStruct(dims, dtype)


def project(x, gain, wq, wk, wv):
    return pl.pallas_call(
        project_kernel,
        name="project",
        out_shape=(
            shape((BLOCK, D), BF),
            shape((SLOTS, TILE, 128), BF),
            shape((CHIPS, BLOCK, 256), BF),
        ),
        in_specs=[VM, VM, ANY, ANY, ANY],
        out_specs=(ANY, ANY, ANY),
        scratch_shapes=[
            pltpu.VMEM((BLOCK, D), BF),
            pltpu.VMEM((3, D, 384), BF),
            pltpu.VMEM((3, BLOCK, 256), BF),
            pltpu.VMEM((3, 2, TILE, 128), BF),
            pltpu.SemaphoreType.DMA((3,)),
            *GATHER_SEMS,
            pltpu.SemaphoreType.DMA((15,)),
            pltpu.SemaphoreType.DMA((CHIPS,)),
            pltpu.SemaphoreType.DMA((CHIPS // 2,)),
            pltpu.SemaphoreType.DMA((6,)),
            pltpu.SemaphoreType.DMA((SLOTS,)),
            pltpu.SemaphoreType.DMA,
        ],
        compiler_params=pltpu.CompilerParams(
            collective_id=0, has_side_effects=True, vmem_limit_bytes=VMEM_LIMIT
        ),
    )(x, gain, wq, wk, wv)


def eye():
    row = lax.broadcasted_iota(jnp.int32, (128, 128), 0)
    col = lax.broadcasted_iota(jnp.int32, (128, 128), 1)
    return jnp.where(row == col, 1.0, 0.0).astype(BF)


def both_maps(q_t):
    top = lax.broadcasted_iota(jnp.int32, q_t.shape, 0) < 64
    return jnp.concatenate([jnp.where(top, q_t, 0.0), jnp.where(top, 0.0, q_t)], axis=1)


def key_mask(start, count, tile, width):
    key = start + lax.broadcasted_iota(jnp.int32, (count, width), 0)
    query = tile * TILE + lax.broadcasted_iota(jnp.int32, (count, width), 1) % TILE
    return key <= query


def group_norm(parts, lam):
    first, second = parts[:, :TILE], parts[:, TILE:]
    differ = first - lam * second
    rms = rms_scale(differ, 0)
    return rms, differ * rms


def attend_kernel(
    tiles_ref, lam_ref, gain_ref, q_ref, kv_ref, mixed_ref, parts_ref, log_ref, v_t, kmax, acc, total
):
    keys = CHIPS * BLOCK
    lam = lam_ref[0]

    @pl.when(tiles_ref[SLOTS - 1] >= 0)
    def _():
        unit = eye()

        def flip(b, best):
            block = kv_ref[pl.ds(b * KB, KB), :]
            v_t[:, pl.ds(pl.multiple_of(b * KB, KB), KB)] = matmul_t(unit, block[:, 128:]).astype(BF)
            k_t = matmul_t(unit, block[:, :128])
            square = k_t * k_t
            return (
                jnp.maximum(best[0], jnp.sum(square[:64], axis=0, keepdims=True)),
                jnp.maximum(best[1], jnp.sum(square[64:], axis=0, keepdims=True)),
            )

        zero = jnp.zeros((1, KB), F32)
        best = lax.fori_loop(0, keys // KB, flip, (zero, zero))
        for m in range(2):
            kmax[m] = jnp.max(best[m])

    for r in range(SLOTS):
        tile = tiles_ref[r]

        @pl.when(tile >= 0)
        def _():
            q_t = q_ref[r].astype(F32).T
            square = q_t * q_t
            bound = SCORE * jnp.concatenate(
                [
                    jnp.sqrt(jnp.sum(square[:64], axis=0, keepdims=True) * kmax[0]),
                    jnp.sqrt(jnp.sum(square[64:], axis=0, keepdims=True) * kmax[1]),
                ],
                axis=1,
            )
            q_both = both_maps(q_t).astype(BF)
            acc[...] = jnp.zeros_like(acc)
            total[...] = jnp.zeros_like(total)

            def step(b, masked):
                start = pl.multiple_of(b * KB, KB)
                score = matmul(kv_ref[pl.ds(start, KB), :128], q_both)
                prob = jnp.exp2(score * SCORE - bound)
                if masked:
                    prob = jnp.where(key_mask(start, KB, tile, 2 * TILE), prob, 0.0)
                total[...] += jnp.sum(prob, axis=0, keepdims=True)
                acc[...] += matmul(v_t[:, pl.ds(start, KB)], prob.astype(BF))

            full = tile * TILE // KB

            def body(b, carry):
                step(b, False)
                return carry

            lax.fori_loop(0, full, body, 0)
            step(full, True)
            parts = acc[...] / total[...]
            parts_ref[r] = parts
            log_ref[r] = bound + jnp.log(total[...]) * LOG2E
            rms, hat = group_norm(parts, lam)
            mixed_ref[r] = (hat * gain_ref[...] * OUT_SCALE).T.astype(BF)


def attend(tiles, lam, gain, q, kv):
    return pl.pallas_call(
        attend_kernel,
        name="attend",
        out_shape=(
            shape((SLOTS, TILE, 128), BF),
            shape((SLOTS, 128, 2 * TILE), F32),
            shape((SLOTS, 1, 2 * TILE), F32),
        ),
        in_specs=[SM, SM, VM, VM, VM],
        out_specs=(VM, VM, VM),
        scratch_shapes=[
            pltpu.VMEM((128, CHIPS * BLOCK), BF),
            pltpu.SMEM((2,), F32),
            pltpu.VMEM((128, 2 * TILE), F32),
            pltpu.VMEM((1, 2 * TILE), F32),
        ],
        compiler_params=pltpu.CompilerParams(vmem_limit_bytes=VMEM_LIMIT),
        cost_estimate=pl.CostEstimate(
            flops=6 * 10**9, bytes_accessed=6 * 2**20, transcendentals=7 * 10**6
        ),
    )(tiles, lam, gain, q, kv)


def middle_kernel(
    x_ref, cot_ref, mask_ref, gain_ref, tiles_ref, wo_ref, wg_ref, wu_ref, wd_ref,
    out_ref, dres_ref, gainpart_ref, ffn_ref, dout_ref, dgate_ref, dup_ref, hid_ref, mix_ref,
    dresall_ref, dmix_ref,
    land, wo, wg, wu, wd, fbuf, obuf, rbuf, dms, *rest,
):
    chip, core, t = place()
    reduces = [rest[9 * k : 9 * k + 9] for k in range(3)]
    gathers = [rest[27 + 2 * k : 29 + 2 * k] for k in range(3)]
    wsem, hsend, hrecv, tsend, trecv, osem = rest[33:]
    loads = [
        weight_load(wo_ref, wo, wsem.at[0], core, 384),
        weight_load(wg_ref, wg, wsem.at[1], core, 1024),
        weight_load(wu_ref, wu, wsem.at[2], core, 1024),
        weight_load(wd_ref, wd, wsem.at[3], core, 1024),
    ]
    for load in loads:
        load.start()
    gather_f = QuadGather(fbuf, *gathers[0], chip, core, t)
    gather_o = QuadGather(obuf, *gathers[1], chip, core, t)
    gather_r = QuadGather(rbuf, *gathers[2], chip, core, t)
    mine = pl.ds(pl.multiple_of(gather_f.mine, ROWS), ROWS)
    dout = cot_ref[...] * mask_ref[...]
    obuf[mine, :] = dout.astype(BF)
    greet_all(chip, core, t)
    home_sends(tiles_ref, land, hsend, hrecv, chip, core, t, True)
    gather_o.start()
    loads[0].wait()
    home_waits(tiles_ref, land, hrecv)
    for j in range(3):
        for u in range(2):
            mix_ref[u * 128 : (u + 1) * 128, j * 128 : (j + 1) * 128] = land[j, u]

    red = QuadReduce(*reduces[0], chip, core, t)
    red.run(lambda k: matmul_t(mix_ref[...], wo[k * CW : (k + 1) * CW, :]))
    resid = x_ref[...] + jnp.concatenate([red.result(k) for k in range(NC)], axis=1)
    ffn_rms = rms_scale(resid)
    ffn_hat = resid * ffn_rms
    fbuf[mine, :] = (ffn_hat * gain_ref[...]).astype(BF)
    gather_f.start()
    gather_o.finish()
    gather_f.finish()
    for load in loads[1:]:
        load.wait()

    def hidden_step(n, carry):
        cols = pl.ds(pl.multiple_of(n * 256, 256), 256)
        gate = matmul(fbuf[...], wg[:, cols])
        up = matmul(fbuf[...], wu[:, cols])
        d_hidden = matmul(obuf[...], wd[:, cols])
        sig = 1.0 / (1.0 + jnp.exp(-gate))
        silu = gate * sig
        hid_ref[:, cols] = (silu * up).astype(BF)
        dgate_ref[:, cols] = (d_hidden * up * sig * (1.0 + gate * (1.0 - sig))).astype(BF)
        dup_ref[:, cols] = (d_hidden * silu).astype(BF)
        return carry

    lax.fori_loop(0, 4, hidden_step, 0)
    red2 = QuadReduce(*reduces[1], chip, core, t)
    red2.run(
        lambda k: matmul_t(dgate_ref[...], wg[k * CW : (k + 1) * CW, :])
        + matmul_t(dup_ref[...], wu[k * CW : (k + 1) * CW, :])
    )
    red3 = QuadReduce(*reduces[2], chip, core, t)
    d_ffn = jnp.concatenate([red2.result(k) for k in range(NC)], axis=1)
    gainpart_ref[...] = jnp.sum(d_ffn * ffn_hat, axis=0, keepdims=True)
    d_resid = dout + norm_back(d_ffn, gain_ref[...], ffn_rms, ffn_hat)
    dres_ref[...] = d_resid
    rbuf[mine, :] = d_resid.astype(BF)
    gather_r.start()
    red3.run(lambda k: matmul_t(hid_ref[...], wd[k * CW : (k + 1) * CW, :]))
    gather_r.finish()
    d_mixed = matmul(rbuf[...], wo[...]).astype(BF)
    for j in range(3):
        for u in range(2):
            dms[j, u] = d_mixed[u * 128 : (u + 1) * 128, j * 128 : (j + 1) * 128]
    tile_sends(dms, dmix_ref, tsend, trecv, chip, core, t, True)
    saves = [
        pltpu.make_async_copy(fbuf, ffn_ref, osem.at[0]),
        pltpu.make_async_copy(obuf, dout_ref, osem.at[1]),
        pltpu.make_async_copy(rbuf, dresall_ref, osem.at[2]),
    ]
    for save in saves:
        save.start()
    out_ref[...] = resid + jnp.concatenate([red3.result(k) for k in range(NC)], axis=1)
    tile_waits(dms, dmix_ref, tsend, trecv, chip, core, t)
    tile_sends(dms, dmix_ref, tsend, trecv, chip, core, t, False)
    home_sends(tiles_ref, land, hsend, hrecv, chip, core, t, False)
    for gather in (gather_f, gather_o, gather_r):
        gather.drain()
    for reduce in (red, red2, red3):
        reduce.drain()
    for save in saves:
        save.wait()


def middle(x, cot, mask, gain, tiles, wo, wg, wu, wd):
    return pl.pallas_call(
        middle_kernel,
        name="middle",
        out_shape=(
            shape((ROWS, D), F32),
            shape((ROWS, D), F32),
            shape((1, D), F32),
            shape((BLOCK, D), BF),
            shape((BLOCK, D), BF),
            shape((BLOCK, 1024), BF),
            shape((BLOCK, 1024), BF),
            shape((BLOCK, 1024), BF),
            shape((BLOCK, 384), BF),
            shape((BLOCK, D), BF),
            shape((SLOTS, TILE, 128), BF),
        ),
        in_specs=[VM, VM, VM, VM, ANY, ANY, ANY, ANY, ANY],
        out_specs=(VM, VM, VM, ANY, ANY, VM, VM, VM, VM, ANY, ANY),
        scratch_shapes=[
            pltpu.VMEM((3, 2, TILE, 128), BF),
            pltpu.VMEM((D, 384), BF),
            pltpu.VMEM((D, 1024), BF),
            pltpu.VMEM((D, 1024), BF),
            pltpu.VMEM((D, 1024), BF),
            pltpu.VMEM((BLOCK, D), BF),
            pltpu.VMEM((BLOCK, D), BF),
            pltpu.VMEM((BLOCK, D), BF),
            pltpu.VMEM((3, 2, TILE, 128), BF),
            *(REDUCE_SCRATCH * 3),
            *(GATHER_SEMS * 3),
            pltpu.SemaphoreType.DMA((4,)),
            pltpu.SemaphoreType.DMA((SLOTS,)),
            pltpu.SemaphoreType.DMA((3, 2)),
            pltpu.SemaphoreType.DMA((6,)),
            pltpu.SemaphoreType.DMA((SLOTS,)),
            pltpu.SemaphoreType.DMA((3,)),
        ],
        compiler_params=pltpu.CompilerParams(
            collective_id=1, has_side_effects=True, vmem_limit_bytes=VMEM_LIMIT
        ),
    )(x, cot, mask, gain, tiles, wo, wg, wu, wd)


BB = 256


def attend_back_kernel(
    tiles_ref, lam_ref, gain_ref, q_ref, kv_ref, dmix_ref, parts_ref, log_ref,
    dq_ref, dkv_ref, sub_ref, dlam_ref,
    k_t, acc, dq_acc, sub_acc, lam_acc,
):
    keys = CHIPS * BLOCK
    lam = lam_ref[0]
    sub_acc[...] = jnp.zeros_like(sub_acc)
    lam_acc[...] = jnp.zeros_like(lam_acc)

    @pl.when(tiles_ref[SLOTS - 1] >= 0)
    def _():
        unit = eye()

        def flip(b, carry):
            rows = pl.ds(pl.multiple_of(b * KB, KB), KB)
            k_t[:, rows] = matmul_t(unit, kv_ref[rows, :128]).astype(BF)
            acc[rows, :] = jnp.zeros((KB, 256), F32)
            return carry

        lax.fori_loop(0, keys // KB, flip, 0)

    for r in range(SLOTS):
        tile = tiles_ref[r]

        @pl.when(tile >= 0)
        def _():
            q_t = q_ref[r].astype(F32).T
            q_both_t = both_maps(q_t).astype(BF)
            q = q_ref[r].astype(F32)
            left = lax.broadcasted_iota(jnp.int32, q.shape, 1) < 64
            q_both = jnp.concatenate(
                [jnp.where(left, q, 0.0), jnp.where(left, 0.0, q)], axis=0
            ).astype(BF)
            parts = parts_ref[r]
            first, second = parts[:, :TILE], parts[:, TILE:]
            rms, hat = group_norm(parts, lam)
            e_t = dmix_ref[r].astype(F32).T * OUT_SCALE
            sub_acc[...] += jnp.sum(e_t * hat, axis=1, keepdims=True)
            d_differ = norm_back(e_t, gain_ref[...], rms, hat, 0).astype(BF)
            d_wide = d_differ.astype(F32)
            d_rows = d_wide.T.astype(BF)
            second_dot = jnp.sum(d_wide * second, axis=0, keepdims=True)
            lam_acc[...] -= second_dot
            first_delta = jnp.sum(d_wide * first, axis=0, keepdims=True)
            second_delta = -lam * second_dot
            log_total = log_ref[r]
            dq_acc[...] = jnp.zeros_like(dq_acc)

            def step(b, masked):
                start = pl.multiple_of(b * BB, BB)
                rows = pl.ds(start, BB)
                block = kv_ref[rows, :]
                score = matmul(block[:, :128], q_both_t)
                prob = jnp.exp2(score * SCORE - log_total)
                if masked:
                    prob = jnp.where(key_mask(start, BB, tile, 2 * TILE), prob, 0.0)
                upper = matmul(block[:, 128:], d_differ)
                p1, p2 = prob[:, :TILE], prob[:, TILE:]
                ds = jnp.concatenate(
                    [p1 * (upper - first_delta), p2 * (-lam * upper - second_delta)], axis=1
                ).astype(BF)
                both = (p1 - lam * p2).astype(BF)
                acc[rows, :128] += matmul(ds, q_both)
                acc[rows, 128:] += matmul(both, d_rows)
                dq_acc[...] += matmul(k_t[:, rows], ds)

            full = tile * TILE // BB

            def body(b, carry):
                step(b, False)
                return carry

            lax.fori_loop(0, full, body, 0)
            step(full, True)
            dq_t = jnp.concatenate([dq_acc[:64, :TILE], dq_acc[64:, TILE:]], axis=0)
            dq_ref[r] = (dq_t * 0.125).T.astype(BF)

    @pl.when(tiles_ref[SLOTS - 1] >= 0)
    def _():
        def save(b, carry):
            rows = pl.ds(pl.multiple_of(b * KB, KB), KB)
            dkv_ref[rows, :128] = (acc[rows, :128] * 0.125).astype(BF)
            dkv_ref[rows, 128:] = acc[rows, 128:].astype(BF)
            return carry

        lax.fori_loop(0, keys // KB, save, 0)

    sub_ref[...] = sub_acc[...]
    dlam_ref[...] = jnp.sum(lam_acc[...], axis=1, keepdims=True)


def attend_back(tiles, lam, gain, q, kv, dmix, parts, logs):
    return pl.pallas_call(
        attend_back_kernel,
        name="attend_back",
        out_shape=(
            shape((SLOTS, TILE, 128), BF),
            shape((CHIPS * BLOCK, 256), BF),
            shape((128, 1), F32),
            shape((1, 1), F32),
        ),
        in_specs=[SM, SM] + [VM] * 6,
        out_specs=(VM, VM, VM, VM),
        scratch_shapes=[
            pltpu.VMEM((128, CHIPS * BLOCK), BF),
            pltpu.VMEM((CHIPS * BLOCK, 256), F32),
            pltpu.VMEM((128, 2 * TILE), F32),
            pltpu.VMEM((128, 1), F32),
            pltpu.VMEM((1, TILE), F32),
        ],
        compiler_params=pltpu.CompilerParams(vmem_limit_bytes=VMEM_LIMIT),
        cost_estimate=pl.CostEstimate(
            flops=2 * 10**10, bytes_accessed=10 * 2**20, transcendentals=7 * 10**6
        ),
    )(tiles, lam, gain, q, kv, dmix, parts, logs)


def finish_kernel(
    x_ref, gain_ref, dres_ref, dq_ref, dkv_ref, wq_ref, wk_ref, wv_ref,
    grad_ref, gainpart_ref, dqkv_ref,
    wbuf, sib, both, home, land, *rest,
):
    chip, core, t = place()
    s = 2 * chip + core
    reduce = rest[:9]
    wsem, dsend, drecv, ksend, krecv, hsend, hrecv = rest[9:]
    loads = [
        weight_load(ref, wbuf.at[k], wsem.at[k], core, 384)
        for k, ref in enumerate((wq_ref, wk_ref, wv_ref))
    ]
    for load in loads:
        load.start()
    greet_all(chip, core, t)
    head = chip // PER_HEAD
    half = CHIPS // 2

    def to_sibling(o):
        return remote(
            dkv_ref.at[2 * o + 1 - core], sib.at[o], dsend.at[o], drecv.at[o], s + 1 - 2 * core, t
        )

    def order(o):
        return lax.rem(chip // 2 + 1 + o, half)

    def to_home(o, start):
        block = 2 * o + core
        target = 2 * block + head // 3
        spot = (head % 3) * PER_HEAD + chip % PER_HEAD

        if start:

            @pl.when(target == s)
            def _():
                pltpu.make_async_copy(both.at[o], home.at[spot], krecv.at[spot]).start()

        @pl.when(target != s)
        def _():
            cp = remote(both.at[o], home.at[spot], ksend.at[o], krecv.at[spot], target, t)
            if start:
                cp.start()
            else:
                cp.wait_send()

    @pl.when(chip < SERVED)
    def _():
        def first(k, carry):
            to_sibling(order(k)).start()
            return carry

        lax.fori_loop(0, half, first, 0)

    home_sends(dq_ref, land, hsend, hrecv, chip, core, t, True)

    @pl.when(chip < SERVED)
    def _():
        def second(k, carry):
            o = order(k)
            to_sibling(o).wait_recv()
            both[o] = (dkv_ref[2 * o + core].astype(F32) + sib[o].astype(F32)).astype(BF)
            to_home(o, True)
            return carry

        lax.fori_loop(0, half, second, 0)

    for load in loads:
        load.wait()
    home_waits(dq_ref, land, hrecv)
    for j in range(3):
        for u in range(2):
            dqkv_ref[u * 128 : (u + 1) * 128, j * 128 : (j + 1) * 128] = land[j, u]
    for j in range(3):
        total = jnp.zeros((BLOCK, 256), F32)
        for p in range(PER_HEAD):
            spot = j * PER_HEAD + p
            pltpu.make_async_copy(both.at[0], home.at[spot], krecv.at[spot]).wait()
            total = total + home[spot].astype(F32)
        dqkv_ref[:, 384 + j * 128 : 512 + j * 128] = total[:, :128].astype(BF)
        dqkv_ref[:, 768 + j * 128 : 896 + j * 128] = total[:, 128:].astype(BF)
    red = QuadReduce(*reduce, chip, core, t)

    def term(k):
        rows = slice(k * CW, (k + 1) * CW)
        return (
            matmul_t(dqkv_ref[:, :384], wbuf[0, rows, :])
            + matmul_t(dqkv_ref[:, 384:768], wbuf[1, rows, :])
            + matmul_t(dqkv_ref[:, 768:], wbuf[2, rows, :])
        )

    red.run(term)
    x = x_ref[...]
    rms = rms_scale(x)
    hat = x * rms
    d_normed = jnp.concatenate([red.result(k) for k in range(NC)], axis=1)
    gainpart_ref[...] = jnp.sum(d_normed * hat, axis=0, keepdims=True)
    grad_ref[...] = dres_ref[...] + norm_back(d_normed, gain_ref[...], rms, hat)
    red.drain()
    home_sends(dq_ref, land, hsend, hrecv, chip, core, t, False)

    @pl.when(chip < SERVED)
    def _():
        def last(o, carry):
            to_sibling(o).wait_send()
            to_home(o, False)
            return carry

        lax.fori_loop(0, half, last, 0)


def finish(x, gain, dres, dq, dkv, wq, wk, wv):
    return pl.pallas_call(
        finish_kernel,
        name="finish",
        out_shape=(shape((ROWS, D), F32), shape((1, D), F32), shape((BLOCK, 1152), BF)),
        in_specs=[VM, VM, VM, ANY, VM, ANY, ANY, ANY],
        out_specs=(VM, VM, VM),
        scratch_shapes=[
            pltpu.VMEM((3, D, 384), BF),
            pltpu.VMEM((CHIPS // 2, BLOCK, 256), BF),
            pltpu.VMEM((CHIPS // 2, BLOCK, 256), BF),
            pltpu.VMEM((3 * PER_HEAD, BLOCK, 256), BF),
            pltpu.VMEM((3, 2, TILE, 128), BF),
            *REDUCE_SCRATCH,
            pltpu.SemaphoreType.DMA((3,)),
            pltpu.SemaphoreType.DMA((CHIPS // 2,)),
            pltpu.SemaphoreType.DMA((CHIPS // 2,)),
            pltpu.SemaphoreType.DMA((CHIPS // 2,)),
            pltpu.SemaphoreType.DMA((3 * PER_HEAD,)),
            pltpu.SemaphoreType.DMA((SLOTS,)),
            pltpu.SemaphoreType.DMA((3, 2)),
        ],
        compiler_params=pltpu.CompilerParams(
            collective_id=2, has_side_effects=True, vmem_limit_bytes=VMEM_LIMIT
        ),
    )(x, gain, dres, dq, dkv, wq, wk, wv)


def row_product(left, right):
    return lax.dot_general(left, right, (((0,), (0,)), ((), ())), preferred_element_type=F32)


def weight_grad(left, right, core):
    part = row_product(left, right).astype(BF)
    groups = [[2 * i + c for i in range(CHIPS)] for c in range(2)]
    rows = lax.psum_scatter(
        part, "seq", scatter_dimension=0, axis_index_groups=groups, tiled=True
    ).astype(F32)
    near = lax.dynamic_slice_in_dim(rows, core * 24, 24, 0)
    away = lax.dynamic_slice_in_dim(rows, (1 - core) * 24, 24, 0)
    got = lax.ppermute(away, "seq", [(i, i ^ 1) for i in range(2 * CHIPS)])
    even = jnp.concatenate([near, got], axis=1)
    odd = jnp.concatenate([got, near], axis=1)
    return jnp.where(core == 0, even, odd)


def on_device(
    hidden_in, cotangent, needle_mask, attn_gain, lambdas, subln_gain, ffn_gain,
    weight_query, weight_key, weight_value, weight_out, weight_gate, weight_up, weight_down,
):
    chip, core, t = place()
    first_exp = jnp.exp(jnp.sum(lambdas[0] * lambdas[1], axis=-1))
    second_exp = jnp.exp(jnp.sum(lambdas[2] * lambdas[3], axis=-1))
    lambda_all = first_exp - second_exp + LAMBDA_INIT
    head = jnp.minimum(t * 6 + chip // PER_HEAD, 11)
    lam = lax.dynamic_slice_in_dim(lambda_all, head, 1)
    slot = (2 * chip + core) % 10
    served = chip < SERVED
    tiles = jnp.stack(
        [
            jnp.where(served if r else jnp.logical_and(served, slot < 4), tile_of(slot, r), -1)
            for r in range(SLOTS)
        ]
    ).astype(jnp.int32)
    attn_row = attn_gain.reshape(1, D)
    ffn_row = ffn_gain.reshape(1, D)
    sub_col = subln_gain.reshape(128, 1)
    mask = needle_mask.astype(F32).reshape(ROWS, 1)

    normed_all, q, kv = project(hidden_in, attn_row, weight_query, weight_key, weight_value)
    kv = kv.reshape(CHIPS * BLOCK, 256)
    mixed_tiles, parts, logs = attend(tiles, lam, sub_col, q, kv)
    (
        output, d_resid, ffn_part, ffn_all, dout_all, d_gate, d_up, hidden, mixed, dres_all, dmix,
    ) = middle(
        hidden_in, cotangent, mask, ffn_row, mixed_tiles, weight_out, weight_gate, weight_up, weight_down
    )
    dq, dkv, sub_part, dlam = attend_back(tiles, lam, sub_col, q, kv, dmix, parts, logs)
    grad_input, attn_part, dqkv = finish(
        hidden_in, attn_row, d_resid, dq, dkv.reshape(CHIPS, BLOCK, 256),
        weight_query, weight_key, weight_value,
    )
    here = jnp.logical_and(jnp.arange(12) == head, served)
    dlam_all = jnp.where(here, dlam[0, 0], 0.0)
    gains = lax.psum(
        jnp.concatenate([attn_part[0], ffn_part[0], sub_part[:, 0], dlam_all]), ("seq", "tp")
    )
    d_lambda = gains[2 * D + 128 :]
    grad_lambdas = jnp.stack(
        [
            (d_lambda * first_exp)[:, None] * lambdas[1],
            (d_lambda * first_exp)[:, None] * lambdas[0],
            -(d_lambda * second_exp)[:, None] * lambdas[3],
            -(d_lambda * second_exp)[:, None] * lambdas[2],
        ]
    )
    return (
        output,
        grad_input,
        weight_grad(normed_all, dqkv[:, :384], core),
        weight_grad(normed_all, dqkv[:, 384:768], core),
        weight_grad(normed_all, dqkv[:, 768:], core),
        weight_grad(dres_all, mixed, core),
        weight_grad(ffn_all, d_gate, core),
        weight_grad(ffn_all, d_up, core),
        weight_grad(dout_all, hidden, core),
        gains[:D],
        grad_lambdas,
        gains[2 * D : 2 * D + 128],
        gains[D : 2 * D],
    )


def solution(mesh):
    split = P(None, "tp")
    rows = P(("seq", "tp"), None)
    both = P("seq", "tp")
    return jax.shard_map(
        on_device,
        mesh=mesh,
        in_specs=(rows, rows, P(("seq", "tp"))) + (P(),) * 4 + (split,) * 7,
        out_specs=(rows, rows) + (both,) * 7 + (P(),) * 4,
        check_vma=False,
    )
```

```python
import math

import jax
import jax.numpy as jnp
from jax import lax
from jax.experimental import pallas as pl
from jax.experimental.pallas import tpu as pltpu
from jax.sharding import PartitionSpec as P

MESH = pl.DeviceIdType.MESH
BF = jnp.bfloat16
F32 = jnp.float32
EPS = 1e-06
LAMBDA_INIT = 0.8 - 0.6 * math.exp(-3.6)
OUT_SCALE = 1.0 - LAMBDA_INIT
D = 1536
CHIPS = 32
SERVED = 30
PER_HEAD = 5
ROWS = 64
BLOCK = 256
TILE = 128
SLOTS = 7
KB = 512
LOG2E = 1.4426950408889634
SCORE = 0.125 * LOG2E
VMEM_LIMIT = 60 * 2**20


def place():
    s = lax.axis_index("seq")
    return s // 2, s % 2, lax.axis_index("tp")


def owner_of(tile):
    step = (tile - 4) // 10
    pos = (tile - 4) % 10
    slot = jnp.where(step % 2 == 0, pos, 9 - pos)
    early = tile < 4
    return jnp.where(early, tile, slot), jnp.where(early, 0, step + 1)


def tile_of(slot, r):
    if r == 0:
        return slot
    return 4 + 10 * (r - 1) + (slot if (r - 1) % 2 == 0 else 9 - slot)


def matmul(a, b):
    return jnp.dot(a, b, preferred_element_type=F32)


def matmul_t(a, b):
    return lax.dot_general(a, b, (((1,), (1,)), ((), ())), preferred_element_type=F32)


def rms_scale(values, axis=-1):
    return lax.rsqrt(jnp.mean(values * values, axis=axis, keepdims=True) + EPS)


def norm_back(grad_normed, gain, rms, hat, axis=-1):
    scaled = grad_normed * gain
    return rms * (scaled - hat * jnp.mean(scaled * hat, axis=axis, keepdims=True))


def greet_all(chip, core, t):
    barrier = pltpu.get_barrier_semaphore()
    s = 2 * chip + core

    def greet(o, carry):
        pl.semaphore_signal(
            barrier, inc=1, device_id=(lax.rem(s + o, 2 * CHIPS), t), device_id_type=MESH
        )
        return carry

    lax.fori_loop(1, 2 * CHIPS, greet, 0)
    pl.semaphore_signal(barrier, inc=1, device_id=(s, 1 - t), device_id_type=MESH)
    pl.semaphore_wait(barrier, 2 * CHIPS)


def remote(src, dst, send_sem, recv_sem, s, t):
    return pltpu.make_async_remote_copy(
        src_ref=src,
        dst_ref=dst,
        send_sem=send_sem,
        recv_sem=recv_sem,
        device_id=(s, t),
        device_id_type=MESH,
    )


def rows_at(ref, start, count):
    return ref.at[pl.ds(pl.multiple_of(start, ROWS), count)]


class QuadGather:
    def __init__(self, buf, send, recv, chip, core, t):
        self.buf, self.send, self.recv = buf, send, recv
        self.chip, self.core, self.t = chip, core, t
        mine = core * 128 + t * ROWS
        self.mine = mine
        self.near = core * 128 + (1 - t) * ROWS
        sib = (2 * chip + 1 - core, t)
        self.to_near = self.copy(mine, 0, (2 * chip + core, 1 - t))
        self.to_sib = self.copy(mine, 1, sib)
        self.forward = self.copy(self.near, 2, sib)

    def copy(self, row, k, target):
        view = rows_at(self.buf, row, ROWS)
        return remote(view, view, self.send.at[k], self.recv.at[k], *target)

    def start(self):
        self.to_near.start()
        self.to_sib.start()

    def finish(self):
        self.to_near.wait_recv()
        self.forward.start()
        self.to_sib.wait_recv()
        self.forward.wait_recv()

    def drain(self):
        self.to_near.wait_send()
        self.to_sib.wait_send()
        self.forward.wait_send()


class RingGather:
    def __init__(self, pieces, land, send, recv, axis, chip, core, t):
        at = chip % 4 if axis == "x" else chip // 8
        self.local = pltpu.make_async_copy(pieces(at), land.at[at], recv.at[at])
        self.copies = []
        for k in (1, 3, 2):
            if axis == "x":
                peer, chip_to = (at + k) % 4, chip - at + (at + k) % 4
            else:
                peer, chip_to = (at + k) % 4, (chip + 8 * k) % CHIPS
            self.copies.append(
                remote(pieces(peer), land.at[at], send.at[k - 1], recv.at[at], 2 * chip_to + core, t)
            )
        self.waits = [
            pltpu.make_async_copy(pieces(at), land.at[k], recv.at[k]) for k in range(4)
        ]

    def start(self):
        self.local.start()
        for cp in self.copies:
            cp.start()

    def finish(self):
        for cp in self.waits:
            cp.wait()

    def drain(self):
        for cp in self.copies:
            cp.wait_send()


RING_SEMS = [pltpu.SemaphoreType.DMA((3,)), pltpu.SemaphoreType.DMA((4,))]


def greet_ring(chip, core, t):
    barrier = pltpu.get_barrier_semaphore()
    x = chip % 4
    for k in (1, 2, 3):
        for peer in ((chip + 8 * k) % CHIPS, chip - x + (x + k) % 4):
            pl.semaphore_signal(
                barrier, inc=1, device_id=(2 * peer + core, t), device_id_type=MESH
            )
    pl.semaphore_wait(barrier, 6)


def block_grad(dst, start, left, right, step):
    width = right.shape[1]

    def one(m, carry):
        cols = pl.ds(pl.multiple_of(m * step, 128), step)
        part = left[:, :, cols].reshape(4 * BLOCK, step)
        dst[cols, start : start + width] = lax.dot_general(
            part, right, (((0,), (0,)), ((), ())), preferred_element_type=F32
        ).astype(BF)
        return carry

    lax.fori_loop(0, left.shape[2] // step, one, 0)


CHUNK = 48


class Scatter:
    def __init__(self, part, land, send, recv, count, first, spot, chip, core, t):
        self.part, self.land, self.send, self.recv = part, land, send, recv
        self.count, self.first, self.spot = count, first, spot
        self.chip, self.core, self.t = chip, core, t

    def source(self, i):
        return self.part.at[pl.ds(pl.multiple_of(i * CHUNK, 16), CHUNK)]

    def each(self, start):
        def one(o, carry):
            i = lax.rem(self.chip + 1 + 3 * o, self.count)
            owner = self.first + i
            cp = remote(
                self.source(i), self.land.at[self.spot], self.send.at[i], self.recv.at[self.spot],
                2 * owner + self.core, self.t,
            )
            if start:

                @pl.when(owner == self.chip)
                def _():
                    pltpu.make_async_copy(
                        self.source(i), self.land.at[self.spot], self.recv.at[self.spot]
                    ).start()

            @pl.when(owner != self.chip)
            def _():
                if start:
                    cp.start()
                else:
                    cp.wait_send()

            return carry

        lax.fori_loop(0, self.count, one, 0)

    def wait(self):
        def one(k, carry):
            pltpu.make_async_copy(self.source(0), self.land.at[k], self.recv.at[k]).wait()
            return carry

        lax.fori_loop(0, self.count, one, 0)

    def total(self, b, cols):
        def one(k, carry):
            return carry + self.land[8 * b + k, :, cols].astype(F32)

        return lax.fori_loop(0, 8, one, jnp.zeros((CHUNK, cols.stop - cols.start), F32))


def scatter_sems(count):
    return [pltpu.SemaphoreType.DMA((count,)), pltpu.SemaphoreType.DMA((count,))]


GATHER_SEMS = [pltpu.SemaphoreType.DMA((3,)), pltpu.SemaphoreType.DMA((3,))]
CW = 512
NC = D // CW


class QuadReduce:
    def __init__(self, part, dsend, drecv, ysend, yrecv, ds, dr, ys, yr, chip, core, t):
        self.part, self.dsend, self.drecv = part, dsend, drecv
        self.ysend, self.yrecv = ysend, yrecv
        self.core, self.t = core, t
        self.d = [
            remote(dsend.at[k], drecv.at[k], ds.at[k], dr.at[k], 2 * chip + 1 - core, t)
            for k in range(NC)
        ]
        self.y = [
            remote(ysend.at[k], yrecv.at[k], ys.at[k], yr.at[k], 2 * chip + core, 1 - t)
            for k in range(NC)
        ]

    def rows(self, start, count, k):
        return self.part[pl.ds(pl.multiple_of(start, ROWS), count), k * CW : (k + 1) * CW]

    def put(self, k, value):
        self.part[:, k * CW : (k + 1) * CW] = value
        self.dsend[k] = self.rows((1 - self.core) * 128, 128, k).astype(BF)
        self.d[k].start()

    def middle(self, k):
        self.d[k].wait_recv()
        near = (1 - self.t) * ROWS
        far = self.rows(self.core * 128 + near, ROWS, k)
        got = self.drecv[k, pl.ds(pl.multiple_of(near, ROWS), ROWS), :]
        self.ysend[k] = (far + got.astype(F32)).astype(BF)
        self.y[k].start()

    def result(self, k):
        mine = self.t * ROWS
        own = self.rows(self.core * 128 + mine, ROWS, k)
        got = self.drecv[k, pl.ds(pl.multiple_of(mine, ROWS), ROWS), :].astype(F32)
        self.y[k].wait_recv()
        return own + got + self.yrecv[k].astype(F32)

    def run(self, term):
        for k in range(NC):
            self.put(k, term(k))
            if k:
                self.middle(k - 1)
        self.middle(NC - 1)

    def drain(self):
        for k in range(NC):
            self.d[k].wait_send()
            self.y[k].wait_send()


REDUCE_SCRATCH = [
    pltpu.VMEM((BLOCK, D), F32),
    pltpu.VMEM((NC, 128, CW), BF),
    pltpu.VMEM((NC, 128, CW), BF),
    pltpu.VMEM((NC, ROWS, CW), BF),
    pltpu.VMEM((NC, ROWS, CW), BF),
] + [pltpu.SemaphoreType.DMA((NC,))] * 4


def tile_sends(tiles, land, send, recv, chip, core, t, start):
    s = 2 * chip + core
    for j in range(3):
        for u in range(2):
            slot, index = owner_of(2 * chip + u)
            target = (core * 3 + j) * 10 + slot
            k = j * 2 + u

            if start:

                @pl.when(target == s)
                def _():
                    pltpu.make_async_copy(tiles.at[j, u], land.at[index], recv.at[index]).start()

            @pl.when(target != s)
            def _():
                cp = remote(tiles.at[j, u], land.at[index], send.at[k], recv.at[index], target, t)
                if start:
                    cp.start()
                else:
                    cp.wait_send()


def tile_waits(tiles, land, send, recv, chip, core, t):
    slot = (2 * chip + core) % 10
    for r in range(SLOTS):
        here = chip < SERVED
        if r == 0:
            here = jnp.logical_and(here, slot < 4)

        @pl.when(here)
        def _():
            pltpu.make_async_copy(tiles.at[0, 0], land.at[r], recv.at[r]).wait()


def home_sends(tiles, land, send, recv, chip, core, t, start):
    s = 2 * chip + core
    slot = s % 10
    head = chip // PER_HEAD
    for r in range(SLOTS):
        here = chip < SERVED
        if r == 0:
            here = jnp.logical_and(here, slot < 4)
        tile = tile_of(slot, r)
        target = (tile // 2) * 2 + head // 3
        j, u = head % 3, tile % 2

        if start:

            @pl.when(jnp.logical_and(here, target == s))
            def _():
                pltpu.make_async_copy(tiles.at[r], land.at[j, u], recv.at[j, u]).start()

        @pl.when(jnp.logical_and(here, target != s))
        def _():
            cp = remote(tiles.at[r], land.at[j, u], send.at[r], recv.at[j, u], target, t)
            if start:
                cp.start()
            else:
                cp.wait_send()


def home_waits(tiles, land, recv):
    for j in range(3):
        for u in range(2):
            pltpu.make_async_copy(tiles.at[0], land.at[j, u], recv.at[j, u]).wait()


def weight_load(ref, buf, sem, core, width):
    return pltpu.make_async_copy(
        ref.at[:, pl.ds(pl.multiple_of(core * width, 128), width)], buf, sem
    )


def project_kernel(
    x_ref, cot_ref, mask_ref, gain_ref, wq_ref, wk_ref, wv_ref,
    normed_ref, dout_ref, q_ref, kv_ref,
    nbuf, obuf, wbuf, kvsrc, qsrc, wsem, nsend, nrecv, osend, orecv, kvsend, kvrecv, fsend, qsend,
    qrecv, osem,
):
    chip, core, t = place()
    s = 2 * chip + core
    loads = [
        weight_load(ref, wbuf.at[k], wsem.at[k], core, 384)
        for k, ref in enumerate((wk_ref, wv_ref, wq_ref))
    ]
    for load in loads:
        load.start()
    x = x_ref[...]
    normed = (x * rms_scale(x) * gain_ref[...]).astype(BF)
    quad = QuadGather(nbuf, nsend, nrecv, chip, core, t)
    mine = pl.ds(pl.multiple_of(quad.mine, ROWS), ROWS)
    nbuf[mine, :] = normed
    quad_o = QuadGather(obuf, osend, orecv, chip, core, t)
    greet_all(chip, core, t)
    quad.start()
    obuf[mine, :] = (cot_ref[...] * mask_ref[...]).astype(BF)
    quad.finish()
    saves = pieces_out(nbuf, normed_ref, osem, 0, 4)
    for k in range(2):
        loads[k].wait()
        value = matmul(nbuf[...], wbuf[k]).astype(BF)
        for j in range(3):
            kvsrc[j, :, k * 128 : (k + 1) * 128] = value[:, j * 128 : (j + 1) * 128]

    def kv_sends(start):
        def one(o, carry):
            w = lax.rem(chip + 7 * o, 3 * PER_HEAD)
            j = w // PER_HEAD
            target = 2 * (core * 3 * PER_HEAD + w) + chip % 2
            if start:

                @pl.when(target == s)
                def _():
                    pltpu.make_async_copy(kvsrc.at[j], kv_ref.at[chip], kvrecv.at[chip]).start()

            @pl.when(target != s)
            def _():
                cp = remote(kvsrc.at[j], kv_ref.at[chip], kvsend.at[w], kvrecv.at[chip], target, t)
                if start:
                    cp.start()
                else:
                    cp.wait_send()

            return carry

        lax.fori_loop(0, 3 * PER_HEAD, one, 0)

    kv_sends(True)
    loads[2].wait()
    value = matmul(nbuf[...], wbuf[2]).astype(BF)
    for j in range(3):
        for u in range(2):
            qsrc[j, u] = value[u * 128 : (u + 1) * 128, j * 128 : (j + 1) * 128]
    tile_sends(qsrc, q_ref, qsend, qrecv, chip, core, t, True)
    quad_o.start()

    @pl.when(chip < SERVED)
    def _():
        def forward(o):
            source = lax.rem((chip // 2 + o) * 2 + core, CHIPS)
            view = kv_ref.at[source]
            return source, remote(view, view, fsend.at[o], kvrecv.at[source], s + 1 - 2 * core, t)

        def take(o, carry):
            source, cp = forward(o)
            pltpu.make_async_copy(kvsrc.at[0], kv_ref.at[source], kvrecv.at[source]).wait()
            cp.start()
            return carry

        lax.fori_loop(0, CHIPS // 2, take, 0)

        def finish(o, carry):
            source = 2 * o + 1 - core
            pltpu.make_async_copy(kvsrc.at[0], kv_ref.at[source], kvrecv.at[source]).wait()
            forward(o)[1].wait_send()
            return carry

        lax.fori_loop(0, CHIPS // 2, finish, 0)

    quad_o.finish()
    saves += pieces_out(obuf, dout_ref, osem, 4, 2)
    tile_waits(qsrc, q_ref, qsend, qrecv, chip, core, t)
    kv_sends(False)
    tile_sends(qsrc, q_ref, qsend, qrecv, chip, core, t, False)
    quad.drain()
    quad_o.drain()
    for save in saves:
        save.wait()


def pieces_out(buf, ref, sem, first, count):
    width = D // count
    copies = [
        pltpu.make_async_copy(
            buf.at[:, a * width : (a + 1) * width], ref.at[a], sem.at[first + a]
        )
        for a in range(count)
    ]
    for cp in copies:
        cp.start()
    return copies


VM = pl.BlockSpec(memory_space=pltpu.VMEM)
SM = pl.BlockSpec(memory_space=pltpu.SMEM)
ANY = pl.BlockSpec(memory_space=pl.ANY)


def shape(dims, dtype):
    return jax.ShapeDtypeStruct(dims, dtype)


HALVES = (2, BLOCK, 768)
QUARTERS = (4, BLOCK, 384)


def project(x, cot, mask, gain, wq, wk, wv):
    return pl.pallas_call(
        project_kernel,
        name="project",
        out_shape=(
            shape(QUARTERS, BF),
            shape(HALVES, BF),
            shape((SLOTS, TILE, 128), BF),
            shape((CHIPS, BLOCK, 256), BF),
        ),
        in_specs=[VM, VM, VM, VM, ANY, ANY, ANY],
        out_specs=(ANY,) * 4,
        scratch_shapes=[
            pltpu.VMEM((BLOCK, D), BF),
            pltpu.VMEM((BLOCK, D), BF),
            pltpu.VMEM((3, D, 384), BF),
            pltpu.VMEM((3, BLOCK, 256), BF),
            pltpu.VMEM((3, 2, TILE, 128), BF),
            pltpu.SemaphoreType.DMA((3,)),
            *(GATHER_SEMS * 2),
            pltpu.SemaphoreType.DMA((15,)),
            pltpu.SemaphoreType.DMA((CHIPS,)),
            pltpu.SemaphoreType.DMA((CHIPS // 2,)),
            pltpu.SemaphoreType.DMA((6,)),
            pltpu.SemaphoreType.DMA((SLOTS,)),
            pltpu.SemaphoreType.DMA((6,)),
        ],
        compiler_params=pltpu.CompilerParams(
            collective_id=0, has_side_effects=True, vmem_limit_bytes=VMEM_LIMIT
        ),
    )(x, cot, mask, gain, wq, wk, wv)


def eye():
    row = lax.broadcasted_iota(jnp.int32, (128, 128), 0)
    col = lax.broadcasted_iota(jnp.int32, (128, 128), 1)
    return jnp.where(row == col, 1.0, 0.0).astype(BF)


def both_maps(q_t):
    top = lax.broadcasted_iota(jnp.int32, q_t.shape, 0) < 64
    return jnp.concatenate([jnp.where(top, q_t, 0.0), jnp.where(top, 0.0, q_t)], axis=1)


def key_mask(start, count, tile, width):
    key = start + lax.broadcasted_iota(jnp.int32, (count, width), 0)
    query = tile * TILE + lax.broadcasted_iota(jnp.int32, (count, width), 1) % TILE
    return key <= query


def group_norm(parts, lam):
    first, second = parts[:, :TILE], parts[:, TILE:]
    differ = first - lam * second
    rms = rms_scale(differ, 0)
    return rms, differ * rms


def lambda_of(lambdas_ref, chip, t):
    first = jnp.exp(jnp.sum(lambdas_ref[0] * lambdas_ref[1], axis=-1, keepdims=True))
    second = jnp.exp(jnp.sum(lambdas_ref[2] * lambdas_ref[3], axis=-1, keepdims=True))
    every = first - second + LAMBDA_INIT
    mine = lax.broadcasted_iota(jnp.int32, every.shape, 0) == 6 * t + chip // PER_HEAD
    return jnp.sum(jnp.where(mine, every, 0.0), axis=0, keepdims=True)


STEP = 2048


def attend_kernel(
    lambdas_ref, gain_ref, q_ref, kv_ref, normed_ref,
    mixed_ref, parts_ref, log_ref, xnormed_ref, znormed_ref,
    v_t, kmax, acc, total, *sems,
):
    chip, core, t = place()
    slot = (2 * chip + core) % 10
    served = chip < SERVED
    keys = CHIPS * BLOCK
    greet_ring(chip, core, t)
    gathers = [
        RingGather(lambda p: normed_ref.at[p], xnormed_ref, *sems[:2], "x", chip, core, t),
        RingGather(lambda p: normed_ref.at[p], znormed_ref, *sems[2:], "z", chip, core, t),
    ]
    for gather in gathers:
        gather.start()
    lam = lambda_of(lambdas_ref, chip, t)

    @pl.when(served)
    def _():
        unit = eye()

        def flip(b, best):
            for u in range(2):
                start = pl.multiple_of(b * 2 * KB + u * KB, KB)
                block = kv_ref[pl.ds(start, KB), :]
                v_t[:, pl.ds(start, KB)] = matmul_t(unit, block[:, 128:]).astype(BF)
                k_t = matmul_t(unit, block[:, :128])
                square = k_t * k_t
                best = (
                    jnp.maximum(best[0], jnp.sum(square[:64], axis=0, keepdims=True)),
                    jnp.maximum(best[1], jnp.sum(square[64:], axis=0, keepdims=True)),
                )
            return best

        zero = jnp.zeros((1, KB), F32)
        best = lax.fori_loop(0, keys // (2 * KB), flip, (zero, zero))
        for m in range(2):
            kmax[m] = jnp.max(best[m])

    for r in range(SLOTS):
        tile = tile_of(slot, r)

        @pl.when(served if r else jnp.logical_and(served, slot < 4))
        def _():
            q_t = q_ref[r].astype(F32).T
            square = q_t * q_t
            bound = SCORE * jnp.concatenate(
                [
                    jnp.sqrt(jnp.sum(square[:64], axis=0, keepdims=True) * kmax[0]),
                    jnp.sqrt(jnp.sum(square[64:], axis=0, keepdims=True) * kmax[1]),
                ],
                axis=1,
            )
            q_both = both_maps(q_t).astype(BF)
            acc[...] = jnp.zeros_like(acc)
            total[...] = jnp.zeros_like(total)

            def step(b, masked):
                sums, out = None, None
                for u in range(STEP // KB):
                    start = pl.multiple_of(b * STEP + u * KB, KB)
                    score = matmul(kv_ref[pl.ds(start, KB), :128], q_both)
                    prob = jnp.exp2(score * SCORE - bound)
                    if masked:
                        prob = jnp.where(key_mask(start, KB, tile, 2 * TILE), prob, 0.0)
                    part = jnp.sum(prob.reshape(KB // 8, 8, 2 * TILE), axis=0)
                    term = matmul(v_t[:, pl.ds(start, KB)], prob.astype(BF))
                    sums = part if sums is None else sums + part
                    out = term if out is None else out + term
                total[...] += sums
                acc[...] += out

            full = tile * TILE // STEP

            def body(b, carry):
                step(b, False)
                return carry

            lax.fori_loop(0, full, body, 0)
            step(full, True)
            whole = jnp.sum(total[...], axis=0, keepdims=True)
            parts = acc[...] / whole
            parts_ref[r] = parts
            log_ref[r] = bound + jnp.log(whole) * LOG2E
            rms, hat = group_norm(parts, lam)
            mixed_ref[r] = (hat * gain_ref[...] * OUT_SCALE).T.astype(BF)

    for gather in gathers:
        gather.finish()
        gather.drain()


GATHERED = (4, BLOCK, 768)
GATHERED_Q = (4, BLOCK, 384)


def attend(lambdas, gain, q, kv, normed):
    return pl.pallas_call(
        attend_kernel,
        name="attend",
        out_shape=(
            shape((SLOTS, TILE, 128), BF),
            shape((SLOTS, 128, 2 * TILE), F32),
            shape((SLOTS, 1, 2 * TILE), F32),
            shape(GATHERED_Q, BF),
            shape(GATHERED_Q, BF),
        ),
        in_specs=[VM, VM, VM, VM, ANY],
        out_specs=(VM, VM, VM, ANY, ANY),
        scratch_shapes=[
            pltpu.VMEM((128, CHIPS * BLOCK), BF),
            pltpu.SMEM((2,), F32),
            pltpu.VMEM((128, 2 * TILE), F32),
            pltpu.VMEM((8, 2 * TILE), F32),
            *(RING_SEMS * 2),
        ],
        compiler_params=pltpu.CompilerParams(
            collective_id=3, has_side_effects=True, vmem_limit_bytes=VMEM_LIMIT
        ),
    )(lambdas, gain, q, kv, normed)


def middle_kernel(
    x_ref, cot_ref, mask_ref, gain_ref, tiles_ref, wo_ref, wg_ref, wu_ref, wd_ref,
    dout_ref,
    out_ref, dres_ref, gainpart_ref, dresall_ref, dmix_ref,
    lffn_ref, lgu_ref, lhid_ref, ldout_ref, lmix_ref,
    land, wo, wg, wu, wd, fbuf, rbuf, dms, doutall_ref, gu_ref, hid_ref, mix_ref, *rest,
):
    chip, core, t = place()
    reduces = [rest[9 * k : 9 * k + 9] for k in range(3)]
    gathers = [rest[27 + 2 * k : 29 + 2 * k] for k in range(2)]
    wsem, hsend, hrecv, tsend, trecv, osem = rest[31:37]
    sems = rest[37:]
    ring_dout = RingGather(lambda p: doutall_ref.at[p // 2], ldout_ref, *sems[0:2], "z", chip, core, t)
    ring_mix = RingGather(lambda p: mix_ref, lmix_ref, *sems[2:4], "x", chip, core, t)
    ring_ffn = RingGather(
        lambda p: fbuf.at[:, pl.ds(pl.multiple_of((p // 2) * 768, 128), 768)],
        lffn_ref, *sems[4:6], "x", chip, core, t,
    )
    ring_hid = RingGather(lambda p: hid_ref.at[p % 2], lhid_ref, *sems[6:8], "z", chip, core, t)
    ring_gu = RingGather(lambda p: gu_ref.at[p % 2], lgu_ref, *sems[8:10], "x", chip, core, t)
    rings = (ring_dout, ring_mix, ring_ffn, ring_hid, ring_gu)
    take_dout = pltpu.make_async_copy(dout_ref, doutall_ref, osem.at[4])
    take_dout.start()
    loads = [
        weight_load(wo_ref, wo, wsem.at[0], core, 384),
        weight_load(wg_ref, wg, wsem.at[1], core, 1024),
        weight_load(wu_ref, wu, wsem.at[2], core, 1024),
        weight_load(wd_ref, wd, wsem.at[3], core, 1024),
    ]
    for load in loads:
        load.start()
    gather_f = QuadGather(fbuf, *gathers[0], chip, core, t)
    gather_r = QuadGather(rbuf, *gathers[1], chip, core, t)
    mine = pl.ds(pl.multiple_of(gather_f.mine, ROWS), ROWS)
    dout = cot_ref[...] * mask_ref[...]
    greet_all(chip, core, t)
    home_sends(tiles_ref, land, hsend, hrecv, chip, core, t, True)
    take_dout.wait()
    ring_dout.start()
    loads[0].wait()
    home_waits(tiles_ref, land, hrecv)
    for j in range(3):
        for u in range(2):
            mix_ref[u * 128 : (u + 1) * 128, j * 128 : (j + 1) * 128] = land[j, u]
    ring_mix.start()
    red = QuadReduce(*reduces[0], chip, core, t)
    red.run(lambda k: matmul_t(mix_ref[...], wo[k * CW : (k + 1) * CW, :]))
    resid = x_ref[...] + jnp.concatenate([red.result(k) for k in range(NC)], axis=1)
    ffn_rms = rms_scale(resid)
    ffn_hat = resid * ffn_rms
    fbuf[mine, :] = (ffn_hat * gain_ref[...]).astype(BF)
    gather_f.start()
    gather_f.finish()
    ring_ffn.start()
    for load in loads[1:]:
        load.wait()

    def hidden_step(n, carry):
        cols = pl.ds(pl.multiple_of(n * 256, 256), 256)
        b, at = n // 2, n % 2
        gate = matmul(fbuf[...], wg[:, cols])
        up = matmul(fbuf[...], wu[:, cols])
        d_hidden = matmul(doutall_ref[0], wd[:768, cols]) + matmul(doutall_ref[1], wd[768:, cols])
        sig = 1.0 / (1.0 + jnp.exp(-gate))
        silu = gate * sig
        to = pl.ds(pl.multiple_of(at * 256, 256), 256)
        up_to = pl.ds(pl.multiple_of(512 + at * 256, 256), 256)
        hid_ref[b, :, to] = (silu * up).astype(BF)
        gu_ref[b, :, to] = (d_hidden * up * sig * (1.0 + gate * (1.0 - sig))).astype(BF)
        gu_ref[b, :, up_to] = (d_hidden * silu).astype(BF)
        return carry

    lax.fori_loop(0, 4, hidden_step, 0)
    ring_hid.start()
    ring_gu.start()
    red2 = QuadReduce(*reduces[1], chip, core, t)

    def ffn_term(k):
        rows = slice(k * CW, (k + 1) * CW)
        return (
            matmul_t(gu_ref[0, :, :512], wg[rows, :512])
            + matmul_t(gu_ref[1, :, :512], wg[rows, 512:])
            + matmul_t(gu_ref[0, :, 512:], wu[rows, :512])
            + matmul_t(gu_ref[1, :, 512:], wu[rows, 512:])
        )

    red2.run(ffn_term)
    red3 = QuadReduce(*reduces[2], chip, core, t)
    d_ffn = jnp.concatenate([red2.result(k) for k in range(NC)], axis=1)
    gainpart_ref[...] = jnp.sum(d_ffn * ffn_hat, axis=0, keepdims=True)
    d_resid = dout + norm_back(d_ffn, gain_ref[...], ffn_rms, ffn_hat)
    dres_ref[...] = d_resid
    rbuf[mine, :] = d_resid.astype(BF)
    gather_r.start()
    red3.run(
        lambda k: matmul_t(hid_ref[0], wd[k * CW : (k + 1) * CW, :512])
        + matmul_t(hid_ref[1], wd[k * CW : (k + 1) * CW, 512:])
    )
    gather_r.finish()
    d_mixed = matmul(rbuf[...], wo[...]).astype(BF)
    for j in range(3):
        for u in range(2):
            dms[j, u] = d_mixed[u * 128 : (u + 1) * 128, j * 128 : (j + 1) * 128]
    tile_sends(dms, dmix_ref, tsend, trecv, chip, core, t, True)
    saves = pieces_out(rbuf, dresall_ref, osem, 0, 4)
    out_ref[...] = resid + jnp.concatenate([red3.result(k) for k in range(NC)], axis=1)
    tile_waits(dms, dmix_ref, tsend, trecv, chip, core, t)
    tile_sends(dms, dmix_ref, tsend, trecv, chip, core, t, False)
    home_sends(tiles_ref, land, hsend, hrecv, chip, core, t, False)
    for gather in (gather_f, gather_r):
        gather.drain()
    for reduce in (red, red2, red3):
        reduce.drain()
    for save in saves:
        save.wait()
    for ring in rings:
        ring.finish()
        ring.drain()


def middle(x, cot, mask, gain, tiles, wo, wg, wu, wd, dout_all):
    return pl.pallas_call(
        middle_kernel,
        name="middle",
        out_shape=(
            shape((ROWS, D), F32),
            shape((ROWS, D), F32),
            shape((1, D), F32),
            shape(QUARTERS, BF),
            shape((SLOTS, TILE, 128), BF),
            shape(GATHERED, BF),
            shape((4, BLOCK, 1024), BF),
            shape((4, BLOCK, 512), BF),
            shape(GATHERED, BF),
            shape(GATHERED_Q, BF),
        ),
        in_specs=[VM, VM, VM, VM] + [ANY] * 6,
        out_specs=(VM, VM, VM) + (ANY,) * 7,
        scratch_shapes=[
            pltpu.VMEM((3, 2, TILE, 128), BF),
            pltpu.VMEM((D, 384), BF),
            pltpu.VMEM((D, 1024), BF),
            pltpu.VMEM((D, 1024), BF),
            pltpu.VMEM((D, 1024), BF),
            pltpu.VMEM((BLOCK, D), BF),
            pltpu.VMEM((BLOCK, D), BF),
            pltpu.VMEM((3, 2, TILE, 128), BF),
            pltpu.VMEM(HALVES, BF),
            pltpu.VMEM((2, BLOCK, 1024), BF),
            pltpu.VMEM((2, BLOCK, 512), BF),
            pltpu.VMEM((BLOCK, 384), BF),
            *(REDUCE_SCRATCH * 3),
            *(GATHER_SEMS * 2),
            pltpu.SemaphoreType.DMA((4,)),
            pltpu.SemaphoreType.DMA((SLOTS,)),
            pltpu.SemaphoreType.DMA((3, 2)),
            pltpu.SemaphoreType.DMA((6,)),
            pltpu.SemaphoreType.DMA((SLOTS,)),
            pltpu.SemaphoreType.DMA((5,)),
            *(RING_SEMS * 5),
        ],
        compiler_params=pltpu.CompilerParams(
            collective_id=1, has_side_effects=True, vmem_limit_bytes=VMEM_LIMIT
        ),
    )(x, cot, mask, gain, tiles, wo, wg, wu, wd, dout_all)


SPAN = 1024
SPANS = CHIPS * BLOCK // SPAN
PER_SPAN = SPAN // BLOCK // 2


def attend_back_kernel(
    lambdas_ref, gain_ref, q_ref, kv_ref, dmix_ref, parts_ref, log_ref,
    lffn_ref, lgu_ref, lhid_ref, ldout_ref, dres_ref,
    dqkv_ref, small_ref, gate_ref, up_ref, down_ref, xdres_ref,
    k_t, acc, q_cols, q_rows, d_cols, d_rows, deltas, dq_acc, dq_out, own, given, sib, both, home, land,
    lffn, lgu, lhid, ldout, pgu, pdown, sgu, sdown, swap, swapped, *sems,
):
    chip, core, t = place()
    s = 2 * chip + core
    slot = s % 10
    head = chip // PER_HEAD
    served = chip < SERVED
    x, z = chip % 4, chip // 8
    loads = [
        pltpu.make_async_copy(src, dst, sems[0].at[k])
        for k, (src, dst) in enumerate(
            ((lhid_ref, lhid), (ldout_ref, ldout), (lffn_ref, lffn), (lgu_ref, lgu))
        )
    ]
    for load in loads:
        load.start()
    lam = lambda_of(lambdas_ref, chip, t)
    greet_all(chip, core, t)
    ring_dres = RingGather(lambda p: dres_ref.at[p], xdres_ref, *sems[1:3], "x", chip, core, t)
    send_down = Scatter(
        pdown, sdown, *sems[3:5], 16, 16 * (z // 2), 8 * (z % 2) + chip % 8, chip, core, t
    )
    send_gu = Scatter(
        pgu, sgu, *sems[5:7], 16, 16 * (x // 2), 8 * (x % 2) + chip // 4, chip, core, t
    )
    swap_sem, dsend, drecv, ksend, krecv, hsend, hrecv = sems[7:]
    loads[0].wait()
    loads[1].wait()
    block_grad(pdown, 0, ldout, lhid[...].reshape(4 * BLOCK, 512), 256)
    send_down.each(True)
    loads[2].wait()
    loads[3].wait()
    block_grad(pgu, 0, lffn, lgu[:, :, :512].reshape(4 * BLOCK, 512), 256)
    block_grad(pgu, 512, lffn, lgu[:, :, 512:].reshape(4 * BLOCK, 512), 256)
    send_gu.each(True)
    ring_dres.start()
    small_ref[...] = jnp.zeros_like(small_ref)

    def to_sibling(o):
        return remote(given.at[o], sib.at[o], dsend.at[o], drecv.at[o], s + 1 - 2 * core, t)

    def to_home(o, start):
        target = 2 * (2 * o + core) + head // 3
        spot = (head % 3) * PER_HEAD + chip % PER_HEAD
        if start:

            @pl.when(target == s)
            def _():
                pltpu.make_async_copy(both.at[o], home.at[spot], krecv.at[spot]).start()

        @pl.when(target != s)
        def _():
            cp = remote(both.at[o], home.at[spot], ksend.at[o], krecv.at[spot], target, t)
            if start:
                cp.start()
            else:
                cp.wait_send()

    def tile_at(r):
        late = 4 + 10 * (r - 1) + jnp.where((r - 1) % 2 == 0, slot, 9 - slot)
        return jnp.where(r == 0, slot, late)

    @pl.when(served)
    def _():
        unit = eye()

        def flip(b, carry):
            for u in range(2):
                rows = pl.ds(pl.multiple_of(b * 2 * KB + u * KB, KB), KB)
                k_t[:, rows] = matmul_t(unit, kv_ref[rows, :128]).astype(BF)
            return carry

        lax.fori_loop(0, SPANS, flip, 0)

    for r in range(SLOTS):

        @pl.when(served if r else jnp.logical_and(served, slot < 4))
        def _():
            q_cols[r] = both_maps(q_ref[r].astype(F32).T).astype(BF)
            q = q_ref[r].astype(F32)
            left = lax.broadcasted_iota(jnp.int32, q.shape, 1) < 64
            q_rows[r] = jnp.concatenate(
                [jnp.where(left, q, 0.0), jnp.where(left, 0.0, q)], axis=0
            ).astype(BF)
            parts = parts_ref[r]
            first, second = parts[:, :TILE], parts[:, TILE:]
            rms, hat = group_norm(parts, lam)
            e_t = dmix_ref[r].astype(F32).T * OUT_SCALE
            column = jnp.sum(e_t * hat, axis=1, keepdims=True)
            d_differ = norm_back(e_t, gain_ref[...], rms, hat, 0).astype(BF)
            d_wide = d_differ.astype(F32)
            d_cols[r] = d_differ
            d_rows[r] = d_wide.T.astype(BF)
            second_dot = jnp.sum(d_wide * second, axis=0, keepdims=True)
            row = lax.broadcasted_iota(jnp.int32, (128, 128), 0)
            lane = lax.broadcasted_iota(jnp.int32, (128, 128), 1)
            small_ref[0:1, :] += jnp.sum(jnp.where(row == lane, column, 0.0), axis=0, keepdims=True)
            here = lax.broadcasted_iota(jnp.int32, (1, 128), 1) == 6 * t + head
            small_ref[1:2, :] -= jnp.where(here, jnp.sum(second_dot, axis=1, keepdims=True), 0.0)
            deltas[r, 0:1, :] = jnp.sum(d_wide * first, axis=0, keepdims=True)
            deltas[r, 1:2, :] = -lam * second_dot
            dq_acc[r] = jnp.zeros((128, 2 * TILE), F32)

    @pl.when(served)
    def _():
        def span(k, carry):
            b = lax.rem(chip + k, SPANS)
            start = pl.multiple_of(b * SPAN, SPAN)
            rows = pl.ds(start, SPAN)
            acc[...] = jnp.zeros_like(acc)

            def step(r, masked):
                block = kv_ref[rows, :]
                score = matmul(block[:, :128], q_cols[r])
                prob = jnp.exp2(score * SCORE - log_ref[r])
                if masked:
                    prob = jnp.where(key_mask(start, SPAN, tile_at(r), 2 * TILE), prob, 0.0)
                upper = matmul(block[:, 128:], d_cols[r])
                p1, p2 = prob[:, :TILE], prob[:, TILE:]
                ds = jnp.concatenate(
                    [p1 * (upper - deltas[r, 0:1, :]), p2 * (-lam * upper - deltas[r, 1:2, :])],
                    axis=1,
                ).astype(BF)
                mix = (p1 - lam * p2).astype(BF)
                acc[:, :128] += matmul(ds, q_rows[r])
                acc[:, 128:] += matmul(mix, d_rows[r])
                dq_acc[r] += matmul(k_t[:, rows], ds)

            def masked_step(r, carry):
                step(r, True)
                return carry

            def full_step(r, carry):
                step(r, False)
                return carry

            reach, past = 0, 0
            for r in range(SLOTS):
                last = tile_of(slot, r) * TILE // SPAN
                counts = (slot < 4) if r == 0 else True
                reach += jnp.where(jnp.logical_and(counts, last >= b), 1, 0)
                past += jnp.where(jnp.logical_and(counts, last > b), 1, 0)
            lax.fori_loop(SLOTS - reach, SLOTS - past, masked_step, 0)
            lax.fori_loop(SLOTS - past, SLOTS, full_step, 0)
            for u in range(PER_SPAN):
                o = PER_SPAN * b + u
                for ref, which in ((given, 1 - core), (own, core)):
                    part = acc[pl.ds(pl.multiple_of((2 * u + which) * BLOCK, BLOCK), BLOCK), :]
                    ref[o, :, :128] = (part[:, :128] * 0.125).astype(BF)
                    ref[o, :, 128:] = part[:, 128:].astype(BF)
                to_sibling(o).start()

            @pl.when(k > 0)
            def _():
                pass_on(k - 1)

            return carry

        def pass_on(k):
            for u in range(PER_SPAN):
                o = PER_SPAN * lax.rem(chip + k, SPANS) + u
                to_sibling(o).wait_recv()
                both[o] = (own[o].astype(F32) + sib[o].astype(F32)).astype(BF)
                to_home(o, True)

        lax.fori_loop(0, SPANS, span, 0)
        pass_on(SPANS - 1)

    for r in range(SLOTS):

        @pl.when(served if r else jnp.logical_and(served, slot < 4))
        def _():
            dq_t = jnp.concatenate([dq_acc[r, :64, :TILE], dq_acc[r, 64:, TILE:]], axis=0)
            dq_out[r] = (dq_t * 0.125).T.astype(BF)

    home_sends(dq_out, land, hsend, hrecv, chip, core, t, True)
    send_down.wait()
    for b in range(2):
        total = send_down.total(b, slice(0, 512))
        for h in range(2):
            swap[h, :, 2048 + b * 512 : 2560 + b * 512] = total[h * 24 : h * 24 + 24]
    send_gu.wait()
    for b in range(2):
        for m in range(2):
            total = send_gu.total(b, slice(m * 512, m * 512 + 512))
            at = m * 1024 + b * 512
            for h in range(2):
                swap[h, :, at : at + 512] = total[h * 24 : h * 24 + 24]
    swap_copy = remote(
        swap.at[1 - core], swapped, swap_sem.at[0], swap_sem.at[1], s + 1 - 2 * core, t
    )
    swap_copy.start()
    home_waits(dq_out, land, hrecv)
    for j in range(3):
        for u in range(2):
            dqkv_ref[0, u * 128 : (u + 1) * 128, j * 128 : (j + 1) * 128] = land[j, u]
    for j in range(3):
        total = jnp.zeros((BLOCK, 256), F32)
        for p in range(PER_HEAD):
            spot = j * PER_HEAD + p
            pltpu.make_async_copy(both.at[0], home.at[spot], krecv.at[spot]).wait()
            total = total + home[spot].astype(F32)
        dqkv_ref[1, :, j * 128 : (j + 1) * 128] = total[:, :128].astype(BF)
        dqkv_ref[2, :, j * 128 : (j + 1) * 128] = total[:, 128:].astype(BF)
    swap_copy.wait()
    swap_out(swap, swapped, ((gate_ref, 0), (up_ref, 1024), (down_ref, 2048)), 1024, core)
    ring_dres.finish()
    ring_dres.drain()
    send_gu.each(False)
    send_down.each(False)
    home_sends(dq_out, land, hsend, hrecv, chip, core, t, False)

    @pl.when(served)
    def _():
        def last(o, carry):
            to_sibling(o).wait_send()
            to_home(o, False)
            return carry

        lax.fori_loop(0, CHIPS // 2, last, 0)


def swap_out(swap, swapped, outs, width, core):
    mine = swap[core]
    for c in range(2):

        @pl.when(core == c)
        def _():
            for ref, at in outs:
                ref[:, c * width : (c + 1) * width] = mine[:, at : at + width]
                other = (1 - c) * width
                ref[:, other : other + width] = swapped[:, at : at + width]


def attend_back(lambdas, gain, q, kv, dmix, parts, logs, lffn, lgu, lhid, ldout, dres):
    half = (CHIPS // 2, BLOCK, 256)
    return pl.pallas_call(
        attend_back_kernel,
        name="attend_back",
        out_shape=(
            shape((3, BLOCK, 384), BF),
            shape((2, 128), F32),
            shape((24, 2048), F32),
            shape((24, 2048), F32),
            shape((24, 2048), F32),
            shape(GATHERED_Q, BF),
        ),
        in_specs=[VM] * 7 + [ANY] * 5,
        out_specs=(VM,) * 5 + (ANY,),
        scratch_shapes=[
            pltpu.VMEM((128, CHIPS * BLOCK), BF),
            pltpu.VMEM((SPAN, 256), F32),
            pltpu.VMEM((SLOTS, 128, 2 * TILE), BF),
            pltpu.VMEM((SLOTS, 2 * TILE, 128), BF),
            pltpu.VMEM((SLOTS, 128, TILE), BF),
            pltpu.VMEM((SLOTS, TILE, 128), BF),
            pltpu.VMEM((SLOTS, 2, TILE), F32),
            pltpu.VMEM((SLOTS, 128, 2 * TILE), F32),
            pltpu.VMEM((SLOTS, TILE, 128), BF),
            pltpu.VMEM(half, BF),
            pltpu.VMEM(half, BF),
            pltpu.VMEM(half, BF),
            pltpu.VMEM(half, BF),
            pltpu.VMEM((3 * PER_HEAD, BLOCK, 256), BF),
            pltpu.VMEM((3, 2, TILE, 128), BF),
            pltpu.VMEM(GATHERED, BF),
            pltpu.VMEM((4, BLOCK, 1024), BF),
            pltpu.VMEM((4, BLOCK, 512), BF),
            pltpu.VMEM(GATHERED, BF),
            pltpu.VMEM((768, 1024), BF),
            pltpu.VMEM((768, 512), BF),
            pltpu.VMEM((16, CHUNK, 1024), BF),
            pltpu.VMEM((16, CHUNK, 512), BF),
            pltpu.VMEM((2, 24, 3072), F32),
            pltpu.VMEM((24, 3072), F32),
            pltpu.SemaphoreType.DMA((4,)),
            *RING_SEMS,
            *scatter_sems(16),
            *scatter_sems(16),
            pltpu.SemaphoreType.DMA((2,)),
            pltpu.SemaphoreType.DMA((CHIPS // 2,)),
            pltpu.SemaphoreType.DMA((CHIPS // 2,)),
            pltpu.SemaphoreType.DMA((CHIPS // 2,)),
            pltpu.SemaphoreType.DMA((3 * PER_HEAD,)),
            pltpu.SemaphoreType.DMA((SLOTS,)),
            pltpu.SemaphoreType.DMA((3, 2)),
        ],
        compiler_params=pltpu.CompilerParams(
            collective_id=4, has_side_effects=True, vmem_limit_bytes=VMEM_LIMIT
        ),
    )(lambdas, gain, q, kv, dmix, parts, logs, lffn, lgu, lhid, ldout, dres)


def finish_kernel(
    x_ref, gain_ref, dres_ref, dqkv_ref, wq_ref, wk_ref, wv_ref,
    xnormed_ref, znormed_ref, xdres_ref, xmix_ref, ffnpart_ref, small_ref,
    grad_ref, gq_ref, gk_ref, gv_ref, go_ref, sums_ref,
    wbuf, xnormed, znormed, xdres, xmix, rq, rk, rv, pqo, pkv, sqo, skv, swap, swapped,
    vec, vecs, quarter, quarters, *rest,
):
    chip, core, t = place()
    s = 2 * chip + core
    x, z = chip % 4, chip // 8
    reduce = rest[:9]
    wsem, lsem = rest[9:11]
    rings = [
        RingGather(lambda p, k=k: dqkv_ref.at[k], land, *sems, axis, chip, core, t)
        for k, land, sems, axis in (
            (1, rk, rest[11:13], "z"), (0, rq, rest[13:15], "x"), (2, rv, rest[15:17], "z")
        )
    ]
    send_qo = Scatter(pqo, sqo, *rest[17:19], 8, 8 * x, chip // 4, chip, core, t)
    send_kv = Scatter(pkv, skv, *rest[19:21], 8, 8 * z, chip % 8, chip, core, t)
    swap_sem, asem, bsem, csem = rest[21:]
    loads = [
        weight_load(ref, wbuf.at[k], wsem.at[k], core, 384)
        for k, ref in enumerate((wq_ref, wk_ref, wv_ref))
    ]
    lefts = [
        pltpu.make_async_copy(src, dst, lsem.at[k])
        for k, (src, dst) in enumerate(
            ((xdres_ref, xdres), (xmix_ref, xmix), (xnormed_ref, xnormed), (znormed_ref, znormed))
        )
    ]
    for load in loads + lefts:
        load.start()
    greet_all(chip, core, t)
    for ring in rings:
        ring.start()
    for load in loads:
        load.wait()
    red = QuadReduce(*reduce, chip, core, t)

    def term(k):
        rows = slice(k * CW, (k + 1) * CW)
        return (
            matmul_t(dqkv_ref[0], wbuf[0, rows, :])
            + matmul_t(dqkv_ref[1], wbuf[1, rows, :])
            + matmul_t(dqkv_ref[2], wbuf[2, rows, :])
        )

    red.run(term)
    for left in lefts:
        left.wait()
    block_grad(pqo, 384, xdres, xmix[...].reshape(4 * BLOCK, 384), 384)
    x = x_ref[...]
    rms = rms_scale(x)
    hat = x * rms
    d_normed = jnp.concatenate([red.result(k) for k in range(NC)], axis=1)
    part = jnp.sum(d_normed * hat, axis=0, keepdims=True)
    vec[...] = jnp.zeros_like(vec)
    for k in range(12):
        vec[k : k + 1, :] = part[:, k * 128 : (k + 1) * 128]
        vec[12 + k : 13 + k, :] = ffnpart_ref[:, k * 128 : (k + 1) * 128]
    vec[24:26, :] = small_ref[...]
    members = ((s + 1 - 2 * core, t), (s, 1 - t), (s + 1 - 2 * core, 1 - t))
    first_sum = [
        remote(vec, vecs.at[k], asem.at[0, k], asem.at[1, k], *member)
        for k, member in enumerate(members)
    ]
    for cp in first_sum:
        cp.start()
    grad_ref[...] = dres_ref[...] + norm_back(d_normed, gain_ref[...], rms, hat)
    for cp in first_sum:
        cp.wait_recv()
    share = pl.ds(pl.multiple_of((2 * core + t) * 8, 8), 8)
    quarter[...] = (vec[share, :] + vecs[0, share, :]) + (vecs[1, share, :] + vecs[2, share, :])

    def spread(k, start):
        to = 2 * lax.rem(chip + k, CHIPS) + core
        cp = remote(quarter, quarters.at[chip], bsem.at[0, k], bsem.at[1, chip], to, t)
        if start:
            cp.start()
        else:
            cp.wait_send()

    def spread_start(k, carry):
        spread(k, True)
        return carry

    def spread_end(k, carry):
        spread(k, False)
        return carry

    own = pltpu.make_async_copy(quarter, quarters.at[chip], bsem.at[1, chip])
    own.start()
    lax.fori_loop(1, CHIPS, spread_start, 0)
    rings[1].finish()
    block_grad(pqo, 0, xnormed, rq[...].reshape(4 * BLOCK, 384), 384)
    send_qo.each(True)
    rings[0].finish()
    block_grad(pkv, 0, znormed, rk[...].reshape(4 * BLOCK, 384), 384)
    rings[2].finish()
    block_grad(pkv, 384, znormed, rv[...].reshape(4 * BLOCK, 384), 384)
    send_kv.each(True)

    def collect(k, total):
        pltpu.make_async_copy(quarter, quarters.at[k], bsem.at[1, k]).wait()
        return total + quarters[k]

    sums_ref[share, :] = lax.fori_loop(0, CHIPS, collect, jnp.zeros((8, 128), F32))
    last_sum = [
        remote(sums_ref.at[share], sums_ref.at[share], csem.at[0, k], csem.at[1, k], *member)
        for k, member in enumerate(members)
    ]
    for cp in last_sum:
        cp.start()
    for send, first in ((send_qo, (0, 3)), (send_kv, (1, 2))):
        send.wait()
        for m in range(2):
            total = send.total(0, slice(m * 384, m * 384 + 384))
            at = first[m] * 384
            for h in range(2):
                swap[h, :, at : at + 384] = total[h * 24 : h * 24 + 24]
    swap_copy = remote(
        swap.at[1 - core], swapped, swap_sem.at[0], swap_sem.at[1], s + 1 - 2 * core, t
    )
    swap_copy.start()
    for cp in last_sum:
        cp.wait()
    for cp in first_sum:
        cp.wait_send()
    lax.fori_loop(1, CHIPS, spread_end, 0)
    send_qo.each(False)
    send_kv.each(False)
    for ring in rings:
        ring.drain()
    red.drain()
    swap_copy.wait()
    outs = ((gq_ref, 0), (gk_ref, 384), (gv_ref, 768), (go_ref, 1152))
    swap_out(swap, swapped, outs, 384, core)


def finish(x, gain, dres, dqkv, wq, wk, wv, xnormed, znormed, xdres, xmix, ffn_part, small):
    return pl.pallas_call(
        finish_kernel,
        name="finish",
        out_shape=(shape((ROWS, D), F32),) + (shape((24, 768), F32),) * 4 + (shape((32, 128), F32),),
        in_specs=[VM] * 4 + [ANY] * 7 + [VM] * 2,
        out_specs=(VM,) * 6,
        scratch_shapes=[
            pltpu.VMEM((3, D, 384), BF),
            *([pltpu.VMEM(GATHERED_Q, BF)] * 7),
            pltpu.VMEM((384, 768), BF),
            pltpu.VMEM((384, 768), BF),
            pltpu.VMEM((8, CHUNK, 768), BF),
            pltpu.VMEM((8, CHUNK, 768), BF),
            pltpu.VMEM((2, 24, 1536), F32),
            pltpu.VMEM((24, 1536), F32),
            pltpu.VMEM((32, 128), F32),
            pltpu.VMEM((3, 32, 128), F32),
            pltpu.VMEM((8, 128), F32),
            pltpu.VMEM((CHIPS, 8, 128), F32),
            *REDUCE_SCRATCH,
            pltpu.SemaphoreType.DMA((3,)),
            pltpu.SemaphoreType.DMA((4,)),
            *(RING_SEMS * 3),
            *scatter_sems(8),
            *scatter_sems(8),
            pltpu.SemaphoreType.DMA((2,)),
            pltpu.SemaphoreType.DMA((2, 3)),
            pltpu.SemaphoreType.DMA((2, CHIPS)),
            pltpu.SemaphoreType.DMA((2, 3)),
        ],
        compiler_params=pltpu.CompilerParams(
            collective_id=2, has_side_effects=True, vmem_limit_bytes=VMEM_LIMIT
        ),
    )(x, gain, dres, dqkv, wq, wk, wv, xnormed, znormed, xdres, xmix, ffn_part, small)


def publish(*arrays):
    count = len(arrays)

    def kernel(*refs):
        copies = [
            pltpu.make_async_copy(refs[k], refs[count + k], refs[2 * count].at[k])
            for k in range(count)
        ]
        for cp in copies:
            cp.start()
        for cp in copies:
            cp.wait()

    return pl.pallas_call(
        kernel,
        name="publish",
        out_shape=tuple(shape(a.shape, a.dtype) for a in arrays),
        in_specs=[ANY] * count,
        out_specs=(ANY,) * count,
        scratch_shapes=[pltpu.SemaphoreType.DMA((count,))],
    )(*arrays)


def on_device(
    hidden_in, cotangent, needle_mask, attn_gain, lambdas, subln_gain, ffn_gain,
    weight_query, weight_key, weight_value, weight_out, weight_gate, weight_up, weight_down,
):
    attn_row = attn_gain.reshape(1, D)
    ffn_row = ffn_gain.reshape(1, D)
    sub_col = subln_gain.reshape(128, 1)
    mask = needle_mask.astype(F32).reshape(ROWS, 1)

    normed, dout, q, kv = project(
        hidden_in, cotangent, mask, attn_row, weight_query, weight_key, weight_value
    )
    kv = kv.reshape(CHIPS * BLOCK, 256)
    mixed, parts, logs, xnormed, znormed = attend(lambdas, sub_col, q, kv, normed)
    output, d_resid, ffn_part, dres, dmix, lffn, lgu, lhid, ldout, xmix = middle(
        hidden_in, cotangent, mask, ffn_row, mixed,
        weight_out, weight_gate, weight_up, weight_down, dout,
    )
    dqkv, small, grad_gate, grad_up, grad_down, xdres = attend_back(
        lambdas, sub_col, q, kv, dmix, parts, logs, lffn, lgu, lhid, ldout, dres
    )
    grad_input, grad_query, grad_key, grad_value, grad_out, sums = finish(
        hidden_in, attn_row, d_resid, dqkv, weight_query, weight_key, weight_value,
        xnormed, znormed, xdres, xmix, ffn_part, small,
    )
    first_exp = jnp.exp(jnp.sum(lambdas[0] * lambdas[1], axis=-1))
    second_exp = jnp.exp(jnp.sum(lambdas[2] * lambdas[3], axis=-1))
    d_first = sums[25, :12] * first_exp
    d_second = -sums[25, :12] * second_exp
    grad_lambdas = jnp.stack(
        [
            d_first[:, None] * lambdas[1],
            d_first[:, None] * lambdas[0],
            d_second[:, None] * lambdas[3],
            d_second[:, None] * lambdas[2],
        ]
    )
    results = publish(
        output, grad_input, grad_query, grad_key, grad_value, grad_out, grad_gate, grad_up, grad_down
    )
    return (
        *results,
        sums[:12].reshape(D),
        grad_lambdas,
        sums[24],
        sums[12:24].reshape(D),
    )


def solution(mesh):
    split = P(None, "tp")
    rows = P(("seq", "tp"), None)
    both = P("seq", "tp")
    return jax.shard_map(
        on_device,
        mesh=mesh,
        in_specs=(rows, rows, P(("seq", "tp"))) + (P(),) * 4 + (split,) * 7,
        out_specs=(rows, rows) + (both,) * 7 + (P(),) * 4,
        check_vma=False,
    )
```

```python
import math

import jax
import jax.numpy as jnp
from jax import lax
from jax.experimental import pallas as pl
from jax.experimental.pallas import tpu as pltpu
from jax.sharding import PartitionSpec as P

MESH = pl.DeviceIdType.MESH
BF = jnp.bfloat16
F32 = jnp.float32
EPS = 1e-06
LAMBDA_INIT = 0.8 - 0.6 * math.exp(-3.6)
OUT_SCALE = 1.0 - LAMBDA_INIT
D = 1536
CHIPS = 32
SERVED = 30
PER_HEAD = 5
ROWS = 64
BLOCK = 256
TILE = 128
SLOTS = 7
KB = 512
LOG2E = 1.4426950408889634
SCORE = 0.125 * LOG2E
VMEM_LIMIT = 60 * 2**20


def place():
    s = lax.axis_index("seq")
    return s // 2, s % 2, lax.axis_index("tp")


def owner_of(tile):
    step = (tile - 4) // 10
    pos = (tile - 4) % 10
    slot = jnp.where(step % 2 == 0, pos, 9 - pos)
    early = tile < 4
    return jnp.where(early, tile, slot), jnp.where(early, 0, step + 1)


def tile_of(slot, r):
    if r == 0:
        return slot
    return 4 + 10 * (r - 1) + (slot if (r - 1) % 2 == 0 else 9 - slot)


def matmul(a, b):
    return jnp.dot(a, b, preferred_element_type=F32)


def matmul_t(a, b):
    return lax.dot_general(a, b, (((1,), (1,)), ((), ())), preferred_element_type=F32)


def rms_scale(values, axis=-1):
    return lax.rsqrt(jnp.mean(values * values, axis=axis, keepdims=True) + EPS)


def norm_back(grad_normed, gain, rms, hat, axis=-1):
    scaled = grad_normed * gain
    return rms * (scaled - hat * jnp.mean(scaled * hat, axis=axis, keepdims=True))


def greet_all(chip, core, t):
    barrier = pltpu.get_barrier_semaphore()
    s = 2 * chip + core

    def greet(o, carry):
        pl.semaphore_signal(
            barrier, inc=1, device_id=(lax.rem(s + o, 2 * CHIPS), t), device_id_type=MESH
        )
        return carry

    lax.fori_loop(1, 2 * CHIPS, greet, 0)
    pl.semaphore_signal(barrier, inc=1, device_id=(s, 1 - t), device_id_type=MESH)
    pl.semaphore_wait(barrier, 2 * CHIPS)


def remote(src, dst, send_sem, recv_sem, s, t):
    return pltpu.make_async_remote_copy(
        src_ref=src,
        dst_ref=dst,
        send_sem=send_sem,
        recv_sem=recv_sem,
        device_id=(s, t),
        device_id_type=MESH,
    )


def rows_at(ref, start, count):
    return ref.at[pl.ds(pl.multiple_of(start, ROWS), count)]


class QuadGather:
    def __init__(self, buf, send, recv, chip, core, t):
        self.buf, self.send, self.recv = buf, send, recv
        self.chip, self.core, self.t = chip, core, t
        mine = core * 128 + t * ROWS
        self.mine = mine
        self.near = core * 128 + (1 - t) * ROWS
        sib = (2 * chip + 1 - core, t)
        self.to_near = self.copy(mine, 0, (2 * chip + core, 1 - t))
        self.to_sib = self.copy(mine, 1, sib)
        self.forward = self.copy(self.near, 2, sib)

    def copy(self, row, k, target):
        view = rows_at(self.buf, row, ROWS)
        return remote(view, view, self.send.at[k], self.recv.at[k], *target)

    def start(self):
        self.to_near.start()
        self.to_sib.start()

    def finish(self):
        self.to_near.wait_recv()
        self.forward.start()
        self.to_sib.wait_recv()
        self.forward.wait_recv()

    def drain(self):
        self.to_near.wait_send()
        self.to_sib.wait_send()
        self.forward.wait_send()


class RingGather:
    def __init__(self, pieces, land, send, recv, axis, chip, core, t):
        at = chip % 4 if axis == "x" else chip // 8
        self.local = pltpu.make_async_copy(pieces(at), land.at[at], recv.at[at])
        self.copies = []
        for k in (1, 3, 2):
            if axis == "x":
                peer, chip_to = (at + k) % 4, chip - at + (at + k) % 4
            else:
                peer, chip_to = (at + k) % 4, (chip + 8 * k) % CHIPS
            self.copies.append(
                remote(pieces(peer), land.at[at], send.at[k - 1], recv.at[at], 2 * chip_to + core, t)
            )
        self.waits = [
            pltpu.make_async_copy(pieces(at), land.at[k], recv.at[k]) for k in range(4)
        ]

    def start(self):
        self.local.start()
        for cp in self.copies:
            cp.start()

    def finish(self):
        for cp in self.waits:
            cp.wait()

    def drain(self):
        for cp in self.copies:
            cp.wait_send()


class RingGatherOnce:
    def __init__(self, pieces, land, send, recv, pass_send, pass_recv, axis, chip, core, t):
        at = chip % 4 if axis == "x" else chip // 8
        self.mine = pl.ds(pl.multiple_of(core * 128, 128), 128)
        self.local = pltpu.make_async_copy(pieces(at), land.at[at], recv.at[0])
        self.local_at = at
        self.copies, self.passes = [], []
        for k in (1, 3, 2):
            peer = (at + k) % 4
            chip_to = chip - at + peer if axis == "x" else (chip + 8 * k) % CHIPS
            self.copies.append(
                remote(
                    pieces(peer).at[self.mine], land.at[at, self.mine],
                    send.at[k - 1], recv.at[4 - k], 2 * chip_to + core, t,
                )
            )
            view = land.at[peer, self.mine]
            self.passes.append(
                (
                    pltpu.make_async_copy(pieces(at).at[self.mine], view, recv.at[k]),
                    remote(view, view, pass_send.at[k - 1], pass_recv.at[k - 1], 2 * chip + 1 - core, t),
                )
            )

    def start(self):
        self.local.start()
        for cp in self.copies:
            cp.start()

    def forward(self):
        for arrive, cp in self.passes:
            arrive.wait()
            cp.start()

    def finish(self):
        self.local.wait()
        for _, cp in self.passes:
            cp.wait_recv()

    def drain(self):
        for cp in self.copies:
            cp.wait_send()
        for _, cp in self.passes:
            cp.wait_send()


ONCE_SEMS = [
    pltpu.SemaphoreType.DMA((3,)),
    pltpu.SemaphoreType.DMA((4,)),
    pltpu.SemaphoreType.DMA((3,)),
    pltpu.SemaphoreType.DMA((3,)),
]
RING_SEMS = [pltpu.SemaphoreType.DMA((3,)), pltpu.SemaphoreType.DMA((4,))]


def block_grad(dst, start, left, right, step):
    width = right.shape[1]

    def one(m, carry):
        cols = pl.ds(pl.multiple_of(m * step, 128), step)
        part = left[:, :, cols].reshape(4 * BLOCK, step)
        dst[cols, start : start + width] = lax.dot_general(
            part, right, (((0,), (0,)), ((), ())), preferred_element_type=F32
        ).astype(BF)
        return carry

    lax.fori_loop(0, left.shape[2] // step, one, 0)


CHUNK = 48


class Scatter:
    def __init__(self, part, land, send, recv, count, first, spot, chip, core, t):
        self.part, self.land, self.send, self.recv = part, land, send, recv
        self.count, self.first, self.spot = count, first, spot
        self.chip, self.core, self.t = chip, core, t

    def source(self, i):
        return self.part.at[pl.ds(pl.multiple_of(i * CHUNK, 16), CHUNK)]

    def each(self, start):
        def one(o, carry):
            i = lax.rem(self.chip + 1 + 3 * o, self.count)
            owner = self.first + i
            cp = remote(
                self.source(i), self.land.at[self.spot], self.send.at[i], self.recv.at[self.spot],
                2 * owner + self.core, self.t,
            )
            if start:

                @pl.when(owner == self.chip)
                def _():
                    pltpu.make_async_copy(
                        self.source(i), self.land.at[self.spot], self.recv.at[self.spot]
                    ).start()

            @pl.when(owner != self.chip)
            def _():
                if start:
                    cp.start()
                else:
                    cp.wait_send()

            return carry

        lax.fori_loop(0, self.count, one, 0)

    def wait(self):
        def one(k, carry):
            pltpu.make_async_copy(self.source(0), self.land.at[k], self.recv.at[k]).wait()
            return carry

        lax.fori_loop(0, self.count, one, 0)

    def total(self, b, cols):
        def one(k, carry):
            return carry + self.land[8 * b + k, :, cols].astype(F32)

        return lax.fori_loop(0, 8, one, jnp.zeros((CHUNK, cols.stop - cols.start), F32))


def scatter_sems(count):
    return [pltpu.SemaphoreType.DMA((count,)), pltpu.SemaphoreType.DMA((count,))]


GATHER_SEMS = [pltpu.SemaphoreType.DMA((3,)), pltpu.SemaphoreType.DMA((3,))]
CW = 512
NC = D // CW


class QuadReduce:
    def __init__(self, part, dsend, drecv, ysend, yrecv, ds, dr, ys, yr, chip, core, t):
        self.part, self.dsend, self.drecv = part, dsend, drecv
        self.ysend, self.yrecv = ysend, yrecv
        self.core, self.t = core, t
        self.d = [
            remote(dsend.at[k], drecv.at[k], ds.at[k], dr.at[k], 2 * chip + 1 - core, t)
            for k in range(NC)
        ]
        self.y = [
            remote(ysend.at[k], yrecv.at[k], ys.at[k], yr.at[k], 2 * chip + core, 1 - t)
            for k in range(NC)
        ]

    def rows(self, start, count, k):
        return self.part[pl.ds(pl.multiple_of(start, ROWS), count), k * CW : (k + 1) * CW]

    def put(self, k, value):
        self.part[:, k * CW : (k + 1) * CW] = value
        self.dsend[k] = self.rows((1 - self.core) * 128, 128, k).astype(BF)
        self.d[k].start()

    def middle(self, k):
        self.d[k].wait_recv()
        near = (1 - self.t) * ROWS
        far = self.rows(self.core * 128 + near, ROWS, k)
        got = self.drecv[k, pl.ds(pl.multiple_of(near, ROWS), ROWS), :]
        self.ysend[k] = (far + got.astype(F32)).astype(BF)
        self.y[k].start()

    def result(self, k):
        mine = self.t * ROWS
        own = self.rows(self.core * 128 + mine, ROWS, k)
        got = self.drecv[k, pl.ds(pl.multiple_of(mine, ROWS), ROWS), :].astype(F32)
        self.y[k].wait_recv()
        return own + got + self.yrecv[k].astype(F32)

    def run(self, term):
        for k in range(NC):
            self.put(k, term(k))
            if k:
                self.middle(k - 1)
        self.middle(NC - 1)

    def drain(self):
        for k in range(NC):
            self.d[k].wait_send()
            self.y[k].wait_send()


REDUCE_SCRATCH = [
    pltpu.VMEM((BLOCK, D), F32),
    pltpu.VMEM((NC, 128, CW), BF),
    pltpu.VMEM((NC, 128, CW), BF),
    pltpu.VMEM((NC, ROWS, CW), BF),
    pltpu.VMEM((NC, ROWS, CW), BF),
] + [pltpu.SemaphoreType.DMA((NC,))] * 4


def tile_sends(tiles, land, send, recv, chip, core, t, start):
    s = 2 * chip + core
    for j in range(3):
        for u in range(2):
            slot, index = owner_of(2 * chip + u)
            target = (core * 3 + j) * 10 + slot
            k = j * 2 + u

            if start:

                @pl.when(target == s)
                def _():
                    pltpu.make_async_copy(tiles.at[j, u], land.at[index], recv.at[index]).start()

            @pl.when(target != s)
            def _():
                cp = remote(tiles.at[j, u], land.at[index], send.at[k], recv.at[index], target, t)
                if start:
                    cp.start()
                else:
                    cp.wait_send()


def tile_waits(tiles, land, send, recv, chip, core, t):
    slot = (2 * chip + core) % 10
    for r in range(SLOTS):
        here = chip < SERVED
        if r == 0:
            here = jnp.logical_and(here, slot < 4)

        @pl.when(here)
        def _():
            pltpu.make_async_copy(tiles.at[0, 0], land.at[r], recv.at[r]).wait()


def home_sends(tiles, land, send, recv, chip, core, t, start):
    s = 2 * chip + core
    slot = s % 10
    head = chip // PER_HEAD
    for r in range(SLOTS):
        here = chip < SERVED
        if r == 0:
            here = jnp.logical_and(here, slot < 4)
        tile = tile_of(slot, r)
        target = (tile // 2) * 2 + head // 3
        j, u = head % 3, tile % 2

        if start:

            @pl.when(jnp.logical_and(here, target == s))
            def _():
                pltpu.make_async_copy(tiles.at[r], land.at[j, u], recv.at[j, u]).start()

        @pl.when(jnp.logical_and(here, target != s))
        def _():
            cp = remote(tiles.at[r], land.at[j, u], send.at[r], recv.at[j, u], target, t)
            if start:
                cp.start()
            else:
                cp.wait_send()


def home_waits(tiles, land, recv):
    for j in range(3):
        for u in range(2):
            pltpu.make_async_copy(tiles.at[0], land.at[j, u], recv.at[j, u]).wait()


def weight_load(ref, buf, sem, core, width):
    return pltpu.make_async_copy(
        ref.at[:, pl.ds(pl.multiple_of(core * width, 128), width)], buf, sem
    )


def pieces_out(buf, ref, sem, first, count):
    width = D // count
    copies = [
        pltpu.make_async_copy(
            buf.at[:, a * width : (a + 1) * width], ref.at[a], sem.at[first + a]
        )
        for a in range(count)
    ]
    for cp in copies:
        cp.start()
    return copies


VM = pl.BlockSpec(memory_space=pltpu.VMEM)
ANY = pl.BlockSpec(memory_space=pl.ANY)


def shape(dims, dtype):
    return jax.ShapeDtypeStruct(dims, dtype)


HALVES = (2, BLOCK, 768)
QUARTERS = (4, BLOCK, 384)
GATHERED = (4, BLOCK, 768)
GATHERED_Q = (4, BLOCK, 384)
KV = (CHIPS, BLOCK, 256)
STEP = 2048


def eye(size):
    row = lax.broadcasted_iota(jnp.int32, (size, size), 0)
    col = lax.broadcasted_iota(jnp.int32, (size, size), 1)
    return jnp.where(row == col, 1.0, 0.0).astype(BF)


def both_maps(q_t):
    top = lax.broadcasted_iota(jnp.int32, q_t.shape, 0) < 64
    return jnp.concatenate([jnp.where(top, q_t, 0.0), jnp.where(top, 0.0, q_t)], axis=1)


def key_mask(start, count, tile, width):
    key = start + lax.broadcasted_iota(jnp.int32, (count, width), 0)
    query = tile * TILE + lax.broadcasted_iota(jnp.int32, (count, width), 1) % TILE
    return key <= query


def group_norm(parts, lam):
    first, second = parts[:, :TILE], parts[:, TILE:]
    differ = first - lam * second
    rms = rms_scale(differ, 0)
    return rms, differ * rms


def lambda_of(lambdas_ref, chip, t):
    first = jnp.exp(jnp.sum(lambdas_ref[0] * lambdas_ref[1], axis=-1, keepdims=True))
    second = jnp.exp(jnp.sum(lambdas_ref[2] * lambdas_ref[3], axis=-1, keepdims=True))
    every = first - second + LAMBDA_INIT
    mine = lax.broadcasted_iota(jnp.int32, every.shape, 0) == 6 * t + chip // PER_HEAD
    return jnp.sum(jnp.where(mine, every, 0.0), axis=0, keepdims=True)


def forward_kernel(
    x_ref, cot_ref, mask_ref, gain_ref, lambdas_ref, sub_ref, wq_ref, wk_ref, wv_ref,
    dout_ref, q_ref, kv_ref, mixed_ref, parts_ref, log_ref, xnormed_ref, znormed_ref,
    nbuf, obuf, wbuf, kvsrc, qsrc, kv, q, v_t, peaks, kmax, acc, total,
    wsem, nsend, nrecv, osend, orecv, kvsend, kvrecv, fsend, qsend, qrecv, osem, *sems,
):
    chip, core, t = place()
    s = 2 * chip + core
    slot = s % 10
    served = chip < SERVED
    loads = [
        weight_load(ref, wbuf.at[k], wsem.at[k], core, 384)
        for k, ref in enumerate((wk_ref, wv_ref, wq_ref))
    ]
    for load in loads:
        load.start()
    x = x_ref[...]
    normed = (x * rms_scale(x) * gain_ref[...]).astype(BF)
    quad = QuadGather(nbuf, nsend, nrecv, chip, core, t)
    mine = pl.ds(pl.multiple_of(quad.mine, ROWS), ROWS)
    nbuf[mine, :] = normed
    quad_o = QuadGather(obuf, osend, orecv, chip, core, t)
    greet_all(chip, core, t)
    quad.start()
    obuf[mine, :] = (cot_ref[...] * mask_ref[...]).astype(BF)
    lam = lambda_of(lambdas_ref, chip, t)
    unit = eye(256)
    quad.finish()
    for k in range(2):
        loads[k].wait()
        value = matmul(nbuf[...], wbuf[k]).astype(BF)
        for j in range(3):
            kvsrc[j, :, k * 128 : (k + 1) * 128] = value[:, j * 128 : (j + 1) * 128]

    def kv_sends(start):
        def one(o, carry):
            w = lax.rem(chip + 7 * o, 3 * PER_HEAD)
            j = w // PER_HEAD
            target = 2 * (core * 3 * PER_HEAD + w) + chip % 2
            if start:

                @pl.when(target == s)
                def _():
                    pltpu.make_async_copy(kvsrc.at[j], kv.at[chip], kvrecv.at[chip]).start()

            @pl.when(target != s)
            def _():
                cp = remote(kvsrc.at[j], kv.at[chip], kvsend.at[w], kvrecv.at[chip], target, t)
                if start:
                    cp.start()
                else:
                    cp.wait_send()

            return carry

        lax.fori_loop(0, 3 * PER_HEAD, one, 0)

    kv_sends(True)
    loads[2].wait()
    value = matmul(nbuf[...], wbuf[2]).astype(BF)
    for j in range(3):
        for u in range(2):
            qsrc[j, u] = value[u * 128 : (u + 1) * 128, j * 128 : (j + 1) * 128]
    tile_sends(qsrc, q, qsend, qrecv, chip, core, t, True)
    quad_o.start()

    def forward(o):
        source = lax.rem((chip // 2 + o) * 2 + core, CHIPS)
        view = kv.at[source]
        return source, remote(view, view, fsend.at[o], kvrecv.at[source], s + 1 - 2 * core, t)

    def turn(source):
        block = kv[source]
        at = pl.ds(pl.multiple_of(source * BLOCK, BLOCK), BLOCK)
        turned = matmul_t(unit, block)
        v_t[:, at] = turned[128:].astype(BF)
        square = turned[:128] * turned[:128]
        for m in range(2):
            largest = jnp.sum(square[64 * m : 64 * m + 64], axis=0, keepdims=True)
            peaks[m : m + 1, :] = jnp.maximum(peaks[m : m + 1, :], largest)

    def gathers():
        def piece(p):
            return nbuf.at[:, pl.ds(pl.multiple_of(p * 384, 128), 384)]

        return [
            RingGather(piece, xnormed_ref, *sems[:2], "x", chip, core, t),
            RingGather(piece, znormed_ref, *sems[2:], "z", chip, core, t),
        ]

    @pl.when(served)
    def _():
        peaks[...] = jnp.zeros_like(peaks)

        def take(o, carry):
            source, cp = forward(o)
            pltpu.make_async_copy(kvsrc.at[0], kv.at[source], kvrecv.at[source]).wait()
            cp.start()
            turn(source)
            return carry

        lax.fori_loop(0, CHIPS // 2, take, 0)

        def finish(o, carry):
            source = lax.rem((chip // 2 + o) * 2 + 1 - core, CHIPS)
            pltpu.make_async_copy(kvsrc.at[0], kv.at[source], kvrecv.at[source]).wait()
            forward(o)[1].wait_send()
            turn(source)
            return carry

        lax.fori_loop(0, CHIPS // 2, finish, 0)
        for m in range(2):
            kmax[m] = jnp.max(peaks[m : m + 1, :])

    quad_o.finish()
    saves = pieces_out(obuf, dout_ref, osem, 0, 2)
    tile_waits(qsrc, q, qsend, qrecv, chip, core, t)
    for ring in gathers():
        ring.start()

    def keep():
        return [
            pltpu.make_async_copy(kv, kv_ref, osem.at[2]),
            pltpu.make_async_copy(q.at[pl.ds(1, SLOTS - 1)], q_ref.at[pl.ds(1, SLOTS - 1)], osem.at[3]),
        ]

    def keep_early():
        return pltpu.make_async_copy(q.at[0], q_ref.at[0], osem.at[4])

    @pl.when(served)
    def _():
        for cp in keep():
            cp.start()

    @pl.when(jnp.logical_and(served, slot < 4))
    def _():
        keep_early().start()

    for r in range(SLOTS):
        tile = tile_of(slot, r)

        @pl.when(served if r else jnp.logical_and(served, slot < 4))
        def _():
            q_t = q[r].astype(F32).T
            square = q_t * q_t
            bound = SCORE * jnp.concatenate(
                [
                    jnp.sqrt(jnp.sum(square[:64], axis=0, keepdims=True) * kmax[0]),
                    jnp.sqrt(jnp.sum(square[64:], axis=0, keepdims=True) * kmax[1]),
                ],
                axis=1,
            )
            q_both = both_maps(q_t).astype(BF)
            acc[...] = jnp.zeros_like(acc)
            total[...] = jnp.zeros_like(total)

            def step(b, masked):
                sums, out = None, None
                for u in range(STEP // KB):
                    start = pl.multiple_of(b * STEP + u * KB, KB)
                    pair = pl.ds(b * (STEP // BLOCK) + u * (KB // BLOCK), KB // BLOCK)
                    score = matmul(kv[pair, :, :128].reshape(KB, 128), q_both)
                    prob = jnp.exp2(score * SCORE - bound)
                    if masked:
                        prob = jnp.where(key_mask(start, KB, tile, 2 * TILE), prob, 0.0)
                    part = jnp.sum(prob.reshape(KB // 8, 8, 2 * TILE), axis=0)
                    term = matmul(v_t[:, pl.ds(start, KB)], prob.astype(BF))
                    sums = part if sums is None else sums + part
                    out = term if out is None else out + term
                total[...] += sums
                acc[...] += out

            full = tile * TILE // STEP

            def body(b, carry):
                step(b, False)
                return carry

            lax.fori_loop(0, full, body, 0)
            step(full, True)
            whole = jnp.sum(total[...], axis=0, keepdims=True)
            parts = acc[...] / whole
            parts_ref[r] = parts
            log_ref[r] = bound + jnp.log(whole) * LOG2E
            rms, hat = group_norm(parts, lam)
            mixed_ref[r] = (hat * sub_ref[...] * OUT_SCALE).T.astype(BF)

    for ring in gathers():
        ring.finish()
        ring.drain()
    kv_sends(False)
    tile_sends(qsrc, q, qsend, qrecv, chip, core, t, False)
    quad.drain()
    quad_o.drain()
    for save in saves:
        save.wait()

    @pl.when(served)
    def _():
        for cp in keep():
            cp.wait()

    @pl.when(jnp.logical_and(served, slot < 4))
    def _():
        keep_early().wait()


def forward_part(x, cot, mask, gain, lambdas, sub, wq, wk, wv):
    return pl.pallas_call(
        forward_kernel,
        name="forward",
        out_shape=(
            shape(HALVES, BF),
            shape((SLOTS, TILE, 128), BF),
            shape(KV, BF),
            shape((SLOTS, TILE, 128), BF),
            shape((SLOTS, 128, 2 * TILE), F32),
            shape((SLOTS, 1, 2 * TILE), F32),
            shape(GATHERED_Q, BF),
            shape(GATHERED_Q, BF),
        ),
        in_specs=[VM] * 6 + [ANY] * 3,
        out_specs=(ANY, ANY, ANY, VM, VM, VM, ANY, ANY),
        scratch_shapes=[
            pltpu.VMEM((BLOCK, D), BF),
            pltpu.VMEM((BLOCK, D), BF),
            pltpu.VMEM((3, D, 384), BF),
            pltpu.VMEM((3, BLOCK, 256), BF),
            pltpu.VMEM((3, 2, TILE, 128), BF),
            pltpu.VMEM(KV, BF),
            pltpu.VMEM((SLOTS, TILE, 128), BF),
            pltpu.VMEM((128, CHIPS * BLOCK), BF),
            pltpu.VMEM((8, BLOCK), F32),
            pltpu.SMEM((2,), F32),
            pltpu.VMEM((128, 2 * TILE), F32),
            pltpu.VMEM((8, 2 * TILE), F32),
            pltpu.SemaphoreType.DMA((3,)),
            *(GATHER_SEMS * 2),
            pltpu.SemaphoreType.DMA((15,)),
            pltpu.SemaphoreType.DMA((CHIPS,)),
            pltpu.SemaphoreType.DMA((CHIPS // 2,)),
            pltpu.SemaphoreType.DMA((6,)),
            pltpu.SemaphoreType.DMA((SLOTS,)),
            pltpu.SemaphoreType.DMA((5,)),
            *(RING_SEMS * 2),
        ],
        compiler_params=pltpu.CompilerParams(
            collective_id=0, has_side_effects=True, vmem_limit_bytes=VMEM_LIMIT
        ),
    )(x, cot, mask, gain, lambdas, sub, wq, wk, wv)


SPAN = 1024
SPANS = CHIPS * BLOCK // SPAN
PER_SPAN = SPAN // BLOCK // 2
EARLY_SPANS = 4


def middle_kernel(
    x_ref, cot_ref, mask_ref, gain_ref, lambdas_ref, sub_ref, tiles_ref, wo_ref, wg_ref, wu_ref, wd_ref,
    dout_ref, q_ref, kv_ref, parts_ref, log_ref,
    out_ref, dres_ref, gainpart_ref, dqkv_ref, small_ref, gate_ref, up_ref, down_ref,
    lmix_ref, xdres_ref,
    land, wo, wg, wu, wd, fbuf, rbuf, dms, dout_all, gu, hid, mix,
    q, kv, parts_all, logs, dmix,
    lffn, lgu, lhid, ldout, pgu, pdown, sgu, sdown, swap, swapped,
    k_t, acc, q_cols, q_rows, d_cols, d_rows, deltas, dq_acc, dq_out, given, sib, both, home, *rest,
):
    chip, core, t = place()
    s = 2 * chip + core
    slot = s % 10
    head = chip // PER_HEAD
    served = chip < SERVED
    x_at, z_at = chip % 4, chip // 8
    taken = iter(rest)

    def take(count):
        return [next(taken) for _ in range(count)]

    reduces = [take(9) for _ in range(2)]
    gather_sems = [take(2) for _ in range(2)]
    ring_sems = [take(2) for _ in range(5)]
    once_sems = take(4)
    scatter = [take(2) for _ in range(2)]
    wsem, osem, hsend, hrecv, tsend, trecv, swap_sem = take(7)
    dsend, drecv, ksend, krecv, gsend, grecv = take(6)

    loads = [
        weight_load(wo_ref, wo, wsem.at[0], core, 384),
        weight_load(wg_ref, wg, wsem.at[1], core, 1024),
        weight_load(wu_ref, wu, wsem.at[2], core, 1024),
        weight_load(wd_ref, wd, wsem.at[3], core, 1024),
    ]
    fetches = [
        pltpu.make_async_copy(src, dst, osem.at[4 + k])
        for k, (src, dst) in enumerate(
            ((dout_ref, dout_all), (q_ref, q), (kv_ref, kv), (parts_ref, parts_all), (log_ref, logs))
        )
    ]
    loads[0].start()
    fetches[0].start()
    for load in loads[1:]:
        load.start()
    for fetch in fetches[1:]:
        fetch.start()
    gather_f = QuadGather(fbuf, *gather_sems[0], chip, core, t)
    gather_r = QuadGather(rbuf, *gather_sems[1], chip, core, t)
    ring_dout = RingGather(lambda p: dout_all.at[p // 2], ldout, *ring_sems[0], "x", chip, core, t)
    ring_mix = RingGather(lambda p: mix, lmix_ref, *ring_sems[1], "x", chip, core, t)
    ring_hid = RingGather(lambda p: hid.at[p % 2], lhid, *ring_sems[2], "x", chip, core, t)
    ring_gu = RingGather(lambda p: gu.at[p % 2], lgu, *ring_sems[3], "z", chip, core, t)
    ring_dres = RingGather(
        lambda p: rbuf.at[:, pl.ds(pl.multiple_of(p * 384, 128), 384)],
        xdres_ref, *ring_sems[4], "x", chip, core, t,
    )
    ring_ffn = RingGatherOnce(
        lambda p: fbuf.at[:, pl.ds(pl.multiple_of((p // 2) * 768, 128), 768)],
        lffn, *once_sems, "z", chip, core, t,
    )
    send_down = Scatter(
        pdown, sdown, *scatter[0], 16, 16 * (x_at // 2), 8 * (x_at % 2) + chip // 4, chip, core, t
    )
    send_gu = Scatter(
        pgu, sgu, *scatter[1], 16, 16 * (z_at // 2), 8 * (z_at % 2) + chip % 8, chip, core, t
    )
    mine = pl.ds(pl.multiple_of(gather_f.mine, ROWS), ROWS)
    dout = cot_ref[...] * mask_ref[...]
    lam = lambda_of(lambdas_ref, chip, t)
    small_ref[...] = jnp.zeros_like(small_ref)
    greet_all(chip, core, t)
    home_sends(tiles_ref, land, hsend, hrecv, chip, core, t, True)
    loads[0].wait()
    home_waits(tiles_ref, land, hrecv)
    for j in range(3):
        for u in range(2):
            mix[u * 128 : (u + 1) * 128, j * 128 : (j + 1) * 128] = land[j, u]
    red = QuadReduce(*reduces[0], chip, core, t)
    red.run(lambda k: matmul_t(mix[...], wo[k * CW : (k + 1) * CW, :]))
    fetches[0].wait()
    ring_dout.start()
    ring_mix.start()
    resid = x_ref[...] + jnp.concatenate([red.result(k) for k in range(NC)], axis=1)
    ffn_rms = rms_scale(resid)
    ffn_hat = resid * ffn_rms
    fbuf[mine, :] = (ffn_hat * gain_ref[...]).astype(BF)
    gather_f.start()
    for load in loads[1:]:
        load.wait()
    red.drain()
    gather_f.finish()
    ring_ffn.start()

    def hidden_step(n, carry):
        cols = pl.ds(pl.multiple_of(n * 256, 256), 256)
        b, at = n // 2, n % 2
        gate = matmul(fbuf[...], wg[:, cols])
        up = matmul(fbuf[...], wu[:, cols])
        d_hidden = matmul(dout_all[0], wd[:768, cols]) + matmul(dout_all[1], wd[768:, cols])
        sig = 1.0 / (1.0 + jnp.exp(-gate))
        silu = gate * sig
        to = pl.ds(pl.multiple_of(at * 256, 256), 256)
        up_to = pl.ds(pl.multiple_of(512 + at * 256, 256), 256)
        hid[b, :, to] = (silu * up).astype(BF)
        gu[b, :, to] = (d_hidden * up * sig * (1.0 + gate * (1.0 - sig))).astype(BF)
        gu[b, :, up_to] = (d_hidden * silu).astype(BF)
        return carry

    lax.fori_loop(0, 4, hidden_step, 0)
    red2 = QuadReduce(*reduces[0], chip, core, t)

    def ffn_term(k):
        rows = slice(k * CW, (k + 1) * CW)
        return (
            matmul_t(gu[0, :, :512], wg[rows, :512])
            + matmul_t(gu[1, :, :512], wg[rows, 512:])
            + matmul_t(gu[0, :, 512:], wu[rows, :512])
            + matmul_t(gu[1, :, 512:], wu[rows, 512:])
        )

    red2.run(ffn_term)
    ring_hid.start()
    ring_gu.start()
    red3 = QuadReduce(*reduces[1], chip, core, t)
    d_ffn = jnp.concatenate([red2.result(k) for k in range(NC)], axis=1)
    gainpart_ref[...] = jnp.sum(d_ffn * ffn_hat, axis=0, keepdims=True)
    d_resid = dout + norm_back(d_ffn, gain_ref[...], ffn_rms, ffn_hat)
    dres_ref[...] = d_resid
    rbuf[mine, :] = d_resid.astype(BF)
    gather_r.start()
    red3.run(
        lambda k: matmul_t(hid[0], wd[k * CW : (k + 1) * CW, :512])
        + matmul_t(hid[1], wd[k * CW : (k + 1) * CW, 512:])
    )
    gather_r.finish()
    d_mixed = matmul(rbuf[...], wo[...]).astype(BF)
    for j in range(3):
        for u in range(2):
            dms[j, u] = d_mixed[u * 128 : (u + 1) * 128, j * 128 : (j + 1) * 128]
    tile_sends(dms, dmix, tsend, trecv, chip, core, t, True)
    ring_ffn.forward()
    out_ref[...] = resid + jnp.concatenate([red3.result(k) for k in range(NC)], axis=1)
    for fetch in fetches[1:]:
        fetch.wait()

    def to_sibling(o):
        at = o % (2 * PER_SPAN)
        return remote(given.at[at], sib.at[o], dsend.at[at], drecv.at[o], s + 1 - 2 * core, t)

    def to_home(o, start):
        target = 2 * (2 * o + core) + head // 3
        spot = (head % 3) * PER_HEAD + chip % PER_HEAD
        if start:

            @pl.when(target == s)
            def _():
                pltpu.make_async_copy(both.at[o], home.at[spot], krecv.at[spot]).start()

        @pl.when(target != s)
        def _():
            cp = remote(both.at[o], home.at[spot], ksend.at[o], krecv.at[spot], target, t)
            if start:
                cp.start()
            else:
                cp.wait_send()

    def tile_at(r):
        late = 4 + 10 * (r - 1) + jnp.where((r - 1) % 2 == 0, slot, 9 - slot)
        return jnp.where(r == 0, slot, late)

    @pl.when(served)
    def _():
        unit = eye(128)

        def flip(b, carry):
            rows = pl.ds(pl.multiple_of(b * KB, KB), KB)
            block = kv[pl.ds(2 * b, 2), :, :128].reshape(KB, 128)
            k_t[:, rows] = matmul_t(unit, block).astype(BF)
            return carry

        lax.fori_loop(0, CHIPS * BLOCK // KB, flip, 0)

    tile_waits(dms, dmix, tsend, trecv, chip, core, t)
    ring_dout.finish()
    ring_hid.finish()
    block_grad(pdown, 0, ldout, lhid[...].reshape(4 * BLOCK, 512), 256)
    send_down.each(True)

    for r in range(SLOTS):

        @pl.when(served if r else jnp.logical_and(served, slot < 4))
        def _():
            q_wide = q[r].astype(F32)
            q_cols[r] = both_maps(q_wide.T).astype(BF)
            left = lax.broadcasted_iota(jnp.int32, q_wide.shape, 1) < 64
            q_rows[r] = jnp.concatenate(
                [jnp.where(left, q_wide, 0.0), jnp.where(left, 0.0, q_wide)], axis=0
            ).astype(BF)
            parts = parts_all[r]
            first, second = parts[:, :TILE], parts[:, TILE:]
            rms, hat = group_norm(parts, lam)
            e_t = dmix[r].astype(F32).T * OUT_SCALE
            column = jnp.sum(e_t * hat, axis=1, keepdims=True)
            d_differ = norm_back(e_t, sub_ref[...], rms, hat, 0).astype(BF)
            d_wide = d_differ.astype(F32)
            d_cols[r] = d_differ
            d_rows[r] = d_wide.T.astype(BF)
            second_dot = jnp.sum(d_wide * second, axis=0, keepdims=True)
            row = lax.broadcasted_iota(jnp.int32, (128, 128), 0)
            lane = lax.broadcasted_iota(jnp.int32, (128, 128), 1)
            small_ref[0:1, :] += jnp.sum(jnp.where(row == lane, column, 0.0), axis=0, keepdims=True)
            here = lax.broadcasted_iota(jnp.int32, (1, 128), 1) == 6 * t + head
            small_ref[1:2, :] -= jnp.where(here, jnp.sum(second_dot, axis=1, keepdims=True), 0.0)
            deltas[r, 0:1, :] = jnp.sum(d_wide * first, axis=0, keepdims=True)
            deltas[r, 1:2, :] = -lam * second_dot
            dq_acc[r] = jnp.zeros((128, 2 * TILE), F32)

    def pass_on(k):
        for u in range(PER_SPAN):
            o = PER_SPAN * lax.rem(chip + k, SPANS) + u
            to_sibling(o).wait_recv()
            both[o] = (both[o].astype(F32) + sib[o].astype(F32)).astype(BF)
            to_home(o, True)

    def span(k, carry):
        b = lax.rem(chip + k, SPANS)
        start = pl.multiple_of(b * SPAN, SPAN)
        rows = pl.ds(start, SPAN)
        blocks = pl.ds(b * (SPAN // BLOCK), SPAN // BLOCK)
        acc[...] = jnp.zeros_like(acc)

        def step(r, masked):
            score = matmul(kv[blocks, :, :128].reshape(SPAN, 128), q_cols[r])
            prob = jnp.exp2(score * SCORE - logs[r])
            if masked:
                prob = jnp.where(key_mask(start, SPAN, tile_at(r), 2 * TILE), prob, 0.0)
            upper = matmul(kv[blocks, :, 128:].reshape(SPAN, 128), d_cols[r])
            p1, p2 = prob[:, :TILE], prob[:, TILE:]
            ds = jnp.concatenate(
                [p1 * (upper - deltas[r, 0:1, :]), p2 * (-lam * upper - deltas[r, 1:2, :])],
                axis=1,
            ).astype(BF)
            mixed = (p1 - lam * p2).astype(BF)
            acc[:, :128] += matmul(ds, q_rows[r])
            acc[:, 128:] += matmul(mixed, d_rows[r])
            dq_acc[r] += matmul(k_t[:, rows], ds)

        def masked_step(r, carry):
            step(r, True)
            return carry

        def full_step(r, carry):
            step(r, False)
            return carry

        reach, past = 0, 0
        for r in range(SLOTS):
            last = tile_of(slot, r) * TILE // SPAN
            counts = (slot < 4) if r == 0 else True
            reach += jnp.where(jnp.logical_and(counts, last >= b), 1, 0)
            past += jnp.where(jnp.logical_and(counts, last > b), 1, 0)
        lax.fori_loop(SLOTS - reach, SLOTS - past, masked_step, 0)
        lax.fori_loop(SLOTS - past, SLOTS, full_step, 0)

        @pl.when(k >= 2)
        def _():
            for u in range(PER_SPAN):
                to_sibling(PER_SPAN * lax.rem(chip + k - 2, SPANS) + u).wait_send()

        for u in range(PER_SPAN):
            o = PER_SPAN * b + u
            for ref, at, which in ((given, o % (2 * PER_SPAN), 1 - core), (both, o, core)):
                part = acc[pl.ds(pl.multiple_of((2 * u + which) * BLOCK, BLOCK), BLOCK), :]
                ref[at, :, :128] = (part[:, :128] * 0.125).astype(BF)
                ref[at, :, 128:] = part[:, 128:].astype(BF)
            to_sibling(o).start()

        @pl.when(k > 0)
        def _():
            pass_on(k - 1)

        return carry

    @pl.when(served)
    def _():
        lax.fori_loop(0, EARLY_SPANS, span, 0)

    ring_ffn.finish()
    ring_gu.finish()
    block_grad(pgu, 0, lffn, lgu[:, :, :512].reshape(4 * BLOCK, 512), 256)
    block_grad(pgu, 512, lffn, lgu[:, :, 512:].reshape(4 * BLOCK, 512), 256)
    send_gu.each(True)

    @pl.when(served)
    def _():
        lax.fori_loop(EARLY_SPANS, SPANS, span, 0)
        pass_on(SPANS - 1)

    for r in range(SLOTS):

        @pl.when(served if r else jnp.logical_and(served, slot < 4))
        def _():
            dq_t = jnp.concatenate([dq_acc[r, :64, :TILE], dq_acc[r, 64:, TILE:]], axis=0)
            dq_out[r] = (dq_t * 0.125).T.astype(BF)

    home_sends(dq_out, land, gsend, grecv, chip, core, t, True)
    ring_dres.start()
    send_down.wait()
    for b in range(2):
        total = send_down.total(b, slice(0, 512))
        for h in range(2):
            swap[h, :, 2048 + b * 512 : 2560 + b * 512] = total[h * 24 : h * 24 + 24]
    home_waits(dq_out, land, grecv)
    for j in range(3):
        for u in range(2):
            dqkv_ref[0, u * 128 : (u + 1) * 128, j * 128 : (j + 1) * 128] = land[j, u]
    for j in range(3):
        total = jnp.zeros((BLOCK, 256), F32)
        for p in range(PER_HEAD):
            spot = j * PER_HEAD + p
            pltpu.make_async_copy(both.at[0], home.at[spot], krecv.at[spot]).wait()
            total = total + home[spot].astype(F32)
        dqkv_ref[1, :, j * 128 : (j + 1) * 128] = total[:, :128].astype(BF)
        dqkv_ref[2, :, j * 128 : (j + 1) * 128] = total[:, 128:].astype(BF)
    send_gu.wait()
    for b in range(2):
        for m in range(2):
            total = send_gu.total(b, slice(m * 512, m * 512 + 512))
            at = m * 1024 + b * 512
            for h in range(2):
                swap[h, :, at : at + 512] = total[h * 24 : h * 24 + 24]
    swap_copy = remote(
        swap.at[1 - core], swapped, swap_sem.at[0], swap_sem.at[1], s + 1 - 2 * core, t
    )
    swap_copy.start()
    ring_mix.finish()
    ring_dres.finish()
    for ring in (ring_dout, ring_mix, ring_hid, ring_gu, ring_dres, ring_ffn):
        ring.drain()
    send_gu.each(False)
    send_down.each(False)
    home_sends(tiles_ref, land, hsend, hrecv, chip, core, t, False)
    home_sends(dq_out, land, gsend, grecv, chip, core, t, False)
    tile_sends(dms, dmix, tsend, trecv, chip, core, t, False)
    for gather in (gather_f, gather_r):
        gather.drain()
    red2.drain()
    red3.drain()

    @pl.when(served)
    def _():
        for k in (SPANS - 2, SPANS - 1):
            for u in range(PER_SPAN):
                to_sibling(PER_SPAN * lax.rem(chip + k, SPANS) + u).wait_send()

        def last(o, carry):
            to_home(o, False)
            return carry

        lax.fori_loop(0, CHIPS // 2, last, 0)

    swap_copy.wait()
    swap_out(swap, swapped, ((gate_ref, 0), (up_ref, 1024), (down_ref, 2048)), 1024, core)


def swap_out(swap, swapped, outs, width, core):
    mine = swap[core]
    for c in range(2):

        @pl.when(core == c)
        def _():
            for ref, at in outs:
                ref[:, c * width : (c + 1) * width] = mine[:, at : at + width]
                other = (1 - c) * width
                ref[:, other : other + width] = swapped[:, at : at + width]


def middle_part(
    x, cot, mask, gain, lambdas, sub, tiles, wo, wg, wu, wd, dout_all, q, kv, parts, logs
):
    half = (CHIPS // 2, BLOCK, 256)
    vm = pltpu.VMEM
    sem = pltpu.SemaphoreType.DMA
    return pl.pallas_call(
        middle_kernel,
        name="middle",
        out_shape=(
            shape((ROWS, D), F32),
            shape((ROWS, D), F32),
            shape((1, D), F32),
            shape((3, BLOCK, 384), BF),
            shape((2, 128), F32),
            shape((24, 2048), F32),
            shape((24, 2048), F32),
            shape((24, 2048), F32),
            shape(GATHERED_Q, BF),
            shape(GATHERED_Q, BF),
        ),
        in_specs=[VM] * 6 + [ANY] * 10,
        out_specs=(VM,) * 8 + (ANY,) * 2,
        scratch_shapes=[
            vm((3, 2, TILE, 128), BF),
            vm((D, 384), BF),
            vm((D, 1024), BF),
            vm((D, 1024), BF),
            vm((D, 1024), BF),
            vm((BLOCK, D), BF),
            vm((BLOCK, D), BF),
            vm((3, 2, TILE, 128), BF),
            vm(HALVES, BF),
            vm((2, BLOCK, 1024), BF),
            vm((2, BLOCK, 512), BF),
            vm((BLOCK, 384), BF),
            vm((SLOTS, TILE, 128), BF),
            vm(KV, BF),
            vm((SLOTS, 128, 2 * TILE), F32),
            vm((SLOTS, 1, 2 * TILE), F32),
            vm((SLOTS, TILE, 128), BF),
            vm(GATHERED, BF),
            vm((4, BLOCK, 1024), BF),
            vm((4, BLOCK, 512), BF),
            vm(GATHERED, BF),
            vm((768, 1024), BF),
            vm((768, 512), BF),
            vm((16, CHUNK, 1024), BF),
            vm((16, CHUNK, 512), BF),
            vm((2, 24, 3072), F32),
            vm((24, 3072), F32),
            vm((128, CHIPS * BLOCK), BF),
            vm((SPAN, 256), F32),
            vm((SLOTS, 128, 2 * TILE), BF),
            vm((SLOTS, 2 * TILE, 128), BF),
            vm((SLOTS, 128, TILE), BF),
            vm((SLOTS, TILE, 128), BF),
            vm((SLOTS, 2, TILE), F32),
            vm((SLOTS, 128, 2 * TILE), F32),
            vm((SLOTS, TILE, 128), BF),
            vm((2 * PER_SPAN, BLOCK, 256), BF),
            vm(half, BF),
            vm(half, BF),
            vm((3 * PER_HEAD, BLOCK, 256), BF),
            *(REDUCE_SCRATCH * 2),
            *(GATHER_SEMS * 2),
            *(RING_SEMS * 5),
            *ONCE_SEMS,
            *scatter_sems(16),
            *scatter_sems(16),
            sem((4,)),
            sem((9,)),
            sem((SLOTS,)),
            sem((3, 2)),
            sem((6,)),
            sem((SLOTS,)),
            sem((2,)),
            sem((2 * PER_SPAN,)),
            sem((CHIPS // 2,)),
            sem((CHIPS // 2,)),
            sem((3 * PER_HEAD,)),
            sem((SLOTS,)),
            sem((3, 2)),
        ],
        compiler_params=pltpu.CompilerParams(
            collective_id=1, has_side_effects=True, vmem_limit_bytes=VMEM_LIMIT
        ),
    )(x, cot, mask, gain, lambdas, sub, tiles, wo, wg, wu, wd, dout_all, q, kv, parts, logs)


def finish_kernel(
    x_ref, gain_ref, dres_ref, dqkv_ref, wq_ref, wk_ref, wv_ref,
    xnormed_ref, znormed_ref, xdres_ref, xmix_ref, ffnpart_ref, small_ref,
    grad_ref, gq_ref, gk_ref, gv_ref, go_ref, sums_ref,
    wbuf, xnormed, znormed, xdres, xmix, rq, rk, rv, pqo, pkv, sqo, skv, swap, swapped,
    vec, vecs, quarter, quarters, *rest,
):
    chip, core, t = place()
    s = 2 * chip + core
    x, z = chip % 4, chip // 8
    reduce = rest[:9]
    wsem, lsem = rest[9:11]
    rings = [
        RingGather(lambda p, k=k: dqkv_ref.at[k], land, *sems, axis, chip, core, t)
        for k, land, sems, axis in (
            (1, rk, rest[11:13], "z"), (0, rq, rest[13:15], "x"), (2, rv, rest[15:17], "z")
        )
    ]
    send_qo = Scatter(pqo, sqo, *rest[17:19], 8, 8 * x, chip // 4, chip, core, t)
    send_kv = Scatter(pkv, skv, *rest[19:21], 8, 8 * z, chip % 8, chip, core, t)
    swap_sem, asem, bsem, csem = rest[21:]
    loads = [
        weight_load(ref, wbuf.at[k], wsem.at[k], core, 384)
        for k, ref in enumerate((wq_ref, wk_ref, wv_ref))
    ]
    lefts = [
        pltpu.make_async_copy(src, dst, lsem.at[k])
        for k, (src, dst) in enumerate(
            ((xdres_ref, xdres), (xmix_ref, xmix), (xnormed_ref, xnormed), (znormed_ref, znormed))
        )
    ]
    for load in loads + lefts:
        load.start()
    greet_all(chip, core, t)
    for ring in rings:
        ring.start()
    for load in loads:
        load.wait()
    red = QuadReduce(*reduce, chip, core, t)

    def term(k):
        rows = slice(k * CW, (k + 1) * CW)
        return (
            matmul_t(dqkv_ref[0], wbuf[0, rows, :])
            + matmul_t(dqkv_ref[1], wbuf[1, rows, :])
            + matmul_t(dqkv_ref[2], wbuf[2, rows, :])
        )

    red.run(term)
    for left in lefts:
        left.wait()
    block_grad(pqo, 384, xdres, xmix[...].reshape(4 * BLOCK, 384), 384)
    x = x_ref[...]
    rms = rms_scale(x)
    hat = x * rms
    d_normed = jnp.concatenate([red.result(k) for k in range(NC)], axis=1)
    part = jnp.sum(d_normed * hat, axis=0, keepdims=True)
    vec[...] = jnp.zeros_like(vec)
    for k in range(12):
        vec[k : k + 1, :] = part[:, k * 128 : (k + 1) * 128]
        vec[12 + k : 13 + k, :] = ffnpart_ref[:, k * 128 : (k + 1) * 128]
    vec[24:26, :] = small_ref[...]
    members = ((s + 1 - 2 * core, t), (s, 1 - t), (s + 1 - 2 * core, 1 - t))
    first_sum = [
        remote(vec, vecs.at[k], asem.at[0, k], asem.at[1, k], *member)
        for k, member in enumerate(members)
    ]
    for cp in first_sum:
        cp.start()
    grad_ref[...] = dres_ref[...] + norm_back(d_normed, gain_ref[...], rms, hat)
    for cp in first_sum:
        cp.wait_recv()
    share = pl.ds(pl.multiple_of((2 * core + t) * 8, 8), 8)
    quarter[...] = (vec[share, :] + vecs[0, share, :]) + (vecs[1, share, :] + vecs[2, share, :])

    def spread(k, start):
        to = 2 * lax.rem(chip + k, CHIPS) + core
        cp = remote(quarter, quarters.at[chip], bsem.at[0, k], bsem.at[1, chip], to, t)
        if start:
            cp.start()
        else:
            cp.wait_send()

    def spread_start(k, carry):
        spread(k, True)
        return carry

    def spread_end(k, carry):
        spread(k, False)
        return carry

    own = pltpu.make_async_copy(quarter, quarters.at[chip], bsem.at[1, chip])
    own.start()
    lax.fori_loop(1, CHIPS, spread_start, 0)
    rings[1].finish()
    block_grad(pqo, 0, xnormed, rq[...].reshape(4 * BLOCK, 384), 384)
    send_qo.each(True)
    rings[0].finish()
    block_grad(pkv, 0, znormed, rk[...].reshape(4 * BLOCK, 384), 384)
    rings[2].finish()
    block_grad(pkv, 384, znormed, rv[...].reshape(4 * BLOCK, 384), 384)
    send_kv.each(True)

    def collect(k, total):
        pltpu.make_async_copy(quarter, quarters.at[k], bsem.at[1, k]).wait()
        return total + quarters[k]

    sums_ref[share, :] = lax.fori_loop(0, CHIPS, collect, jnp.zeros((8, 128), F32))
    last_sum = [
        remote(sums_ref.at[share], sums_ref.at[share], csem.at[0, k], csem.at[1, k], *member)
        for k, member in enumerate(members)
    ]
    for cp in last_sum:
        cp.start()
    for send, first in ((send_qo, (0, 3)), (send_kv, (1, 2))):
        send.wait()
        for m in range(2):
            total = send.total(0, slice(m * 384, m * 384 + 384))
            at = first[m] * 384
            for h in range(2):
                swap[h, :, at : at + 384] = total[h * 24 : h * 24 + 24]
    swap_copy = remote(
        swap.at[1 - core], swapped, swap_sem.at[0], swap_sem.at[1], s + 1 - 2 * core, t
    )
    swap_copy.start()
    for cp in last_sum:
        cp.wait()
    for cp in first_sum:
        cp.wait_send()
    lax.fori_loop(1, CHIPS, spread_end, 0)
    send_qo.each(False)
    send_kv.each(False)
    for ring in rings:
        ring.drain()
    red.drain()
    swap_copy.wait()
    outs = ((gq_ref, 0), (gk_ref, 384), (gv_ref, 768), (go_ref, 1152))
    swap_out(swap, swapped, outs, 384, core)


def finish(x, gain, dres, dqkv, wq, wk, wv, xnormed, znormed, xdres, xmix, ffn_part, small):
    return pl.pallas_call(
        finish_kernel,
        name="finish",
        out_shape=(shape((ROWS, D), F32),) + (shape((24, 768), F32),) * 4 + (shape((32, 128), F32),),
        in_specs=[VM] * 4 + [ANY] * 7 + [VM] * 2,
        out_specs=(VM,) * 6,
        scratch_shapes=[
            pltpu.VMEM((3, D, 384), BF),
            *([pltpu.VMEM(GATHERED_Q, BF)] * 7),
            pltpu.VMEM((384, 768), BF),
            pltpu.VMEM((384, 768), BF),
            pltpu.VMEM((8, CHUNK, 768), BF),
            pltpu.VMEM((8, CHUNK, 768), BF),
            pltpu.VMEM((2, 24, 1536), F32),
            pltpu.VMEM((24, 1536), F32),
            pltpu.VMEM((32, 128), F32),
            pltpu.VMEM((3, 32, 128), F32),
            pltpu.VMEM((8, 128), F32),
            pltpu.VMEM((CHIPS, 8, 128), F32),
            *REDUCE_SCRATCH,
            pltpu.SemaphoreType.DMA((3,)),
            pltpu.SemaphoreType.DMA((4,)),
            *(RING_SEMS * 3),
            *scatter_sems(8),
            *scatter_sems(8),
            pltpu.SemaphoreType.DMA((2,)),
            pltpu.SemaphoreType.DMA((2, 3)),
            pltpu.SemaphoreType.DMA((2, CHIPS)),
            pltpu.SemaphoreType.DMA((2, 3)),
        ],
        compiler_params=pltpu.CompilerParams(
            collective_id=2, has_side_effects=True, vmem_limit_bytes=VMEM_LIMIT
        ),
    )(x, gain, dres, dqkv, wq, wk, wv, xnormed, znormed, xdres, xmix, ffn_part, small)


def publish(*arrays):
    count = len(arrays)

    def kernel(*refs):
        for k in range(count):
            refs[count + k][...] = refs[k][...]

    return pl.pallas_call(
        kernel,
        name="publish",
        out_shape=tuple(shape(a.shape, a.dtype) for a in arrays),
        in_specs=[VM] * count,
        out_specs=(VM,) * count,
    )(*arrays)


def on_device(
    hidden_in, cotangent, needle_mask, attn_gain, lambdas, subln_gain, ffn_gain,
    weight_query, weight_key, weight_value, weight_out, weight_gate, weight_up, weight_down,
):
    attn_row = attn_gain.reshape(1, D)
    ffn_row = ffn_gain.reshape(1, D)
    sub_col = subln_gain.reshape(128, 1)
    mask = needle_mask.astype(F32).reshape(ROWS, 1)

    dout, q, kv, mixed, parts, logs, xnormed, znormed = forward_part(
        hidden_in, cotangent, mask, attn_row, lambdas, sub_col, weight_query, weight_key, weight_value
    )
    output, d_resid, ffn_part, dqkv, small, grad_gate, grad_up, grad_down, xmix, xdres = middle_part(
        hidden_in, cotangent, mask, ffn_row, lambdas, sub_col, mixed,
        weight_out, weight_gate, weight_up, weight_down, dout, q, kv, parts, logs,
    )
    grad_input, grad_query, grad_key, grad_value, grad_out, sums = finish(
        hidden_in, attn_row, d_resid, dqkv, weight_query, weight_key, weight_value,
        xnormed, znormed, xdres, xmix, ffn_part, small,
    )
    first_exp = jnp.exp(jnp.sum(lambdas[0] * lambdas[1], axis=-1))
    second_exp = jnp.exp(jnp.sum(lambdas[2] * lambdas[3], axis=-1))
    d_first = sums[25, :12] * first_exp
    d_second = -sums[25, :12] * second_exp
    grad_lambdas = jnp.stack(
        [
            d_first[:, None] * lambdas[1],
            d_first[:, None] * lambdas[0],
            d_second[:, None] * lambdas[3],
            d_second[:, None] * lambdas[2],
        ]
    )
    results = publish(
        output, grad_input, grad_query, grad_key, grad_value, grad_out, grad_gate, grad_up, grad_down
    )
    return (
        *results,
        sums[:12].reshape(D),
        grad_lambdas,
        sums[24],
        sums[12:24].reshape(D),
    )


def solution(mesh):
    split = P(None, "tp")
    rows = P(("seq", "tp"), None)
    both = P("seq", "tp")
    return jax.shard_map(
        on_device,
        mesh=mesh,
        in_specs=(rows, rows, P(("seq", "tp"))) + (P(),) * 4 + (split,) * 7,
        out_specs=(rows, rows) + (both,) * 7 + (P(),) * 4,
        check_vma=False,
    )
```

```python
import math

import jax
import jax.numpy as jnp
from jax import lax
from jax.experimental import pallas as pl
from jax.experimental.pallas import tpu as pltpu
from jax.sharding import PartitionSpec as P

MESH = pl.DeviceIdType.MESH
BF = jnp.bfloat16
F32 = jnp.float32
EPS = 1e-06
LAMBDA_INIT = 0.8 - 0.6 * math.exp(-3.6)
OUT_SCALE = 1.0 - LAMBDA_INIT
D = 1536
CHIPS = 32
PER_HEAD = 5
WORKERS = 15
ROWS = 64
BLOCK = 256
TILE = 128
SLOTS = 7
KB = 512
LOG2E = 1.4426950408889634
SCORE = 0.125 * LOG2E
VMEM_LIMIT = 63 * 2**20


def place():
    s = lax.axis_index("seq")
    return s // 2, s % 2, lax.axis_index("tp")


def worker(chip, core):
    x, y, z = chip % 4, chip // 4 % 2, chip // 8
    at = 4 * z + x
    return (x + y + z) % 2, at, at % PER_HEAD * 2 + core, at < WORKERS


def worker_chip(parity, at):
    x, z = at % 4, at // 4
    return (2 * z + (x + z + parity) % 2) * 4 + x


def owner_of(tile):
    step = (tile - 4) // 10
    pos = (tile - 4) % 10
    slot = jnp.where(step % 2 == 0, pos, 9 - pos)
    early = tile < 4
    return jnp.where(early, tile, slot), jnp.where(early, 0, step + 1)


def tile_of(slot, r):
    if r == 0:
        return slot
    return 4 + 10 * (r - 1) + (slot if (r - 1) % 2 == 0 else 9 - slot)


def matmul(a, b):
    return jnp.dot(a, b, preferred_element_type=F32)


def matmul_t(a, b):
    return lax.dot_general(a, b, (((1,), (1,)), ((), ())), preferred_element_type=F32)


def rms_scale(values, axis=-1):
    return lax.rsqrt(jnp.mean(values * values, axis=axis, keepdims=True) + EPS)


def norm_back(grad_normed, gain, rms, hat, axis=-1):
    scaled = grad_normed * gain
    return rms * (scaled - hat * jnp.mean(scaled * hat, axis=axis, keepdims=True))


def greet_all(chip, core, t):
    barrier = pltpu.get_barrier_semaphore()
    s = 2 * chip + core

    def greet(o, carry):
        pl.semaphore_signal(
            barrier, inc=1, device_id=(lax.rem(s + o, 2 * CHIPS), t), device_id_type=MESH
        )
        return carry

    lax.fori_loop(1, 2 * CHIPS, greet, 0)
    pl.semaphore_signal(barrier, inc=1, device_id=(s, 1 - t), device_id_type=MESH)
    pl.semaphore_wait(barrier, 2 * CHIPS)


def remote(src, dst, send_sem, recv_sem, s, t):
    return pltpu.make_async_remote_copy(
        src_ref=src,
        dst_ref=dst,
        send_sem=send_sem,
        recv_sem=recv_sem,
        device_id=(s, t),
        device_id_type=MESH,
    )


def rows_at(ref, start, count):
    return ref.at[pl.ds(pl.multiple_of(start, ROWS), count)]


class QuadGather:
    def __init__(self, buf, send, recv, chip, core, t):
        self.buf, self.send, self.recv = buf, send, recv
        self.chip, self.core, self.t = chip, core, t
        mine = core * 128 + t * ROWS
        self.mine = mine
        self.near = core * 128 + (1 - t) * ROWS
        sib = (2 * chip + 1 - core, t)
        self.to_near = self.copy(mine, 0, (2 * chip + core, 1 - t))
        self.to_sib = self.copy(mine, 1, sib)
        self.forward = self.copy(self.near, 2, sib)

    def copy(self, row, k, target):
        view = rows_at(self.buf, row, ROWS)
        return remote(view, view, self.send.at[k], self.recv.at[k], *target)

    def start(self):
        self.to_near.start()
        self.to_sib.start()

    def finish(self):
        self.to_near.wait_recv()
        self.forward.start()
        self.to_sib.wait_recv()
        self.forward.wait_recv()

    def drain(self):
        self.to_near.wait_send()
        self.to_sib.wait_send()
        self.forward.wait_send()


class RingGather:
    def __init__(self, pieces, land, send, recv, axis, chip, core, t):
        at = chip % 4 if axis == "x" else chip // 8
        self.local = pltpu.make_async_copy(pieces(at), land.at[at], recv.at[at])
        self.copies = []
        for k in (1, 3, 2):
            if axis == "x":
                peer, chip_to = (at + k) % 4, chip - at + (at + k) % 4
            else:
                peer, chip_to = (at + k) % 4, (chip + 8 * k) % CHIPS
            self.copies.append(
                remote(pieces(peer), land.at[at], send.at[k - 1], recv.at[at], 2 * chip_to + core, t)
            )
        self.waits = [
            pltpu.make_async_copy(pieces(at), land.at[k], recv.at[k]) for k in range(4)
        ]

    def start(self):
        self.local.start()
        for cp in self.copies:
            cp.start()

    def finish(self):
        for cp in self.waits:
            cp.wait()

    def drain(self):
        for cp in self.copies:
            cp.wait_send()


class RingGatherOnce:
    def __init__(self, pieces, land, send, recv, pass_send, pass_recv, axis, chip, core, t):
        at = chip % 4 if axis == "x" else chip // 8
        self.mine = pl.ds(pl.multiple_of(core * 128, 128), 128)
        self.local = pltpu.make_async_copy(pieces(at), land.at[at], recv.at[0])
        self.local_at = at
        self.copies, self.passes = [], []
        for k in (1, 3, 2):
            peer = (at + k) % 4
            chip_to = chip - at + peer if axis == "x" else (chip + 8 * k) % CHIPS
            self.copies.append(
                remote(
                    pieces(peer).at[self.mine], land.at[at, self.mine],
                    send.at[k - 1], recv.at[4 - k], 2 * chip_to + core, t,
                )
            )
            view = land.at[peer, self.mine]
            self.passes.append(
                (
                    pltpu.make_async_copy(pieces(at).at[self.mine], view, recv.at[k]),
                    remote(view, view, pass_send.at[k - 1], pass_recv.at[k - 1], 2 * chip + 1 - core, t),
                )
            )

    def start(self):
        self.local.start()
        for cp in self.copies:
            cp.start()

    def forward(self):
        for arrive, cp in self.passes:
            arrive.wait()
            cp.start()

    def finish(self):
        self.local.wait()
        for _, cp in self.passes:
            cp.wait_recv()

    def drain(self):
        for cp in self.copies:
            cp.wait_send()
        for _, cp in self.passes:
            cp.wait_send()


ONCE_SEMS = [
    pltpu.SemaphoreType.DMA((3,)),
    pltpu.SemaphoreType.DMA((4,)),
    pltpu.SemaphoreType.DMA((3,)),
    pltpu.SemaphoreType.DMA((3,)),
]
RING_SEMS = [pltpu.SemaphoreType.DMA((3,)), pltpu.SemaphoreType.DMA((4,))]


def block_grad(dst, start, left, right, step, at=0, total=768):
    width = right.shape[1]

    def one(m, carry):
        cols = pl.ds(pl.multiple_of(m * step, 128), step)
        part = left[:, :, pl.ds(pl.multiple_of(at + m * step, 128), step)].reshape(4 * BLOCK, step)
        dst[cols, start : start + width] = lax.dot_general(
            part, right, (((0,), (0,)), ((), ())), preferred_element_type=F32
        ).astype(BF)
        return carry

    lax.fori_loop(0, total // step, one, 0)


CHUNK = 48


class Scatter:
    def __init__(self, part, land, send, recv, count, first, spot, chip, core, t):
        self.part, self.land, self.send, self.recv = part, land, send, recv
        self.count, self.first, self.spot = count, first, spot
        self.chip, self.core, self.t = chip, core, t

    def source(self, i):
        return self.part.at[pl.ds(pl.multiple_of(i * CHUNK, 16), CHUNK)]

    def each(self, start):
        self.some(0, self.count, start)

    def some(self, first, end, start):
        def one(o, carry):
            i = lax.rem(self.chip + 1 + 3 * o, self.count)
            owner = self.first + i
            cp = remote(
                self.source(i), self.land.at[self.spot], self.send.at[i], self.recv.at[self.spot],
                2 * owner + self.core, self.t,
            )
            if start:

                @pl.when(owner == self.chip)
                def _():
                    pltpu.make_async_copy(
                        self.source(i), self.land.at[self.spot], self.recv.at[self.spot]
                    ).start()

            @pl.when(owner != self.chip)
            def _():
                if start:
                    cp.start()
                else:
                    cp.wait_send()

            return carry

        lax.fori_loop(first, end, one, 0)

    def wait(self):
        def one(k, carry):
            pltpu.make_async_copy(self.source(0), self.land.at[k], self.recv.at[k]).wait()
            return carry

        lax.fori_loop(0, self.count, one, 0)

    def total(self, b, cols):
        def one(k, carry):
            return carry + self.land[8 * b + k, :, cols].astype(F32)

        return lax.fori_loop(0, 8, one, jnp.zeros((CHUNK, cols.stop - cols.start), F32))


def scatter_sems(count):
    return [pltpu.SemaphoreType.DMA((count,)), pltpu.SemaphoreType.DMA((count,))]


GATHER_SEMS = [pltpu.SemaphoreType.DMA((3,)), pltpu.SemaphoreType.DMA((3,))]
CW = 512
NC = D // CW


class QuadReduce:
    def __init__(self, part, dsend, drecv, ysend, yrecv, ds, dr, ys, yr, chip, core, t):
        self.part, self.dsend, self.drecv = part, dsend, drecv
        self.ysend, self.yrecv = ysend, yrecv
        self.core, self.t = core, t
        self.d = [
            remote(dsend.at[k], drecv.at[k], ds.at[k], dr.at[k], 2 * chip + 1 - core, t)
            for k in range(NC)
        ]
        self.y = [
            remote(ysend.at[k], yrecv.at[k], ys.at[k], yr.at[k], 2 * chip + core, 1 - t)
            for k in range(NC)
        ]

    def rows(self, start, count, k):
        return self.part[pl.ds(pl.multiple_of(start, ROWS), count), k * CW : (k + 1) * CW]

    def put(self, k, value):
        self.part[:, k * CW : (k + 1) * CW] = value
        self.dsend[k] = self.rows((1 - self.core) * 128, 128, k).astype(BF)
        self.d[k].start()

    def middle(self, k):
        self.d[k].wait_recv()
        near = (1 - self.t) * ROWS
        far = self.rows(self.core * 128 + near, ROWS, k)
        got = self.drecv[k, pl.ds(pl.multiple_of(near, ROWS), ROWS), :]
        self.ysend[k] = (far + got.astype(F32)).astype(BF)
        self.y[k].start()

    def result(self, k):
        mine = self.t * ROWS
        own = self.rows(self.core * 128 + mine, ROWS, k)
        got = self.drecv[k, pl.ds(pl.multiple_of(mine, ROWS), ROWS), :].astype(F32)
        self.y[k].wait_recv()
        return own + got + self.yrecv[k].astype(F32)

    def run(self, term):
        for k in range(NC):
            self.put(k, term(k))
            if k:
                self.middle(k - 1)
        self.middle(NC - 1)

    def drain(self):
        for k in range(NC):
            self.d[k].wait_send()
            self.y[k].wait_send()


REDUCE_SCRATCH = [
    pltpu.VMEM((BLOCK, D), F32),
    pltpu.VMEM((NC, 128, CW), BF),
    pltpu.VMEM((NC, 128, CW), BF),
    pltpu.VMEM((NC, ROWS, CW), BF),
    pltpu.VMEM((NC, ROWS, CW), BF),
] + [pltpu.SemaphoreType.DMA((NC,))] * 4


def tile_sends(tiles, land, send, recv, chip, core, t, start):
    s = 2 * chip + core
    for j in range(3):
        for u in range(2):
            slot, index = owner_of(2 * chip + u)
            target = 2 * worker_chip(core, j * PER_HEAD + slot // 2) + slot % 2
            k = j * 2 + u

            if start:

                @pl.when(target == s)
                def _():
                    pltpu.make_async_copy(tiles.at[j, u], land.at[index], recv.at[index]).start()

            @pl.when(target != s)
            def _():
                cp = remote(tiles.at[j, u], land.at[index], send.at[k], recv.at[index], target, t)
                if start:
                    cp.start()
                else:
                    cp.wait_send()


def tile_waits(tiles, land, send, recv, chip, core, t):
    _, _, slot, served = worker(chip, core)
    for r in range(SLOTS):
        here = served
        if r == 0:
            here = jnp.logical_and(here, slot < 4)

        @pl.when(here)
        def _():
            pltpu.make_async_copy(tiles.at[0, 0], land.at[r], recv.at[r]).wait()


def home_sends(tiles, land, send, recv, chip, core, t, start):
    s = 2 * chip + core
    parity, at, slot, served = worker(chip, core)
    for r in range(SLOTS):
        here = served
        if r == 0:
            here = jnp.logical_and(here, slot < 4)
        tile = tile_of(slot, r)
        target = (tile // 2) * 2 + parity
        j, u = at // PER_HEAD, tile % 2

        if start:

            @pl.when(jnp.logical_and(here, target == s))
            def _():
                pltpu.make_async_copy(tiles.at[r], land.at[j, u], recv.at[j, u]).start()

        @pl.when(jnp.logical_and(here, target != s))
        def _():
            cp = remote(tiles.at[r], land.at[j, u], send.at[r], recv.at[j, u], target, t)
            if start:
                cp.start()
            else:
                cp.wait_send()


def home_waits(tiles, land, recv):
    for j in range(3):
        for u in range(2):
            pltpu.make_async_copy(tiles.at[0], land.at[j, u], recv.at[j, u]).wait()


def weight_load(ref, buf, sem, core, width):
    return pltpu.make_async_copy(
        ref.at[:, pl.ds(pl.multiple_of(core * width, 128), width)], buf, sem
    )


def pieces_out(buf, ref, sem, first, count):
    width = D // count
    copies = [
        pltpu.make_async_copy(
            buf.at[:, a * width : (a + 1) * width], ref.at[a], sem.at[first + a]
        )
        for a in range(count)
    ]
    for cp in copies:
        cp.start()
    return copies


VM = pl.BlockSpec(memory_space=pltpu.VMEM)
ANY = pl.BlockSpec(memory_space=pl.ANY)


def shape(dims, dtype):
    return jax.ShapeDtypeStruct(dims, dtype)


HALVES = (2, BLOCK, 768)
QUARTERS = (4, BLOCK, 384)
GATHERED = (4, BLOCK, 768)
GATHERED_Q = (4, BLOCK, 384)
KV = (CHIPS, BLOCK, 256)
STEP = 2048


def eye(size):
    row = lax.broadcasted_iota(jnp.int32, (size, size), 0)
    col = lax.broadcasted_iota(jnp.int32, (size, size), 1)
    return jnp.where(row == col, 1.0, 0.0).astype(BF)


def both_maps(q_t):
    top = lax.broadcasted_iota(jnp.int32, q_t.shape, 0) < 64
    return jnp.concatenate([jnp.where(top, q_t, 0.0), jnp.where(top, 0.0, q_t)], axis=1)


def key_mask(start, count, tile, width):
    key = start + lax.broadcasted_iota(jnp.int32, (count, width), 0)
    query = tile * TILE + lax.broadcasted_iota(jnp.int32, (count, width), 1) % TILE
    return key <= query


def group_norm(parts, lam):
    first, second = parts[:, :TILE], parts[:, TILE:]
    differ = first - lam * second
    rms = rms_scale(differ, 0)
    return rms, differ * rms


def long_row(ref):
    return jnp.concatenate([ref[k : k + 1, :] for k in range(12)], axis=1)


def as_column(row):
    return jnp.broadcast_to(row, (128, 128)).T


def mask_column(mask_ref):
    mask = mask_ref[...].astype(F32)
    return as_column(jnp.concatenate([mask, mask], axis=1))[:ROWS, :1]


def lambda_parts(lambdas_ref):
    vectors = [lambdas_ref[:, k, :] for k in range(4)]
    first = jnp.exp(jnp.sum(vectors[0] * vectors[1], axis=-1, keepdims=True))
    second = jnp.exp(jnp.sum(vectors[2] * vectors[3], axis=-1, keepdims=True))
    return vectors, first, second


def lambda_of(lambdas_ref, head):
    _, first, second = lambda_parts(lambdas_ref)
    every = first - second + LAMBDA_INIT
    mine = lax.broadcasted_iota(jnp.int32, every.shape, 0) == head
    return jnp.sum(jnp.where(mine, every, 0.0), axis=0, keepdims=True)


def forward_kernel(
    x_ref, cot_ref, mask_ref, attn_ref, sub_ref, lambdas_ref, wq_ref, wk_ref, wv_ref,
    dout_ref, normed_ref, q_ref, kv_ref, mixed_ref, parts_ref, log_ref,
    nbuf, obuf, wbuf, kvsrc, qsrc, kv, q, v_t, peaks, kmax, acc, total,
    wsem, nsend, nrecv, osend, orecv, kvsend, kvrecv, fsend, qsend, qrecv, osem,
):
    chip, core, t = place()
    s = 2 * chip + core
    parity, place_at, slot, served = worker(chip, core)
    loads = [
        weight_load(ref, wbuf.at[k], wsem.at[k], core, 384)
        for k, ref in enumerate((wk_ref, wv_ref, wq_ref))
    ]
    for load in loads:
        load.start()
    x = x_ref[...]
    normed = (x * rms_scale(x) * long_row(attn_ref)).astype(BF)
    quad = QuadGather(nbuf, nsend, nrecv, chip, core, t)
    mine = pl.ds(pl.multiple_of(quad.mine, ROWS), ROWS)
    nbuf[mine, :] = normed
    quad_o = QuadGather(obuf, osend, orecv, chip, core, t)
    greet_all(chip, core, t)
    quad.start()
    obuf[mine, :] = (cot_ref[...] * mask_column(mask_ref)).astype(BF)
    lam = lambda_of(lambdas_ref, 6 * t + 3 * parity + place_at // PER_HEAD)
    sub = as_column(sub_ref[...])
    unit = eye(256)
    quad.finish()
    for k in range(2):
        loads[k].wait()
        value = matmul(nbuf[...], wbuf[k]).astype(BF)
        for j in range(3):
            kvsrc[j, :, k * 128 : (k + 1) * 128] = value[:, j * 128 : (j + 1) * 128]

    def kv_sends(start):
        def one(o, carry):
            w = lax.rem(chip + 7 * o, WORKERS)
            j = w // PER_HEAD
            target = 2 * worker_chip(core, w) + chip % 2
            if start:

                @pl.when(target == s)
                def _():
                    pltpu.make_async_copy(kvsrc.at[j], kv.at[chip], kvrecv.at[chip]).start()

            @pl.when(target != s)
            def _():
                cp = remote(kvsrc.at[j], kv.at[chip], kvsend.at[w], kvrecv.at[chip], target, t)
                if start:
                    cp.start()
                else:
                    cp.wait_send()

            return carry

        lax.fori_loop(0, WORKERS, one, 0)

    kv_sends(True)
    saves = pieces_out(nbuf, normed_ref, osem, 5, 4)
    loads[2].wait()
    value = matmul(nbuf[...], wbuf[2]).astype(BF)
    for j in range(3):
        for u in range(2):
            qsrc[j, u] = value[u * 128 : (u + 1) * 128, j * 128 : (j + 1) * 128]
    tile_sends(qsrc, q, qsend, qrecv, chip, core, t, True)
    quad_o.start()

    def forward(o):
        source = lax.rem((chip // 2 + o) * 2 + core, CHIPS)
        view = kv.at[source]
        return source, remote(view, view, fsend.at[o], kvrecv.at[source], s + 1 - 2 * core, t)

    def turn(source):
        block = kv[source]
        at = pl.ds(pl.multiple_of(source * BLOCK, BLOCK), BLOCK)
        turned = matmul_t(unit, block)
        v_t[:, at] = turned[128:].astype(BF)
        square = turned[:128] * turned[:128]
        for m in range(2):
            largest = jnp.sum(square[64 * m : 64 * m + 64], axis=0, keepdims=True)
            peaks[m : m + 1, :] = jnp.maximum(peaks[m : m + 1, :], largest)

    @pl.when(served)
    def _():
        peaks[...] = jnp.zeros_like(peaks)

        def take(o, carry):
            source, cp = forward(o)
            pltpu.make_async_copy(kvsrc.at[0], kv.at[source], kvrecv.at[source]).wait()
            cp.start()
            turn(source)
            return carry

        lax.fori_loop(0, CHIPS // 2, take, 0)

        def finish(o, carry):
            source = lax.rem((chip // 2 + o) * 2 + 1 - core, CHIPS)
            pltpu.make_async_copy(kvsrc.at[0], kv.at[source], kvrecv.at[source]).wait()
            forward(o)[1].wait_send()
            turn(source)
            return carry

        lax.fori_loop(0, CHIPS // 2, finish, 0)
        for m in range(2):
            kmax[m] = jnp.max(peaks[m : m + 1, :])

    quad_o.finish()
    saves += pieces_out(obuf, dout_ref, osem, 0, 2)
    tile_waits(qsrc, q, qsend, qrecv, chip, core, t)
    def keep():
        return [
            pltpu.make_async_copy(kv, kv_ref, osem.at[2]),
            pltpu.make_async_copy(q.at[pl.ds(1, SLOTS - 1)], q_ref.at[pl.ds(1, SLOTS - 1)], osem.at[3]),
        ]

    def keep_early():
        return pltpu.make_async_copy(q.at[0], q_ref.at[0], osem.at[4])

    @pl.when(served)
    def _():
        for cp in keep():
            cp.start()

    @pl.when(jnp.logical_and(served, slot < 4))
    def _():
        keep_early().start()

    for r in range(SLOTS):
        tile = tile_of(slot, r)

        @pl.when(served if r else jnp.logical_and(served, slot < 4))
        def _():
            q_t = q[r].astype(F32).T
            square = q_t * q_t
            bound = SCORE * jnp.concatenate(
                [
                    jnp.sqrt(jnp.sum(square[:64], axis=0, keepdims=True) * kmax[0]),
                    jnp.sqrt(jnp.sum(square[64:], axis=0, keepdims=True) * kmax[1]),
                ],
                axis=1,
            )
            q_both = both_maps(q_t).astype(BF)
            acc[...] = jnp.zeros_like(acc)
            total[...] = jnp.zeros_like(total)

            def step(b, masked):
                sums, out = None, None
                for u in range(STEP // KB):
                    start = pl.multiple_of(b * STEP + u * KB, KB)
                    pair = pl.ds(b * (STEP // BLOCK) + u * (KB // BLOCK), KB // BLOCK)
                    score = matmul(kv[pair, :, :128].reshape(KB, 128), q_both)
                    prob = jnp.exp2(score * SCORE - bound)
                    if masked:
                        prob = jnp.where(key_mask(start, KB, tile, 2 * TILE), prob, 0.0)
                    part = jnp.sum(prob.reshape(KB // 8, 8, 2 * TILE), axis=0)
                    term = matmul(v_t[:, pl.ds(start, KB)], prob.astype(BF))
                    sums = part if sums is None else sums + part
                    out = term if out is None else out + term
                total[...] += sums
                acc[...] += out

            full = tile * TILE // STEP

            def body(b, carry):
                step(b, False)
                return carry

            lax.fori_loop(0, full, body, 0)
            step(full, True)
            whole = jnp.sum(total[...], axis=0, keepdims=True)
            parts = acc[...] / whole
            parts_ref[r] = parts
            log_ref[r] = bound + jnp.log(whole) * LOG2E
            rms, hat = group_norm(parts, lam)
            mixed_ref[r] = (hat * sub * OUT_SCALE).T.astype(BF)

    kv_sends(False)
    tile_sends(qsrc, q, qsend, qrecv, chip, core, t, False)
    quad.drain()
    quad_o.drain()
    for save in saves:
        save.wait()

    @pl.when(served)
    def _():
        for cp in keep():
            cp.wait()

    @pl.when(jnp.logical_and(served, slot < 4))
    def _():
        keep_early().wait()


def forward_part(x, cot, mask, attn, sub, lambdas, wq, wk, wv):
    return pl.pallas_call(
        forward_kernel,
        name="forward",
        out_shape=(
            shape(HALVES, BF),
            shape(QUARTERS, BF),
            shape((SLOTS, TILE, 128), BF),
            shape(KV, BF),
            shape((SLOTS, TILE, 128), BF),
            shape((SLOTS, 128, 2 * TILE), F32),
            shape((SLOTS, 1, 2 * TILE), F32),
        ),
        in_specs=[VM] * 6 + [ANY] * 3,
        out_specs=(ANY, ANY, ANY, ANY, VM, VM, VM),
        scratch_shapes=[
            pltpu.VMEM((BLOCK, D), BF),
            pltpu.VMEM((BLOCK, D), BF),
            pltpu.VMEM((3, D, 384), BF),
            pltpu.VMEM((3, BLOCK, 256), BF),
            pltpu.VMEM((3, 2, TILE, 128), BF),
            pltpu.VMEM(KV, BF),
            pltpu.VMEM((SLOTS, TILE, 128), BF),
            pltpu.VMEM((128, CHIPS * BLOCK), BF),
            pltpu.VMEM((8, BLOCK), F32),
            pltpu.SMEM((2,), F32),
            pltpu.VMEM((128, 2 * TILE), F32),
            pltpu.VMEM((8, 2 * TILE), F32),
            pltpu.SemaphoreType.DMA((3,)),
            *(GATHER_SEMS * 2),
            pltpu.SemaphoreType.DMA((15,)),
            pltpu.SemaphoreType.DMA((CHIPS,)),
            pltpu.SemaphoreType.DMA((CHIPS // 2,)),
            pltpu.SemaphoreType.DMA((6,)),
            pltpu.SemaphoreType.DMA((SLOTS,)),
            pltpu.SemaphoreType.DMA((9,)),
        ],
        compiler_params=pltpu.CompilerParams(
            collective_id=0, has_side_effects=True, vmem_limit_bytes=VMEM_LIMIT
        ),
    )(x, cot, mask, attn, sub, lambdas, wq, wk, wv)


SPAN = 1024
SPANS = CHIPS * BLOCK // SPAN
PER_SPAN = SPAN // BLOCK // 2
EARLY_SPANS = 3


def middle_kernel(
    x_ref, cot_ref, mask_ref, attn_ref, ffn_ref, sub_ref, lambdas_ref, tiles_ref,
    wq_ref, wk_ref, wv_ref, wo_ref, wg_ref, wu_ref, wd_ref,
    dout_ref, normed_ref, q_ref, kv_ref, parts_ref, log_ref,
    out_ref, grad_ref, gq_ref, gk_ref, gv_ref, go_ref, gate_ref, up_ref, down_ref, sums_ref,
    xnormed_ref, znormed_ref,
    dres, dqkv_ref, rq, rk, rv, xmix, xdres, pqo, pkv, sqo, skv, swap2, swapped2,
    vec, vecs, quarter, quarters,
    land, wo, wg, wu, wd, fbuf, rbuf, dms, dout_all, dgate, dup, hid, mix,
    q, kv, parts_all, logs, dmix,
    lffn, lgate, lup, lhid, ldout, pgate, pup, pdown, sgate, sup, sdown, swap, swapped,
    k_t, acc, q_cols, q_rows, d_cols, d_rows, deltas, dq_acc, dq_out, given, sib, both, home, *rest,
):
    chip, core, t = place()
    s = 2 * chip + core
    parity, place_at, slot, served = worker(chip, core)
    head = 3 * parity + place_at // PER_HEAD
    x_at, z_at = chip % 4, chip // 8
    taken = iter(rest)

    def take(count):
        return [next(taken) for _ in range(count)]

    reduces = [take(9) for _ in range(2)]
    gather_sems = [take(2) for _ in range(2)]
    ring_sems = [take(2) for _ in range(11)]
    once_sems = take(4)
    scatter = [take(2) for _ in range(5)]
    wsem, osem, hsend, hrecv, tsend, trecv, swap_sem = take(7)
    dsend, drecv, ksend, krecv, gsend, grecv = take(6)
    w2sem, lsem, swap2_sem, asem, bsem, csem = take(6)

    loads = [
        weight_load(wo_ref, wo, wsem.at[0], core, 384),
        weight_load(wg_ref, wg, wsem.at[1], core, 1024),
        weight_load(wu_ref, wu, wsem.at[2], core, 1024),
        weight_load(wd_ref, wd, wsem.at[3], core, 1024),
    ]
    fetches = [
        pltpu.make_async_copy(src, dst, osem.at[4 + k])
        for k, (src, dst) in enumerate(
            ((dout_ref, dout_all), (q_ref, q), (kv_ref, kv), (parts_ref, parts_all), (log_ref, logs))
        )
    ]
    loads[0].start()
    fetches[0].start()
    for load in loads[1:]:
        load.start()
    for fetch in fetches[1:]:
        fetch.start()
    gather_f = QuadGather(fbuf, *gather_sems[0], chip, core, t)
    gather_r = QuadGather(rbuf, *gather_sems[1], chip, core, t)
    ring_dout = RingGather(lambda p: dout_all.at[p // 2], ldout, *ring_sems[0], "x", chip, core, t)
    ring_mix = RingGather(lambda p: mix, xmix, *ring_sems[1], "x", chip, core, t)
    ring_hid = RingGather(lambda p: hid.at[p % 2], lhid, *ring_sems[2], "x", chip, core, t)
    ring_gate = RingGather(lambda p: dgate.at[p % 2], lgate, *ring_sems[3], "z", chip, core, t)
    ring_up = RingGather(lambda p: dup.at[p % 2], lup, *ring_sems[10], "z", chip, core, t)
    ring_dres = RingGather(
        lambda p: rbuf.at[:, pl.ds(pl.multiple_of(p * 384, 128), 384)],
        xdres, *ring_sems[4], "x", chip, core, t,
    )
    ring_xn = RingGather(lambda p: normed_ref.at[p], xnormed_ref, *ring_sems[5], "x", chip, core, t)
    ring_zn = RingGather(lambda p: normed_ref.at[p], znormed_ref, *ring_sems[6], "z", chip, core, t)
    ring_q = RingGather(lambda p: dqkv_ref.at[0], rq, *ring_sems[7], "x", chip, core, t)
    ring_k = RingGather(lambda p: dqkv_ref.at[1], rk, *ring_sems[8], "z", chip, core, t)
    ring_v = RingGather(lambda p: dqkv_ref.at[2], rv, *ring_sems[9], "z", chip, core, t)
    send_qo = Scatter(pqo, sqo, *scatter[2], 8, 8 * x_at, chip // 4, chip, core, t)
    send_kv = Scatter(pkv, skv, *scatter[3], 8, 8 * z_at, chip % 8, chip, core, t)
    members = ((s + 1 - 2 * core, t), (s, 1 - t), (s + 1 - 2 * core, 1 - t))
    ring_ffn = RingGatherOnce(
        lambda p: fbuf.at[:, pl.ds(pl.multiple_of((p // 2) * 768, 128), 768)],
        lffn, *once_sems, "z", chip, core, t,
    )
    send_down = Scatter(
        pdown, sdown, *scatter[0], 16, 16 * (x_at // 2), 8 * (x_at % 2) + chip // 4, chip, core, t
    )
    send_gate, send_up = (
        Scatter(
            part, to, *sems, 16, 16 * (z_at // 2), 8 * (z_at % 2) + chip % 8, chip, core, t
        )
        for part, to, sems in ((pgate, sgate, scatter[1]), (pup, sup, scatter[4]))
    )
    mine = pl.ds(pl.multiple_of(gather_f.mine, ROWS), ROWS)
    dout = cot_ref[...] * mask_column(mask_ref)
    lam = lambda_of(lambdas_ref, 6 * t + head)
    sub = as_column(sub_ref[...])
    ffn_gain = long_row(ffn_ref)
    vec[...] = jnp.zeros_like(vec)
    greet_all(chip, core, t)
    home_sends(tiles_ref, land, hsend, hrecv, chip, core, t, True)
    ring_zn.start()
    ring_xn.start()
    loads[0].wait()
    home_waits(tiles_ref, land, hrecv)
    for j in range(3):
        for u in range(2):
            mix[u * 128 : (u + 1) * 128, j * 128 : (j + 1) * 128] = land[j, u]
    red = QuadReduce(*reduces[0], chip, core, t)
    red.run(lambda k: matmul_t(mix[...], wo[k * CW : (k + 1) * CW, :]))
    fetches[0].wait()
    ring_dout.start()
    ring_mix.start()
    resid = x_ref[...] + jnp.concatenate([red.result(k) for k in range(NC)], axis=1)
    ffn_rms = rms_scale(resid)
    ffn_hat = resid * ffn_rms
    fbuf[mine, :] = (ffn_hat * ffn_gain).astype(BF)
    gather_f.start()
    for load in loads[1:]:
        load.wait()
    red.drain()
    gather_f.finish()
    ring_ffn.start()

    def hidden_step(n, carry):
        cols = pl.ds(pl.multiple_of(n * 256, 256), 256)
        b, at = n // 2, n % 2
        gate = matmul(fbuf[...], wg[:, cols])
        up = matmul(fbuf[...], wu[:, cols])
        d_hidden = matmul(dout_all[0], wd[:768, cols]) + matmul(dout_all[1], wd[768:, cols])
        sig = 1.0 / (1.0 + jnp.exp(-gate))
        silu = gate * sig
        to = pl.ds(pl.multiple_of(at * 256, 256), 256)
        hid[b, :, to] = (silu * up).astype(BF)
        dgate[b, :, to] = (d_hidden * up * sig * (1.0 + gate * (1.0 - sig))).astype(BF)
        dup[b, :, to] = (d_hidden * silu).astype(BF)
        return carry

    lax.fori_loop(0, 4, hidden_step, 0)
    ring_gate.start()
    ring_hid.start()
    red2 = QuadReduce(*reduces[0], chip, core, t)

    def ffn_term(k):
        rows = slice(k * CW, (k + 1) * CW)
        return (
            matmul_t(dgate[0], wg[rows, :512])
            + matmul_t(dgate[1], wg[rows, 512:])
            + matmul_t(dup[0], wu[rows, :512])
            + matmul_t(dup[1], wu[rows, 512:])
        )

    red2.run(ffn_term)
    late_loads = [
        weight_load(ref, buf.at[:, k * 384 : (k + 1) * 384], w2sem.at[i], core, 384)
        for i, (ref, buf, k) in enumerate(((wq_ref, wg, 0), (wk_ref, wg, 1), (wv_ref, wu, 0)))
    ]
    for load in late_loads:
        load.start()
    red3 = QuadReduce(*reduces[1], chip, core, t)
    d_ffn = jnp.concatenate([red2.result(k) for k in range(NC)], axis=1)
    part = jnp.sum(d_ffn * ffn_hat, axis=0, keepdims=True)
    for k in range(12):
        vec[12 + k : 13 + k, :] = part[:, k * 128 : (k + 1) * 128]
    d_resid = dout + norm_back(d_ffn, ffn_gain, ffn_rms, ffn_hat)
    dres[...] = d_resid
    rbuf[mine, :] = d_resid.astype(BF)
    gather_r.start()
    ring_ffn.forward()
    red3.run(
        lambda k: matmul_t(hid[0], wd[k * CW : (k + 1) * CW, :512])
        + matmul_t(hid[1], wd[k * CW : (k + 1) * CW, 512:])
    )
    gather_r.finish()
    d_mixed = matmul(rbuf[...], wo[...]).astype(BF)
    for j in range(3):
        for u in range(2):
            dms[j, u] = d_mixed[u * 128 : (u + 1) * 128, j * 128 : (j + 1) * 128]
    tile_sends(dms, dmix, tsend, trecv, chip, core, t, True)
    ring_up.start()
    ring_dres.start()
    out_ref[...] = resid + jnp.concatenate([red3.result(k) for k in range(NC)], axis=1)
    for fetch in fetches[1:]:
        fetch.wait()

    def to_sibling(o):
        at = o % (2 * PER_SPAN)
        return remote(given.at[at], sib.at[o], dsend.at[at], drecv.at[o], s + 1 - 2 * core, t)

    def to_home(o, start):
        target = 2 * (2 * o + core) + parity
        spot = place_at
        if start:

            @pl.when(target == s)
            def _():
                pltpu.make_async_copy(both.at[o], home.at[spot], krecv.at[spot]).start()

        @pl.when(target != s)
        def _():
            cp = remote(both.at[o], home.at[spot], ksend.at[o], krecv.at[spot], target, t)
            if start:
                cp.start()
            else:
                cp.wait_send()

    def tile_at(r):
        late = 4 + 10 * (r - 1) + jnp.where((r - 1) % 2 == 0, slot, 9 - slot)
        return jnp.where(r == 0, slot, late)

    @pl.when(served)
    def _():
        unit = eye(128)

        def flip(b, carry):
            rows = pl.ds(pl.multiple_of(b * KB, KB), KB)
            block = kv[pl.ds(2 * b, 2), :, :128].reshape(KB, 128)
            k_t[:, rows] = matmul_t(unit, block).astype(BF)
            return carry

        lax.fori_loop(0, CHIPS * BLOCK // KB, flip, 0)

    ring_dout.finish()
    ring_hid.finish()
    block_grad(pdown, 0, ldout, lhid[...].reshape(4 * BLOCK, 512), 256)
    ring_xn.finish()
    ring_zn.finish()
    lefts = [
        pltpu.make_async_copy(src, ldout.at[:, :, k * 384 : (k + 1) * 384], lsem.at[k])
        for k, src in enumerate((xnormed_ref, znormed_ref))
    ]
    for left in lefts:
        left.start()
    tile_waits(dms, dmix, tsend, trecv, chip, core, t)
    send_down.each(True)
    ring_ffn.finish()
    ring_gate.finish()
    block_grad(pgate, 0, lffn, lgate[...].reshape(4 * BLOCK, 512), 256)

    for r in range(SLOTS):

        @pl.when(served if r else jnp.logical_and(served, slot < 4))
        def _():
            q_wide = q[r].astype(F32)
            q_cols[r] = both_maps(q_wide.T).astype(BF)
            left = lax.broadcasted_iota(jnp.int32, q_wide.shape, 1) < 64
            q_rows[r] = jnp.concatenate(
                [jnp.where(left, q_wide, 0.0), jnp.where(left, 0.0, q_wide)], axis=0
            ).astype(BF)
            parts = parts_all[r]
            first, second = parts[:, :TILE], parts[:, TILE:]
            rms, hat = group_norm(parts, lam)
            e_t = dmix[r].astype(F32).T * OUT_SCALE
            column = jnp.sum(e_t * hat, axis=1, keepdims=True)
            d_differ = norm_back(e_t, sub, rms, hat, 0).astype(BF)
            d_wide = d_differ.astype(F32)
            d_cols[r] = d_differ
            d_rows[r] = d_wide.T.astype(BF)
            second_dot = jnp.sum(d_wide * second, axis=0, keepdims=True)
            row = lax.broadcasted_iota(jnp.int32, (128, 128), 0)
            lane = lax.broadcasted_iota(jnp.int32, (128, 128), 1)
            vec[24:25, :] += jnp.sum(jnp.where(row == lane, column, 0.0), axis=0, keepdims=True)
            here = lax.broadcasted_iota(jnp.int32, (1, 128), 1) == 6 * t + head
            vec[25:26, :] -= jnp.where(here, jnp.sum(second_dot, axis=1, keepdims=True), 0.0)
            deltas[r, 0:1, :] = jnp.sum(d_wide * first, axis=0, keepdims=True)
            deltas[r, 1:2, :] = -lam * second_dot
            dq_acc[r] = jnp.zeros((128, 2 * TILE), F32)

    def pass_on(k):
        for u in range(PER_SPAN):
            o = PER_SPAN * lax.rem(chip + k, SPANS) + u
            to_sibling(o).wait_recv()
            both[o] = (both[o].astype(F32) + sib[o].astype(F32)).astype(BF)
            to_home(o, True)

    def span(k, carry):
        b = lax.rem(chip + k, SPANS)
        start = pl.multiple_of(b * SPAN, SPAN)
        rows = pl.ds(start, SPAN)
        blocks = pl.ds(b * (SPAN // BLOCK), SPAN // BLOCK)
        acc[...] = jnp.zeros_like(acc)

        def step(r, masked):
            score = matmul(kv[blocks, :, :128].reshape(SPAN, 128), q_cols[r])
            prob = jnp.exp2(score * SCORE - logs[r])
            if masked:
                prob = jnp.where(key_mask(start, SPAN, tile_at(r), 2 * TILE), prob, 0.0)
            upper = matmul(kv[blocks, :, 128:].reshape(SPAN, 128), d_cols[r])
            p1, p2 = prob[:, :TILE], prob[:, TILE:]
            ds = jnp.concatenate(
                [p1 * (upper - deltas[r, 0:1, :]), p2 * (-lam * upper - deltas[r, 1:2, :])],
                axis=1,
            ).astype(BF)
            mixed = (p1 - lam * p2).astype(BF)
            acc[:, :128] += matmul(ds, q_rows[r])
            acc[:, 128:] += matmul(mixed, d_rows[r])
            dq_acc[r] += matmul(k_t[:, rows], ds)

        def masked_step(r, carry):
            step(r, True)
            return carry

        def full_step(r, carry):
            step(r, False)
            return carry

        reach, past = 0, 0
        for r in range(SLOTS):
            last = tile_of(slot, r) * TILE // SPAN
            counts = (slot < 4) if r == 0 else True
            reach += jnp.where(jnp.logical_and(counts, last >= b), 1, 0)
            past += jnp.where(jnp.logical_and(counts, last > b), 1, 0)
        lax.fori_loop(SLOTS - reach, SLOTS - past, masked_step, 0)
        lax.fori_loop(SLOTS - past, SLOTS, full_step, 0)

        @pl.when(k >= 2)
        def _():
            for u in range(PER_SPAN):
                to_sibling(PER_SPAN * lax.rem(chip + k - 2, SPANS) + u).wait_send()

        for u in range(PER_SPAN):
            o = PER_SPAN * b + u
            for ref, at, which in ((given, o % (2 * PER_SPAN), 1 - core), (both, o, core)):
                part = acc[pl.ds(pl.multiple_of((2 * u + which) * BLOCK, BLOCK), BLOCK), :]
                ref[at, :, :128] = (part[:, :128] * 0.125).astype(BF)
                ref[at, :, 128:] = part[:, 128:].astype(BF)
            to_sibling(o).start()

        @pl.when(k > 0)
        def _():
            pass_on(k - 1)

        return carry

    def early(k, carry):
        span(k, carry)

        @pl.when(k < 2)
        def _():
            send_gate.some(8 * k, 8 * k + 8, True)

        return carry

    def late(k, carry):
        span(k, carry)

        @pl.when(k < EARLY_SPANS + 4)
        def _():
            at = 4 * (k - EARLY_SPANS)
            send_up.some(at, at + 4, True)

        return carry

    @pl.when(served)
    def _():
        lax.fori_loop(0, EARLY_SPANS, early, 0)

    @pl.when(jnp.logical_not(served))
    def _():
        send_gate.each(True)

    ring_up.finish()
    block_grad(pup, 0, lffn, lup[...].reshape(4 * BLOCK, 512), 256)

    @pl.when(jnp.logical_not(served))
    def _():
        send_up.each(True)

    @pl.when(served)
    def _():
        lax.fori_loop(EARLY_SPANS, SPANS, late, 0)
        pass_on(SPANS - 1)

    for r in range(SLOTS):

        @pl.when(served if r else jnp.logical_and(served, slot < 4))
        def _():
            dq_t = jnp.concatenate([dq_acc[r, :64, :TILE], dq_acc[r, 64:, TILE:]], axis=0)
            dq_out[r] = (dq_t * 0.125).T.astype(BF)

    home_sends(dq_out, land, gsend, grecv, chip, core, t, True)
    home_waits(dq_out, land, grecv)
    for j in range(3):
        for u in range(2):
            dqkv_ref[0, u * 128 : (u + 1) * 128, j * 128 : (j + 1) * 128] = land[j, u]
    ring_q.start()
    for j in range(3):
        total = jnp.zeros((BLOCK, 256), F32)
        for p in range(PER_HEAD):
            spot = j * PER_HEAD + p
            pltpu.make_async_copy(both.at[0], home.at[spot], krecv.at[spot]).wait()
            total = total + home[spot].astype(F32)
        dqkv_ref[1, :, j * 128 : (j + 1) * 128] = total[:, :128].astype(BF)
        dqkv_ref[2, :, j * 128 : (j + 1) * 128] = total[:, 128:].astype(BF)
    ring_k.start()
    ring_v.start()

    for load in late_loads:
        load.wait()
    red2.drain()
    red4 = QuadReduce(*reduces[0], chip, core, t)

    def normed_term(k):
        rows = slice(k * CW, (k + 1) * CW)
        return (
            matmul_t(dqkv_ref[0], wg[rows, :384])
            + matmul_t(dqkv_ref[1], wg[rows, 384:768])
            + matmul_t(dqkv_ref[2], wu[rows, :384])
        )

    red4.run(normed_term)
    ring_mix.finish()
    ring_dres.finish()
    block_grad(pqo, 384, xdres, xmix[...].reshape(4 * BLOCK, 384), 384, 0, 384)
    x = x_ref[...]
    rms = rms_scale(x)
    hat = x * rms
    d_normed = jnp.concatenate([red4.result(k) for k in range(NC)], axis=1)
    part = jnp.sum(d_normed * hat, axis=0, keepdims=True)
    for k in range(12):
        vec[k : k + 1, :] = part[:, k * 128 : (k + 1) * 128]
    first_sum = [
        remote(vec, vecs.at[k], asem.at[0, k], asem.at[1, k], *member)
        for k, member in enumerate(members)
    ]
    for cp in first_sum:
        cp.start()
    grad_ref[...] = dres[...] + norm_back(d_normed, long_row(attn_ref), rms, hat)
    for left in lefts:
        left.wait()
    ring_q.finish()
    block_grad(pqo, 0, ldout, rq[...].reshape(4 * BLOCK, 384), 384, 0, 384)
    send_qo.each(True)
    ring_k.finish()
    block_grad(pkv, 0, ldout, rk[...].reshape(4 * BLOCK, 384), 384, 384, 384)
    ring_v.finish()
    block_grad(pkv, 384, ldout, rv[...].reshape(4 * BLOCK, 384), 384, 384, 384)
    send_kv.each(True)
    for cp in first_sum:
        cp.wait_recv()
    share = pl.ds(pl.multiple_of((2 * core + t) * 8, 8), 8)
    quarter[...] = (vec[share, :] + vecs[0, share, :]) + (vecs[1, share, :] + vecs[2, share, :])

    def spread(k, start):
        to = 2 * lax.rem(chip + k, CHIPS) + core
        cp = remote(quarter, quarters.at[chip], bsem.at[0, k], bsem.at[1, chip], to, t)
        if start:
            cp.start()
        else:
            cp.wait_send()

    def spread_start(k, carry):
        spread(k, True)
        return carry

    def spread_end(k, carry):
        spread(k, False)
        return carry

    own = pltpu.make_async_copy(quarter, quarters.at[chip], bsem.at[1, chip])
    own.start()
    lax.fori_loop(1, CHIPS, spread_start, 0)

    send_down.wait()
    for b in range(2):
        total = send_down.total(b, slice(0, 512))
        for h in range(2):
            swap[h, :, 2048 + b * 512 : 2560 + b * 512] = total[h * 24 : h * 24 + 24]
    for m, send in enumerate((send_gate, send_up)):
        send.wait()
        for b in range(2):
            total = send.total(b, slice(0, 512))
            at = m * 1024 + b * 512
            for h in range(2):
                swap[h, :, at : at + 512] = total[h * 24 : h * 24 + 24]
    sibling = s + 1 - 2 * core
    swap_copy = remote(swap.at[1 - core], swapped, swap_sem.at[0], swap_sem.at[1], sibling, t)
    swap_copy.start()

    def collect(k, total):
        pltpu.make_async_copy(quarter, quarters.at[k], bsem.at[1, k]).wait()
        return total + quarters[k]

    sums_ref[share, :] = lax.fori_loop(0, CHIPS, collect, jnp.zeros((8, 128), F32))
    last_sum = [
        remote(sums_ref.at[share], sums_ref.at[share], csem.at[0, k], csem.at[1, k], *member)
        for k, member in enumerate(members)
    ]
    for cp in last_sum:
        cp.start()
    for send, first in ((send_qo, (0, 3)), (send_kv, (1, 2))):
        send.wait()
        for m in range(2):
            total = send.total(0, slice(m * 384, m * 384 + 384))
            at = first[m] * 384
            for h in range(2):
                swap2[h, :, at : at + 384] = total[h * 24 : h * 24 + 24]
    swap2_copy = remote(swap2.at[1 - core], swapped2, swap2_sem.at[0], swap2_sem.at[1], sibling, t)
    swap2_copy.start()
    swap_copy.wait()
    swap_out(swap, swapped, ((gate_ref, 0), (up_ref, 1024), (down_ref, 2048)), 1024, core)

    for ring in (
        ring_dout, ring_mix, ring_hid, ring_gate, ring_up, ring_dres, ring_ffn, ring_xn, ring_zn, ring_q, ring_k,
        ring_v,
    ):
        ring.drain()
    for send in (send_gate, send_up, send_down, send_qo, send_kv):
        send.each(False)
    home_sends(tiles_ref, land, hsend, hrecv, chip, core, t, False)
    home_sends(dq_out, land, gsend, grecv, chip, core, t, False)
    tile_sends(dms, dmix, tsend, trecv, chip, core, t, False)
    for gather in (gather_f, gather_r):
        gather.drain()
    red3.drain()
    red4.drain()

    @pl.when(served)
    def _():
        for k in (SPANS - 2, SPANS - 1):
            for u in range(PER_SPAN):
                to_sibling(PER_SPAN * lax.rem(chip + k, SPANS) + u).wait_send()

        def last(o, carry):
            to_home(o, False)
            return carry

        lax.fori_loop(0, CHIPS // 2, last, 0)

    for cp in last_sum:
        cp.wait()
    for cp in first_sum:
        cp.wait_send()
    lax.fori_loop(1, CHIPS, spread_end, 0)
    swap2_copy.wait()
    outs = ((gq_ref, 0), (gk_ref, 384), (gv_ref, 768), (go_ref, 1152))
    swap_out(swap2, swapped2, outs, 384, core)


def swap_out(swap, swapped, outs, width, core):
    mine = swap[core]
    for c in range(2):

        @pl.when(core == c)
        def _():
            for ref, at in outs:
                ref[:, c * width : (c + 1) * width] = mine[:, at : at + width]
                other = (1 - c) * width
                ref[:, other : other + width] = swapped[:, at : at + width]


def middle_part(
    x, cot, mask, attn, ffn, sub, lambdas, tiles, wq, wk, wv, wo, wg, wu, wd,
    dout_all, normed, q, kv, parts, logs,
):
    half = (CHIPS // 2, BLOCK, 256)
    vm = pltpu.VMEM
    sem = pltpu.SemaphoreType.DMA
    return pl.pallas_call(
        middle_kernel,
        name="middle",
        out_shape=(
            shape((ROWS, D), F32),
            shape((ROWS, D), F32),
            *([shape((24, 768), F32)] * 4),
            *([shape((24, 2048), F32)] * 3),
            shape((32, 128), F32),
            shape(GATHERED_Q, BF),
            shape(GATHERED_Q, BF),
        ),
        in_specs=[VM] * 7 + [ANY] * 14,
        out_specs=(VM,) * 10 + (ANY,) * 2,
        scratch_shapes=[
            vm((ROWS, D), F32),
            vm((3, BLOCK, 384), BF),
            *([vm(GATHERED_Q, BF)] * 5),
            vm((384, 768), BF),
            vm((384, 768), BF),
            vm((8, CHUNK, 768), BF),
            vm((8, CHUNK, 768), BF),
            vm((2, 24, 1536), F32),
            vm((24, 1536), F32),
            vm((32, 128), F32),
            vm((3, 32, 128), F32),
            vm((8, 128), F32),
            vm((CHIPS, 8, 128), F32),
            vm((3, 2, TILE, 128), BF),
            vm((D, 384), BF),
            vm((D, 1024), BF),
            vm((D, 1024), BF),
            vm((D, 1024), BF),
            vm((BLOCK, D), BF),
            vm((BLOCK, D), BF),
            vm((3, 2, TILE, 128), BF),
            vm(HALVES, BF),
            vm((2, BLOCK, 512), BF),
            vm((2, BLOCK, 512), BF),
            vm((2, BLOCK, 512), BF),
            vm((BLOCK, 384), BF),
            vm((SLOTS, TILE, 128), BF),
            vm(KV, BF),
            vm((SLOTS, 128, 2 * TILE), F32),
            vm((SLOTS, 1, 2 * TILE), F32),
            vm((SLOTS, TILE, 128), BF),
            vm(GATHERED, BF),
            *([vm((4, BLOCK, 512), BF)] * 3),
            vm(GATHERED, BF),
            *([vm((768, 512), BF)] * 3),
            *([vm((16, CHUNK, 512), BF)] * 3),
            vm((2, 24, 3072), F32),
            vm((24, 3072), F32),
            vm((128, CHIPS * BLOCK), BF),
            vm((SPAN, 256), F32),
            vm((SLOTS, 128, 2 * TILE), BF),
            vm((SLOTS, 2 * TILE, 128), BF),
            vm((SLOTS, 128, TILE), BF),
            vm((SLOTS, TILE, 128), BF),
            vm((SLOTS, 2, TILE), F32),
            vm((SLOTS, 128, 2 * TILE), F32),
            vm((SLOTS, TILE, 128), BF),
            vm((2 * PER_SPAN, BLOCK, 256), BF),
            vm(half, BF),
            vm(half, BF),
            vm((3 * PER_HEAD, BLOCK, 256), BF),
            *(REDUCE_SCRATCH * 2),
            *(GATHER_SEMS * 2),
            *(RING_SEMS * 11),
            *ONCE_SEMS,
            *(scatter_sems(16) * 2),
            *(scatter_sems(8) * 2),
            *scatter_sems(16),
            sem((4,)),
            sem((9,)),
            sem((SLOTS,)),
            sem((3, 2)),
            sem((6,)),
            sem((SLOTS,)),
            sem((2,)),
            sem((2 * PER_SPAN,)),
            sem((CHIPS // 2,)),
            sem((CHIPS // 2,)),
            sem((3 * PER_HEAD,)),
            sem((SLOTS,)),
            sem((3, 2)),
            sem((3,)),
            sem((2,)),
            sem((2,)),
            sem((2, 3)),
            sem((2, CHIPS)),
            sem((2, 3)),
        ],
        compiler_params=pltpu.CompilerParams(
            collective_id=1, has_side_effects=True, vmem_limit_bytes=VMEM_LIMIT
        ),
    )(
        x, cot, mask, attn, ffn, sub, lambdas, tiles, wq, wk, wv, wo, wg, wu, wd,
        dout_all, normed, q, kv, parts, logs,
    )


def publish(lambdas, sums, arrays):
    count = len(arrays)

    def kernel(lambdas_ref, sums_ref, *refs):
        for k in range(count):
            refs[count + k][...] = refs[k][...]
        attn_ref, ffn_ref, sub_ref, grad_ref = refs[2 * count :]
        attn_ref[...] = sums_ref[0:12, :]
        ffn_ref[...] = sums_ref[12:24, :]
        sub_ref[...] = sums_ref[24:25, :]
        vectors, first, second = lambda_parts(lambdas_ref)
        d_lam = as_column(sums_ref[25:26, :])[:12, :1]
        factors = (d_lam * first, d_lam * first, -d_lam * second, -d_lam * second)
        for k, other in enumerate((1, 0, 3, 2)):
            grad_ref[:, k, :] = factors[k] * vectors[other]

    return pl.pallas_call(
        kernel,
        name="publish",
        out_shape=tuple(shape(a.shape, a.dtype) for a in arrays)
        + (shape((12, 128), F32), shape((12, 128), F32), shape((1, 128), F32), shape((12, 4, 64), F32)),
        in_specs=[VM] * (count + 2),
        out_specs=(VM,) * (count + 4),
    )(lambdas, sums, *arrays)


def on_device(
    hidden_in, cotangent, needle_mask, attn_gain, lambdas, subln_gain, ffn_gain,
    weight_query, weight_key, weight_value, weight_out, weight_gate, weight_up, weight_down,
):
    mask = needle_mask.reshape(1, ROWS)
    attn = attn_gain.reshape(12, 128)
    sub = subln_gain.reshape(1, 128)
    by_head = jnp.transpose(lambdas, (1, 0, 2))
    dout, normed, q, kv, mixed, parts, logs = forward_part(
        hidden_in, cotangent, mask, attn, sub, by_head, weight_query, weight_key, weight_value
    )
    *results, sums, _, _ = middle_part(
        hidden_in, cotangent, mask, attn, ffn_gain.reshape(12, 128), sub, by_head, mixed,
        weight_query, weight_key, weight_value, weight_out, weight_gate, weight_up, weight_down,
        dout, normed, q, kv, parts, logs,
    )
    *results, attn_grad, ffn_grad, sub_grad, lambda_grad = publish(by_head, sums, results)
    return (
        *results,
        attn_grad.reshape(D),
        jnp.transpose(lambda_grad, (1, 0, 2)),
        sub_grad.reshape(128),
        ffn_grad.reshape(D),
    )


def solution(mesh):
    split = P(None, "tp")
    rows = P(("seq", "tp"), None)
    both = P("seq", "tp")
    return jax.shard_map(
        on_device,
        mesh=mesh,
        in_specs=(rows, rows, P(("seq", "tp"))) + (P(),) * 4 + (split,) * 7,
        out_specs=(rows, rows) + (both,) * 7 + (P(),) * 4,
        check_vma=False,
    )
```

```python
import math

import jax
import jax.numpy as jnp
from jax import lax
from jax.experimental import pallas as pl
from jax.experimental.pallas import tpu as pltpu
from jax.sharding import PartitionSpec as P

MESH = pl.DeviceIdType.MESH
BF = jnp.bfloat16
F32 = jnp.float32
EPS = 1e-06
LAMBDA_INIT = 0.8 - 0.6 * math.exp(-3.6)
OUT_SCALE = 1.0 - LAMBDA_INIT
D = 1536
CHIPS = 32
PER_HEAD = 5
WORKERS = 15
ROWS = 64
BLOCK = 256
TILE = 128
SLOTS = 7
KB = 512
LOG2E = 1.4426950408889634
SCORE = 0.125 * LOG2E
VMEM_LIMIT = 63 * 2**20


def place():
    s = lax.axis_index("seq")
    return s // 2, s % 2, lax.axis_index("tp")


def worker(chip, core):
    x, y, z = chip % 4, chip // 4 % 2, chip // 8
    at = 4 * z + x
    return (x + y + z) % 2, at, at % PER_HEAD * 2 + core, at < WORKERS


def worker_chip(parity, at):
    x, z = at % 4, at // 4
    return (2 * z + (x + z + parity) % 2) * 4 + x


def owner_of(tile):
    step = (tile - 4) // 10
    pos = (tile - 4) % 10
    slot = jnp.where(step % 2 == 0, pos, 9 - pos)
    early = tile < 4
    return jnp.where(early, tile, slot), jnp.where(early, 0, step + 1)


def tile_of(slot, r):
    if r == 0:
        return slot
    return 4 + 10 * (r - 1) + (slot if (r - 1) % 2 == 0 else 9 - slot)


def matmul(a, b):
    return jnp.dot(a, b, preferred_element_type=F32)


def matmul_t(a, b):
    return lax.dot_general(a, b, (((1,), (1,)), ((), ())), preferred_element_type=F32)


def rms_scale(values, axis=-1):
    return lax.rsqrt(jnp.mean(values * values, axis=axis, keepdims=True) + EPS)


def norm_back(grad_normed, gain, rms, hat, axis=-1):
    scaled = grad_normed * gain
    return rms * (scaled - hat * jnp.mean(scaled * hat, axis=axis, keepdims=True))


def greet_all(chip, core, t):
    barrier = pltpu.get_barrier_semaphore()
    s = 2 * chip + core

    def greet(o, carry):
        pl.semaphore_signal(
            barrier, inc=1, device_id=(lax.rem(s + o, 2 * CHIPS), t), device_id_type=MESH
        )
        return carry

    lax.fori_loop(1, 2 * CHIPS, greet, 0)
    pl.semaphore_signal(barrier, inc=1, device_id=(s, 1 - t), device_id_type=MESH)
    pl.semaphore_wait(barrier, 2 * CHIPS)


def remote(src, dst, send_sem, recv_sem, s, t):
    return pltpu.make_async_remote_copy(
        src_ref=src,
        dst_ref=dst,
        send_sem=send_sem,
        recv_sem=recv_sem,
        device_id=(s, t),
        device_id_type=MESH,
    )


def rows_at(ref, start, count):
    return ref.at[pl.ds(pl.multiple_of(start, ROWS), count)]


class QuadGather:
    def __init__(self, buf, send, recv, chip, core, t):
        self.buf, self.send, self.recv = buf, send, recv
        self.chip, self.core, self.t = chip, core, t
        mine = core * 128 + t * ROWS
        self.mine = mine
        self.near = core * 128 + (1 - t) * ROWS
        sib = (2 * chip + 1 - core, t)
        self.to_near = self.copy(mine, 0, (2 * chip + core, 1 - t))
        self.to_sib = self.copy(mine, 1, sib)
        self.forward = self.copy(self.near, 2, sib)

    def copy(self, row, k, target):
        view = rows_at(self.buf, row, ROWS)
        return remote(view, view, self.send.at[k], self.recv.at[k], *target)

    def start(self):
        self.to_near.start()
        self.to_sib.start()

    def finish(self):
        self.to_near.wait_recv()
        self.forward.start()
        self.to_sib.wait_recv()
        self.forward.wait_recv()

    def drain(self):
        self.to_near.wait_send()
        self.to_sib.wait_send()
        self.forward.wait_send()


class RingGather:
    def __init__(self, pieces, land, send, recv, axis, chip, core, t):
        at = chip % 4 if axis == "x" else chip // 8
        self.local = pltpu.make_async_copy(pieces(at), land.at[at], recv.at[at])
        self.copies = []
        for k in (1, 3, 2):
            if axis == "x":
                peer, chip_to = (at + k) % 4, chip - at + (at + k) % 4
            else:
                peer, chip_to = (at + k) % 4, (chip + 8 * k) % CHIPS
            self.copies.append(
                remote(pieces(peer), land.at[at], send.at[k - 1], recv.at[at], 2 * chip_to + core, t)
            )
        self.waits = [
            pltpu.make_async_copy(pieces(at), land.at[k], recv.at[k]) for k in range(4)
        ]

    def start(self):
        self.local.start()
        for cp in self.copies:
            cp.start()

    def finish(self):
        for cp in self.waits:
            cp.wait()

    def drain(self):
        for cp in self.copies:
            cp.wait_send()


class RingGatherOnce:
    def __init__(self, pieces, land, send, recv, pass_send, pass_recv, axis, chip, core, t):
        at = chip % 4 if axis == "x" else chip // 8
        self.mine = pl.ds(pl.multiple_of(core * 128, 128), 128)
        self.local = pltpu.make_async_copy(pieces(at), land.at[at], recv.at[0])
        self.local_at = at
        self.copies, self.passes = [], []
        for k in (1, 3, 2):
            peer = (at + k) % 4
            chip_to = chip - at + peer if axis == "x" else (chip + 8 * k) % CHIPS
            self.copies.append(
                remote(
                    pieces(peer).at[self.mine], land.at[at, self.mine],
                    send.at[k - 1], recv.at[4 - k], 2 * chip_to + core, t,
                )
            )
            view = land.at[peer, self.mine]
            self.passes.append(
                (
                    pltpu.make_async_copy(pieces(at).at[self.mine], view, recv.at[k]),
                    remote(view, view, pass_send.at[k - 1], pass_recv.at[k - 1], 2 * chip + 1 - core, t),
                )
            )

    def start(self):
        self.local.start()
        for cp in self.copies:
            cp.start()

    def forward(self):
        for arrive, cp in self.passes:
            arrive.wait()
            cp.start()

    def finish(self):
        self.local.wait()
        for _, cp in self.passes:
            cp.wait_recv()

    def drain(self):
        for cp in self.copies:
            cp.wait_send()
        for _, cp in self.passes:
            cp.wait_send()


ONCE_SEMS = [
    pltpu.SemaphoreType.DMA((3,)),
    pltpu.SemaphoreType.DMA((4,)),
    pltpu.SemaphoreType.DMA((3,)),
    pltpu.SemaphoreType.DMA((3,)),
]
RING_SEMS = [pltpu.SemaphoreType.DMA((3,)), pltpu.SemaphoreType.DMA((4,))]


def block_grad(dst, start, left, right, step, at=0, total=768):
    width = right.shape[1]

    def one(m, carry):
        cols = pl.ds(pl.multiple_of(m * step, 128), step)
        part = left[:, :, pl.ds(pl.multiple_of(at + m * step, 128), step)].reshape(4 * BLOCK, step)
        dst[cols, start : start + width] = lax.dot_general(
            part, right, (((0,), (0,)), ((), ())), preferred_element_type=F32
        ).astype(BF)
        return carry

    lax.fori_loop(0, total // step, one, 0)


CHUNK = 48


class Scatter:
    def __init__(self, part, land, send, recv, count, first, spot, chip, core, t):
        self.part, self.land, self.send, self.recv = part, land, send, recv
        self.count, self.first, self.spot = count, first, spot
        self.chip, self.core, self.t = chip, core, t

    def source(self, i):
        return self.part.at[pl.ds(pl.multiple_of(i * CHUNK, 16), CHUNK)]

    def each(self, start):
        self.some(0, self.count, start)

    def some(self, first, end, start):
        def one(o, carry):
            i = lax.rem(self.chip + 1 + 3 * o, self.count)
            owner = self.first + i
            cp = remote(
                self.source(i), self.land.at[self.spot], self.send.at[i], self.recv.at[self.spot],
                2 * owner + self.core, self.t,
            )
            if start:

                @pl.when(owner == self.chip)
                def _():
                    pltpu.make_async_copy(
                        self.source(i), self.land.at[self.spot], self.recv.at[self.spot]
                    ).start()

            @pl.when(owner != self.chip)
            def _():
                if start:
                    cp.start()
                else:
                    cp.wait_send()

            return carry

        lax.fori_loop(first, end, one, 0)

    def wait(self):
        def one(k, carry):
            pltpu.make_async_copy(self.source(0), self.land.at[k], self.recv.at[k]).wait()
            return carry

        lax.fori_loop(0, self.count, one, 0)

    def total(self, b, cols):
        def one(k, carry):
            return carry + self.land[8 * b + k, :, cols].astype(F32)

        return lax.fori_loop(0, 8, one, jnp.zeros((CHUNK, cols.stop - cols.start), F32))


def scatter_sems(count):
    return [pltpu.SemaphoreType.DMA((count,)), pltpu.SemaphoreType.DMA((count,))]


GATHER_SEMS = [pltpu.SemaphoreType.DMA((3,)), pltpu.SemaphoreType.DMA((3,))]
CW = 512
NC = D // CW


class QuadReduce:
    def __init__(self, part, dsend, drecv, ysend, yrecv, ds, dr, ys, yr, chip, core, t):
        self.part, self.dsend, self.drecv = part, dsend, drecv
        self.ysend, self.yrecv = ysend, yrecv
        self.core, self.t = core, t
        self.d = [
            remote(dsend.at[k], drecv.at[k], ds.at[k], dr.at[k], 2 * chip + 1 - core, t)
            for k in range(NC)
        ]
        self.y = [
            remote(ysend.at[k], yrecv.at[k], ys.at[k], yr.at[k], 2 * chip + core, 1 - t)
            for k in range(NC)
        ]

    def rows(self, start, count, k):
        return self.part[pl.ds(pl.multiple_of(start, ROWS), count), k * CW : (k + 1) * CW]

    def put(self, k, value):
        self.part[:, k * CW : (k + 1) * CW] = value
        self.dsend[k] = self.rows((1 - self.core) * 128, 128, k).astype(BF)
        self.d[k].start()

    def middle(self, k):
        self.d[k].wait_recv()
        near = (1 - self.t) * ROWS
        far = self.rows(self.core * 128 + near, ROWS, k)
        got = self.drecv[k, pl.ds(pl.multiple_of(near, ROWS), ROWS), :]
        self.ysend[k] = (far + got.astype(F32)).astype(BF)
        self.y[k].start()

    def result(self, k):
        mine = self.t * ROWS
        own = self.rows(self.core * 128 + mine, ROWS, k)
        got = self.drecv[k, pl.ds(pl.multiple_of(mine, ROWS), ROWS), :].astype(F32)
        self.y[k].wait_recv()
        return own + got + self.yrecv[k].astype(F32)

    def run(self, term):
        for k in range(NC):
            self.put(k, term(k))
            if k:
                self.middle(k - 1)
        self.middle(NC - 1)

    def drain(self):
        for k in range(NC):
            self.d[k].wait_send()
            self.y[k].wait_send()


REDUCE_SCRATCH = [
    pltpu.VMEM((BLOCK, D), F32),
    pltpu.VMEM((NC, 128, CW), BF),
    pltpu.VMEM((NC, 128, CW), BF),
    pltpu.VMEM((NC, ROWS, CW), BF),
    pltpu.VMEM((NC, ROWS, CW), BF),
] + [pltpu.SemaphoreType.DMA((NC,))] * 4


def tile_sends(tiles, land, send, recv, chip, core, t, start):
    s = 2 * chip + core
    for j in range(3):
        for u in range(2):
            slot, index = owner_of(2 * chip + u)
            target = 2 * worker_chip(core, j * PER_HEAD + slot // 2) + slot % 2
            k = j * 2 + u

            if start:

                @pl.when(target == s)
                def _():
                    pltpu.make_async_copy(tiles.at[j, u], land.at[index], recv.at[index]).start()

            @pl.when(target != s)
            def _():
                cp = remote(tiles.at[j, u], land.at[index], send.at[k], recv.at[index], target, t)
                if start:
                    cp.start()
                else:
                    cp.wait_send()


def tile_waits(tiles, land, send, recv, chip, core, t):
    _, _, slot, served = worker(chip, core)
    for r in range(SLOTS):
        here = served
        if r == 0:
            here = jnp.logical_and(here, slot < 4)

        @pl.when(here)
        def _():
            pltpu.make_async_copy(tiles.at[0, 0], land.at[r], recv.at[r]).wait()


def home_sends(tiles, land, send, recv, chip, core, t, start):
    s = 2 * chip + core
    parity, at, slot, served = worker(chip, core)
    for r in range(SLOTS):
        here = served
        if r == 0:
            here = jnp.logical_and(here, slot < 4)
        tile = tile_of(slot, r)
        target = (tile // 2) * 2 + parity
        j, u = at // PER_HEAD, tile % 2

        if start:

            @pl.when(jnp.logical_and(here, target == s))
            def _():
                pltpu.make_async_copy(tiles.at[r], land.at[j, u], recv.at[j, u]).start()

        @pl.when(jnp.logical_and(here, target != s))
        def _():
            cp = remote(tiles.at[r], land.at[j, u], send.at[r], recv.at[j, u], target, t)
            if start:
                cp.start()
            else:
                cp.wait_send()


def home_waits(tiles, land, recv):
    for j in range(3):
        for u in range(2):
            pltpu.make_async_copy(tiles.at[0], land.at[j, u], recv.at[j, u]).wait()


def weight_load(ref, buf, sem, core, width):
    return pltpu.make_async_copy(
        ref.at[:, pl.ds(pl.multiple_of(core * width, 128), width)], buf, sem
    )


VM = pl.BlockSpec(memory_space=pltpu.VMEM)
ANY = pl.BlockSpec(memory_space=pl.ANY)


def shape(dims, dtype):
    return jax.ShapeDtypeStruct(dims, dtype)


HALVES = (2, BLOCK, 768)
QUARTERS = (4, BLOCK, 384)
GATHERED = (4, BLOCK, 768)
GATHERED_Q = (4, BLOCK, 384)
KV = (CHIPS, BLOCK, 256)
STEP = 2048


def eye(size):
    row = lax.broadcasted_iota(jnp.int32, (size, size), 0)
    col = lax.broadcasted_iota(jnp.int32, (size, size), 1)
    return jnp.where(row == col, 1.0, 0.0).astype(BF)


def both_maps(q_t):
    top = lax.broadcasted_iota(jnp.int32, q_t.shape, 0) < 64
    return jnp.concatenate([jnp.where(top, q_t, 0.0), jnp.where(top, 0.0, q_t)], axis=1)


def key_mask(start, count, tile, width):
    key = start + lax.broadcasted_iota(jnp.int32, (count, width), 0)
    query = tile * TILE + lax.broadcasted_iota(jnp.int32, (count, width), 1) % TILE
    return key <= query


def group_norm(parts, lam):
    first, second = parts[:, :TILE], parts[:, TILE:]
    differ = first - lam * second
    rms = rms_scale(differ, 0)
    return rms, differ * rms


def long_row(ref):
    return jnp.concatenate([ref[k : k + 1, :] for k in range(12)], axis=1)


def as_column(row):
    return jnp.broadcast_to(row, (128, 128)).T


def mask_column(mask_ref):
    mask = mask_ref[...].astype(F32)
    return as_column(jnp.concatenate([mask, mask], axis=1))[:ROWS, :1]


def lambda_parts(lambdas_ref):
    vectors = [lambdas_ref[:, k, :] for k in range(4)]
    first = jnp.exp(jnp.sum(vectors[0] * vectors[1], axis=-1, keepdims=True))
    second = jnp.exp(jnp.sum(vectors[2] * vectors[3], axis=-1, keepdims=True))
    return vectors, first, second


def lambda_of(lambdas_ref, head):
    _, first, second = lambda_parts(lambdas_ref)
    every = first - second + LAMBDA_INIT
    mine = lax.broadcasted_iota(jnp.int32, every.shape, 0) == head
    return jnp.sum(jnp.where(mine, every, 0.0), axis=0, keepdims=True)


SPAN = 1024
SPANS = CHIPS * BLOCK // SPAN
PER_SPAN = SPAN // BLOCK // 2
EARLY_SPANS = 3


def layer_kernel(
    x_ref, cot_ref, mask_ref, attn_ref, ffn_ref, sub_ref, lambdas_ref,
    wq_ref, wk_ref, wv_ref, wo_ref, wg_ref, wu_ref, wd_ref,
    out_ref, grad_ref, gq_ref, gk_ref, gv_ref, go_ref, gate_ref, up_ref, down_ref, sums_ref,
    xnormed_ref, znormed_ref,
    dres, dqkv_ref, rq, rk, rv, xmix, xdres, pqo, pkv, sqo, skv, swap2, swapped2,
    vec, vecs, quarter, quarters,
    land, wo, wg, wu, wd, fbuf, nbuf, dms, obuf, dgate, dup, hid, mix,
    q, kv, parts_all, logs, dmix,
    lffn, lgate, lup, lhid, ldout, pgate, pup, pdown, sgate, sup, sdown, swap, swapped,
    turned, acc, q_cols, q_rows, d_cols, d_rows, deltas, dq_acc, dq_out, given, sib, both, home,
    peaks, kmax, total, *rest,
):
    chip, core, t = place()
    s = 2 * chip + core
    parity, place_at, slot, served = worker(chip, core)
    head = 3 * parity + place_at // PER_HEAD
    x_at, z_at = chip % 4, chip // 8
    taken = iter(rest)

    def take(count):
        return [next(taken) for _ in range(count)]

    reduces = [take(9) for _ in range(2)]
    gather_sems = [take(2) for _ in range(4)]
    ring_sems = [take(2) for _ in range(11)]
    once_sems = take(4)
    scatter = [take(2) for _ in range(5)]
    wsem, hsend, hrecv, tsend, trecv, swap_sem = take(6)
    dsend, drecv, ksend, krecv, gsend, grecv = take(6)
    w2sem, lsem, swap2_sem, asem, bsem, csem = take(6)
    kvsend, kvrecv, fsend, qsend, qrecv = take(5)
    rbuf = nbuf
    front = dq_acc.at[0]


    def halves(ref):
        return lambda p: ref.at[:, pl.ds(pl.multiple_of(p // 2 * 768, 128), 768)]

    def quarters_of(ref):
        return lambda p: ref.at[:, pl.ds(pl.multiple_of(p * 384, 128), 384)]

    gather_f = QuadGather(fbuf, *gather_sems[0], chip, core, t)
    gather_r = QuadGather(rbuf, *gather_sems[1], chip, core, t)
    ring_dout = RingGather(halves(obuf), ldout, *ring_sems[0], "x", chip, core, t)
    ring_mix = RingGather(lambda p: mix, xmix, *ring_sems[1], "x", chip, core, t)
    ring_hid = RingGather(lambda p: hid.at[p % 2], lhid, *ring_sems[2], "x", chip, core, t)
    ring_gate = RingGather(lambda p: dgate.at[p % 2], lgate, *ring_sems[3], "z", chip, core, t)
    ring_up = RingGather(lambda p: dup.at[p % 2], lup, *ring_sems[10], "z", chip, core, t)
    ring_dres = RingGather(
        quarters_of(rbuf), xdres, *ring_sems[4], "x", chip, core, t,
    )
    ring_xn = RingGather(quarters_of(nbuf), xnormed_ref, *ring_sems[5], "x", chip, core, t)
    ring_zn = RingGather(quarters_of(nbuf), znormed_ref, *ring_sems[6], "z", chip, core, t)
    ring_q = RingGather(lambda p: dqkv_ref.at[0], rq, *ring_sems[7], "x", chip, core, t)
    ring_k = RingGather(lambda p: dqkv_ref.at[1], rk, *ring_sems[8], "z", chip, core, t)
    ring_v = RingGather(lambda p: dqkv_ref.at[2], rv, *ring_sems[9], "z", chip, core, t)
    send_qo = Scatter(pqo, sqo, *scatter[2], 8, 8 * x_at, chip // 4, chip, core, t)
    send_kv = Scatter(pkv, skv, *scatter[3], 8, 8 * z_at, chip % 8, chip, core, t)
    members = ((s + 1 - 2 * core, t), (s, 1 - t), (s + 1 - 2 * core, 1 - t))
    ring_ffn = RingGatherOnce(
        halves(fbuf), lffn, *once_sems, "z", chip, core, t,
    )
    send_down = Scatter(
        pdown, sdown, *scatter[0], 16, 16 * (x_at // 2), 8 * (x_at % 2) + chip // 4, chip, core, t
    )
    send_gate, send_up = (
        Scatter(
            part, to, *sems, 16, 16 * (z_at // 2), 8 * (z_at % 2) + chip % 8, chip, core, t
        )
        for part, to, sems in ((pgate, sgate, scatter[1]), (pup, sup, scatter[4]))
    )
    first_loads = [
        weight_load(ref, buf.at[:, k * 384 : (k + 1) * 384], w2sem.at[i], core, 384)
        for i, (ref, buf, k) in enumerate(((wk_ref, wg, 0), (wv_ref, wg, 1), (wq_ref, wu, 0)))
    ]
    loads = [
        weight_load(wo_ref, wo, wsem.at[0], core, 384),
        weight_load(wg_ref, wg, wsem.at[1], core, 1024),
        weight_load(wu_ref, wu, wsem.at[2], core, 1024),
        weight_load(wd_ref, wd, wsem.at[3], core, 1024),
    ]
    for load in first_loads + loads[:1]:
        load.start()
    quad = QuadGather(nbuf, *gather_sems[2], chip, core, t)
    quad_o = QuadGather(obuf, *gather_sems[3], chip, core, t)
    mine = pl.ds(pl.multiple_of(quad.mine, ROWS), ROWS)
    x = x_ref[...]
    normed = (x * rms_scale(x) * long_row(attn_ref)).astype(BF)
    nbuf[mine, :] = normed
    greet_all(chip, core, t)
    quad.start()
    dout = cot_ref[...] * mask_column(mask_ref)
    obuf[mine, :] = dout.astype(BF)
    lam = lambda_of(lambdas_ref, 6 * t + head)
    sub = as_column(sub_ref[...])
    ffn_gain = long_row(ffn_ref)
    vec[...] = jnp.zeros_like(vec)
    unit = eye(256)
    quad.finish()
    for k in range(2):
        first_loads[k].wait()
        value = matmul(nbuf[...], wg[:, k * 384 : (k + 1) * 384]).astype(BF)
        for j in range(3):
            dqkv_ref[j, :, k * 128 : (k + 1) * 128] = value[:, j * 128 : (j + 1) * 128]

    def kv_piece(j):
        return dqkv_ref.at[j, :, :256]

    def kv_sends(start):
        def one(o, carry):
            w = lax.rem(chip + 7 * o, WORKERS)
            j = w // PER_HEAD
            target = 2 * worker_chip(core, w) + chip % 2
            if start:

                @pl.when(target == s)
                def _():
                    pltpu.make_async_copy(kv_piece(j), kv.at[chip], kvrecv.at[chip]).start()

            @pl.when(target != s)
            def _():
                cp = remote(kv_piece(j), kv.at[chip], kvsend.at[w], kvrecv.at[chip], target, t)
                if start:
                    cp.start()
                else:
                    cp.wait_send()

            return carry

        lax.fori_loop(0, WORKERS, one, 0)

    kv_sends(True)
    first_loads[2].wait()
    value = matmul(nbuf[...], wu[:, :384]).astype(BF)
    for j in range(3):
        for u in range(2):
            dms[j, u] = value[u * 128 : (u + 1) * 128, j * 128 : (j + 1) * 128]
    tile_sends(dms, q, qsend, qrecv, chip, core, t, True)
    quad_o.start()
    for load in loads[1:]:
        load.start()

    def forward(o):
        source = lax.rem((chip // 2 + o) * 2 + core, CHIPS)
        view = kv.at[source]
        return source, remote(view, view, fsend.at[o], kvrecv.at[source], s + 1 - 2 * core, t)

    def turn(source):
        block = kv[source]
        at = pl.ds(pl.multiple_of(source * BLOCK, BLOCK), BLOCK)
        both_t = matmul_t(unit, block)
        turned[:, at] = both_t[128:].astype(BF)
        square = both_t[:128] * both_t[:128]
        for m in range(2):
            largest = jnp.sum(square[64 * m : 64 * m + 64], axis=0, keepdims=True)
            peaks[m : m + 1, :] = jnp.maximum(peaks[m : m + 1, :], largest)

    @pl.when(served)
    def _():
        peaks[...] = jnp.zeros_like(peaks)

        def take(o, carry):
            source, cp = forward(o)
            pltpu.make_async_copy(kv_piece(0), kv.at[source], kvrecv.at[source]).wait()
            cp.start()
            turn(source)
            return carry

        lax.fori_loop(0, CHIPS // 2, take, 0)

        def finish(o, carry):
            source = lax.rem((chip // 2 + o) * 2 + 1 - core, CHIPS)
            pltpu.make_async_copy(kv_piece(0), kv.at[source], kvrecv.at[source]).wait()
            forward(o)[1].wait_send()
            turn(source)
            return carry

        lax.fori_loop(0, CHIPS // 2, finish, 0)
        for m in range(2):
            kmax[m] = jnp.max(peaks[m : m + 1, :])

    quad_o.finish()
    tile_waits(dms, q, qsend, qrecv, chip, core, t)
    ring_zn.start()
    ring_dout.start()

    for r in range(SLOTS):
        tile = tile_of(slot, r)

        @pl.when(served if r else jnp.logical_and(served, slot < 4))
        def _():
            q_t = q[r].astype(F32).T
            square = q_t * q_t
            bound = SCORE * jnp.concatenate(
                [
                    jnp.sqrt(jnp.sum(square[:64], axis=0, keepdims=True) * kmax[0]),
                    jnp.sqrt(jnp.sum(square[64:], axis=0, keepdims=True) * kmax[1]),
                ],
                axis=1,
            )
            q_both = both_maps(q_t).astype(BF)
            front[...] = jnp.zeros_like(front)
            total[...] = jnp.zeros_like(total)

            def step(b, masked):
                sums, out = None, None
                for u in range(STEP // KB):
                    start = pl.multiple_of(b * STEP + u * KB, KB)
                    pair = pl.ds(b * (STEP // BLOCK) + u * (KB // BLOCK), KB // BLOCK)
                    score = matmul(kv[pair, :, :128].reshape(KB, 128), q_both)
                    prob = jnp.exp2(score * SCORE - bound)
                    if masked:
                        prob = jnp.where(key_mask(start, KB, tile, 2 * TILE), prob, 0.0)
                    part = jnp.sum(prob.reshape(KB // 8, 8, 2 * TILE), axis=0)
                    term = matmul(turned[:, pl.ds(start, KB)], prob.astype(BF))
                    sums = part if sums is None else sums + part
                    out = term if out is None else out + term
                total[...] += sums
                front[...] += out

            full = tile * TILE // STEP

            def body(b, carry):
                step(b, False)
                return carry

            lax.fori_loop(0, full, body, 0)
            step(full, True)
            whole = jnp.sum(total[...], axis=0, keepdims=True)
            parts = front[...] / whole
            parts_all[r] = parts
            logs[r] = bound + jnp.log(whole) * LOG2E
            rms, hat = group_norm(parts, lam)
            dq_out[r] = (hat * sub * OUT_SCALE).T.astype(BF)


    home_sends(dq_out, land, hsend, hrecv, chip, core, t, True)
    loads[0].wait()
    home_waits(dq_out, land, hrecv)
    for j in range(3):
        for u in range(2):
            mix[u * 128 : (u + 1) * 128, j * 128 : (j + 1) * 128] = land[j, u]
    red = QuadReduce(*reduces[0], chip, core, t)
    red.run(lambda k: matmul_t(mix[...], wo[k * CW : (k + 1) * CW, :]))
    ring_xn.start()
    ring_mix.start()
    home_sends(dq_out, land, hsend, hrecv, chip, core, t, False)
    kv_sends(False)
    tile_sends(dms, q, qsend, qrecv, chip, core, t, False)
    resid = x_ref[...] + jnp.concatenate([red.result(k) for k in range(NC)], axis=1)
    ffn_rms = rms_scale(resid)
    ffn_hat = resid * ffn_rms
    fbuf[mine, :] = (ffn_hat * ffn_gain).astype(BF)
    gather_f.start()
    for load in loads[1:]:
        load.wait()
    red.drain()
    gather_f.finish()
    ring_ffn.start()

    def hidden_step(n, carry):
        cols = pl.ds(pl.multiple_of(n * 256, 256), 256)
        b, at = n // 2, n % 2
        gate = matmul(fbuf[...], wg[:, cols])
        up = matmul(fbuf[...], wu[:, cols])
        d_hidden = matmul(obuf[...], wd[:, cols])
        sig = 1.0 / (1.0 + jnp.exp(-gate))
        silu = gate * sig
        to = pl.ds(pl.multiple_of(at * 256, 256), 256)
        hid[b, :, to] = (silu * up).astype(BF)
        dgate[b, :, to] = (d_hidden * up * sig * (1.0 + gate * (1.0 - sig))).astype(BF)
        dup[b, :, to] = (d_hidden * silu).astype(BF)
        return carry

    lax.fori_loop(0, 4, hidden_step, 0)
    ring_gate.start()
    ring_hid.start()
    red2 = QuadReduce(*reduces[0], chip, core, t)

    def ffn_term(k):
        rows = slice(k * CW, (k + 1) * CW)
        return (
            matmul_t(dgate[0], wg[rows, :512])
            + matmul_t(dgate[1], wg[rows, 512:])
            + matmul_t(dup[0], wu[rows, :512])
            + matmul_t(dup[1], wu[rows, 512:])
        )

    quad.drain()
    quad_o.drain()
    for ring in (ring_zn, ring_xn):
        ring.finish()
        ring.drain()
    red2.run(ffn_term)
    late_loads = [
        weight_load(ref, buf.at[:, k * 384 : (k + 1) * 384], w2sem.at[i], core, 384)
        for i, (ref, buf, k) in enumerate(((wq_ref, wg, 0), (wk_ref, wg, 1), (wv_ref, wu, 0)))
    ]
    for load in late_loads:
        load.start()
    red3 = QuadReduce(*reduces[1], chip, core, t)
    d_ffn = jnp.concatenate([red2.result(k) for k in range(NC)], axis=1)
    part = jnp.sum(d_ffn * ffn_hat, axis=0, keepdims=True)
    for k in range(12):
        vec[12 + k : 13 + k, :] = part[:, k * 128 : (k + 1) * 128]
    d_resid = dout + norm_back(d_ffn, ffn_gain, ffn_rms, ffn_hat)
    dres[...] = d_resid
    rbuf[mine, :] = d_resid.astype(BF)
    gather_r.start()
    ring_ffn.forward()
    red3.run(
        lambda k: matmul_t(hid[0], wd[k * CW : (k + 1) * CW, :512])
        + matmul_t(hid[1], wd[k * CW : (k + 1) * CW, 512:])
    )
    gather_r.finish()
    d_mixed = matmul(rbuf[...], wo[...]).astype(BF)
    for j in range(3):
        for u in range(2):
            dms[j, u] = d_mixed[u * 128 : (u + 1) * 128, j * 128 : (j + 1) * 128]
    tile_sends(dms, dmix, tsend, trecv, chip, core, t, True)
    ring_up.start()
    ring_dres.start()
    out_ref[...] = resid + jnp.concatenate([red3.result(k) for k in range(NC)], axis=1)

    def to_sibling(o):
        at = o % (2 * PER_SPAN)
        return remote(given.at[at], sib.at[o], dsend.at[at], drecv.at[o], s + 1 - 2 * core, t)

    def to_home(o, start):
        target = 2 * (2 * o + core) + parity
        spot = place_at
        if start:

            @pl.when(target == s)
            def _():
                pltpu.make_async_copy(both.at[o], home.at[spot], krecv.at[spot]).start()

        @pl.when(target != s)
        def _():
            cp = remote(both.at[o], home.at[spot], ksend.at[o], krecv.at[spot], target, t)
            if start:
                cp.start()
            else:
                cp.wait_send()

    def tile_at(r):
        late = 4 + 10 * (r - 1) + jnp.where((r - 1) % 2 == 0, slot, 9 - slot)
        return jnp.where(r == 0, slot, late)

    @pl.when(served)
    def _():
        unit = eye(128)

        def flip(b, carry):
            rows = pl.ds(pl.multiple_of(b * KB, KB), KB)
            block = kv[pl.ds(2 * b, 2), :, :128].reshape(KB, 128)
            turned[:, rows] = matmul_t(unit, block).astype(BF)
            return carry

        lax.fori_loop(0, CHIPS * BLOCK // KB, flip, 0)

    ring_dout.finish()
    ring_hid.finish()
    block_grad(pdown, 0, ldout, lhid[...].reshape(4 * BLOCK, 512), 256)
    lefts = [
        pltpu.make_async_copy(src, ldout.at[:, :, k * 384 : (k + 1) * 384], lsem.at[k])
        for k, src in enumerate((xnormed_ref, znormed_ref))
    ]
    for left in lefts:
        left.start()
    tile_waits(dms, dmix, tsend, trecv, chip, core, t)
    send_down.each(True)
    ring_ffn.finish()
    ring_gate.finish()
    block_grad(pgate, 0, lffn, lgate[...].reshape(4 * BLOCK, 512), 256)

    for r in range(SLOTS):

        @pl.when(served if r else jnp.logical_and(served, slot < 4))
        def _():
            q_wide = q[r].astype(F32)
            q_cols[r] = both_maps(q_wide.T).astype(BF)
            left = lax.broadcasted_iota(jnp.int32, q_wide.shape, 1) < 64
            q_rows[r] = jnp.concatenate(
                [jnp.where(left, q_wide, 0.0), jnp.where(left, 0.0, q_wide)], axis=0
            ).astype(BF)
            parts = parts_all[r]
            first, second = parts[:, :TILE], parts[:, TILE:]
            rms, hat = group_norm(parts, lam)
            e_t = dmix[r].astype(F32).T * OUT_SCALE
            column = jnp.sum(e_t * hat, axis=1, keepdims=True)
            d_differ = norm_back(e_t, sub, rms, hat, 0).astype(BF)
            d_wide = d_differ.astype(F32)
            d_cols[r] = d_differ
            d_rows[r] = d_wide.T.astype(BF)
            second_dot = jnp.sum(d_wide * second, axis=0, keepdims=True)
            row = lax.broadcasted_iota(jnp.int32, (128, 128), 0)
            lane = lax.broadcasted_iota(jnp.int32, (128, 128), 1)
            vec[24:25, :] += jnp.sum(jnp.where(row == lane, column, 0.0), axis=0, keepdims=True)
            here = lax.broadcasted_iota(jnp.int32, (1, 128), 1) == 6 * t + head
            vec[25:26, :] -= jnp.where(here, jnp.sum(second_dot, axis=1, keepdims=True), 0.0)
            deltas[r, 0:1, :] = jnp.sum(d_wide * first, axis=0, keepdims=True)
            deltas[r, 1:2, :] = -lam * second_dot
            dq_acc[r] = jnp.zeros((128, 2 * TILE), F32)

    def pass_on(k):
        for u in range(PER_SPAN):
            o = PER_SPAN * lax.rem(chip + k, SPANS) + u
            to_sibling(o).wait_recv()
            both[o] = (both[o].astype(F32) + sib[o].astype(F32)).astype(BF)
            to_home(o, True)

    def span(k, carry):
        b = lax.rem(chip + k, SPANS)
        start = pl.multiple_of(b * SPAN, SPAN)
        rows = pl.ds(start, SPAN)
        blocks = pl.ds(b * (SPAN // BLOCK), SPAN // BLOCK)
        acc[...] = jnp.zeros_like(acc)

        def step(r, masked):
            score = matmul(kv[blocks, :, :128].reshape(SPAN, 128), q_cols[r])
            prob = jnp.exp2(score * SCORE - logs[r])
            if masked:
                prob = jnp.where(key_mask(start, SPAN, tile_at(r), 2 * TILE), prob, 0.0)
            upper = matmul(kv[blocks, :, 128:].reshape(SPAN, 128), d_cols[r])
            p1, p2 = prob[:, :TILE], prob[:, TILE:]
            ds = jnp.concatenate(
                [p1 * (upper - deltas[r, 0:1, :]), p2 * (-lam * upper - deltas[r, 1:2, :])],
                axis=1,
            ).astype(BF)
            mixed = (p1 - lam * p2).astype(BF)
            acc[:, :128] += matmul(ds, q_rows[r])
            acc[:, 128:] += matmul(mixed, d_rows[r])
            dq_acc[r] += matmul(turned[:, rows], ds)

        def masked_step(r, carry):
            step(r, True)
            return carry

        def full_step(r, carry):
            step(r, False)
            return carry

        reach, past = 0, 0
        for r in range(SLOTS):
            last = tile_of(slot, r) * TILE // SPAN
            counts = (slot < 4) if r == 0 else True
            reach += jnp.where(jnp.logical_and(counts, last >= b), 1, 0)
            past += jnp.where(jnp.logical_and(counts, last > b), 1, 0)
        lax.fori_loop(SLOTS - reach, SLOTS - past, masked_step, 0)
        lax.fori_loop(SLOTS - past, SLOTS, full_step, 0)

        @pl.when(k >= 2)
        def _():
            for u in range(PER_SPAN):
                to_sibling(PER_SPAN * lax.rem(chip + k - 2, SPANS) + u).wait_send()

        for u in range(PER_SPAN):
            o = PER_SPAN * b + u
            for ref, at, which in ((given, o % (2 * PER_SPAN), 1 - core), (both, o, core)):
                part = acc[pl.ds(pl.multiple_of((2 * u + which) * BLOCK, BLOCK), BLOCK), :]
                ref[at, :, :128] = (part[:, :128] * 0.125).astype(BF)
                ref[at, :, 128:] = part[:, 128:].astype(BF)
            to_sibling(o).start()

        @pl.when(k > 0)
        def _():
            pass_on(k - 1)

        return carry

    @pl.when(served)
    def _():
        lax.fori_loop(0, EARLY_SPANS, span, 0)

    ring_up.finish()
    block_grad(pup, 0, lffn, lup[...].reshape(4 * BLOCK, 512), 256)

    @pl.when(served)
    def _():
        lax.fori_loop(EARLY_SPANS, SPANS, span, 0)
        pass_on(SPANS - 1)

    for r in range(SLOTS):

        @pl.when(served if r else jnp.logical_and(served, slot < 4))
        def _():
            dq_t = jnp.concatenate([dq_acc[r, :64, :TILE], dq_acc[r, 64:, TILE:]], axis=0)
            dq_out[r] = (dq_t * 0.125).T.astype(BF)

    home_sends(dq_out, land, gsend, grecv, chip, core, t, True)
    home_waits(dq_out, land, grecv)
    for j in range(3):
        for u in range(2):
            dqkv_ref[0, u * 128 : (u + 1) * 128, j * 128 : (j + 1) * 128] = land[j, u]
    ring_q.start()
    for j in range(3):
        total = jnp.zeros((BLOCK, 256), F32)
        for p in range(PER_HEAD):
            spot = j * PER_HEAD + p
            pltpu.make_async_copy(both.at[0], home.at[spot], krecv.at[spot]).wait()
            total = total + home[spot].astype(F32)
        dqkv_ref[1, :, j * 128 : (j + 1) * 128] = total[:, :128].astype(BF)
        dqkv_ref[2, :, j * 128 : (j + 1) * 128] = total[:, 128:].astype(BF)
    ring_k.start()
    ring_v.start()
    send_gate.each(True)
    send_up.each(True)

    for load in late_loads:
        load.wait()
    red2.drain()
    red4 = QuadReduce(*reduces[0], chip, core, t)

    def normed_term(k):
        rows = slice(k * CW, (k + 1) * CW)
        return (
            matmul_t(dqkv_ref[0], wg[rows, :384])
            + matmul_t(dqkv_ref[1], wg[rows, 384:768])
            + matmul_t(dqkv_ref[2], wu[rows, :384])
        )

    red4.run(normed_term)
    ring_mix.finish()
    ring_dres.finish()
    block_grad(pqo, 384, xdres, xmix[...].reshape(4 * BLOCK, 384), 384, 0, 384)
    x = x_ref[...]
    rms = rms_scale(x)
    hat = x * rms
    d_normed = jnp.concatenate([red4.result(k) for k in range(NC)], axis=1)
    part = jnp.sum(d_normed * hat, axis=0, keepdims=True)
    for k in range(12):
        vec[k : k + 1, :] = part[:, k * 128 : (k + 1) * 128]
    first_sum = [
        remote(vec, vecs.at[k], asem.at[0, k], asem.at[1, k], *member)
        for k, member in enumerate(members)
    ]
    for cp in first_sum:
        cp.start()
    grad_ref[...] = dres[...] + norm_back(d_normed, long_row(attn_ref), rms, hat)
    for left in lefts:
        left.wait()
    ring_q.finish()
    block_grad(pqo, 0, ldout, rq[...].reshape(4 * BLOCK, 384), 384, 0, 384)
    send_qo.each(True)
    ring_k.finish()
    block_grad(pkv, 0, ldout, rk[...].reshape(4 * BLOCK, 384), 384, 384, 384)
    for cp in first_sum:
        cp.wait_recv()
    share = pl.ds(pl.multiple_of((2 * core + t) * 8, 8), 8)
    quarter[...] = (vec[share, :] + vecs[0, share, :]) + (vecs[1, share, :] + vecs[2, share, :])

    def spread(k, start):
        to = 2 * lax.rem(chip + k, CHIPS) + core
        cp = remote(quarter, quarters.at[chip], bsem.at[0, k], bsem.at[1, chip], to, t)
        if start:
            cp.start()
        else:
            cp.wait_send()

    def spread_start(k, carry):
        spread(k, True)
        return carry

    def spread_end(k, carry):
        spread(k, False)
        return carry

    own = pltpu.make_async_copy(quarter, quarters.at[chip], bsem.at[1, chip])
    own.start()
    lax.fori_loop(1, CHIPS, spread_start, 0)
    ring_v.finish()
    block_grad(pkv, 384, ldout, rv[...].reshape(4 * BLOCK, 384), 384, 384, 384)
    send_kv.each(True)

    send_down.wait()
    for b in range(2):
        total = send_down.total(b, slice(0, 512))
        for h in range(2):
            swap[h, :, 2048 + b * 512 : 2560 + b * 512] = total[h * 24 : h * 24 + 24]
    for m, send in enumerate((send_gate, send_up)):
        send.wait()
        for b in range(2):
            total = send.total(b, slice(0, 512))
            at = m * 1024 + b * 512
            for h in range(2):
                swap[h, :, at : at + 512] = total[h * 24 : h * 24 + 24]
    sibling = s + 1 - 2 * core
    swap_copy = remote(swap.at[1 - core], swapped, swap_sem.at[0], swap_sem.at[1], sibling, t)
    swap_copy.start()

    def collect(k, total):
        pltpu.make_async_copy(quarter, quarters.at[k], bsem.at[1, k]).wait()
        return total + quarters[k]

    sums_ref[share, :] = lax.fori_loop(0, CHIPS, collect, jnp.zeros((8, 128), F32))
    last_sum = [
        remote(sums_ref.at[share], sums_ref.at[share], csem.at[0, k], csem.at[1, k], *member)
        for k, member in enumerate(members)
    ]
    for cp in last_sum:
        cp.start()
    for send, first in ((send_qo, (0, 3)), (send_kv, (1, 2))):
        send.wait()
        for m in range(2):
            total = send.total(0, slice(m * 384, m * 384 + 384))
            at = first[m] * 384
            for h in range(2):
                swap2[h, :, at : at + 384] = total[h * 24 : h * 24 + 24]
    swap2_copy = remote(swap2.at[1 - core], swapped2, swap2_sem.at[0], swap2_sem.at[1], sibling, t)
    swap2_copy.start()
    swap_copy.wait()
    swap_out(swap, swapped, ((gate_ref, 0), (up_ref, 1024), (down_ref, 2048)), 1024, core)

    for ring in (
        ring_dout, ring_mix, ring_hid, ring_gate, ring_up, ring_dres, ring_ffn, ring_q, ring_k, ring_v,
    ):
        ring.drain()
    for send in (send_gate, send_up, send_down, send_qo, send_kv):
        send.each(False)
    home_sends(dq_out, land, gsend, grecv, chip, core, t, False)
    tile_sends(dms, dmix, tsend, trecv, chip, core, t, False)
    for gather in (gather_f, gather_r):
        gather.drain()
    red3.drain()
    red4.drain()

    @pl.when(served)
    def _():
        for k in (SPANS - 2, SPANS - 1):
            for u in range(PER_SPAN):
                to_sibling(PER_SPAN * lax.rem(chip + k, SPANS) + u).wait_send()

        def last(o, carry):
            to_home(o, False)
            return carry

        lax.fori_loop(0, CHIPS // 2, last, 0)

    for cp in last_sum:
        cp.wait()
    for cp in first_sum:
        cp.wait_send()
    lax.fori_loop(1, CHIPS, spread_end, 0)
    swap2_copy.wait()
    outs = ((gq_ref, 0), (gk_ref, 384), (gv_ref, 768), (go_ref, 1152))
    swap_out(swap2, swapped2, outs, 384, core)


def swap_out(swap, swapped, outs, width, core):
    mine = swap[core]
    for c in range(2):

        @pl.when(core == c)
        def _():
            for ref, at in outs:
                ref[:, c * width : (c + 1) * width] = mine[:, at : at + width]
                other = (1 - c) * width
                ref[:, other : other + width] = swapped[:, at : at + width]


def layer(x, cot, mask, attn, ffn, sub, lambdas, wq, wk, wv, wo, wg, wu, wd):
    half = (CHIPS // 2, BLOCK, 256)
    vm = pltpu.VMEM
    sem = pltpu.SemaphoreType.DMA
    return pl.pallas_call(
        layer_kernel,
        name="layer",
        out_shape=(
            shape((ROWS, D), F32),
            shape((ROWS, D), F32),
            *([shape((24, 768), F32)] * 4),
            *([shape((24, 2048), F32)] * 3),
            shape((32, 128), F32),
            shape(GATHERED_Q, BF),
            shape(GATHERED_Q, BF),
        ),
        in_specs=[VM] * 7 + [ANY] * 7,
        out_specs=(VM,) * 10 + (ANY,) * 2,
        scratch_shapes=[
            vm((ROWS, D), F32),
            vm((3, BLOCK, 384), BF),
            *([vm(GATHERED_Q, BF)] * 5),
            vm((384, 768), BF),
            vm((384, 768), BF),
            vm((8, CHUNK, 768), BF),
            vm((8, CHUNK, 768), BF),
            vm((2, 24, 1536), F32),
            vm((24, 1536), F32),
            vm((32, 128), F32),
            vm((3, 32, 128), F32),
            vm((8, 128), F32),
            vm((CHIPS, 8, 128), F32),
            vm((3, 2, TILE, 128), BF),
            vm((D, 384), BF),
            vm((D, 1024), BF),
            vm((D, 1024), BF),
            vm((D, 1024), BF),
            vm((BLOCK, D), BF),
            vm((BLOCK, D), BF),
            vm((3, 2, TILE, 128), BF),
            vm((BLOCK, D), BF),
            vm((2, BLOCK, 512), BF),
            vm((2, BLOCK, 512), BF),
            vm((2, BLOCK, 512), BF),
            vm((BLOCK, 384), BF),
            vm((SLOTS, TILE, 128), BF),
            vm(KV, BF),
            vm((SLOTS, 128, 2 * TILE), F32),
            vm((SLOTS, 1, 2 * TILE), F32),
            vm((SLOTS, TILE, 128), BF),
            vm(GATHERED, BF),
            *([vm((4, BLOCK, 512), BF)] * 3),
            vm(GATHERED, BF),
            *([vm((768, 512), BF)] * 3),
            *([vm((16, CHUNK, 512), BF)] * 3),
            vm((2, 24, 3072), F32),
            vm((24, 3072), F32),
            vm((128, CHIPS * BLOCK), BF),
            vm((SPAN, 256), F32),
            vm((SLOTS, 128, 2 * TILE), BF),
            vm((SLOTS, 2 * TILE, 128), BF),
            vm((SLOTS, 128, TILE), BF),
            vm((SLOTS, TILE, 128), BF),
            vm((SLOTS, 2, TILE), F32),
            vm((SLOTS, 128, 2 * TILE), F32),
            vm((SLOTS, TILE, 128), BF),
            vm((2 * PER_SPAN, BLOCK, 256), BF),
            vm(half, BF),
            vm(half, BF),
            vm((3 * PER_HEAD, BLOCK, 256), BF),
            vm((8, BLOCK), F32),
            pltpu.SMEM((2,), F32),
            vm((8, 2 * TILE), F32),
            *(REDUCE_SCRATCH * 2),
            *(GATHER_SEMS * 4),
            *(RING_SEMS * 11),
            *ONCE_SEMS,
            *(scatter_sems(16) * 2),
            *(scatter_sems(8) * 2),
            *scatter_sems(16),
            sem((4,)),
            sem((SLOTS,)),
            sem((3, 2)),
            sem((6,)),
            sem((SLOTS,)),
            sem((2,)),
            sem((2 * PER_SPAN,)),
            sem((CHIPS // 2,)),
            sem((CHIPS // 2,)),
            sem((3 * PER_HEAD,)),
            sem((SLOTS,)),
            sem((3, 2)),
            sem((3,)),
            sem((2,)),
            sem((2,)),
            sem((2, 3)),
            sem((2, CHIPS)),
            sem((2, 3)),
            sem((WORKERS,)),
            sem((CHIPS,)),
            sem((CHIPS // 2,)),
            sem((6,)),
            sem((SLOTS,)),
        ],
        compiler_params=pltpu.CompilerParams(
            collective_id=0, has_side_effects=True, vmem_limit_bytes=VMEM_LIMIT
        ),
    )(x, cot, mask, attn, ffn, sub, lambdas, wq, wk, wv, wo, wg, wu, wd)


def publish(lambdas, sums, arrays):
    count = len(arrays)

    def kernel(lambdas_ref, sums_ref, *refs):
        for k in range(count):
            refs[count + k][...] = refs[k][...]
        attn_ref, ffn_ref, sub_ref, grad_ref = refs[2 * count :]
        attn_ref[...] = sums_ref[0:12, :]
        ffn_ref[...] = sums_ref[12:24, :]
        sub_ref[...] = sums_ref[24:25, :]
        vectors, first, second = lambda_parts(lambdas_ref)
        d_lam = as_column(sums_ref[25:26, :])[:12, :1]
        factors = (d_lam * first, d_lam * first, -d_lam * second, -d_lam * second)
        for k, other in enumerate((1, 0, 3, 2)):
            grad_ref[:, k, :] = factors[k] * vectors[other]

    return pl.pallas_call(
        kernel,
        name="publish",
        out_shape=tuple(shape(a.shape, a.dtype) for a in arrays)
        + (shape((12, 128), F32), shape((12, 128), F32), shape((1, 128), F32), shape((12, 4, 64), F32)),
        in_specs=[VM] * (count + 2),
        out_specs=(VM,) * (count + 4),
    )(lambdas, sums, *arrays)


def on_device(
    hidden_in, cotangent, needle_mask, attn_gain, lambdas, subln_gain, ffn_gain,
    weight_query, weight_key, weight_value, weight_out, weight_gate, weight_up, weight_down,
):
    mask = needle_mask.reshape(1, ROWS)
    attn = attn_gain.reshape(12, 128)
    sub = subln_gain.reshape(1, 128)
    by_head = jnp.transpose(lambdas, (1, 0, 2))
    *results, sums, _, _ = layer(
        hidden_in, cotangent, mask, attn, ffn_gain.reshape(12, 128), sub, by_head,
        weight_query, weight_key, weight_value, weight_out, weight_gate, weight_up, weight_down,
    )
    *results, attn_grad, ffn_grad, sub_grad, lambda_grad = publish(by_head, sums, results)
    return (
        *results,
        attn_grad.reshape(D),
        jnp.transpose(lambda_grad, (1, 0, 2)),
        sub_grad.reshape(128),
        ffn_grad.reshape(D),
    )


def solution(mesh):
    split = P(None, "tp")
    rows = P(("seq", "tp"), None)
    both = P("seq", "tp")
    return jax.shard_map(
        on_device,
        mesh=mesh,
        in_specs=(rows, rows, P(("seq", "tp"))) + (P(),) * 4 + (split,) * 7,
        out_specs=(rows, rows) + (both,) * 7 + (P(),) * 4,
        check_vma=False,
    )
```

```python
import math

import jax
import jax.numpy as jnp
from jax import lax
from jax.experimental import pallas as pl
from jax.experimental.pallas import tpu as pltpu
from jax.sharding import PartitionSpec as P

MESH = pl.DeviceIdType.MESH
BF = jnp.bfloat16
F32 = jnp.float32
EPS = 1e-06
LAMBDA_INIT = 0.8 - 0.6 * math.exp(-3.6)
OUT_SCALE = 1.0 - LAMBDA_INIT
D = 1536
CHIPS = 32
PER_HEAD = 5
WORKERS = 15
ROWS = 64
BLOCK = 256
TILE = 128
SLOTS = 7
KB = 512
LOG2E = 1.4426950408889634
SCORE = 0.125 * LOG2E
VMEM_LIMIT = 63 * 2**20


def place():
    s = lax.axis_index("seq")
    return s // 2, s % 2, lax.axis_index("tp")


def worker(chip, core):
    x, y, z = chip % 4, chip // 4 % 2, chip // 8
    at = 4 * z + x
    return (x + y + z) % 2, at, at % PER_HEAD * 2 + core, at < WORKERS


def worker_chip(parity, at):
    x, z = at % 4, at // 4
    return (2 * z + (x + z + parity) % 2) * 4 + x


def owner_of(tile):
    step = (tile - 4) // 10
    pos = (tile - 4) % 10
    slot = jnp.where(step % 2 == 0, pos, 9 - pos)
    early = tile < 4
    return jnp.where(early, tile, slot), jnp.where(early, 0, step + 1)


def tile_of(slot, r):
    if r == 0:
        return slot
    return 4 + 10 * (r - 1) + (slot if (r - 1) % 2 == 0 else 9 - slot)


def matmul(a, b):
    return jnp.dot(a, b, preferred_element_type=F32)


def matmul_t(a, b):
    return lax.dot_general(a, b, (((1,), (1,)), ((), ())), preferred_element_type=F32)


def rms_scale(values, axis=-1):
    return lax.rsqrt(jnp.mean(values * values, axis=axis, keepdims=True) + EPS)


def norm_back(grad_normed, gain, rms, hat, axis=-1):
    scaled = grad_normed * gain
    return rms * (scaled - hat * jnp.mean(scaled * hat, axis=axis, keepdims=True))


def greet_all(chip, core, t):
    barrier = pltpu.get_barrier_semaphore()
    s = 2 * chip + core

    def greet(o, carry):
        pl.semaphore_signal(
            barrier, inc=1, device_id=(lax.rem(s + o, 2 * CHIPS), t), device_id_type=MESH
        )
        return carry

    lax.fori_loop(1, 2 * CHIPS, greet, 0)
    pl.semaphore_signal(barrier, inc=1, device_id=(s, 1 - t), device_id_type=MESH)
    pl.semaphore_wait(barrier, 2 * CHIPS)


def remote(src, dst, send_sem, recv_sem, s, t):
    return pltpu.make_async_remote_copy(
        src_ref=src,
        dst_ref=dst,
        send_sem=send_sem,
        recv_sem=recv_sem,
        device_id=(s, t),
        device_id_type=MESH,
    )


def rows_at(ref, start, count):
    return ref.at[pl.ds(pl.multiple_of(start, ROWS), count)]


class QuadGather:
    def __init__(self, buf, send, recv, chip, core, t):
        self.buf, self.send, self.recv = buf, send, recv
        self.chip, self.core, self.t = chip, core, t
        mine = core * 128 + t * ROWS
        self.mine = mine
        self.near = core * 128 + (1 - t) * ROWS
        sib = (2 * chip + 1 - core, t)
        self.to_near = self.copy(mine, 0, (2 * chip + core, 1 - t))
        self.to_sib = self.copy(mine, 1, sib)
        self.forward = self.copy(self.near, 2, sib)

    def copy(self, row, k, target):
        view = rows_at(self.buf, row, ROWS)
        return remote(view, view, self.send.at[k], self.recv.at[k], *target)

    def start(self):
        self.to_near.start()
        self.to_sib.start()

    def finish(self):
        self.to_near.wait_recv()
        self.forward.start()
        self.to_sib.wait_recv()
        self.forward.wait_recv()

    def drain(self):
        self.to_near.wait_send()
        self.to_sib.wait_send()
        self.forward.wait_send()


class RingGather:
    def __init__(self, pieces, land, send, recv, axis, chip, core, t):
        at = chip % 4 if axis == "x" else chip // 8
        self.local = pltpu.make_async_copy(pieces(at), land.at[at], recv.at[at])
        self.copies = []
        for k in (1, 3, 2):
            if axis == "x":
                peer, chip_to = (at + k) % 4, chip - at + (at + k) % 4
            else:
                peer, chip_to = (at + k) % 4, (chip + 8 * k) % CHIPS
            self.copies.append(
                remote(pieces(peer), land.at[at], send.at[k - 1], recv.at[at], 2 * chip_to + core, t)
            )
        self.waits = [
            pltpu.make_async_copy(pieces(at), land.at[k], recv.at[k]) for k in range(4)
        ]

    def start(self):
        self.local.start()
        for cp in self.copies:
            cp.start()

    def finish(self):
        for cp in self.waits:
            cp.wait()

    def drain(self):
        for cp in self.copies:
            cp.wait_send()


class RingGatherOnce:
    def __init__(self, pieces, land, send, recv, pass_send, pass_recv, axis, chip, core, t):
        at = chip % 4 if axis == "x" else chip // 8
        self.mine = pl.ds(pl.multiple_of(core * 128, 128), 128)
        self.local = pltpu.make_async_copy(pieces(at), land.at[at], recv.at[0])
        self.local_at = at
        self.copies, self.passes = [], []
        for k in (1, 3, 2):
            peer = (at + k) % 4
            chip_to = chip - at + peer if axis == "x" else (chip + 8 * k) % CHIPS
            self.copies.append(
                remote(
                    pieces(peer).at[self.mine], land.at[at, self.mine],
                    send.at[k - 1], recv.at[4 - k], 2 * chip_to + core, t,
                )
            )
            view = land.at[peer, self.mine]
            self.passes.append(
                (
                    pltpu.make_async_copy(pieces(at).at[self.mine], view, recv.at[k]),
                    remote(view, view, pass_send.at[k - 1], pass_recv.at[k - 1], 2 * chip + 1 - core, t),
                )
            )

    def start(self):
        self.local.start()
        for cp in self.copies:
            cp.start()

    def forward(self):
        for arrive, cp in self.passes:
            arrive.wait()
            cp.start()

    def finish(self):
        self.local.wait()
        for _, cp in self.passes:
            cp.wait_recv()

    def drain(self):
        for cp in self.copies:
            cp.wait_send()
        for _, cp in self.passes:
            cp.wait_send()


ONCE_SEMS = [
    pltpu.SemaphoreType.DMA((3,)),
    pltpu.SemaphoreType.DMA((4,)),
    pltpu.SemaphoreType.DMA((3,)),
    pltpu.SemaphoreType.DMA((3,)),
]
RING_SEMS = [pltpu.SemaphoreType.DMA((3,)), pltpu.SemaphoreType.DMA((4,))]


def block_grad(dst, start, left, right, step, at=0, total=768):
    width = right.shape[1]

    def one(m, carry):
        cols = pl.ds(pl.multiple_of(m * step, 128), step)
        part = left[:, :, pl.ds(pl.multiple_of(at + m * step, 128), step)].reshape(4 * BLOCK, step)
        dst[cols, start : start + width] = lax.dot_general(
            part, right, (((0,), (0,)), ((), ())), preferred_element_type=F32
        ).astype(BF)
        return carry

    lax.fori_loop(0, total // step, one, 0)


CHUNK = 48


class Scatter:
    def __init__(self, part, land, send, recv, count, first, spot, chip, core, t):
        self.part, self.land, self.send, self.recv = part, land, send, recv
        self.count, self.first, self.spot = count, first, spot
        self.chip, self.core, self.t = chip, core, t

    def source(self, i):
        return self.part.at[pl.ds(pl.multiple_of(i * CHUNK, 16), CHUNK)]

    def each(self, start):
        self.some(0, self.count, start)

    def some(self, first, end, start):
        def one(o, carry):
            i = lax.rem(self.chip + 1 + 3 * o, self.count)
            owner = self.first + i
            cp = remote(
                self.source(i), self.land.at[self.spot], self.send.at[i], self.recv.at[self.spot],
                2 * owner + self.core, self.t,
            )
            if start:

                @pl.when(owner == self.chip)
                def _():
                    pltpu.make_async_copy(
                        self.source(i), self.land.at[self.spot], self.recv.at[self.spot]
                    ).start()

            @pl.when(owner != self.chip)
            def _():
                if start:
                    cp.start()
                else:
                    cp.wait_send()

            return carry

        lax.fori_loop(first, end, one, 0)

    def wait(self):
        def one(k, carry):
            pltpu.make_async_copy(self.source(0), self.land.at[k], self.recv.at[k]).wait()
            return carry

        lax.fori_loop(0, self.count, one, 0)

    def total(self, b, cols):
        def one(k, carry):
            return carry + self.land[8 * b + k, :, cols].astype(F32)

        return lax.fori_loop(0, 8, one, jnp.zeros((CHUNK, cols.stop - cols.start), F32))


def scatter_sems(count):
    return [pltpu.SemaphoreType.DMA((count,)), pltpu.SemaphoreType.DMA((count,))]


GATHER_SEMS = [pltpu.SemaphoreType.DMA((3,)), pltpu.SemaphoreType.DMA((3,))]
CW = 512
NC = D // CW


class QuadReduce:
    def __init__(self, part, dsend, drecv, ysend, yrecv, ds, dr, ys, yr, chip, core, t):
        self.part, self.dsend, self.drecv = part, dsend, drecv
        self.ysend, self.yrecv = ysend, yrecv
        self.core, self.t = core, t
        self.d = [
            remote(dsend.at[k], drecv.at[k], ds.at[k], dr.at[k], 2 * chip + 1 - core, t)
            for k in range(NC)
        ]
        self.y = [
            remote(ysend.at[k], yrecv.at[k], ys.at[k], yr.at[k], 2 * chip + core, 1 - t)
            for k in range(NC)
        ]

    def rows(self, start, count, k):
        return self.part[pl.ds(pl.multiple_of(start, ROWS), count), k * CW : (k + 1) * CW]

    def put(self, k, value):
        self.part[:, k * CW : (k + 1) * CW] = value
        self.dsend[k] = self.rows((1 - self.core) * 128, 128, k).astype(BF)
        self.d[k].start()

    def middle(self, k):
        self.d[k].wait_recv()
        near = (1 - self.t) * ROWS
        far = self.rows(self.core * 128 + near, ROWS, k)
        got = self.drecv[k, pl.ds(pl.multiple_of(near, ROWS), ROWS), :]
        self.ysend[k] = (far + got.astype(F32)).astype(BF)
        self.y[k].start()

    def result(self, k):
        mine = self.t * ROWS
        own = self.rows(self.core * 128 + mine, ROWS, k)
        got = self.drecv[k, pl.ds(pl.multiple_of(mine, ROWS), ROWS), :].astype(F32)
        self.y[k].wait_recv()
        return own + got + self.yrecv[k].astype(F32)

    def run(self, term):
        for k in range(NC):
            self.put(k, term(k))
            if k:
                self.middle(k - 1)
        self.middle(NC - 1)

    def drain(self):
        for k in range(NC):
            self.d[k].wait_send()
            self.y[k].wait_send()


REDUCE_SCRATCH = [
    pltpu.VMEM((BLOCK, D), F32),
    pltpu.VMEM((NC, 128, CW), BF),
    pltpu.VMEM((NC, 128, CW), BF),
    pltpu.VMEM((NC, ROWS, CW), BF),
    pltpu.VMEM((NC, ROWS, CW), BF),
] + [pltpu.SemaphoreType.DMA((NC,))] * 4


def tile_sends(tiles, land, send, recv, chip, core, t, start):
    s = 2 * chip + core
    for j in range(3):
        for u in range(2):
            slot, index = owner_of(2 * chip + u)
            target = 2 * worker_chip(core, j * PER_HEAD + slot // 2) + slot % 2
            k = j * 2 + u

            if start:

                @pl.when(target == s)
                def _():
                    pltpu.make_async_copy(tiles.at[j, u], land.at[index], recv.at[index]).start()

            @pl.when(target != s)
            def _():
                cp = remote(tiles.at[j, u], land.at[index], send.at[k], recv.at[index], target, t)
                if start:
                    cp.start()
                else:
                    cp.wait_send()


def tile_waits(tiles, land, send, recv, chip, core, t):
    _, _, slot, served = worker(chip, core)
    for r in range(SLOTS):
        here = served
        if r == 0:
            here = jnp.logical_and(here, slot < 4)

        @pl.when(here)
        def _():
            pltpu.make_async_copy(tiles.at[0, 0], land.at[r], recv.at[r]).wait()


def home_sends(tiles, land, send, recv, chip, core, t, start):
    s = 2 * chip + core
    parity, at, slot, served = worker(chip, core)
    for r in range(SLOTS):
        here = served
        if r == 0:
            here = jnp.logical_and(here, slot < 4)
        tile = tile_of(slot, r)
        target = (tile // 2) * 2 + parity
        j, u = at // PER_HEAD, tile % 2

        if start:

            @pl.when(jnp.logical_and(here, target == s))
            def _():
                pltpu.make_async_copy(tiles.at[r], land.at[j, u], recv.at[j, u]).start()

        @pl.when(jnp.logical_and(here, target != s))
        def _():
            cp = remote(tiles.at[r], land.at[j, u], send.at[r], recv.at[j, u], target, t)
            if start:
                cp.start()
            else:
                cp.wait_send()


def home_waits(tiles, land, recv):
    for j in range(3):
        for u in range(2):
            pltpu.make_async_copy(tiles.at[0], land.at[j, u], recv.at[j, u]).wait()


def weight_load(ref, buf, sem, core, width):
    return pltpu.make_async_copy(
        ref.at[:, pl.ds(pl.multiple_of(core * width, 128), width)], buf, sem
    )


VM = pl.BlockSpec(memory_space=pltpu.VMEM)
ANY = pl.BlockSpec(memory_space=pl.ANY)


def shape(dims, dtype):
    return jax.ShapeDtypeStruct(dims, dtype)


HALVES = (2, BLOCK, 768)
QUARTERS = (4, BLOCK, 384)
GATHERED = (4, BLOCK, 768)
GATHERED_Q = (4, BLOCK, 384)
KV = (CHIPS, BLOCK, 256)
STEP = 2048


def eye(size):
    row = lax.broadcasted_iota(jnp.int32, (size, size), 0)
    col = lax.broadcasted_iota(jnp.int32, (size, size), 1)
    return jnp.where(row == col, 1.0, 0.0).astype(BF)


def both_maps(q_t):
    top = lax.broadcasted_iota(jnp.int32, q_t.shape, 0) < 64
    return jnp.concatenate([jnp.where(top, q_t, 0.0), jnp.where(top, 0.0, q_t)], axis=1)


def key_mask(start, count, tile, width):
    key = start + lax.broadcasted_iota(jnp.int32, (count, width), 0)
    query = tile * TILE + lax.broadcasted_iota(jnp.int32, (count, width), 1) % TILE
    return key <= query


def group_norm(parts, lam):
    first, second = parts[:, :TILE], parts[:, TILE:]
    differ = first - lam * second
    rms = rms_scale(differ, 0)
    return rms, differ * rms


def long_row(ref):
    return jnp.concatenate([ref[k : k + 1, :] for k in range(12)], axis=1)


def as_column(row):
    return jnp.broadcast_to(row, (128, 128)).T


def mask_column(mask_ref):
    mask = mask_ref[...].astype(F32)
    return as_column(jnp.concatenate([mask, mask], axis=1))[:ROWS, :1]


def lambda_parts(lambdas_ref):
    vectors = [lambdas_ref[:, k, :] for k in range(4)]
    first = jnp.exp(jnp.sum(vectors[0] * vectors[1], axis=-1, keepdims=True))
    second = jnp.exp(jnp.sum(vectors[2] * vectors[3], axis=-1, keepdims=True))
    return vectors, first, second


def lambda_of(lambdas_ref, head):
    _, first, second = lambda_parts(lambdas_ref)
    every = first - second + LAMBDA_INIT
    mine = lax.broadcasted_iota(jnp.int32, every.shape, 0) == head
    return jnp.sum(jnp.where(mine, every, 0.0), axis=0, keepdims=True)


SPAN = 1024
SPANS = CHIPS * BLOCK // SPAN
PER_SPAN = SPAN // BLOCK // 2
EARLY_SPANS = 3


def layer_kernel(
    x_ref, cot_ref, mask_ref, attn_ref, ffn_ref, sub_ref, lambdas_ref,
    wq_ref, wk_ref, wv_ref, wo_ref, wg_ref, wu_ref, wd_ref,
    out_to, grad_to, gq_to, gk_to, gv_to, go_to, gate_to, up_to, down_to, sums_ref,
    xnormed_ref, znormed_ref,
    out_ref, grad_ref, gq_ref, gk_ref, gv_ref, go_ref, gate_ref, up_ref, down_ref,
    dres, dqkv_ref, rq, rk, rvx, rvz, xmix, xdres, pqo, pkv, sqo, skv, swap2, swapped2,
    vec, vecs, quarter, quarters,
    land, wo, wg, wu, wd, fbuf, nbuf, dms, obuf, dgate, dup, hid, mix,
    q, kv, parts_all, logs, dmix,
    lffn, lgate, lup, lhid, ldout, pgate, pup, pdown, sgate, sup, sdown, swap, swapped,
    turned, acc, q_cols, q_rows, d_cols, d_rows, deltas, dq_acc, dq_out, given, sib, both, home,
    peaks, kmax, total, *rest,
):
    chip, core, t = place()
    s = 2 * chip + core
    parity, place_at, slot, served = worker(chip, core)
    head = 3 * parity + place_at // PER_HEAD
    x_at, z_at = chip % 4, chip // 8
    taken = iter(rest)

    def take(count):
        return [next(taken) for _ in range(count)]

    reduces = [take(9) for _ in range(2)]
    gather_sems = [take(2) for _ in range(4)]
    ring_sems = [take(2) for _ in range(12)]
    once_sems = take(4)
    scatter = [take(2) for _ in range(5)]
    wsem, hsend, hrecv, tsend, trecv, swap_sem = take(6)
    dsend, drecv, ksend, krecv, gsend, grecv = take(6)
    w2sem, lsem, swap2_sem, asem, bsem, csem = take(6)
    (osem,) = take(1)
    results = [
        pltpu.make_async_copy(src, dst, osem.at[k])
        for k, (src, dst) in enumerate(
            (
                (out_ref, out_to), (grad_ref, grad_to), (gq_ref, gq_to), (gk_ref, gk_to),
                (gv_ref, gv_to), (go_ref, go_to), (gate_ref, gate_to), (up_ref, up_to),
                (down_ref, down_to),
            )
        )
    ]
    kvsend, kvrecv, fsend, qsend, qrecv = take(5)
    rbuf = nbuf
    front = dq_acc.at[0]


    def halves(ref):
        return lambda p: ref.at[:, pl.ds(pl.multiple_of(p // 2 * 768, 128), 768)]

    def quarters_of(ref):
        return lambda p: ref.at[:, pl.ds(pl.multiple_of(p * 384, 128), 384)]

    gather_f = QuadGather(fbuf, *gather_sems[0], chip, core, t)
    gather_r = QuadGather(rbuf, *gather_sems[1], chip, core, t)
    ring_dout = RingGather(halves(obuf), ldout, *ring_sems[0], "x", chip, core, t)
    ring_mix = RingGather(lambda p: mix, xmix, *ring_sems[1], "x", chip, core, t)
    ring_hid = RingGather(lambda p: hid.at[p % 2], lhid, *ring_sems[2], "x", chip, core, t)
    ring_gate = RingGather(lambda p: dgate.at[p % 2], lgate, *ring_sems[3], "z", chip, core, t)
    ring_up = RingGather(lambda p: dup.at[p % 2], lup, *ring_sems[10], "z", chip, core, t)
    ring_dres = RingGather(
        quarters_of(rbuf), xdres, *ring_sems[4], "x", chip, core, t,
    )
    ring_xn = RingGather(quarters_of(nbuf), xnormed_ref, *ring_sems[5], "x", chip, core, t)
    ring_zn = RingGather(quarters_of(nbuf), znormed_ref, *ring_sems[6], "z", chip, core, t)
    ring_q = RingGather(lambda p: dqkv_ref.at[0], rq, *ring_sems[7], "x", chip, core, t)
    ring_k = RingGather(lambda p: dqkv_ref.at[1], rk, *ring_sems[8], "z", chip, core, t)
    ring_vx = RingGather(
        lambda p: dqkv_ref.at[2, :, :128], rvx, *ring_sems[9], "x", chip, core, t
    )
    ring_vz = RingGather(
        lambda p: dqkv_ref.at[2, :, 128:], rvz, *ring_sems[11], "z", chip, core, t
    )
    send_qo = Scatter(pqo, sqo, *scatter[2], 8, 8 * x_at, chip // 4, chip, core, t)
    send_kv = Scatter(pkv, skv, *scatter[3], 8, 8 * z_at, chip % 8, chip, core, t)
    members = ((s + 1 - 2 * core, t), (s, 1 - t), (s + 1 - 2 * core, 1 - t))
    ring_ffn = RingGatherOnce(
        halves(fbuf), lffn, *once_sems, "z", chip, core, t,
    )
    send_down = Scatter(
        pdown, sdown, *scatter[0], 16, 16 * (x_at // 2), 8 * (x_at % 2) + chip // 4, chip, core, t
    )
    send_gate, send_up = (
        Scatter(
            part, to, *sems, 16, 16 * (z_at // 2), 8 * (z_at % 2) + chip % 8, chip, core, t
        )
        for part, to, sems in ((pgate, sgate, scatter[1]), (pup, sup, scatter[4]))
    )
    first_loads = [
        weight_load(ref, buf.at[:, k * 384 : (k + 1) * 384], w2sem.at[i], core, 384)
        for i, (ref, buf, k) in enumerate(((wk_ref, wg, 0), (wv_ref, wg, 1), (wq_ref, wu, 0)))
    ]
    loads = [
        weight_load(wo_ref, wo, wsem.at[0], core, 384),
        weight_load(wg_ref, wg, wsem.at[1], core, 1024),
        weight_load(wu_ref, wu, wsem.at[2], core, 1024),
        weight_load(wd_ref, wd, wsem.at[3], core, 1024),
    ]
    for load in first_loads + loads[:1]:
        load.start()
    quad = QuadGather(nbuf, *gather_sems[2], chip, core, t)
    quad_o = QuadGather(obuf, *gather_sems[3], chip, core, t)
    mine = pl.ds(pl.multiple_of(quad.mine, ROWS), ROWS)
    x = x_ref[...]
    normed = (x * rms_scale(x) * long_row(attn_ref)).astype(BF)
    nbuf[mine, :] = normed
    greet_all(chip, core, t)
    quad.start()
    dout = cot_ref[...] * mask_column(mask_ref)
    obuf[mine, :] = dout.astype(BF)
    lam = lambda_of(lambdas_ref, 6 * t + head)
    sub = as_column(sub_ref[...])
    ffn_gain = long_row(ffn_ref)
    vec[...] = jnp.zeros_like(vec)
    unit = eye(256)
    quad.finish()
    for k in range(2):
        first_loads[k].wait()
        value = matmul(nbuf[...], wg[:, k * 384 : (k + 1) * 384]).astype(BF)
        for j in range(3):
            dqkv_ref[j, :, k * 128 : (k + 1) * 128] = value[:, j * 128 : (j + 1) * 128]

    def kv_piece(j):
        return dqkv_ref.at[j, :, :256]

    def kv_sends(start):
        def one(o, carry):
            w = lax.rem(chip + 7 * o, WORKERS)
            j = w // PER_HEAD
            target = 2 * worker_chip(core, w) + chip % 2
            if start:

                @pl.when(target == s)
                def _():
                    pltpu.make_async_copy(kv_piece(j), kv.at[chip], kvrecv.at[chip]).start()

            @pl.when(target != s)
            def _():
                cp = remote(kv_piece(j), kv.at[chip], kvsend.at[w], kvrecv.at[chip], target, t)
                if start:
                    cp.start()
                else:
                    cp.wait_send()

            return carry

        lax.fori_loop(0, WORKERS, one, 0)

    kv_sends(True)
    first_loads[2].wait()
    value = matmul(nbuf[...], wu[:, :384]).astype(BF)
    for j in range(3):
        for u in range(2):
            dms[j, u] = value[u * 128 : (u + 1) * 128, j * 128 : (j + 1) * 128]
    tile_sends(dms, q, qsend, qrecv, chip, core, t, True)
    quad_o.start()
    for load in loads[1:]:
        load.start()

    def forward(o):
        source = lax.rem((chip // 2 + o) * 2 + core, CHIPS)
        view = kv.at[source]
        return source, remote(view, view, fsend.at[o], kvrecv.at[source], s + 1 - 2 * core, t)

    def turn(source):
        block = kv[source]
        at = pl.ds(pl.multiple_of(source * BLOCK, BLOCK), BLOCK)
        both_t = matmul_t(unit, block)
        turned[:, at] = both_t[128:].astype(BF)
        square = both_t[:128] * both_t[:128]
        for m in range(2):
            largest = jnp.sum(square[64 * m : 64 * m + 64], axis=0, keepdims=True)
            peaks[m : m + 1, :] = jnp.maximum(peaks[m : m + 1, :], largest)

    @pl.when(served)
    def _():
        peaks[...] = jnp.zeros_like(peaks)

        def take(o, carry):
            source, cp = forward(o)
            pltpu.make_async_copy(kv_piece(0), kv.at[source], kvrecv.at[source]).wait()
            cp.start()
            turn(source)
            return carry

        lax.fori_loop(0, CHIPS // 2, take, 0)

        def finish(o, carry):
            source = lax.rem((chip // 2 + o) * 2 + 1 - core, CHIPS)
            pltpu.make_async_copy(kv_piece(0), kv.at[source], kvrecv.at[source]).wait()
            forward(o)[1].wait_send()
            turn(source)
            return carry

        lax.fori_loop(0, CHIPS // 2, finish, 0)
        for m in range(2):
            kmax[m] = jnp.max(peaks[m : m + 1, :])

    quad_o.finish()
    tile_waits(dms, q, qsend, qrecv, chip, core, t)
    ring_zn.start()
    ring_dout.start()

    for r in range(SLOTS):
        tile = tile_of(slot, r)

        @pl.when(served if r else jnp.logical_and(served, slot < 4))
        def _():
            q_t = q[r].astype(F32).T
            square = q_t * q_t
            bound = SCORE * jnp.concatenate(
                [
                    jnp.sqrt(jnp.sum(square[:64], axis=0, keepdims=True) * kmax[0]),
                    jnp.sqrt(jnp.sum(square[64:], axis=0, keepdims=True) * kmax[1]),
                ],
                axis=1,
            )
            q_both = both_maps(q_t).astype(BF)
            front[...] = jnp.zeros_like(front)
            total[...] = jnp.zeros_like(total)

            def step(b, masked):
                sums, out = None, None
                for u in range(STEP // KB):
                    start = pl.multiple_of(b * STEP + u * KB, KB)
                    pair = pl.ds(b * (STEP // BLOCK) + u * (KB // BLOCK), KB // BLOCK)
                    score = matmul(kv[pair, :, :128].reshape(KB, 128), q_both)
                    prob = jnp.exp2(score * SCORE - bound)
                    if masked:
                        prob = jnp.where(key_mask(start, KB, tile, 2 * TILE), prob, 0.0)
                    part = jnp.sum(prob.reshape(KB // 8, 8, 2 * TILE), axis=0)
                    term = matmul(turned[:, pl.ds(start, KB)], prob.astype(BF))
                    sums = part if sums is None else sums + part
                    out = term if out is None else out + term
                total[...] += sums
                front[...] += out

            full = tile * TILE // STEP

            def body(b, carry):
                step(b, False)
                return carry

            lax.fori_loop(0, full, body, 0)
            step(full, True)
            whole = jnp.sum(total[...], axis=0, keepdims=True)
            parts = front[...] / whole
            parts_all[r] = parts
            logs[r] = bound + jnp.log(whole) * LOG2E
            rms, hat = group_norm(parts, lam)
            dq_out[r] = (hat * sub * OUT_SCALE).T.astype(BF)


    home_sends(dq_out, land, hsend, hrecv, chip, core, t, True)
    loads[0].wait()
    home_waits(dq_out, land, hrecv)
    for j in range(3):
        for u in range(2):
            mix[u * 128 : (u + 1) * 128, j * 128 : (j + 1) * 128] = land[j, u]
    red = QuadReduce(*reduces[0], chip, core, t)
    red.run(lambda k: matmul_t(mix[...], wo[k * CW : (k + 1) * CW, :]))
    ring_xn.start()
    ring_mix.start()
    home_sends(dq_out, land, hsend, hrecv, chip, core, t, False)
    kv_sends(False)
    tile_sends(dms, q, qsend, qrecv, chip, core, t, False)
    resid = x_ref[...] + jnp.concatenate([red.result(k) for k in range(NC)], axis=1)
    ffn_rms = rms_scale(resid)
    ffn_hat = resid * ffn_rms
    fbuf[mine, :] = (ffn_hat * ffn_gain).astype(BF)
    gather_f.start()
    for load in loads[1:]:
        load.wait()
    red.drain()
    gather_f.finish()
    ring_ffn.start()

    def hidden_step(n, carry):
        cols = pl.ds(pl.multiple_of(n * 256, 256), 256)
        b, at = n // 2, n % 2
        gate = matmul(fbuf[...], wg[:, cols])
        up = matmul(fbuf[...], wu[:, cols])
        d_hidden = matmul(obuf[...], wd[:, cols])
        sig = 1.0 / (1.0 + jnp.exp(-gate))
        silu = gate * sig
        to = pl.ds(pl.multiple_of(at * 256, 256), 256)
        hid[b, :, to] = (silu * up).astype(BF)
        dgate[b, :, to] = (d_hidden * up * sig * (1.0 + gate * (1.0 - sig))).astype(BF)
        dup[b, :, to] = (d_hidden * silu).astype(BF)
        return carry

    lax.fori_loop(0, 4, hidden_step, 0)
    ring_gate.start()
    ring_hid.start()
    red2 = QuadReduce(*reduces[0], chip, core, t)

    def ffn_term(k):
        rows = slice(k * CW, (k + 1) * CW)
        return (
            matmul_t(dgate[0], wg[rows, :512])
            + matmul_t(dgate[1], wg[rows, 512:])
            + matmul_t(dup[0], wu[rows, :512])
            + matmul_t(dup[1], wu[rows, 512:])
        )

    quad.drain()
    quad_o.drain()
    for ring in (ring_zn, ring_xn):
        ring.finish()
        ring.drain()
    red2.run(ffn_term)
    late_loads = [
        weight_load(ref, buf.at[:, k * 384 : (k + 1) * 384], w2sem.at[i], core, 384)
        for i, (ref, buf, k) in enumerate(((wq_ref, wg, 0), (wk_ref, wg, 1), (wv_ref, wu, 0)))
    ]
    for load in late_loads:
        load.start()
    red3 = QuadReduce(*reduces[1], chip, core, t)
    d_ffn = jnp.concatenate([red2.result(k) for k in range(NC)], axis=1)
    part = jnp.sum(d_ffn * ffn_hat, axis=0, keepdims=True)
    for k in range(12):
        vec[12 + k : 13 + k, :] = part[:, k * 128 : (k + 1) * 128]
    d_resid = dout + norm_back(d_ffn, ffn_gain, ffn_rms, ffn_hat)
    dres[...] = d_resid
    rbuf[mine, :] = d_resid.astype(BF)
    gather_r.start()
    ring_ffn.forward()
    red3.run(
        lambda k: matmul_t(hid[0], wd[k * CW : (k + 1) * CW, :512])
        + matmul_t(hid[1], wd[k * CW : (k + 1) * CW, 512:])
    )
    gather_r.finish()
    d_mixed = matmul(rbuf[...], wo[...]).astype(BF)
    for j in range(3):
        for u in range(2):
            dms[j, u] = d_mixed[u * 128 : (u + 1) * 128, j * 128 : (j + 1) * 128]
    tile_sends(dms, dmix, tsend, trecv, chip, core, t, True)
    ring_up.start()
    ring_dres.start()
    out_ref[...] = resid + jnp.concatenate([red3.result(k) for k in range(NC)], axis=1)
    results[0].start()

    def to_sibling(o):
        at = o % (2 * PER_SPAN)
        return remote(given.at[at], sib.at[o], dsend.at[at], drecv.at[o], s + 1 - 2 * core, t)

    def to_home(o, start):
        target = 2 * (2 * o + core) + parity
        spot = place_at
        if start:

            @pl.when(target == s)
            def _():
                pltpu.make_async_copy(both.at[o], home.at[spot], krecv.at[spot]).start()

        @pl.when(target != s)
        def _():
            cp = remote(both.at[o], home.at[spot], ksend.at[o], krecv.at[spot], target, t)
            if start:
                cp.start()
            else:
                cp.wait_send()

    def tile_at(r):
        late = 4 + 10 * (r - 1) + jnp.where((r - 1) % 2 == 0, slot, 9 - slot)
        return jnp.where(r == 0, slot, late)

    @pl.when(served)
    def _():
        unit = eye(128)

        def flip(b, carry):
            rows = pl.ds(pl.multiple_of(b * KB, KB), KB)
            block = kv[pl.ds(2 * b, 2), :, :128].reshape(KB, 128)
            turned[:, rows] = matmul_t(unit, block).astype(BF)
            return carry

        lax.fori_loop(0, CHIPS * BLOCK // KB, flip, 0)

    ring_dout.finish()
    ring_hid.finish()
    block_grad(pdown, 0, ldout, lhid[...].reshape(4 * BLOCK, 512), 256)
    lefts = [
        pltpu.make_async_copy(src, ldout.at[:, :, k * 384 : (k + 1) * 384], lsem.at[k])
        for k, src in enumerate((xnormed_ref, znormed_ref))
    ]
    for left in lefts:
        left.start()
    tile_waits(dms, dmix, tsend, trecv, chip, core, t)
    send_down.each(True)
    ring_ffn.finish()
    ring_gate.finish()
    block_grad(pgate, 0, lffn, lgate[...].reshape(4 * BLOCK, 512), 256)

    for r in range(SLOTS):

        @pl.when(served if r else jnp.logical_and(served, slot < 4))
        def _():
            q_wide = q[r].astype(F32)
            q_cols[r] = both_maps(q_wide.T).astype(BF)
            left = lax.broadcasted_iota(jnp.int32, q_wide.shape, 1) < 64
            q_rows[r] = jnp.concatenate(
                [jnp.where(left, q_wide, 0.0), jnp.where(left, 0.0, q_wide)], axis=0
            ).astype(BF)
            parts = parts_all[r]
            first, second = parts[:, :TILE], parts[:, TILE:]
            rms, hat = group_norm(parts, lam)
            e_t = dmix[r].astype(F32).T * OUT_SCALE
            column = jnp.sum(e_t * hat, axis=1, keepdims=True)
            d_differ = norm_back(e_t, sub, rms, hat, 0).astype(BF)
            d_wide = d_differ.astype(F32)
            d_cols[r] = d_differ
            d_rows[r] = d_wide.T.astype(BF)
            second_dot = jnp.sum(d_wide * second, axis=0, keepdims=True)
            row = lax.broadcasted_iota(jnp.int32, (128, 128), 0)
            lane = lax.broadcasted_iota(jnp.int32, (128, 128), 1)
            vec[24:25, :] += jnp.sum(jnp.where(row == lane, column, 0.0), axis=0, keepdims=True)
            here = lax.broadcasted_iota(jnp.int32, (1, 128), 1) == 6 * t + head
            vec[25:26, :] -= jnp.where(here, jnp.sum(second_dot, axis=1, keepdims=True), 0.0)
            deltas[r, 0:1, :] = jnp.sum(d_wide * first, axis=0, keepdims=True)
            deltas[r, 1:2, :] = -lam * second_dot
            dq_acc[r] = jnp.zeros((128, 2 * TILE), F32)

    def pass_on(k):
        for u in range(PER_SPAN):
            o = PER_SPAN * lax.rem(chip + k, SPANS) + u
            to_sibling(o).wait_recv()
            both[o] = (both[o].astype(F32) + sib[o].astype(F32)).astype(BF)
            to_home(o, True)

    def span(k, carry):
        b = lax.rem(chip + k, SPANS)
        start = pl.multiple_of(b * SPAN, SPAN)
        rows = pl.ds(start, SPAN)
        blocks = pl.ds(b * (SPAN // BLOCK), SPAN // BLOCK)
        acc[...] = jnp.zeros_like(acc)

        def step(r, masked):
            score = matmul(kv[blocks, :, :128].reshape(SPAN, 128), q_cols[r])
            prob = jnp.exp2(score * SCORE - logs[r])
            if masked:
                prob = jnp.where(key_mask(start, SPAN, tile_at(r), 2 * TILE), prob, 0.0)
            upper = matmul(kv[blocks, :, 128:].reshape(SPAN, 128), d_cols[r])
            p1, p2 = prob[:, :TILE], prob[:, TILE:]
            ds = jnp.concatenate(
                [p1 * (upper - deltas[r, 0:1, :]), p2 * (-lam * upper - deltas[r, 1:2, :])],
                axis=1,
            ).astype(BF)
            mixed = (p1 - lam * p2).astype(BF)
            acc[:, :128] += matmul(ds, q_rows[r])
            acc[:, 128:] += matmul(mixed, d_rows[r])
            dq_acc[r] += matmul(turned[:, rows], ds)

        def masked_step(r, carry):
            step(r, True)
            return carry

        def full_step(r, carry):
            step(r, False)
            return carry

        reach, past = 0, 0
        for r in range(SLOTS):
            last = tile_of(slot, r) * TILE // SPAN
            counts = (slot < 4) if r == 0 else True
            reach += jnp.where(jnp.logical_and(counts, last >= b), 1, 0)
            past += jnp.where(jnp.logical_and(counts, last > b), 1, 0)
        lax.fori_loop(SLOTS - reach, SLOTS - past, masked_step, 0)
        lax.fori_loop(SLOTS - past, SLOTS, full_step, 0)

        @pl.when(k >= 2)
        def _():
            for u in range(PER_SPAN):
                to_sibling(PER_SPAN * lax.rem(chip + k - 2, SPANS) + u).wait_send()

        for u in range(PER_SPAN):
            o = PER_SPAN * b + u
            for ref, at, which in ((given, o % (2 * PER_SPAN), 1 - core), (both, o, core)):
                part = acc[pl.ds(pl.multiple_of((2 * u + which) * BLOCK, BLOCK), BLOCK), :]
                ref[at, :, :128] = (part[:, :128] * 0.125).astype(BF)
                ref[at, :, 128:] = part[:, 128:].astype(BF)
            to_sibling(o).start()

        @pl.when(k > 0)
        def _():
            pass_on(k - 1)

        return carry

    def early(k, carry):
        span(k, carry)

        @pl.when(k < 2)
        def _():
            send_gate.some(8 * k, 8 * k + 8, True)

        return carry

    def late(k, carry):
        span(k, carry)

        @pl.when(k < EARLY_SPANS + 4)
        def _():
            at = 4 * (k - EARLY_SPANS)
            send_up.some(at, at + 4, True)

        return carry

    @pl.when(served)
    def _():
        lax.fori_loop(0, EARLY_SPANS, early, 0)

    @pl.when(jnp.logical_not(served))
    def _():
        send_gate.each(True)

    ring_up.finish()
    block_grad(pup, 0, lffn, lup[...].reshape(4 * BLOCK, 512), 256)

    @pl.when(jnp.logical_not(served))
    def _():
        send_up.each(True)

    @pl.when(served)
    def _():
        lax.fori_loop(EARLY_SPANS, SPANS, late, 0)
        pass_on(SPANS - 1)

    for r in range(SLOTS):

        @pl.when(served if r else jnp.logical_and(served, slot < 4))
        def _():
            dq_t = jnp.concatenate([dq_acc[r, :64, :TILE], dq_acc[r, 64:, TILE:]], axis=0)
            dq_out[r] = (dq_t * 0.125).T.astype(BF)

    home_sends(dq_out, land, gsend, grecv, chip, core, t, True)
    home_waits(dq_out, land, grecv)
    for j in range(3):
        for u in range(2):
            dqkv_ref[0, u * 128 : (u + 1) * 128, j * 128 : (j + 1) * 128] = land[j, u]
    ring_q.start()
    for j in range(3):
        total = jnp.zeros((BLOCK, 256), F32)
        for p in range(PER_HEAD):
            spot = j * PER_HEAD + p
            pltpu.make_async_copy(both.at[0], home.at[spot], krecv.at[spot]).wait()
            total = total + home[spot].astype(F32)
        dqkv_ref[1, :, j * 128 : (j + 1) * 128] = total[:, :128].astype(BF)
        dqkv_ref[2, :, j * 128 : (j + 1) * 128] = total[:, 128:].astype(BF)
    ring_k.start()
    ring_vx.start()
    ring_vz.start()

    for load in late_loads:
        load.wait()
    red2.drain()
    red4 = QuadReduce(*reduces[0], chip, core, t)

    def normed_term(k):
        rows = slice(k * CW, (k + 1) * CW)
        return (
            matmul_t(dqkv_ref[0], wg[rows, :384])
            + matmul_t(dqkv_ref[1], wg[rows, 384:768])
            + matmul_t(dqkv_ref[2], wu[rows, :384])
        )

    red4.run(normed_term)
    ring_mix.finish()
    ring_dres.finish()
    block_grad(pqo, 384, xdres, xmix[...].reshape(4 * BLOCK, 384), 384, 0, 384)
    x = x_ref[...]
    rms = rms_scale(x)
    hat = x * rms
    d_normed = jnp.concatenate([red4.result(k) for k in range(NC)], axis=1)
    part = jnp.sum(d_normed * hat, axis=0, keepdims=True)
    for k in range(12):
        vec[k : k + 1, :] = part[:, k * 128 : (k + 1) * 128]
    first_sum = [
        remote(vec, vecs.at[k], asem.at[0, k], asem.at[1, k], *member)
        for k, member in enumerate(members)
    ]
    for cp in first_sum:
        cp.start()
    grad_ref[...] = dres[...] + norm_back(d_normed, long_row(attn_ref), rms, hat)
    results[1].start()
    for left in lefts:
        left.wait()
    ring_q.finish()
    block_grad(pqo, 0, ldout, rq[...].reshape(4 * BLOCK, 384), 384, 0, 384)
    ring_vx.finish()
    block_grad(pqo, 768, ldout, rvx[...].reshape(4 * BLOCK, 128), 384, 0, 384)
    send_qo.each(True)
    ring_k.finish()
    block_grad(pkv, 0, ldout, rk[...].reshape(4 * BLOCK, 384), 384, 384, 384)
    for cp in first_sum:
        cp.wait_recv()
    share = pl.ds(pl.multiple_of((2 * core + t) * 8, 8), 8)
    quarter[...] = (vec[share, :] + vecs[0, share, :]) + (vecs[1, share, :] + vecs[2, share, :])

    def spread(k, start):
        to = 2 * lax.rem(chip + k, CHIPS) + core
        cp = remote(quarter, quarters.at[chip], bsem.at[0, k], bsem.at[1, chip], to, t)
        if start:
            cp.start()
        else:
            cp.wait_send()

    def spread_start(k, carry):
        spread(k, True)
        return carry

    def spread_end(k, carry):
        spread(k, False)
        return carry

    own = pltpu.make_async_copy(quarter, quarters.at[chip], bsem.at[1, chip])
    own.start()
    lax.fori_loop(1, CHIPS, spread_start, 0)
    ring_vz.finish()
    block_grad(pkv, 384, ldout, rvz[...].reshape(4 * BLOCK, 256), 384, 384, 384)
    send_kv.each(True)

    send_down.wait()
    for b in range(2):
        total = send_down.total(b, slice(0, 512))
        for h in range(2):
            swap[h, :, 2048 + b * 512 : 2560 + b * 512] = total[h * 24 : h * 24 + 24]
    for m, send in enumerate((send_gate, send_up)):
        send.wait()
        for b in range(2):
            total = send.total(b, slice(0, 512))
            at = m * 1024 + b * 512
            for h in range(2):
                swap[h, :, at : at + 512] = total[h * 24 : h * 24 + 24]
    sibling = s + 1 - 2 * core
    swap_copy = remote(swap.at[1 - core], swapped, swap_sem.at[0], swap_sem.at[1], sibling, t)
    swap_copy.start()

    def collect(k, total):
        pltpu.make_async_copy(quarter, quarters.at[k], bsem.at[1, k]).wait()
        return total + quarters[k]

    sums_ref[share, :] = lax.fori_loop(0, CHIPS, collect, jnp.zeros((8, 128), F32))
    last_sum = [
        remote(sums_ref.at[share], sums_ref.at[share], csem.at[0, k], csem.at[1, k], *member)
        for k, member in enumerate(members)
    ]
    for cp in last_sum:
        cp.start()
    for send, spots in (
        (send_qo, ((0, 384, 0), (384, 384, 1152), (768, 128, 768))),
        (send_kv, ((0, 384, 384), (384, 256, 896))),
    ):
        send.wait()
        for first, width, at in spots:
            total = send.total(0, slice(first, first + width))
            for h in range(2):
                swap2[h, :, at : at + width] = total[h * 24 : h * 24 + 24]
    swap2_copy = remote(swap2.at[1 - core], swapped2, swap2_sem.at[0], swap2_sem.at[1], sibling, t)
    swap2_copy.start()
    swap_copy.wait()
    swap_out(swap, swapped, ((gate_ref, 0), (up_ref, 1024), (down_ref, 2048)), 1024, core)
    for cp in results[6:]:
        cp.start()

    for ring in (
        ring_dout, ring_mix, ring_hid, ring_gate, ring_up, ring_dres, ring_ffn, ring_q, ring_k, ring_vx,
        ring_vz,
    ):
        ring.drain()
    for send in (send_gate, send_up, send_down, send_qo, send_kv):
        send.each(False)
    home_sends(dq_out, land, gsend, grecv, chip, core, t, False)
    tile_sends(dms, dmix, tsend, trecv, chip, core, t, False)
    for gather in (gather_f, gather_r):
        gather.drain()
    red3.drain()
    red4.drain()

    @pl.when(served)
    def _():
        for k in (SPANS - 2, SPANS - 1):
            for u in range(PER_SPAN):
                to_sibling(PER_SPAN * lax.rem(chip + k, SPANS) + u).wait_send()

        def last(o, carry):
            to_home(o, False)
            return carry

        lax.fori_loop(0, CHIPS // 2, last, 0)

    for cp in last_sum:
        cp.wait()
    for cp in first_sum:
        cp.wait_send()
    lax.fori_loop(1, CHIPS, spread_end, 0)
    swap2_copy.wait()
    outs = ((gq_ref, 0), (gk_ref, 384), (gv_ref, 768), (go_ref, 1152))
    swap_out(swap2, swapped2, outs, 384, core)
    for cp in results[2:6]:
        cp.start()
    for cp in results:
        cp.wait()


def swap_out(swap, swapped, outs, width, core):
    mine = swap[core]
    for c in range(2):

        @pl.when(core == c)
        def _():
            for ref, at in outs:
                ref[:, c * width : (c + 1) * width] = mine[:, at : at + width]
                other = (1 - c) * width
                ref[:, other : other + width] = swapped[:, at : at + width]


def layer(x, cot, mask, attn, ffn, sub, lambdas, wq, wk, wv, wo, wg, wu, wd):
    half = (CHIPS // 2, BLOCK, 256)
    vm = pltpu.VMEM
    sem = pltpu.SemaphoreType.DMA
    return pl.pallas_call(
        layer_kernel,
        name="layer",
        out_shape=(
            shape((ROWS, D), F32),
            shape((ROWS, D), F32),
            *([shape((24, 768), F32)] * 4),
            *([shape((24, 2048), F32)] * 3),
            shape((32, 128), F32),
            shape(GATHERED_Q, BF),
            shape(GATHERED_Q, BF),
        ),
        in_specs=[VM] * 7 + [ANY] * 7,
        out_specs=(ANY,) * 9 + (VM,) + (ANY,) * 2,
        scratch_shapes=[
            vm((ROWS, D), F32),
            vm((ROWS, D), F32),
            *([vm((24, 768), F32)] * 4),
            *([vm((24, 2048), F32)] * 3),
            vm((ROWS, D), F32),
            vm((3, BLOCK, 384), BF),
            *([vm(GATHERED_Q, BF)] * 2),
            vm((4, BLOCK, 128), BF),
            vm((4, BLOCK, 256), BF),
            *([vm(GATHERED_Q, BF)] * 2),
            vm((384, 896), BF),
            vm((384, 640), BF),
            vm((8, CHUNK, 896), BF),
            vm((8, CHUNK, 640), BF),
            vm((2, 24, 1536), F32),
            vm((24, 1536), F32),
            vm((32, 128), F32),
            vm((3, 32, 128), F32),
            vm((8, 128), F32),
            vm((CHIPS, 8, 128), F32),
            vm((3, 2, TILE, 128), BF),
            vm((D, 384), BF),
            vm((D, 1024), BF),
            vm((D, 1024), BF),
            vm((D, 1024), BF),
            vm((BLOCK, D), BF),
            vm((BLOCK, D), BF),
            vm((3, 2, TILE, 128), BF),
            vm((BLOCK, D), BF),
            vm((2, BLOCK, 512), BF),
            vm((2, BLOCK, 512), BF),
            vm((2, BLOCK, 512), BF),
            vm((BLOCK, 384), BF),
            vm((SLOTS, TILE, 128), BF),
            vm(KV, BF),
            vm((SLOTS, 128, 2 * TILE), F32),
            vm((SLOTS, 1, 2 * TILE), F32),
            vm((SLOTS, TILE, 128), BF),
            vm(GATHERED, BF),
            *([vm((4, BLOCK, 512), BF)] * 3),
            vm(GATHERED, BF),
            *([vm((768, 512), BF)] * 3),
            *([vm((16, CHUNK, 512), BF)] * 3),
            vm((2, 24, 3072), F32),
            vm((24, 3072), F32),
            vm((128, CHIPS * BLOCK), BF),
            vm((SPAN, 256), F32),
            vm((SLOTS, 128, 2 * TILE), BF),
            vm((SLOTS, 2 * TILE, 128), BF),
            vm((SLOTS, 128, TILE), BF),
            vm((SLOTS, TILE, 128), BF),
            vm((SLOTS, 2, TILE), F32),
            vm((SLOTS, 128, 2 * TILE), F32),
            vm((SLOTS, TILE, 128), BF),
            vm((2 * PER_SPAN, BLOCK, 256), BF),
            vm(half, BF),
            vm(half, BF),
            vm((3 * PER_HEAD, BLOCK, 256), BF),
            vm((8, BLOCK), F32),
            pltpu.SMEM((2,), F32),
            vm((8, 2 * TILE), F32),
            *(REDUCE_SCRATCH * 2),
            *(GATHER_SEMS * 4),
            *(RING_SEMS * 12),
            *ONCE_SEMS,
            *(scatter_sems(16) * 2),
            *(scatter_sems(8) * 2),
            *scatter_sems(16),
            sem((4,)),
            sem((SLOTS,)),
            sem((3, 2)),
            sem((6,)),
            sem((SLOTS,)),
            sem((2,)),
            sem((2 * PER_SPAN,)),
            sem((CHIPS // 2,)),
            sem((CHIPS // 2,)),
            sem((3 * PER_HEAD,)),
            sem((SLOTS,)),
            sem((3, 2)),
            sem((3,)),
            sem((2,)),
            sem((2,)),
            sem((2, 3)),
            sem((2, CHIPS)),
            sem((2, 3)),
            sem((9,)),
            sem((WORKERS,)),
            sem((CHIPS,)),
            sem((CHIPS // 2,)),
            sem((6,)),
            sem((SLOTS,)),
        ],
        compiler_params=pltpu.CompilerParams(
            collective_id=0, has_side_effects=True, vmem_limit_bytes=VMEM_LIMIT
        ),
    )(x, cot, mask, attn, ffn, sub, lambdas, wq, wk, wv, wo, wg, wu, wd)


def publish(lambdas, sums, arrays):
    count = len(arrays)

    def kernel(lambdas_ref, sums_ref, *refs):
        for k in range(count):
            refs[count + k][...] = refs[k][...]
        attn_ref, ffn_ref, sub_ref, grad_ref = refs[2 * count :]
        attn_ref[...] = sums_ref[0:12, :]
        ffn_ref[...] = sums_ref[12:24, :]
        sub_ref[...] = sums_ref[24:25, :]
        vectors, first, second = lambda_parts(lambdas_ref)
        d_lam = as_column(sums_ref[25:26, :])[:12, :1]
        factors = (d_lam * first, d_lam * first, -d_lam * second, -d_lam * second)
        for k, other in enumerate((1, 0, 3, 2)):
            grad_ref[:, k, :] = factors[k] * vectors[other]

    return pl.pallas_call(
        kernel,
        name="publish",
        out_shape=tuple(shape(a.shape, a.dtype) for a in arrays)
        + (shape((12, 128), F32), shape((12, 128), F32), shape((1, 128), F32), shape((12, 4, 64), F32)),
        in_specs=[VM] * (count + 2),
        out_specs=(VM,) * (count + 4),
    )(lambdas, sums, *arrays)


def on_device(
    hidden_in, cotangent, needle_mask, attn_gain, lambdas, subln_gain, ffn_gain,
    weight_query, weight_key, weight_value, weight_out, weight_gate, weight_up, weight_down,
):
    mask = needle_mask.reshape(1, ROWS)
    attn = attn_gain.reshape(12, 128)
    sub = subln_gain.reshape(1, 128)
    by_head = jnp.transpose(lambdas, (1, 0, 2))
    *results, sums, _, _ = layer(
        hidden_in, cotangent, mask, attn, ffn_gain.reshape(12, 128), sub, by_head,
        weight_query, weight_key, weight_value, weight_out, weight_gate, weight_up, weight_down,
    )
    *results, attn_grad, ffn_grad, sub_grad, lambda_grad = publish(by_head, sums, results)
    return (
        *results,
        attn_grad.reshape(D),
        jnp.transpose(lambda_grad, (1, 0, 2)),
        sub_grad.reshape(128),
        ffn_grad.reshape(D),
    )


def solution(mesh):
    split = P(None, "tp")
    rows = P(("seq", "tp"), None)
    both = P("seq", "tp")
    return jax.shard_map(
        on_device,
        mesh=mesh,
        in_specs=(rows, rows, P(("seq", "tp"))) + (P(),) * 4 + (split,) * 7,
        out_specs=(rows, rows) + (both,) * 7 + (P(),) * 4,
        check_vma=False,
    )
```

```python
import math

import jax
import jax.numpy as jnp
from jax import lax
from jax.experimental import pallas as pl
from jax.experimental.pallas import tpu as pltpu
from jax.sharding import PartitionSpec as P

MESH = pl.DeviceIdType.MESH
BF = jnp.bfloat16
F32 = jnp.float32
EPS = 1e-06
LAMBDA_INIT = 0.8 - 0.6 * math.exp(-3.6)
OUT_SCALE = 1.0 - LAMBDA_INIT
D = 1536
CHIPS = 32
PER_HEAD = 5
WORKERS = 15
ROWS = 64
BLOCK = 256
TILE = 128
SLOTS = 7
KB = 512
LOG2E = 1.4426950408889634
SCORE = 0.125 * LOG2E
LOWEST = -1e30
VMEM_LIMIT = 63 * 2**20


def place():
    s = lax.axis_index("seq")
    return s // 2, s % 2, lax.axis_index("tp")


def worker(chip, core):
    x, y, z = chip % 4, chip // 4 % 2, chip // 8
    at = 4 * z + x
    return (x + y + z) % 2, at, at % PER_HEAD * 2 + core, at < WORKERS


def worker_chip(parity, at):
    x, z = at % 4, at // 4
    return (2 * z + (x + z + parity) % 2) * 4 + x


def owner_of(tile):
    step = (tile - 4) // 10
    pos = (tile - 4) % 10
    slot = jnp.where(step % 2 == 0, pos, 9 - pos)
    early = tile < 4
    return jnp.where(early, tile, slot), jnp.where(early, 0, step + 1)


def tile_of(slot, r):
    if r == 0:
        return slot
    return 4 + 10 * (r - 1) + (slot if (r - 1) % 2 == 0 else 9 - slot)


def matmul(a, b):
    return jnp.dot(a, b, preferred_element_type=F32)


def matmul_t(a, b):
    return lax.dot_general(a, b, (((1,), (1,)), ((), ())), preferred_element_type=F32)


def rms_scale(values, axis=-1):
    return lax.rsqrt(jnp.mean(values * values, axis=axis, keepdims=True) + EPS)


def norm_back(grad_normed, gain, rms, hat, axis=-1):
    scaled = grad_normed * gain
    return rms * (scaled - hat * jnp.mean(scaled * hat, axis=axis, keepdims=True))


def greet_all(chip, core, t):
    barrier = pltpu.get_barrier_semaphore()
    s = 2 * chip + core

    def greet(o, carry):
        pl.semaphore_signal(
            barrier, inc=1, device_id=(lax.rem(s + o, 2 * CHIPS), t), device_id_type=MESH
        )
        return carry

    lax.fori_loop(1, 2 * CHIPS, greet, 0)
    pl.semaphore_signal(barrier, inc=1, device_id=(s, 1 - t), device_id_type=MESH)
    pl.semaphore_wait(barrier, 2 * CHIPS)


def remote(src, dst, send_sem, recv_sem, s, t):
    return pltpu.make_async_remote_copy(
        src_ref=src,
        dst_ref=dst,
        send_sem=send_sem,
        recv_sem=recv_sem,
        device_id=(s, t),
        device_id_type=MESH,
    )


def rows_at(ref, start, count):
    return ref.at[pl.ds(pl.multiple_of(start, ROWS), count)]


class QuadGather:
    def __init__(self, buf, send, recv, chip, core, t):
        self.buf, self.send, self.recv = buf, send, recv
        self.chip, self.core, self.t = chip, core, t
        mine = core * 128 + t * ROWS
        self.mine = mine
        self.near = core * 128 + (1 - t) * ROWS
        sib = (2 * chip + 1 - core, t)
        self.to_near = self.copy(mine, 0, (2 * chip + core, 1 - t))
        self.to_sib = self.copy(mine, 1, sib)
        self.forward = self.copy(self.near, 2, sib)

    def copy(self, row, k, target):
        view = rows_at(self.buf, row, ROWS)
        return remote(view, view, self.send.at[k], self.recv.at[k], *target)

    def start(self):
        self.to_near.start()
        self.to_sib.start()

    def finish(self):
        self.to_near.wait_recv()
        self.forward.start()
        self.to_sib.wait_recv()
        self.forward.wait_recv()

    def drain(self):
        self.to_near.wait_send()
        self.to_sib.wait_send()
        self.forward.wait_send()


class RingGather:
    def __init__(self, pieces, land, send, recv, axis, chip, core, t):
        at = chip % 4 if axis == "x" else chip // 8
        self.local = pltpu.make_async_copy(pieces(at), land.at[at], recv.at[0])
        self.land, self.send, self.recv = land, send, recv
        self.copies = []
        for k in (1, 3, 2):
            if axis == "x":
                peer, chip_to = (at + k) % 4, chip - at + (at + k) % 4
            else:
                peer, chip_to = (at + k) % 4, (chip + 8 * k) % CHIPS
            self.copies.append(
                remote(pieces(peer), land.at[at], send.at[0], recv.at[0], 2 * chip_to + core, t)
            )

    def start(self):
        self.local.start()
        for cp in self.copies:
            cp.start()

    def finish(self):
        pltpu.make_async_copy(self.land, self.land, self.recv.at[0]).wait()

    def drain(self):
        three = self.land.at[pl.ds(0, 3)]
        pltpu.make_async_copy(three, three, self.send.at[0]).wait()


class RingGatherOnce:
    def __init__(self, pieces, land, send, recv, pass_send, pass_recv, axis, chip, core, t):
        at = chip % 4 if axis == "x" else chip // 8
        self.mine = pl.ds(pl.multiple_of(core * 128, 128), 128)
        self.local = pltpu.make_async_copy(pieces(at), land.at[at], recv.at[0])
        self.local_at = at
        self.copies, self.passes = [], []
        for k in (1, 3, 2):
            peer = (at + k) % 4
            chip_to = chip - at + peer if axis == "x" else (chip + 8 * k) % CHIPS
            self.copies.append(
                remote(
                    pieces(peer).at[self.mine], land.at[at, self.mine],
                    send.at[k - 1], recv.at[4 - k], 2 * chip_to + core, t,
                )
            )
            view = land.at[peer, self.mine]
            self.passes.append(
                (
                    pltpu.make_async_copy(pieces(at).at[self.mine], view, recv.at[k]),
                    remote(view, view, pass_send.at[k - 1], pass_recv.at[k - 1], 2 * chip + 1 - core, t),
                )
            )

    def start(self):
        self.local.start()
        for cp in self.copies:
            cp.start()

    def forward(self):
        for arrive, cp in self.passes:
            arrive.wait()
            cp.start()

    def finish(self):
        self.local.wait()
        for _, cp in self.passes:
            cp.wait_recv()

    def drain(self):
        for cp in self.copies:
            cp.wait_send()
        for _, cp in self.passes:
            cp.wait_send()


ONCE_SEMS = [
    pltpu.SemaphoreType.DMA((3,)),
    pltpu.SemaphoreType.DMA((4,)),
    pltpu.SemaphoreType.DMA((3,)),
    pltpu.SemaphoreType.DMA((3,)),
]
RING_SEMS = [pltpu.SemaphoreType.DMA((1,)), pltpu.SemaphoreType.DMA((1,))]


def block_grad(dst, start, left, right, step, at=0, total=768):
    width = right.shape[1]

    def one(m, carry):
        cols = pl.ds(pl.multiple_of(m * step, 128), step)
        part = left[:, :, pl.ds(pl.multiple_of(at + m * step, 128), step)].reshape(4 * BLOCK, step)
        dst[cols, start : start + width] = lax.dot_general(
            part, right, (((0,), (0,)), ((), ())), preferred_element_type=F32
        ).astype(BF)
        return carry

    lax.fori_loop(0, total // step, one, 0)


CHUNK = 48


class Scatter:
    def __init__(self, part, land, send, recv, count, first, spot, chip, core, t):
        self.part, self.land, self.send, self.recv = part, land, send, recv
        self.count, self.first, self.spot = count, first, spot
        self.chip, self.core, self.t = chip, core, t

    def source(self, i):
        return self.part.at[pl.ds(pl.multiple_of(i * CHUNK, 16), CHUNK)]

    def each(self):
        self.some(0, self.count)

    def some(self, first, end):
        def one(o, carry):
            i = lax.rem(self.chip + 1 + 3 * o, self.count)
            owner = self.first + i
            to = self.land.at[self.spot]

            @pl.when(owner == self.chip)
            def _():
                pltpu.make_async_copy(self.source(i), to, self.recv.at[0]).start()

            @pl.when(owner != self.chip)
            def _():
                remote(
                    self.source(i), to, self.send.at[0], self.recv.at[0], 2 * owner + self.core, self.t
                ).start()

            return carry

        lax.fori_loop(first, end, one, 0)

    def wait(self):
        pltpu.make_async_copy(self.land, self.land, self.recv.at[0]).wait()

    def drain(self):
        own = jnp.logical_and(self.chip >= self.first, self.chip < self.first + self.count)
        for count, case in ((self.count - 1, own), (self.count, jnp.logical_not(own))):

            @pl.when(case)
            def _():
                sent = self.part.at[pl.ds(0, count * CHUNK)]
                pltpu.make_async_copy(sent, sent, self.send.at[0]).wait()

    def total(self, b, cols):
        def one(k, carry):
            return carry + self.land[8 * b + k, :, cols].astype(F32)

        return lax.fori_loop(0, 8, one, jnp.zeros((CHUNK, cols.stop - cols.start), F32))


GATHER_SEMS = [pltpu.SemaphoreType.DMA((3,)), pltpu.SemaphoreType.DMA((3,))]
CW = 512
NC = D // CW


class QuadReduce:
    def __init__(self, part, dsend, drecv, ysend, yrecv, ds, dr, ys, yr, chip, core, t):
        self.part, self.dsend, self.drecv = part, dsend, drecv
        self.ysend, self.yrecv = ysend, yrecv
        self.core, self.t = core, t
        self.ds, self.ys = ds, ys
        self.d = [
            remote(dsend.at[k], drecv.at[k], ds.at[0], dr.at[k], 2 * chip + 1 - core, t)
            for k in range(NC)
        ]
        self.y = [
            remote(ysend.at[k], yrecv.at[k], ys.at[0], yr.at[k], 2 * chip + core, 1 - t)
            for k in range(NC)
        ]

    def rows(self, start, count, k):
        return self.part[pl.ds(pl.multiple_of(start, ROWS), count), k * CW : (k + 1) * CW]

    def put(self, k, value):
        self.part[:, k * CW : (k + 1) * CW] = value
        self.dsend[k] = self.rows((1 - self.core) * 128, 128, k).astype(BF)
        self.d[k].start()

    def middle(self, k):
        self.d[k].wait_recv()
        near = (1 - self.t) * ROWS
        far = self.rows(self.core * 128 + near, ROWS, k)
        got = self.drecv[k, pl.ds(pl.multiple_of(near, ROWS), ROWS), :]
        self.ysend[k] = (far + got.astype(F32)).astype(BF)
        self.y[k].start()

    def result(self, k):
        mine = self.t * ROWS
        own = self.rows(self.core * 128 + mine, ROWS, k)
        got = self.drecv[k, pl.ds(pl.multiple_of(mine, ROWS), ROWS), :].astype(F32)
        self.y[k].wait_recv()
        return own + got + self.yrecv[k].astype(F32)

    def run(self, term):
        for k in range(NC):
            self.put(k, term(k))
            if k:
                self.middle(k - 1)
        self.middle(NC - 1)

    def drain(self):
        pltpu.make_async_copy(self.dsend, self.dsend, self.ds.at[0]).wait()
        pltpu.make_async_copy(self.ysend, self.ysend, self.ys.at[0]).wait()


REDUCE_SCRATCH = [
    pltpu.VMEM((BLOCK, D), F32),
    pltpu.VMEM((NC, 128, CW), BF),
    pltpu.VMEM((NC, 128, CW), BF),
    pltpu.VMEM((NC, ROWS, CW), BF),
    pltpu.VMEM((NC, ROWS, CW), BF),
] + [pltpu.SemaphoreType.DMA((n,)) for n in (1, NC, 1, NC)]


def tile_sends(tiles, land, send, recv, chip, core, t, start):
    s = 2 * chip + core
    for j in range(3):
        for u in range(2):
            slot, index = owner_of(2 * chip + u)
            target = 2 * worker_chip(core, j * PER_HEAD + slot // 2) + slot % 2
            k = j * 2 + u

            if start:

                @pl.when(target == s)
                def _():
                    pltpu.make_async_copy(tiles.at[j, u], land.at[index], recv.at[index]).start()

            @pl.when(target != s)
            def _():
                cp = remote(tiles.at[j, u], land.at[index], send.at[k], recv.at[index], target, t)
                if start:
                    cp.start()
                else:
                    cp.wait_send()


def tile_waits(tiles, land, send, recv, chip, core, t):
    _, _, slot, served = worker(chip, core)
    for r in range(SLOTS):
        here = served
        if r == 0:
            here = jnp.logical_and(here, slot < 4)

        @pl.when(here)
        def _():
            pltpu.make_async_copy(tiles.at[0, 0], land.at[r], recv.at[r]).wait()


def home_sends(tiles, land, send, recv, chip, core, t, start):
    s = 2 * chip + core
    parity, at, slot, served = worker(chip, core)
    for r in range(SLOTS):
        here = served
        if r == 0:
            here = jnp.logical_and(here, slot < 4)
        tile = tile_of(slot, r)
        target = (tile // 2) * 2 + parity
        j, u = at // PER_HEAD, tile % 2

        if start:

            @pl.when(jnp.logical_and(here, target == s))
            def _():
                pltpu.make_async_copy(tiles.at[r], land.at[j, u], recv.at[j, u]).start()

        @pl.when(jnp.logical_and(here, target != s))
        def _():
            cp = remote(tiles.at[r], land.at[j, u], send.at[r], recv.at[j, u], target, t)
            if start:
                cp.start()
            else:
                cp.wait_send()


def home_waits(tiles, land, recv):
    for j in range(3):
        for u in range(2):
            pltpu.make_async_copy(tiles.at[0], land.at[j, u], recv.at[j, u]).wait()


def weight_load(ref, buf, sem, core, width):
    return pltpu.make_async_copy(
        ref.at[:, pl.ds(pl.multiple_of(core * width, 128), width)], buf, sem
    )


VM = pl.BlockSpec(memory_space=pltpu.VMEM)
ANY = pl.BlockSpec(memory_space=pl.ANY)


def shape(dims, dtype):
    return jax.ShapeDtypeStruct(dims, dtype)


HALVES = (2, BLOCK, 768)
QUARTERS = (4, BLOCK, 384)
GATHERED = (4, BLOCK, 768)
GATHERED_Q = (4, BLOCK, 384)
KV = (CHIPS, BLOCK, 256)
STEP = 2048


def eye(size):
    row = lax.broadcasted_iota(jnp.int32, (size, size), 0)
    col = lax.broadcasted_iota(jnp.int32, (size, size), 1)
    return jnp.where(row == col, 1.0, 0.0).astype(BF)


def both_maps(q_t):
    top = lax.broadcasted_iota(jnp.int32, q_t.shape, 0) < 64
    return jnp.concatenate([jnp.where(top, q_t, 0.0), jnp.where(top, 0.0, q_t)], axis=1)


def key_mask(start, count, tile, width):
    key = start + lax.broadcasted_iota(jnp.int32, (count, width), 0)
    query = tile * TILE + lax.broadcasted_iota(jnp.int32, (count, width), 1) % TILE
    return key <= query


def group_norm(parts, lam):
    first, second = parts[:, :TILE], parts[:, TILE:]
    differ = first - lam * second
    rms = rms_scale(differ, 0)
    return rms, differ * rms


def long_row(ref):
    return jnp.concatenate([ref[k : k + 1, :] for k in range(12)], axis=1)


def as_column(row):
    return jnp.broadcast_to(row, (128, 128)).T


def mask_column(mask_ref):
    mask = mask_ref[...].astype(F32)
    return as_column(jnp.concatenate([mask, mask], axis=1))[:ROWS, :1]


def lambda_parts(lambdas_ref):
    vectors = [lambdas_ref[:, k, :] for k in range(4)]
    first = jnp.exp(jnp.sum(vectors[0] * vectors[1], axis=-1, keepdims=True))
    second = jnp.exp(jnp.sum(vectors[2] * vectors[3], axis=-1, keepdims=True))
    return vectors, first, second


def lambda_of(lambdas_ref, head):
    _, first, second = lambda_parts(lambdas_ref)
    every = first - second + LAMBDA_INIT
    mine = lax.broadcasted_iota(jnp.int32, every.shape, 0) == head
    return jnp.sum(jnp.where(mine, every, 0.0), axis=0, keepdims=True)


SPAN = 1024
SPANS = CHIPS * BLOCK // SPAN
PER_SPAN = SPAN // BLOCK // 2
EARLY_SPANS = 3


def layer_kernel(
    x_ref, cot_ref, mask_ref, attn_ref, ffn_ref, sub_ref, lambdas_ref,
    wq_ref, wk_ref, wv_ref, wo_ref, wg_ref, wu_ref, wd_ref,
    out_to, grad_to, gq_to, gk_to, gv_to, go_to, gate_to, up_to, down_to, sums_ref,
    xnormed_ref, znormed_ref,
    out_ref, grad_ref, gq_ref, gk_ref, gv_ref, go_ref, gate_ref, up_ref, down_ref,
    dres, dqkv_ref, rq, rk, rvx, rvz, xmix, xdres, pqo, pkv, sqo, skv, swap2, swapped2,
    vec, vecs, quarter, quarters,
    land, wo, wg, wu, wd, fbuf, nbuf, dms, obuf, dgate, dup, hid, mix,
    q, kv, parts_all, logs, dmix,
    lffn, lgate, lup, lhid, ldout, pgate, pup, pdown, sgate, sup, sdown, swap, swapped,
    turned, acc, q_cols, q_rows, d_cols, d_rows, deltas, dq_acc, dq_out, given, sib, both, home,
    peaks, *rest,
):
    chip, core, t = place()
    s = 2 * chip + core
    parity, place_at, slot, served = worker(chip, core)
    head = 3 * parity + place_at // PER_HEAD
    x_at, z_at = chip % 4, chip // 8
    taken = iter(rest)

    def take(count):
        return [next(taken) for _ in range(count)]

    reduces = [take(9) for _ in range(2)]
    gather_sems = [take(2) for _ in range(4)]
    ring_sems = [take(2) for _ in range(12)]
    once_sems = take(4)
    scatter = [take(2) for _ in range(5)]
    wsem, hsend, hrecv, tsend, trecv, swap_sem = take(6)
    dsend, drecv, ksend, krecv, gsend, grecv = take(6)
    w2sem, lsem, swap2_sem, asem, bsem, csem = take(6)
    (osem,) = take(1)
    results = [
        pltpu.make_async_copy(src, dst, osem.at[k])
        for k, (src, dst) in enumerate(
            (
                (out_ref, out_to), (grad_ref, grad_to), (gq_ref, gq_to), (gk_ref, gk_to),
                (gv_ref, gv_to), (go_ref, go_to), (gate_ref, gate_to), (up_ref, up_to),
                (down_ref, down_to),
            )
        )
    ]
    kvsend, kvrecv, fsend, qsend, qrecv = take(5)
    rbuf = nbuf


    def halves(ref):
        return lambda p: ref.at[:, pl.ds(pl.multiple_of(p // 2 * 768, 128), 768)]

    def quarters_of(ref):
        return lambda p: ref.at[:, pl.ds(pl.multiple_of(p * 384, 128), 384)]

    gather_f = QuadGather(fbuf, *gather_sems[0], chip, core, t)
    gather_r = QuadGather(rbuf, *gather_sems[1], chip, core, t)
    ring_dout = RingGather(halves(obuf), ldout, *ring_sems[0], "x", chip, core, t)
    ring_mix = RingGather(lambda p: mix, xmix, *ring_sems[1], "x", chip, core, t)
    ring_hid = RingGather(lambda p: hid.at[p % 2], lhid, *ring_sems[2], "x", chip, core, t)
    ring_gate = RingGather(lambda p: dgate.at[p % 2], lgate, *ring_sems[3], "z", chip, core, t)
    ring_up = RingGather(lambda p: dup.at[p % 2], lup, *ring_sems[10], "z", chip, core, t)
    ring_dres = RingGather(
        quarters_of(rbuf), xdres, *ring_sems[4], "x", chip, core, t,
    )
    ring_xn = RingGather(quarters_of(nbuf), xnormed_ref, *ring_sems[5], "x", chip, core, t)
    ring_zn = RingGather(quarters_of(nbuf), znormed_ref, *ring_sems[6], "z", chip, core, t)
    ring_q = RingGather(lambda p: dqkv_ref.at[0], rq, *ring_sems[7], "x", chip, core, t)
    ring_k = RingGather(lambda p: dqkv_ref.at[1], rk, *ring_sems[8], "z", chip, core, t)
    ring_vx = RingGather(
        lambda p: dqkv_ref.at[2, :, :128], rvx, *ring_sems[9], "x", chip, core, t
    )
    ring_vz = RingGather(
        lambda p: dqkv_ref.at[2, :, 128:], rvz, *ring_sems[11], "z", chip, core, t
    )
    send_qo = Scatter(pqo, sqo, *scatter[2], 8, 8 * x_at, chip // 4, chip, core, t)
    send_kv = Scatter(pkv, skv, *scatter[3], 8, 8 * z_at, chip % 8, chip, core, t)
    members = ((s + 1 - 2 * core, t), (s, 1 - t), (s + 1 - 2 * core, 1 - t))
    ring_ffn = RingGatherOnce(
        halves(fbuf), lffn, *once_sems, "z", chip, core, t,
    )
    send_down = Scatter(
        pdown, sdown, *scatter[0], 16, 16 * (x_at // 2), 8 * (x_at % 2) + chip // 4, chip, core, t
    )
    send_gate, send_up = (
        Scatter(
            part, to, *sems, 16, 16 * (z_at // 2), 8 * (z_at % 2) + chip % 8, chip, core, t
        )
        for part, to, sems in ((pgate, sgate, scatter[1]), (pup, sup, scatter[4]))
    )
    first_loads = [
        weight_load(ref, buf.at[:, k * 384 : (k + 1) * 384], w2sem.at[i], core, 384)
        for i, (ref, buf, k) in enumerate(((wk_ref, wg, 0), (wv_ref, wg, 1), (wq_ref, wu, 0)))
    ]
    loads = [
        weight_load(wo_ref, wo, wsem.at[0], core, 384),
        weight_load(wg_ref, wg, wsem.at[1], core, 1024),
        weight_load(wu_ref, wu, wsem.at[2], core, 1024),
        weight_load(wd_ref, wd, wsem.at[3], core, 1024),
    ]
    for load in (first_loads[2], *first_loads[:2], loads[0]):
        load.start()
    quad = QuadGather(nbuf, *gather_sems[2], chip, core, t)
    quad_o = QuadGather(obuf, *gather_sems[3], chip, core, t)
    mine = pl.ds(pl.multiple_of(quad.mine, ROWS), ROWS)
    x = x_ref[...]
    normed = (x * rms_scale(x) * long_row(attn_ref)).astype(BF)
    nbuf[mine, :] = normed
    greet_all(chip, core, t)
    quad.start()
    dout = cot_ref[...] * mask_column(mask_ref)
    obuf[mine, :] = dout.astype(BF)
    lam = lambda_of(lambdas_ref, 6 * t + head)
    sub = as_column(sub_ref[...])
    ffn_gain = long_row(ffn_ref)
    vec[...] = jnp.zeros_like(vec)
    unit = eye(128)
    quad.finish()
    def kv_piece(j):
        return dqkv_ref.at[j, :, :256]

    self_served = jnp.logical_and(parity == core, chip % 2 == core)

    def kv_sends():
        def one(o, carry):
            w = lax.rem(chip + 7 * o, WORKERS)
            j = w // PER_HEAD
            target = 2 * worker_chip(core, w) + chip % 2

            @pl.when(target == s)
            def _():
                pltpu.make_async_copy(kv_piece(j), kv.at[chip], kvrecv.at[chip]).start()

            @pl.when(target != s)
            def _():
                remote(kv_piece(j), kv.at[chip], kvsend.at[0], kvrecv.at[chip], target, t).start()

            return carry

        lax.fori_loop(0, WORKERS, one, 0)

    first_loads[2].wait()
    value = matmul(nbuf[...], wu[:, :384]).astype(BF)
    for j in range(3):
        for u in range(2):
            dms[j, u] = value[u * 128 : (u + 1) * 128, j * 128 : (j + 1) * 128]
    tile_sends(dms, q, qsend, qrecv, chip, core, t, True)
    for k in range(2):
        first_loads[k].wait()
        value = matmul(nbuf[...], wg[:, k * 384 : (k + 1) * 384]).astype(BF)
        for j in range(3):
            dqkv_ref[j, :, k * 128 : (k + 1) * 128] = value[:, j * 128 : (j + 1) * 128]

    kv_sends()
    quad_o.start()
    for load in loads[1:]:
        load.start()

    def tile_at(r):
        late = 4 + 10 * (r - 1) + jnp.where((r - 1) % 2 == 0, slot, 9 - slot)
        return jnp.where(r == 0, slot, late)

    def tiles_from(first, span):
        reach, past = 0, 0
        for r in range(SLOTS):
            last = tile_of(slot, r) * TILE // span
            counts = (slot < 4) if r == 0 else True
            reach += jnp.where(jnp.logical_and(counts, last >= first), 1, 0)
            past += jnp.where(jnp.logical_and(counts, last > first), 1, 0)
        return SLOTS - reach, SLOTS - past

    def each_tile(first, span, step):
        reach, past = tiles_from(first, span)

        def masked_step(r, carry):
            step(r, True)
            return carry

        def full_step(r, carry):
            step(r, False)
            return carry

        lax.fori_loop(reach, past, masked_step, 0)
        lax.fori_loop(past, SLOTS, full_step, 0)

    tile_waits(dms, q, qsend, qrecv, chip, core, t)
    for r in range(SLOTS):

        @pl.when(served if r else jnp.logical_and(served, slot < 4))
        def _():
            q_cols[r] = both_maps(q[r].astype(F32).T).astype(BF)
            dq_acc[r] = jnp.zeros((128, 2 * TILE), F32)
            peaks[r, 0:1, :] = jnp.full((1, 2 * TILE), LOWEST, F32)
            peaks[r, 1:2, :] = jnp.zeros((1, 2 * TILE), F32)

    def pair_of(o):
        return lax.rem(chip // 2 + o, CHIPS // 2)

    def arrive(source):
        pltpu.make_async_copy(kv_piece(0), kv.at[source], kvrecv.at[source]).wait()

    def use(o):
        pair = pair_of(o)
        arrive(2 * pair + 1 - core)
        start = pl.multiple_of(pair * KB, KB)
        rows, blocks = pl.ds(start, KB), pl.ds(2 * pair, 2)
        turned[:, rows] = matmul_t(unit, kv[blocks, :, 128:].reshape(KB, 128)).astype(BF)

        def step(r, masked):
            score = matmul(kv[blocks, :, :128].reshape(KB, 128), q_cols[r])
            if masked:
                score = jnp.where(key_mask(start, KB, tile_at(r), 2 * TILE), score, LOWEST)
            old = peaks[r, 0:1, :]
            peak = jnp.maximum(old, jnp.max(score, axis=0, keepdims=True))
            shrink = jnp.exp2((old - peak) * SCORE)
            prob = jnp.exp2((score - peak) * SCORE)
            peaks[r, 0:1, :] = peak
            peaks[r, 1:2, :] = peaks[r, 1:2, :] * shrink + jnp.sum(prob, axis=0, keepdims=True)
            dq_acc[r] = dq_acc[r] * shrink + matmul(turned[:, rows], prob.astype(BF))

        each_tile(pair, KB, step)

    @pl.when(served)
    def _():
        def take(o, carry):
            source = 2 * pair_of(o) + core
            arrive(source)
            view = kv.at[source]
            remote(view, view, fsend.at[0], kvrecv.at[source], s + 1 - 2 * core, t).start()

            @pl.when(o > 0)
            def _():
                use(o - 1)

            return carry

        lax.fori_loop(0, CHIPS // 2, take, 0)

    quad_o.finish()
    ring_zn.start()
    ring_dout.start()

    @pl.when(served)
    def _():
        use(CHIPS // 2 - 1)
        passed = kv.at[pl.ds(0, CHIPS // 2)]
        pltpu.make_async_copy(passed, passed, fsend.at[0]).wait()

    for r in range(SLOTS):

        @pl.when(served if r else jnp.logical_and(served, slot < 4))
        def _():
            whole = peaks[r, 1:2, :]
            parts = dq_acc[r] / whole
            parts_all[r] = parts
            logs[r] = peaks[r, 0:1, :] * SCORE + jnp.log(whole) * LOG2E
            rms, hat = group_norm(parts, lam)
            dq_out[r] = (hat * sub * OUT_SCALE).T.astype(BF)

    home_sends(dq_out, land, hsend, hrecv, chip, core, t, True)
    loads[0].wait()
    home_waits(dq_out, land, hrecv)
    for j in range(3):
        for u in range(2):
            mix[u * 128 : (u + 1) * 128, j * 128 : (j + 1) * 128] = land[j, u]
    red = QuadReduce(*reduces[0], chip, core, t)
    red.run(lambda k: matmul_t(mix[...], wo[k * CW : (k + 1) * CW, :]))
    ring_xn.start()
    ring_mix.start()
    home_sends(dq_out, land, hsend, hrecv, chip, core, t, False)
    own_kv = jnp.logical_and(self_served, served)
    for count, case in ((WORKERS - 1, own_kv), (WORKERS, jnp.logical_not(own_kv))):

        @pl.when(case)
        def _():
            sent = kv.at[pl.ds(0, count)]
            pltpu.make_async_copy(sent, sent, kvsend.at[0]).wait()

    tile_sends(dms, q, qsend, qrecv, chip, core, t, False)
    resid = x_ref[...] + jnp.concatenate([red.result(k) for k in range(NC)], axis=1)
    ffn_rms = rms_scale(resid)
    ffn_hat = resid * ffn_rms
    fbuf[mine, :] = (ffn_hat * ffn_gain).astype(BF)
    gather_f.start()
    for load in loads[1:]:
        load.wait()
    red.drain()
    gather_f.finish()
    ring_ffn.start()

    def hidden_step(n, carry):
        cols = pl.ds(pl.multiple_of(n * 256, 256), 256)
        b, at = n // 2, n % 2
        gate = matmul(fbuf[...], wg[:, cols])
        up = matmul(fbuf[...], wu[:, cols])
        d_hidden = matmul(obuf[...], wd[:, cols])
        sig = 1.0 / (1.0 + jnp.exp(-gate))
        silu = gate * sig
        to = pl.ds(pl.multiple_of(at * 256, 256), 256)
        hid[b, :, to] = (silu * up).astype(BF)
        dgate[b, :, to] = (d_hidden * up * sig * (1.0 + gate * (1.0 - sig))).astype(BF)
        dup[b, :, to] = (d_hidden * silu).astype(BF)
        return carry

    lax.fori_loop(0, 4, hidden_step, 0)
    ring_gate.start()
    ring_hid.start()
    red2 = QuadReduce(*reduces[0], chip, core, t)

    def ffn_term(k):
        rows = slice(k * CW, (k + 1) * CW)
        return (
            matmul_t(dgate[0], wg[rows, :512])
            + matmul_t(dgate[1], wg[rows, 512:])
            + matmul_t(dup[0], wu[rows, :512])
            + matmul_t(dup[1], wu[rows, 512:])
        )

    quad.drain()
    quad_o.drain()
    for ring in (ring_zn, ring_xn):
        ring.finish()
        ring.drain()
    red2.run(ffn_term)
    late_loads = [
        weight_load(ref, buf.at[:, k * 384 : (k + 1) * 384], w2sem.at[i], core, 384)
        for i, (ref, buf, k) in enumerate(((wq_ref, wg, 0), (wk_ref, wg, 1), (wv_ref, wu, 0)))
    ]
    for load in late_loads:
        load.start()
    red3 = QuadReduce(*reduces[1], chip, core, t)
    d_ffn = jnp.concatenate([red2.result(k) for k in range(NC)], axis=1)
    part = jnp.sum(d_ffn * ffn_hat, axis=0, keepdims=True)
    for k in range(12):
        vec[12 + k : 13 + k, :] = part[:, k * 128 : (k + 1) * 128]
    d_resid = dout + norm_back(d_ffn, ffn_gain, ffn_rms, ffn_hat)
    dres[...] = d_resid
    rbuf[mine, :] = d_resid.astype(BF)
    gather_r.start()
    ring_ffn.forward()
    red3.run(
        lambda k: matmul_t(hid[0], wd[k * CW : (k + 1) * CW, :512])
        + matmul_t(hid[1], wd[k * CW : (k + 1) * CW, 512:])
    )
    gather_r.finish()
    d_mixed = matmul(rbuf[...], wo[...]).astype(BF)
    for j in range(3):
        for u in range(2):
            dms[j, u] = d_mixed[u * 128 : (u + 1) * 128, j * 128 : (j + 1) * 128]
    tile_sends(dms, dmix, tsend, trecv, chip, core, t, True)
    ring_up.start()
    ring_dres.start()
    out_ref[...] = resid + jnp.concatenate([red3.result(k) for k in range(NC)], axis=1)
    results[0].start()

    def to_sibling(o):
        at = o % (2 * PER_SPAN)
        return remote(given.at[at], sib.at[o], dsend.at[at], drecv.at[o], s + 1 - 2 * core, t)

    def to_home(o):
        target = 2 * (2 * o + core) + parity
        spot = home.at[place_at]

        @pl.when(target == s)
        def _():
            pltpu.make_async_copy(both.at[o], spot, krecv.at[0]).start()

        @pl.when(target != s)
        def _():
            remote(both.at[o], spot, ksend.at[0], krecv.at[0], target, t).start()

    @pl.when(served)
    def _():
        def flip(b, carry):
            rows = pl.ds(pl.multiple_of(b * KB, KB), KB)
            block = kv[pl.ds(2 * b, 2), :, :128].reshape(KB, 128)
            turned[:, rows] = matmul_t(unit, block).astype(BF)
            return carry

        lax.fori_loop(0, CHIPS * BLOCK // KB, flip, 0)

    ring_dout.finish()
    ring_hid.finish()
    block_grad(pdown, 0, ldout, lhid[...].reshape(4 * BLOCK, 512), 256)
    lefts = [
        pltpu.make_async_copy(src, ldout.at[:, :, k * 384 : (k + 1) * 384], lsem.at[k])
        for k, src in enumerate((xnormed_ref, znormed_ref))
    ]
    for left in lefts:
        left.start()
    tile_waits(dms, dmix, tsend, trecv, chip, core, t)
    send_down.each()
    ring_ffn.finish()
    ring_gate.finish()
    block_grad(pgate, 0, lffn, lgate[...].reshape(4 * BLOCK, 512), 256)

    for r in range(SLOTS):

        @pl.when(served if r else jnp.logical_and(served, slot < 4))
        def _():
            q_wide = q[r].astype(F32)
            left = lax.broadcasted_iota(jnp.int32, q_wide.shape, 1) < 64
            q_rows[r] = jnp.concatenate(
                [jnp.where(left, q_wide, 0.0), jnp.where(left, 0.0, q_wide)], axis=0
            ).astype(BF)
            parts = parts_all[r]
            first, second = parts[:, :TILE], parts[:, TILE:]
            rms, hat = group_norm(parts, lam)
            e_t = dmix[r].astype(F32).T * OUT_SCALE
            column = jnp.sum(e_t * hat, axis=1, keepdims=True)
            d_differ = norm_back(e_t, sub, rms, hat, 0).astype(BF)
            d_wide = d_differ.astype(F32)
            d_cols[r] = d_differ
            d_rows[r] = d_wide.T.astype(BF)
            second_dot = jnp.sum(d_wide * second, axis=0, keepdims=True)
            row = lax.broadcasted_iota(jnp.int32, (128, 128), 0)
            lane = lax.broadcasted_iota(jnp.int32, (128, 128), 1)
            vec[24:25, :] += jnp.sum(jnp.where(row == lane, column, 0.0), axis=0, keepdims=True)
            here = lax.broadcasted_iota(jnp.int32, (1, 128), 1) == 6 * t + head
            vec[25:26, :] -= jnp.where(here, jnp.sum(second_dot, axis=1, keepdims=True), 0.0)
            deltas[r, 0:1, :] = jnp.sum(d_wide * first, axis=0, keepdims=True)
            deltas[r, 1:2, :] = -lam * second_dot
            dq_acc[r] = jnp.zeros((128, 2 * TILE), F32)

    def pass_on(k):
        for u in range(PER_SPAN):
            o = PER_SPAN * lax.rem(chip + k, SPANS) + u
            to_sibling(o).wait_recv()
            both[o] = (both[o].astype(F32) + sib[o].astype(F32)).astype(BF)
            to_home(o)

    def span(k, carry):
        b = lax.rem(chip + k, SPANS)
        start = pl.multiple_of(b * SPAN, SPAN)
        rows = pl.ds(start, SPAN)
        blocks = pl.ds(b * (SPAN // BLOCK), SPAN // BLOCK)
        acc[...] = jnp.zeros_like(acc)

        def step(r, masked):
            score = matmul(kv[blocks, :, :128].reshape(SPAN, 128), q_cols[r])
            prob = jnp.exp2(score * SCORE - logs[r])
            if masked:
                prob = jnp.where(key_mask(start, SPAN, tile_at(r), 2 * TILE), prob, 0.0)
            upper = matmul(kv[blocks, :, 128:].reshape(SPAN, 128), d_cols[r])
            p1, p2 = prob[:, :TILE], prob[:, TILE:]
            ds = jnp.concatenate(
                [p1 * (upper - deltas[r, 0:1, :]), p2 * (-lam * upper - deltas[r, 1:2, :])],
                axis=1,
            ).astype(BF)
            mixed = (p1 - lam * p2).astype(BF)
            acc[:, :128] += matmul(ds, q_rows[r])
            acc[:, 128:] += matmul(mixed, d_rows[r])
            dq_acc[r] += matmul(turned[:, rows], ds)

        each_tile(b, SPAN, step)

        @pl.when(k >= 2)
        def _():
            for u in range(PER_SPAN):
                to_sibling(PER_SPAN * lax.rem(chip + k - 2, SPANS) + u).wait_send()

        for u in range(PER_SPAN):
            o = PER_SPAN * b + u
            for ref, at, which in ((given, o % (2 * PER_SPAN), 1 - core), (both, o, core)):
                part = acc[pl.ds(pl.multiple_of((2 * u + which) * BLOCK, BLOCK), BLOCK), :]
                ref[at, :, :128] = (part[:, :128] * 0.125).astype(BF)
                ref[at, :, 128:] = part[:, 128:].astype(BF)
            to_sibling(o).start()

        @pl.when(k > 0)
        def _():
            pass_on(k - 1)

        return carry

    def early(k, carry):
        span(k, carry)

        @pl.when(k < 2)
        def _():
            send_gate.some(8 * k, 8 * k + 8)

        return carry

    def late(k, carry):
        span(k, carry)

        @pl.when(k < EARLY_SPANS + 4)
        def _():
            at = 4 * (k - EARLY_SPANS)
            send_up.some(at, at + 4)

        return carry

    @pl.when(served)
    def _():
        lax.fori_loop(0, EARLY_SPANS, early, 0)

    @pl.when(jnp.logical_not(served))
    def _():
        send_gate.each()

    ring_up.finish()
    block_grad(pup, 0, lffn, lup[...].reshape(4 * BLOCK, 512), 256)

    @pl.when(jnp.logical_not(served))
    def _():
        send_up.each()

    @pl.when(served)
    def _():
        lax.fori_loop(EARLY_SPANS, SPANS, late, 0)
        pass_on(SPANS - 1)

    for r in range(SLOTS):

        @pl.when(served if r else jnp.logical_and(served, slot < 4))
        def _():
            dq_t = jnp.concatenate([dq_acc[r, :64, :TILE], dq_acc[r, 64:, TILE:]], axis=0)
            dq_out[r] = (dq_t * 0.125).T.astype(BF)

    home_sends(dq_out, land, gsend, grecv, chip, core, t, True)
    home_waits(dq_out, land, grecv)
    for j in range(3):
        for u in range(2):
            dqkv_ref[0, u * 128 : (u + 1) * 128, j * 128 : (j + 1) * 128] = land[j, u]
    ring_q.start()
    pltpu.make_async_copy(home, home, krecv.at[0]).wait()
    for j in range(3):
        total = jnp.zeros((BLOCK, 256), F32)
        for p in range(PER_HEAD):
            spot = j * PER_HEAD + p
            total = total + home[spot].astype(F32)
        dqkv_ref[1, :, j * 128 : (j + 1) * 128] = total[:, :128].astype(BF)
        dqkv_ref[2, :, j * 128 : (j + 1) * 128] = total[:, 128:].astype(BF)
    ring_k.start()
    ring_vx.start()
    ring_vz.start()

    for load in late_loads:
        load.wait()
    red2.drain()
    red4 = QuadReduce(*reduces[0], chip, core, t)

    def normed_term(k):
        rows = slice(k * CW, (k + 1) * CW)
        return (
            matmul_t(dqkv_ref[0], wg[rows, :384])
            + matmul_t(dqkv_ref[1], wg[rows, 384:768])
            + matmul_t(dqkv_ref[2], wu[rows, :384])
        )

    red4.run(normed_term)
    ring_mix.finish()
    ring_dres.finish()
    block_grad(pqo, 384, xdres, xmix[...].reshape(4 * BLOCK, 384), 384, 0, 384)
    x = x_ref[...]
    rms = rms_scale(x)
    hat = x * rms
    d_normed = jnp.concatenate([red4.result(k) for k in range(NC)], axis=1)
    part = jnp.sum(d_normed * hat, axis=0, keepdims=True)
    for k in range(12):
        vec[k : k + 1, :] = part[:, k * 128 : (k + 1) * 128]
    first_sum = [
        remote(vec, vecs.at[k], asem.at[0, k], asem.at[1, k], *member)
        for k, member in enumerate(members)
    ]
    for cp in first_sum:
        cp.start()
    grad_ref[...] = dres[...] + norm_back(d_normed, long_row(attn_ref), rms, hat)
    results[1].start()
    for left in lefts:
        left.wait()
    ring_q.finish()
    block_grad(pqo, 0, ldout, rq[...].reshape(4 * BLOCK, 384), 384, 0, 384)
    ring_vx.finish()
    block_grad(pqo, 768, ldout, rvx[...].reshape(4 * BLOCK, 128), 384, 0, 384)
    send_qo.each()
    ring_k.finish()
    block_grad(pkv, 0, ldout, rk[...].reshape(4 * BLOCK, 384), 384, 384, 384)
    for cp in first_sum:
        cp.wait_recv()
    share = pl.ds(pl.multiple_of((2 * core + t) * 8, 8), 8)
    quarter[...] = (vec[share, :] + vecs[0, share, :]) + (vecs[1, share, :] + vecs[2, share, :])

    def spread(k, carry):
        to = 2 * lax.rem(chip + k, CHIPS) + core
        remote(quarter, quarters.at[chip], bsem.at[0], bsem.at[1], to, t).start()
        return carry

    own = pltpu.make_async_copy(quarter, quarters.at[chip], bsem.at[1])
    own.start()
    lax.fori_loop(1, CHIPS, spread, 0)
    ring_vz.finish()
    block_grad(pkv, 384, ldout, rvz[...].reshape(4 * BLOCK, 256), 384, 384, 384)
    send_kv.each()

    send_down.wait()
    for b in range(2):
        total = send_down.total(b, slice(0, 512))
        for h in range(2):
            swap[h, :, 2048 + b * 512 : 2560 + b * 512] = total[h * 24 : h * 24 + 24]
    for m, send in enumerate((send_gate, send_up)):
        send.wait()
        for b in range(2):
            total = send.total(b, slice(0, 512))
            at = m * 1024 + b * 512
            for h in range(2):
                swap[h, :, at : at + 512] = total[h * 24 : h * 24 + 24]
    sibling = s + 1 - 2 * core
    swap_copy = remote(swap.at[1 - core], swapped, swap_sem.at[0], swap_sem.at[1], sibling, t)
    swap_copy.start()

    pltpu.make_async_copy(quarters, quarters, bsem.at[1]).wait()

    def collect(k, total):
        return total + quarters[k]

    sums_ref[share, :] = lax.fori_loop(0, CHIPS, collect, jnp.zeros((8, 128), F32))
    last_sum = [
        remote(sums_ref.at[share], sums_ref.at[share], csem.at[0, k], csem.at[1, k], *member)
        for k, member in enumerate(members)
    ]
    for cp in last_sum:
        cp.start()
    for send, spots in (
        (send_qo, ((0, 384, 0), (384, 384, 1152), (768, 128, 768))),
        (send_kv, ((0, 384, 384), (384, 256, 896))),
    ):
        send.wait()
        for first, width, at in spots:
            total = send.total(0, slice(first, first + width))
            for h in range(2):
                swap2[h, :, at : at + width] = total[h * 24 : h * 24 + 24]
    swap2_copy = remote(swap2.at[1 - core], swapped2, swap2_sem.at[0], swap2_sem.at[1], sibling, t)
    swap2_copy.start()
    swap_copy.wait()
    swap_out(swap, swapped, ((gate_ref, 0), (up_ref, 1024), (down_ref, 2048)), 1024, core)
    for cp in results[6:]:
        cp.start()

    for ring in (
        ring_dout, ring_mix, ring_hid, ring_gate, ring_up, ring_dres, ring_ffn, ring_q, ring_k, ring_vx,
        ring_vz,
    ):
        ring.drain()
    for send in (send_gate, send_up, send_down, send_qo, send_kv):
        send.drain()
    home_sends(dq_out, land, gsend, grecv, chip, core, t, False)
    tile_sends(dms, dmix, tsend, trecv, chip, core, t, False)
    for gather in (gather_f, gather_r):
        gather.drain()
    red3.drain()
    red4.drain()

    @pl.when(served)
    def _():
        for k in (SPANS - 2, SPANS - 1):
            for u in range(PER_SPAN):
                to_sibling(PER_SPAN * lax.rem(chip + k, SPANS) + u).wait_send()

    for count, case in ((CHIPS // 2 - 1, self_served), (CHIPS // 2, jnp.logical_not(self_served))):

        @pl.when(jnp.logical_and(served, case))
        def _():
            sent = both.at[pl.ds(0, count)]
            pltpu.make_async_copy(sent, sent, ksend.at[0]).wait()

    for cp in last_sum:
        cp.wait()
    for cp in first_sum:
        cp.wait_send()
    others = quarters.at[pl.ds(0, CHIPS - 1)]
    pltpu.make_async_copy(others, others, bsem.at[0]).wait()
    swap2_copy.wait()
    outs = ((gq_ref, 0), (gk_ref, 384), (gv_ref, 768), (go_ref, 1152))
    swap_out(swap2, swapped2, outs, 384, core)
    for cp in results[2:6]:
        cp.start()
    for cp in results:
        cp.wait()


def swap_out(swap, swapped, outs, width, core):
    mine = swap[core]
    for c in range(2):

        @pl.when(core == c)
        def _():
            for ref, at in outs:
                ref[:, c * width : (c + 1) * width] = mine[:, at : at + width]
                other = (1 - c) * width
                ref[:, other : other + width] = swapped[:, at : at + width]


def layer(x, cot, mask, attn, ffn, sub, lambdas, wq, wk, wv, wo, wg, wu, wd):
    half = (CHIPS // 2, BLOCK, 256)
    vm = pltpu.VMEM
    sem = pltpu.SemaphoreType.DMA
    return pl.pallas_call(
        layer_kernel,
        name="layer",
        out_shape=(
            shape((ROWS, D), F32),
            shape((ROWS, D), F32),
            *([shape((24, 768), F32)] * 4),
            *([shape((24, 2048), F32)] * 3),
            shape((32, 128), F32),
            shape(GATHERED_Q, BF),
            shape(GATHERED_Q, BF),
        ),
        in_specs=[VM] * 7 + [ANY] * 7,
        out_specs=(ANY,) * 9 + (VM,) + (ANY,) * 2,
        scratch_shapes=[
            vm((ROWS, D), F32),
            vm((ROWS, D), F32),
            *([vm((24, 768), F32)] * 4),
            *([vm((24, 2048), F32)] * 3),
            vm((ROWS, D), F32),
            vm((3, BLOCK, 384), BF),
            *([vm(GATHERED_Q, BF)] * 2),
            vm((4, BLOCK, 128), BF),
            vm((4, BLOCK, 256), BF),
            *([vm(GATHERED_Q, BF)] * 2),
            vm((384, 896), BF),
            vm((384, 640), BF),
            vm((8, CHUNK, 896), BF),
            vm((8, CHUNK, 640), BF),
            vm((2, 24, 1536), F32),
            vm((24, 1536), F32),
            vm((32, 128), F32),
            vm((3, 32, 128), F32),
            vm((8, 128), F32),
            vm((CHIPS, 8, 128), F32),
            vm((3, 2, TILE, 128), BF),
            vm((D, 384), BF),
            vm((D, 1024), BF),
            vm((D, 1024), BF),
            vm((D, 1024), BF),
            vm((BLOCK, D), BF),
            vm((BLOCK, D), BF),
            vm((3, 2, TILE, 128), BF),
            vm((BLOCK, D), BF),
            vm((2, BLOCK, 512), BF),
            vm((2, BLOCK, 512), BF),
            vm((2, BLOCK, 512), BF),
            vm((BLOCK, 384), BF),
            vm((SLOTS, TILE, 128), BF),
            vm(KV, BF),
            vm((SLOTS, 128, 2 * TILE), F32),
            vm((SLOTS, 1, 2 * TILE), F32),
            vm((SLOTS, TILE, 128), BF),
            vm(GATHERED, BF),
            *([vm((4, BLOCK, 512), BF)] * 3),
            vm(GATHERED, BF),
            *([vm((768, 512), BF)] * 3),
            *([vm((16, CHUNK, 512), BF)] * 3),
            vm((2, 24, 3072), F32),
            vm((24, 3072), F32),
            vm((128, CHIPS * BLOCK), BF),
            vm((SPAN, 256), F32),
            vm((SLOTS, 128, 2 * TILE), BF),
            vm((SLOTS, 2 * TILE, 128), BF),
            vm((SLOTS, 128, TILE), BF),
            vm((SLOTS, TILE, 128), BF),
            vm((SLOTS, 2, TILE), F32),
            vm((SLOTS, 128, 2 * TILE), F32),
            vm((SLOTS, TILE, 128), BF),
            vm((2 * PER_SPAN, BLOCK, 256), BF),
            vm(half, BF),
            vm(half, BF),
            vm((3 * PER_HEAD, BLOCK, 256), BF),
            vm((SLOTS, 2, 2 * TILE), F32),
            *(REDUCE_SCRATCH * 2),
            *(GATHER_SEMS * 4),
            *(RING_SEMS * 12),
            *ONCE_SEMS,
            *(RING_SEMS * 5),
            sem((4,)),
            sem((SLOTS,)),
            sem((3, 2)),
            sem((6,)),
            sem((SLOTS,)),
            sem((2,)),
            sem((2 * PER_SPAN,)),
            sem((CHIPS // 2,)),
            sem((1,)),
            sem((1,)),
            sem((SLOTS,)),
            sem((3, 2)),
            sem((3,)),
            sem((2,)),
            sem((2,)),
            sem((2, 3)),
            sem((2,)),
            sem((2, 3)),
            sem((9,)),
            sem((1,)),
            sem((CHIPS,)),
            sem((1,)),
            sem((6,)),
            sem((SLOTS,)),
        ],
        compiler_params=pltpu.CompilerParams(
            collective_id=0, has_side_effects=True, vmem_limit_bytes=VMEM_LIMIT
        ),
    )(x, cot, mask, attn, ffn, sub, lambdas, wq, wk, wv, wo, wg, wu, wd)


def publish(lambdas, sums, arrays):
    count = len(arrays)

    def kernel(lambdas_ref, sums_ref, *refs):
        for k in range(count):
            refs[count + k][...] = refs[k][...]
        attn_ref, ffn_ref, sub_ref, grad_ref = refs[2 * count :]
        attn_ref[...] = sums_ref[0:12, :]
        ffn_ref[...] = sums_ref[12:24, :]
        sub_ref[...] = sums_ref[24:25, :]
        vectors, first, second = lambda_parts(lambdas_ref)
        d_lam = as_column(sums_ref[25:26, :])[:12, :1]
        factors = (d_lam * first, d_lam * first, -d_lam * second, -d_lam * second)
        for k, other in enumerate((1, 0, 3, 2)):
            grad_ref[:, k, :] = factors[k] * vectors[other]

    return pl.pallas_call(
        kernel,
        name="publish",
        out_shape=tuple(shape(a.shape, a.dtype) for a in arrays)
        + (shape((12, 128), F32), shape((12, 128), F32), shape((1, 128), F32), shape((12, 4, 64), F32)),
        in_specs=[VM] * (count + 2),
        out_specs=(VM,) * (count + 4),
    )(lambdas, sums, *arrays)


def on_device(
    hidden_in, cotangent, needle_mask, attn_gain, lambdas, subln_gain, ffn_gain,
    weight_query, weight_key, weight_value, weight_out, weight_gate, weight_up, weight_down,
):
    mask = needle_mask.reshape(1, ROWS)
    attn = attn_gain.reshape(12, 128)
    sub = subln_gain.reshape(1, 128)
    by_head = jnp.transpose(lambdas, (1, 0, 2))
    *results, sums, _, _ = layer(
        hidden_in, cotangent, mask, attn, ffn_gain.reshape(12, 128), sub, by_head,
        weight_query, weight_key, weight_value, weight_out, weight_gate, weight_up, weight_down,
    )
    *results, attn_grad, ffn_grad, sub_grad, lambda_grad = publish(by_head, sums, results)
    return (
        *results,
        attn_grad.reshape(D),
        jnp.transpose(lambda_grad, (1, 0, 2)),
        sub_grad.reshape(128),
        ffn_grad.reshape(D),
    )


def solution(mesh):
    split = P(None, "tp")
    rows = P(("seq", "tp"), None)
    both = P("seq", "tp")
    return jax.shard_map(
        on_device,
        mesh=mesh,
        in_specs=(rows, rows, P(("seq", "tp"))) + (P(),) * 4 + (split,) * 7,
        out_specs=(rows, rows) + (both,) * 7 + (P(),) * 4,
        check_vma=False,
    )
```

```python
import math

import jax
import jax.numpy as jnp
from jax import lax
from jax.experimental import pallas as pl
from jax.experimental.pallas import tpu as pltpu
from jax.sharding import PartitionSpec as P

MESH = pl.DeviceIdType.MESH
BF = jnp.bfloat16
F32 = jnp.float32
EPS = 1e-06
LAMBDA_INIT = 0.8 - 0.6 * math.exp(-3.6)
OUT_SCALE = 1.0 - LAMBDA_INIT
D = 1536
CHIPS = 32
PER_HEAD = 5
WORKERS = 15
ROWS = 64
BLOCK = 256
TILE = 128
SLOTS = 7
KB = 512
LOG2E = 1.4426950408889634
SCORE = 0.125 * LOG2E
VMEM_LIMIT = 63 * 2**20


def place():
    s = lax.axis_index("seq")
    return s // 2, s % 2, lax.axis_index("tp")


def worker(chip, core):
    x, y, z = chip % 4, chip // 4 % 2, chip // 8
    at = 4 * z + x
    return (x + y + z) % 2, at, at % PER_HEAD * 2 + core, at < WORKERS


def worker_chip(parity, at):
    x, z = at % 4, at // 4
    return (2 * z + (x + z + parity) % 2) * 4 + x


def owner_of(tile):
    step = (tile - 4) // 10
    pos = (tile - 4) % 10
    slot = jnp.where(step % 2 == 0, pos, 9 - pos)
    early = tile < 4
    return jnp.where(early, tile, slot), jnp.where(early, 0, step + 1)


def tile_of(slot, r):
    if r == 0:
        return slot
    return 4 + 10 * (r - 1) + (slot if (r - 1) % 2 == 0 else 9 - slot)


def matmul(a, b):
    return jnp.dot(a, b, preferred_element_type=F32)


def matmul_t(a, b):
    return lax.dot_general(a, b, (((1,), (1,)), ((), ())), preferred_element_type=F32)


def rms_scale(values, axis=-1):
    return lax.rsqrt(jnp.mean(values * values, axis=axis, keepdims=True) + EPS)


def norm_back(grad_normed, gain, rms, hat, axis=-1):
    scaled = grad_normed * gain
    return rms * (scaled - hat * jnp.mean(scaled * hat, axis=axis, keepdims=True))


def greet_all(chip, core, t):
    barrier = pltpu.get_barrier_semaphore()
    s = 2 * chip + core

    def greet(o, carry):
        pl.semaphore_signal(
            barrier, inc=1, device_id=(lax.rem(s + o, 2 * CHIPS), t), device_id_type=MESH
        )
        return carry

    lax.fori_loop(1, 2 * CHIPS, greet, 0)
    pl.semaphore_signal(barrier, inc=1, device_id=(s, 1 - t), device_id_type=MESH)
    pl.semaphore_wait(barrier, 2 * CHIPS)


def remote(src, dst, send_sem, recv_sem, s, t):
    return pltpu.make_async_remote_copy(
        src_ref=src,
        dst_ref=dst,
        send_sem=send_sem,
        recv_sem=recv_sem,
        device_id=(s, t),
        device_id_type=MESH,
    )


def rows_at(ref, start, count):
    return ref.at[pl.ds(pl.multiple_of(start, ROWS), count)]


class QuadGather:
    def __init__(self, buf, send, recv, chip, core, t):
        self.buf, self.send, self.recv = buf, send, recv
        self.chip, self.core, self.t = chip, core, t
        mine = core * 128 + t * ROWS
        self.mine = mine
        self.near = core * 128 + (1 - t) * ROWS
        sib = (2 * chip + 1 - core, t)
        self.to_near = self.copy(mine, 0, (2 * chip + core, 1 - t))
        self.to_sib = self.copy(mine, 1, sib)
        self.forward = self.copy(self.near, 2, sib)

    def copy(self, row, k, target):
        view = rows_at(self.buf, row, ROWS)
        return remote(view, view, self.send.at[k], self.recv.at[k], *target)

    def start(self):
        self.to_near.start()
        self.to_sib.start()

    def finish(self):
        self.to_near.wait_recv()
        self.forward.start()
        self.to_sib.wait_recv()
        self.forward.wait_recv()

    def drain(self):
        self.to_near.wait_send()
        self.to_sib.wait_send()
        self.forward.wait_send()


class RingGather:
    def __init__(self, pieces, land, send, recv, axis, chip, core, t):
        at = chip % 4 if axis == "x" else chip // 8
        self.local = pltpu.make_async_copy(pieces(at), land.at[at], recv.at[0])
        self.land, self.send, self.recv = land, send, recv
        self.copies = []
        for k in (1, 3, 2):
            if axis == "x":
                peer, chip_to = (at + k) % 4, chip - at + (at + k) % 4
            else:
                peer, chip_to = (at + k) % 4, (chip + 8 * k) % CHIPS
            self.copies.append(
                remote(pieces(peer), land.at[at], send.at[0], recv.at[0], 2 * chip_to + core, t)
            )

    def start(self):
        self.local.start()
        for cp in self.copies:
            cp.start()

    def finish(self):
        pltpu.make_async_copy(self.land, self.land, self.recv.at[0]).wait()

    def drain(self):
        three = self.land.at[pl.ds(0, 3)]
        pltpu.make_async_copy(three, three, self.send.at[0]).wait()


class RingGatherOnce:
    def __init__(self, pieces, land, send, recv, pass_send, pass_recv, axis, chip, core, t):
        at = chip % 4 if axis == "x" else chip // 8
        self.mine = pl.ds(pl.multiple_of(core * 128, 128), 128)
        self.local = pltpu.make_async_copy(pieces(at), land.at[at], recv.at[0])
        self.local_at = at
        self.copies, self.passes = [], []
        for k in (1, 3, 2):
            peer = (at + k) % 4
            chip_to = chip - at + peer if axis == "x" else (chip + 8 * k) % CHIPS
            self.copies.append(
                remote(
                    pieces(peer).at[self.mine], land.at[at, self.mine],
                    send.at[k - 1], recv.at[4 - k], 2 * chip_to + core, t,
                )
            )
            view = land.at[peer, self.mine]
            self.passes.append(
                (
                    pltpu.make_async_copy(pieces(at).at[self.mine], view, recv.at[k]),
                    remote(view, view, pass_send.at[k - 1], pass_recv.at[k - 1], 2 * chip + 1 - core, t),
                )
            )

    def start(self):
        self.local.start()
        for cp in self.copies:
            cp.start()

    def forward(self):
        for arrive, cp in self.passes:
            arrive.wait()
            cp.start()

    def finish(self):
        self.local.wait()
        for _, cp in self.passes:
            cp.wait_recv()

    def drain(self):
        for cp in self.copies:
            cp.wait_send()
        for _, cp in self.passes:
            cp.wait_send()


ONCE_SEMS = [
    pltpu.SemaphoreType.DMA((3,)),
    pltpu.SemaphoreType.DMA((4,)),
    pltpu.SemaphoreType.DMA((3,)),
    pltpu.SemaphoreType.DMA((3,)),
]
RING_SEMS = [pltpu.SemaphoreType.DMA((1,)), pltpu.SemaphoreType.DMA((1,))]


def block_grad(dst, start, left, right, step, at=0, total=768):
    width = right.shape[1]

    def one(m, carry):
        cols = pl.ds(pl.multiple_of(m * step, 128), step)
        part = left[:, :, pl.ds(pl.multiple_of(at + m * step, 128), step)].reshape(4 * BLOCK, step)
        dst[cols, start : start + width] = lax.dot_general(
            part, right, (((0,), (0,)), ((), ())), preferred_element_type=F32
        ).astype(BF)
        return carry

    lax.fori_loop(0, total // step, one, 0)


CHUNK = 48


class Scatter:
    def __init__(self, part, land, send, recv, count, first, spot, chip, core, t):
        self.part, self.land, self.send, self.recv = part, land, send, recv
        self.count, self.first, self.spot = count, first, spot
        self.chip, self.core, self.t = chip, core, t

    def source(self, i):
        return self.part.at[pl.ds(pl.multiple_of(i * CHUNK, 16), CHUNK)]

    def each(self):
        self.some(0, self.count)

    def some(self, first, end):
        def one(o, carry):
            i = lax.rem(self.chip + 1 + 3 * o, self.count)
            owner = self.first + i
            to = self.land.at[self.spot]

            @pl.when(owner == self.chip)
            def _():
                pltpu.make_async_copy(self.source(i), to, self.recv.at[0]).start()

            @pl.when(owner != self.chip)
            def _():
                remote(
                    self.source(i), to, self.send.at[0], self.recv.at[0], 2 * owner + self.core, self.t
                ).start()

            return carry

        lax.fori_loop(first, end, one, 0)

    def wait(self):
        pltpu.make_async_copy(self.land, self.land, self.recv.at[0]).wait()

    def drain(self):
        own = jnp.logical_and(self.chip >= self.first, self.chip < self.first + self.count)
        for count, case in ((self.count - 1, own), (self.count, jnp.logical_not(own))):

            @pl.when(case)
            def _():
                sent = self.part.at[pl.ds(0, count * CHUNK)]
                pltpu.make_async_copy(sent, sent, self.send.at[0]).wait()

    def total(self, b, cols):
        def one(k, carry):
            return carry + self.land[8 * b + k, :, cols].astype(F32)

        return lax.fori_loop(0, 8, one, jnp.zeros((CHUNK, cols.stop - cols.start), F32))


GATHER_SEMS = [pltpu.SemaphoreType.DMA((3,)), pltpu.SemaphoreType.DMA((3,))]
CW = 512
NC = D // CW


class QuadReduce:
    def __init__(self, part, dsend, drecv, ysend, yrecv, ds, dr, ys, yr, chip, core, t):
        self.part, self.dsend, self.drecv = part, dsend, drecv
        self.ysend, self.yrecv = ysend, yrecv
        self.core, self.t = core, t
        self.ds, self.ys = ds, ys
        self.d = [
            remote(dsend.at[k], drecv.at[k], ds.at[0], dr.at[k], 2 * chip + 1 - core, t)
            for k in range(NC)
        ]
        self.y = [
            remote(ysend.at[k], yrecv.at[k], ys.at[0], yr.at[k], 2 * chip + core, 1 - t)
            for k in range(NC)
        ]

    def rows(self, start, count, k):
        return self.part[pl.ds(pl.multiple_of(start, ROWS), count), k * CW : (k + 1) * CW]

    def put(self, k, value):
        self.part[:, k * CW : (k + 1) * CW] = value
        self.dsend[k] = self.rows((1 - self.core) * 128, 128, k).astype(BF)
        self.d[k].start()

    def middle(self, k):
        self.d[k].wait_recv()
        near = (1 - self.t) * ROWS
        far = self.rows(self.core * 128 + near, ROWS, k)
        got = self.drecv[k, pl.ds(pl.multiple_of(near, ROWS), ROWS), :]
        self.ysend[k] = (far + got.astype(F32)).astype(BF)
        self.y[k].start()

    def result(self, k):
        mine = self.t * ROWS
        own = self.rows(self.core * 128 + mine, ROWS, k)
        got = self.drecv[k, pl.ds(pl.multiple_of(mine, ROWS), ROWS), :].astype(F32)
        self.y[k].wait_recv()
        return own + got + self.yrecv[k].astype(F32)

    def run(self, term):
        for k in range(NC):
            self.put(k, term(k))
            if k:
                self.middle(k - 1)
        self.middle(NC - 1)

    def drain(self):
        pltpu.make_async_copy(self.dsend, self.dsend, self.ds.at[0]).wait()
        pltpu.make_async_copy(self.ysend, self.ysend, self.ys.at[0]).wait()


REDUCE_SCRATCH = [
    pltpu.VMEM((BLOCK, D), F32),
    pltpu.VMEM((NC, 128, CW), BF),
    pltpu.VMEM((NC, 128, CW), BF),
    pltpu.VMEM((NC, ROWS, CW), BF),
    pltpu.VMEM((NC, ROWS, CW), BF),
] + [pltpu.SemaphoreType.DMA((n,)) for n in (1, NC, 1, NC)]


def tile_sends(tiles, land, send, recv, chip, core, t, start):
    s = 2 * chip + core
    for j in range(3):
        for u in range(2):
            slot, index = owner_of(2 * chip + u)
            target = 2 * worker_chip(core, j * PER_HEAD + slot // 2) + slot % 2
            k = j * 2 + u

            if start:

                @pl.when(target == s)
                def _():
                    pltpu.make_async_copy(tiles.at[j, u], land.at[index], recv.at[index]).start()

            @pl.when(target != s)
            def _():
                cp = remote(tiles.at[j, u], land.at[index], send.at[k], recv.at[index], target, t)
                if start:
                    cp.start()
                else:
                    cp.wait_send()


def tile_waits(tiles, land, send, recv, chip, core, t):
    _, _, slot, served = worker(chip, core)
    for r in range(SLOTS):
        here = served
        if r == 0:
            here = jnp.logical_and(here, slot < 4)

        @pl.when(here)
        def _():
            pltpu.make_async_copy(tiles.at[0, 0], land.at[r], recv.at[r]).wait()


def home_sends(tiles, land, send, recv, chip, core, t, start):
    s = 2 * chip + core
    parity, at, slot, served = worker(chip, core)
    for r in range(SLOTS):
        here = served
        if r == 0:
            here = jnp.logical_and(here, slot < 4)
        tile = tile_of(slot, r)
        target = (tile // 2) * 2 + parity
        j, u = at // PER_HEAD, tile % 2

        if start:

            @pl.when(jnp.logical_and(here, target == s))
            def _():
                pltpu.make_async_copy(tiles.at[r], land.at[j, u], recv.at[j, u]).start()

        @pl.when(jnp.logical_and(here, target != s))
        def _():
            cp = remote(tiles.at[r], land.at[j, u], send.at[r], recv.at[j, u], target, t)
            if start:
                cp.start()
            else:
                cp.wait_send()


def home_waits(tiles, land, recv):
    for j in range(3):
        for u in range(2):
            pltpu.make_async_copy(tiles.at[0], land.at[j, u], recv.at[j, u]).wait()


def weight_load(ref, buf, sem, core, width):
    return pltpu.make_async_copy(
        ref.at[:, pl.ds(pl.multiple_of(core * width, 128), width)], buf, sem
    )


VM = pl.BlockSpec(memory_space=pltpu.VMEM)
ANY = pl.BlockSpec(memory_space=pl.ANY)


def shape(dims, dtype):
    return jax.ShapeDtypeStruct(dims, dtype)


HALVES = (2, BLOCK, 768)
QUARTERS = (4, BLOCK, 384)
GATHERED = (4, BLOCK, 768)
GATHERED_Q = (4, BLOCK, 384)
KV = (CHIPS, BLOCK, 256)
STEP = 2048


def eye(size):
    row = lax.broadcasted_iota(jnp.int32, (size, size), 0)
    col = lax.broadcasted_iota(jnp.int32, (size, size), 1)
    return jnp.where(row == col, 1.0, 0.0).astype(BF)


def both_maps(q_t):
    top = lax.broadcasted_iota(jnp.int32, q_t.shape, 0) < 64
    return jnp.concatenate([jnp.where(top, q_t, 0.0), jnp.where(top, 0.0, q_t)], axis=1)


def key_mask(start, count, tile, width):
    key = start + lax.broadcasted_iota(jnp.int32, (count, width), 0)
    query = tile * TILE + lax.broadcasted_iota(jnp.int32, (count, width), 1) % TILE
    return key <= query


def group_norm(parts, lam):
    first, second = parts[:, :TILE], parts[:, TILE:]
    differ = first - lam * second
    rms = rms_scale(differ, 0)
    return rms, differ * rms


def long_row(ref):
    return jnp.concatenate([ref[k : k + 1, :] for k in range(12)], axis=1)


def as_column(row):
    return jnp.broadcast_to(row, (128, 128)).T


def mask_column(mask_ref):
    mask = mask_ref[...].astype(F32)
    return as_column(jnp.concatenate([mask, mask], axis=1))[:ROWS, :1]


def lambda_parts(lambdas_ref):
    vectors = [lambdas_ref[:, k, :] for k in range(4)]
    first = jnp.exp(jnp.sum(vectors[0] * vectors[1], axis=-1, keepdims=True))
    second = jnp.exp(jnp.sum(vectors[2] * vectors[3], axis=-1, keepdims=True))
    return vectors, first, second


def lambda_of(lambdas_ref, head):
    _, first, second = lambda_parts(lambdas_ref)
    every = first - second + LAMBDA_INIT
    mine = lax.broadcasted_iota(jnp.int32, every.shape, 0) == head
    return jnp.sum(jnp.where(mine, every, 0.0), axis=0, keepdims=True)


SPAN = 1024
SPANS = CHIPS * BLOCK // SPAN
PER_SPAN = SPAN // BLOCK // 2
EARLY_SPANS = 3


def layer_kernel(
    x_ref, cot_ref, mask_ref, attn_ref, ffn_ref, sub_ref, lambdas_ref,
    wq_ref, wk_ref, wv_ref, wo_ref, wg_ref, wu_ref, wd_ref,
    out_to, grad_to, gq_to, gk_to, gv_to, go_to, gate_to, up_to, down_to, sums_ref,
    xnormed_ref, znormed_ref,
    out_ref, grad_ref, gq_ref, gk_ref, gv_ref, go_ref, gate_ref, up_ref, down_ref,
    dres, dqkv_ref, rq, rk, rvx, rvz, xmix, xdres, pqo, pkv, sqo, skv, swap2, swapped2,
    vec, vecs, quarter, quarters,
    land, wo, wg, wu, wd, fbuf, nbuf, dms, obuf, dgate, dup, hid, mix,
    q, kv, parts_all, logs, dmix,
    lffn, lgate, lup, lhid, ldout, pgate, pup, pdown, sgate, sup, sdown, swap, swapped,
    turned, acc, q_cols, q_rows, d_cols, d_rows, deltas, dq_acc, dq_out, given, sib, both, home,
    crest, kmax, weights, *rest,
):
    chip, core, t = place()
    s = 2 * chip + core
    parity, place_at, slot, served = worker(chip, core)
    head = 3 * parity + place_at // PER_HEAD
    x_at, z_at = chip % 4, chip // 8
    taken = iter(rest)

    def take(count):
        return [next(taken) for _ in range(count)]

    reduces = [take(9) for _ in range(2)]
    gather_sems = [take(2) for _ in range(4)]
    ring_sems = [take(2) for _ in range(12)]
    once_sems = take(4)
    scatter = [take(2) for _ in range(5)]
    wsem, hsend, hrecv, tsend, trecv, swap_sem = take(6)
    dsend, drecv, ksend, krecv, gsend, grecv = take(6)
    w2sem, lsem, swap2_sem, asem, bsem, csem = take(6)
    (osem,) = take(1)
    results = [
        pltpu.make_async_copy(src, dst, osem.at[k])
        for k, (src, dst) in enumerate(
            (
                (out_ref, out_to), (grad_ref, grad_to), (gq_ref, gq_to), (gk_ref, gk_to),
                (gv_ref, gv_to), (go_ref, go_to), (gate_ref, gate_to), (up_ref, up_to),
                (down_ref, down_to),
            )
        )
    ]
    kvsend, kvrecv, fsend, qsend, qrecv = take(5)
    rbuf = nbuf


    def halves(ref):
        return lambda p: ref.at[:, pl.ds(pl.multiple_of(p // 2 * 768, 128), 768)]

    def quarters_of(ref):
        return lambda p: ref.at[:, pl.ds(pl.multiple_of(p * 384, 128), 384)]

    gather_f = QuadGather(fbuf, *gather_sems[0], chip, core, t)
    gather_r = QuadGather(rbuf, *gather_sems[1], chip, core, t)
    ring_dout = RingGather(halves(obuf), ldout, *ring_sems[0], "x", chip, core, t)
    ring_mix = RingGather(lambda p: mix, xmix, *ring_sems[1], "x", chip, core, t)
    ring_hid = RingGather(lambda p: hid.at[p % 2], lhid, *ring_sems[2], "x", chip, core, t)
    ring_gate = RingGather(lambda p: dgate.at[p % 2], lgate, *ring_sems[3], "z", chip, core, t)
    ring_up = RingGather(lambda p: dup.at[p % 2], lup, *ring_sems[10], "z", chip, core, t)
    ring_dres = RingGather(
        quarters_of(rbuf), xdres, *ring_sems[4], "x", chip, core, t,
    )
    ring_xn = RingGather(quarters_of(nbuf), xnormed_ref, *ring_sems[5], "x", chip, core, t)
    ring_zn = RingGather(quarters_of(nbuf), znormed_ref, *ring_sems[6], "z", chip, core, t)
    ring_q = RingGather(lambda p: dqkv_ref.at[0], rq, *ring_sems[7], "x", chip, core, t)
    ring_k = RingGather(lambda p: dqkv_ref.at[1], rk, *ring_sems[8], "z", chip, core, t)
    ring_vx = RingGather(
        lambda p: dqkv_ref.at[2, :, :128], rvx, *ring_sems[9], "x", chip, core, t
    )
    ring_vz = RingGather(
        lambda p: dqkv_ref.at[2, :, 128:], rvz, *ring_sems[11], "z", chip, core, t
    )
    send_qo = Scatter(pqo, sqo, *scatter[2], 8, 8 * x_at, chip // 4, chip, core, t)
    send_kv = Scatter(pkv, skv, *scatter[3], 8, 8 * z_at, chip % 8, chip, core, t)
    members = ((s + 1 - 2 * core, t), (s, 1 - t), (s + 1 - 2 * core, 1 - t))
    ring_ffn = RingGatherOnce(
        halves(fbuf), lffn, *once_sems, "z", chip, core, t,
    )
    send_down = Scatter(
        pdown, sdown, *scatter[0], 16, 16 * (x_at // 2), 8 * (x_at % 2) + chip // 4, chip, core, t
    )
    send_gate, send_up = (
        Scatter(
            part, to, *sems, 16, 16 * (z_at // 2), 8 * (z_at % 2) + chip % 8, chip, core, t
        )
        for part, to, sems in ((pgate, sgate, scatter[1]), (pup, sup, scatter[4]))
    )
    first_loads = [
        weight_load(ref, buf.at[:, k * 384 : (k + 1) * 384], w2sem.at[i], core, 384)
        for i, (ref, buf, k) in enumerate(((wk_ref, wg, 0), (wv_ref, wg, 1), (wq_ref, wu, 0)))
    ]
    loads = [
        weight_load(wo_ref, wo, wsem.at[0], core, 384),
        weight_load(wg_ref, wg, wsem.at[1], core, 1024),
        weight_load(wu_ref, wu, wsem.at[2], core, 1024),
        weight_load(wd_ref, wd, wsem.at[3], core, 1024),
    ]
    for load in (first_loads[2], *first_loads[:2], loads[0]):
        load.start()
    quad = QuadGather(nbuf, *gather_sems[2], chip, core, t)
    quad_o = QuadGather(obuf, *gather_sems[3], chip, core, t)
    mine = pl.ds(pl.multiple_of(quad.mine, ROWS), ROWS)
    x = x_ref[...]
    normed = (x * rms_scale(x) * long_row(attn_ref)).astype(BF)
    nbuf[mine, :] = normed
    greet_all(chip, core, t)
    quad.start()
    dout = cot_ref[...] * mask_column(mask_ref)
    obuf[mine, :] = dout.astype(BF)
    lam = lambda_of(lambdas_ref, 6 * t + head)
    sub = as_column(sub_ref[...])
    ffn_gain = long_row(ffn_ref)
    vec[...] = jnp.zeros_like(vec)
    unit = eye(128)
    quad.finish()
    def kv_piece(j):
        return dqkv_ref.at[j, :, :256]

    self_served = jnp.logical_and(parity == core, chip % 2 == core)

    def kv_sends():
        def one(o, carry):
            w = lax.rem(chip + 7 * o, WORKERS)
            j = w // PER_HEAD
            target = 2 * worker_chip(core, w) + chip % 2

            @pl.when(target == s)
            def _():
                pltpu.make_async_copy(kv_piece(j), kv.at[chip], kvrecv.at[chip]).start()

            @pl.when(target != s)
            def _():
                remote(kv_piece(j), kv.at[chip], kvsend.at[0], kvrecv.at[chip], target, t).start()

            return carry

        lax.fori_loop(0, WORKERS, one, 0)

    first_loads[2].wait()
    value = matmul(nbuf[...], wu[:, :384]).astype(BF)
    for j in range(3):
        for u in range(2):
            dms[j, u] = value[u * 128 : (u + 1) * 128, j * 128 : (j + 1) * 128]
    tile_sends(dms, q, qsend, qrecv, chip, core, t, True)
    for k in range(2):
        first_loads[k].wait()
        value = matmul(nbuf[...], wg[:, k * 384 : (k + 1) * 384]).astype(BF)
        for j in range(3):
            dqkv_ref[j, :, k * 128 : (k + 1) * 128] = value[:, j * 128 : (j + 1) * 128]

    kv_sends()
    quad_o.start()
    for load in loads[1:]:
        load.start()

    def tile_at(r):
        late = 4 + 10 * (r - 1) + jnp.where((r - 1) % 2 == 0, slot, 9 - slot)
        return jnp.where(r == 0, slot, late)

    def tiles_from(first, span):
        reach, past = 0, 0
        for r in range(SLOTS):
            last = tile_of(slot, r) * TILE // span
            counts = (slot < 4) if r == 0 else True
            reach += jnp.where(jnp.logical_and(counts, last >= first), 1, 0)
            past += jnp.where(jnp.logical_and(counts, last > first), 1, 0)
        return SLOTS - reach, SLOTS - past

    def each_tile(first, span, step):
        reach, past = tiles_from(first, span)

        def masked_step(r, carry):
            step(r, True)
            return carry

        def full_step(r, carry):
            step(r, False)
            return carry

        lax.fori_loop(reach, past, masked_step, 0)
        lax.fori_loop(past, SLOTS, full_step, 0)

    def source_of(o, half):
        return lax.rem((chip // 2 + o) * 2 + half, CHIPS)

    def arrive(source):
        pltpu.make_async_copy(kv_piece(0), kv.at[source], kvrecv.at[source]).wait()

    def turn(source):
        both_t = matmul_t(eye(256), kv[source])
        turned[:, pl.ds(pl.multiple_of(source * BLOCK, BLOCK), BLOCK)] = both_t[128:].astype(BF)
        square = both_t[:128] * both_t[:128]
        for m in range(2):
            largest = jnp.sum(square[64 * m : 64 * m + 64], axis=0, keepdims=True)
            crest[m : m + 1, :] = jnp.maximum(crest[m : m + 1, :], largest)

    @pl.when(served)
    def _():
        crest[...] = jnp.zeros_like(crest)

        def take(o, carry):
            source = source_of(o, core)
            arrive(source)
            view = kv.at[source]
            remote(view, view, fsend.at[0], kvrecv.at[source], s + 1 - 2 * core, t).start()
            turn(source)
            return carry

        lax.fori_loop(0, CHIPS // 2, take, 0)

        def take_passed(o, carry):
            source = source_of(o, 1 - core)
            arrive(source)
            turn(source)
            return carry

        lax.fori_loop(0, CHIPS // 2, take_passed, 0)
        for m in range(2):
            kmax[m] = jnp.max(crest[m : m + 1, :])

    quad_o.finish()
    tile_waits(dms, q, qsend, qrecv, chip, core, t)
    ring_zn.start()
    ring_dout.start()
    front = dq_acc.at[0]

    for r in range(SLOTS):
        tile = tile_of(slot, r)

        @pl.when(served if r else jnp.logical_and(served, slot < 4))
        def _():
            q_t = q[r].astype(F32).T
            square = q_t * q_t
            bound = SCORE * jnp.concatenate(
                [
                    jnp.sqrt(jnp.sum(square[:64], axis=0, keepdims=True) * kmax[0]),
                    jnp.sqrt(jnp.sum(square[64:], axis=0, keepdims=True) * kmax[1]),
                ],
                axis=1,
            )
            q_both = both_maps(q_t).astype(BF)
            q_cols[r] = q_both
            front[...] = jnp.zeros((128, 2 * TILE), F32)
            weights[...] = jnp.zeros_like(weights)

            def step(b, masked):
                sums, out = None, None
                for u in range(STEP // KB):
                    start = pl.multiple_of(b * STEP + u * KB, KB)
                    pair = pl.ds(b * (STEP // BLOCK) + u * (KB // BLOCK), KB // BLOCK)
                    score = matmul(kv[pair, :, :128].reshape(KB, 128), q_both)
                    prob = jnp.exp2(score * SCORE - bound)
                    if masked:
                        prob = jnp.where(key_mask(start, KB, tile, 2 * TILE), prob, 0.0)
                    part = jnp.sum(prob.reshape(KB // 8, 8, 2 * TILE), axis=0)
                    term = matmul(turned[:, pl.ds(start, KB)], prob.astype(BF))
                    sums = part if sums is None else sums + part
                    out = term if out is None else out + term
                weights[...] += sums
                front[...] += out

            full = tile * TILE // STEP

            def body(b, carry):
                step(b, False)
                return carry

            lax.fori_loop(0, full, body, 0)
            step(full, True)
            whole = jnp.sum(weights[...], axis=0, keepdims=True)
            parts = front[...] / whole
            parts_all[r] = parts
            logs[r] = bound + jnp.log(whole) * LOG2E
            rms, hat = group_norm(parts, lam)
            dq_out[r] = (hat * sub * OUT_SCALE).T.astype(BF)

    @pl.when(served)
    def _():
        passed = kv.at[pl.ds(0, CHIPS // 2)]
        pltpu.make_async_copy(passed, passed, fsend.at[0]).wait()

    home_sends(dq_out, land, hsend, hrecv, chip, core, t, True)
    loads[0].wait()
    home_waits(dq_out, land, hrecv)
    for j in range(3):
        for u in range(2):
            mix[u * 128 : (u + 1) * 128, j * 128 : (j + 1) * 128] = land[j, u]
    red = QuadReduce(*reduces[0], chip, core, t)
    red.run(lambda k: matmul_t(mix[...], wo[k * CW : (k + 1) * CW, :]))
    ring_xn.start()
    ring_mix.start()
    home_sends(dq_out, land, hsend, hrecv, chip, core, t, False)
    own_kv = jnp.logical_and(self_served, served)
    for count, case in ((WORKERS - 1, own_kv), (WORKERS, jnp.logical_not(own_kv))):

        @pl.when(case)
        def _():
            sent = kv.at[pl.ds(0, count)]
            pltpu.make_async_copy(sent, sent, kvsend.at[0]).wait()

    tile_sends(dms, q, qsend, qrecv, chip, core, t, False)
    resid = x_ref[...] + jnp.concatenate([red.result(k) for k in range(NC)], axis=1)
    ffn_rms = rms_scale(resid)
    ffn_hat = resid * ffn_rms
    fbuf[mine, :] = (ffn_hat * ffn_gain).astype(BF)
    gather_f.start()
    for load in loads[1:]:
        load.wait()
    red.drain()
    gather_f.finish()
    ring_ffn.start()

    def hidden_step(n, carry):
        cols = pl.ds(pl.multiple_of(n * 256, 256), 256)
        b, at = n // 2, n % 2
        gate = matmul(fbuf[...], wg[:, cols])
        up = matmul(fbuf[...], wu[:, cols])
        d_hidden = matmul(obuf[...], wd[:, cols])
        sig = 1.0 / (1.0 + jnp.exp(-gate))
        silu = gate * sig
        to = pl.ds(pl.multiple_of(at * 256, 256), 256)
        hid[b, :, to] = (silu * up).astype(BF)
        dgate[b, :, to] = (d_hidden * up * sig * (1.0 + gate * (1.0 - sig))).astype(BF)
        dup[b, :, to] = (d_hidden * silu).astype(BF)
        return carry

    lax.fori_loop(0, 4, hidden_step, 0)
    ring_gate.start()
    ring_hid.start()
    red2 = QuadReduce(*reduces[0], chip, core, t)

    def ffn_term(k):
        rows = slice(k * CW, (k + 1) * CW)
        return (
            matmul_t(dgate[0], wg[rows, :512])
            + matmul_t(dgate[1], wg[rows, 512:])
            + matmul_t(dup[0], wu[rows, :512])
            + matmul_t(dup[1], wu[rows, 512:])
        )

    quad.drain()
    quad_o.drain()
    for ring in (ring_zn, ring_xn):
        ring.finish()
        ring.drain()
    red2.run(ffn_term)
    late_loads = [
        weight_load(ref, buf.at[:, k * 384 : (k + 1) * 384], w2sem.at[i], core, 384)
        for i, (ref, buf, k) in enumerate(((wq_ref, wg, 0), (wk_ref, wg, 1), (wv_ref, wu, 0)))
    ]
    for load in late_loads:
        load.start()
    red3 = QuadReduce(*reduces[1], chip, core, t)
    d_ffn = jnp.concatenate([red2.result(k) for k in range(NC)], axis=1)
    part = jnp.sum(d_ffn * ffn_hat, axis=0, keepdims=True)
    for k in range(12):
        vec[12 + k : 13 + k, :] = part[:, k * 128 : (k + 1) * 128]
    d_resid = dout + norm_back(d_ffn, ffn_gain, ffn_rms, ffn_hat)
    dres[...] = d_resid
    rbuf[mine, :] = d_resid.astype(BF)
    gather_r.start()
    ring_ffn.forward()
    red3.run(
        lambda k: matmul_t(hid[0], wd[k * CW : (k + 1) * CW, :512])
        + matmul_t(hid[1], wd[k * CW : (k + 1) * CW, 512:])
    )
    gather_r.finish()
    d_mixed = matmul(rbuf[...], wo[...]).astype(BF)
    for j in range(3):
        for u in range(2):
            dms[j, u] = d_mixed[u * 128 : (u + 1) * 128, j * 128 : (j + 1) * 128]
    tile_sends(dms, dmix, tsend, trecv, chip, core, t, True)
    ring_up.start()
    ring_dres.start()
    out_ref[...] = resid + jnp.concatenate([red3.result(k) for k in range(NC)], axis=1)
    results[0].start()

    def to_sibling(o):
        at = o % (2 * PER_SPAN)
        return remote(given.at[at], sib.at[o], dsend.at[at], drecv.at[o], s + 1 - 2 * core, t)

    def to_home(o):
        target = 2 * (2 * o + core) + parity
        spot = home.at[place_at]

        @pl.when(target == s)
        def _():
            pltpu.make_async_copy(both.at[o], spot, krecv.at[0]).start()

        @pl.when(target != s)
        def _():
            remote(both.at[o], spot, ksend.at[0], krecv.at[0], target, t).start()

    @pl.when(served)
    def _():
        def flip(b, carry):
            rows = pl.ds(pl.multiple_of(b * KB, KB), KB)
            block = kv[pl.ds(2 * b, 2), :, :128].reshape(KB, 128)
            turned[:, rows] = matmul_t(unit, block).astype(BF)
            return carry

        lax.fori_loop(0, CHIPS * BLOCK // KB, flip, 0)

    ring_dout.finish()
    ring_hid.finish()
    block_grad(pdown, 0, ldout, lhid[...].reshape(4 * BLOCK, 512), 256)
    lefts = [
        pltpu.make_async_copy(src, ldout.at[:, :, k * 384 : (k + 1) * 384], lsem.at[k])
        for k, src in enumerate((xnormed_ref, znormed_ref))
    ]
    for left in lefts:
        left.start()
    tile_waits(dms, dmix, tsend, trecv, chip, core, t)
    send_down.each()
    ring_ffn.finish()
    ring_gate.finish()
    block_grad(pgate, 0, lffn, lgate[...].reshape(4 * BLOCK, 512), 256)

    for r in range(SLOTS):

        @pl.when(served if r else jnp.logical_and(served, slot < 4))
        def _():
            q_wide = q[r].astype(F32)
            left = lax.broadcasted_iota(jnp.int32, q_wide.shape, 1) < 64
            q_rows[r] = jnp.concatenate(
                [jnp.where(left, q_wide, 0.0), jnp.where(left, 0.0, q_wide)], axis=0
            ).astype(BF)
            parts = parts_all[r]
            first, second = parts[:, :TILE], parts[:, TILE:]
            rms, hat = group_norm(parts, lam)
            e_t = dmix[r].astype(F32).T * OUT_SCALE
            column = jnp.sum(e_t * hat, axis=1, keepdims=True)
            d_differ = norm_back(e_t, sub, rms, hat, 0).astype(BF)
            d_wide = d_differ.astype(F32)
            d_cols[r] = d_differ
            d_rows[r] = d_wide.T.astype(BF)
            second_dot = jnp.sum(d_wide * second, axis=0, keepdims=True)
            row = lax.broadcasted_iota(jnp.int32, (128, 128), 0)
            lane = lax.broadcasted_iota(jnp.int32, (128, 128), 1)
            vec[24:25, :] += jnp.sum(jnp.where(row == lane, column, 0.0), axis=0, keepdims=True)
            here = lax.broadcasted_iota(jnp.int32, (1, 128), 1) == 6 * t + head
            vec[25:26, :] -= jnp.where(here, jnp.sum(second_dot, axis=1, keepdims=True), 0.0)
            deltas[r, 0:1, :] = jnp.sum(d_wide * first, axis=0, keepdims=True)
            deltas[r, 1:2, :] = -lam * second_dot
            dq_acc[r] = jnp.zeros((128, 2 * TILE), F32)

    def pass_on(k):
        for u in range(PER_SPAN):
            o = PER_SPAN * lax.rem(chip + k, SPANS) + u
            to_sibling(o).wait_recv()
            both[o] = (both[o].astype(F32) + sib[o].astype(F32)).astype(BF)
            to_home(o)

    def span(k, carry):
        b = lax.rem(chip + k, SPANS)
        start = pl.multiple_of(b * SPAN, SPAN)
        rows = pl.ds(start, SPAN)
        blocks = pl.ds(b * (SPAN // BLOCK), SPAN // BLOCK)
        acc[...] = jnp.zeros_like(acc)

        def step(r, masked):
            score = matmul(kv[blocks, :, :128].reshape(SPAN, 128), q_cols[r])
            prob = jnp.exp2(score * SCORE - logs[r])
            if masked:
                prob = jnp.where(key_mask(start, SPAN, tile_at(r), 2 * TILE), prob, 0.0)
            upper = matmul(kv[blocks, :, 128:].reshape(SPAN, 128), d_cols[r])
            p1, p2 = prob[:, :TILE], prob[:, TILE:]
            ds = jnp.concatenate(
                [p1 * (upper - deltas[r, 0:1, :]), p2 * (-lam * upper - deltas[r, 1:2, :])],
                axis=1,
            ).astype(BF)
            mixed = (p1 - lam * p2).astype(BF)
            acc[:, :128] += matmul(ds, q_rows[r])
            acc[:, 128:] += matmul(mixed, d_rows[r])
            dq_acc[r] += matmul(turned[:, rows], ds)

        each_tile(b, SPAN, step)

        @pl.when(k >= 2)
        def _():
            for u in range(PER_SPAN):
                to_sibling(PER_SPAN * lax.rem(chip + k - 2, SPANS) + u).wait_send()

        for u in range(PER_SPAN):
            o = PER_SPAN * b + u
            for ref, at, which in ((given, o % (2 * PER_SPAN), 1 - core), (both, o, core)):
                part = acc[pl.ds(pl.multiple_of((2 * u + which) * BLOCK, BLOCK), BLOCK), :]
                ref[at, :, :128] = (part[:, :128] * 0.125).astype(BF)
                ref[at, :, 128:] = part[:, 128:].astype(BF)
            to_sibling(o).start()

        @pl.when(k > 0)
        def _():
            pass_on(k - 1)

        return carry

    def early(k, carry):
        span(k, carry)

        @pl.when(k < 2)
        def _():
            send_gate.some(8 * k, 8 * k + 8)

        return carry

    def late(k, carry):
        span(k, carry)

        @pl.when(k < EARLY_SPANS + 4)
        def _():
            at = 4 * (k - EARLY_SPANS)
            send_up.some(at, at + 4)

        return carry

    @pl.when(served)
    def _():
        lax.fori_loop(0, EARLY_SPANS, early, 0)

    @pl.when(jnp.logical_not(served))
    def _():
        send_gate.each()

    ring_up.finish()
    block_grad(pup, 0, lffn, lup[...].reshape(4 * BLOCK, 512), 256)

    @pl.when(jnp.logical_not(served))
    def _():
        send_up.each()

    @pl.when(served)
    def _():
        lax.fori_loop(EARLY_SPANS, SPANS, late, 0)
        pass_on(SPANS - 1)

    for r in range(SLOTS):

        @pl.when(served if r else jnp.logical_and(served, slot < 4))
        def _():
            dq_t = jnp.concatenate([dq_acc[r, :64, :TILE], dq_acc[r, 64:, TILE:]], axis=0)
            dq_out[r] = (dq_t * 0.125).T.astype(BF)

    home_sends(dq_out, land, gsend, grecv, chip, core, t, True)
    home_waits(dq_out, land, grecv)
    for j in range(3):
        for u in range(2):
            dqkv_ref[0, u * 128 : (u + 1) * 128, j * 128 : (j + 1) * 128] = land[j, u]
    ring_q.start()
    pltpu.make_async_copy(home, home, krecv.at[0]).wait()
    for j in range(3):
        total = jnp.zeros((BLOCK, 256), F32)
        for p in range(PER_HEAD):
            spot = j * PER_HEAD + p
            total = total + home[spot].astype(F32)
        dqkv_ref[1, :, j * 128 : (j + 1) * 128] = total[:, :128].astype(BF)
        dqkv_ref[2, :, j * 128 : (j + 1) * 128] = total[:, 128:].astype(BF)
    ring_k.start()
    ring_vx.start()
    ring_vz.start()

    for load in late_loads:
        load.wait()
    red2.drain()
    red4 = QuadReduce(*reduces[0], chip, core, t)

    def normed_term(k):
        rows = slice(k * CW, (k + 1) * CW)
        return (
            matmul_t(dqkv_ref[0], wg[rows, :384])
            + matmul_t(dqkv_ref[1], wg[rows, 384:768])
            + matmul_t(dqkv_ref[2], wu[rows, :384])
        )

    red4.run(normed_term)
    ring_mix.finish()
    ring_dres.finish()
    block_grad(pqo, 384, xdres, xmix[...].reshape(4 * BLOCK, 384), 384, 0, 384)
    x = x_ref[...]
    rms = rms_scale(x)
    hat = x * rms
    d_normed = jnp.concatenate([red4.result(k) for k in range(NC)], axis=1)
    part = jnp.sum(d_normed * hat, axis=0, keepdims=True)
    for k in range(12):
        vec[k : k + 1, :] = part[:, k * 128 : (k + 1) * 128]
    first_sum = [
        remote(vec, vecs.at[k], asem.at[0, k], asem.at[1, k], *member)
        for k, member in enumerate(members)
    ]
    for cp in first_sum:
        cp.start()
    grad_ref[...] = dres[...] + norm_back(d_normed, long_row(attn_ref), rms, hat)
    results[1].start()
    for cp in first_sum:
        cp.wait_recv()
    share = pl.ds(pl.multiple_of((2 * core + t) * 8, 8), 8)
    quarter[...] = (vec[share, :] + vecs[0, share, :]) + (vecs[1, share, :] + vecs[2, share, :])

    def spread(k, carry):
        to = 2 * lax.rem(chip + k, CHIPS) + core
        remote(quarter, quarters.at[chip], bsem.at[0], bsem.at[1], to, t).start()
        return carry

    own = pltpu.make_async_copy(quarter, quarters.at[chip], bsem.at[1])
    own.start()
    lax.fori_loop(1, CHIPS, spread, 0)
    for left in lefts:
        left.wait()
    ring_q.finish()
    block_grad(pqo, 0, ldout, rq[...].reshape(4 * BLOCK, 384), 384, 0, 384)
    ring_vx.finish()
    block_grad(pqo, 768, ldout, rvx[...].reshape(4 * BLOCK, 128), 384, 0, 384)
    send_qo.each()
    ring_k.finish()
    block_grad(pkv, 0, ldout, rk[...].reshape(4 * BLOCK, 384), 384, 384, 384)
    ring_vz.finish()
    block_grad(pkv, 384, ldout, rvz[...].reshape(4 * BLOCK, 256), 384, 384, 384)
    send_kv.each()

    send_down.wait()
    for b in range(2):
        total = send_down.total(b, slice(0, 512))
        for h in range(2):
            swap[h, :, 2048 + b * 512 : 2560 + b * 512] = total[h * 24 : h * 24 + 24]
    for m, send in enumerate((send_gate, send_up)):
        send.wait()
        for b in range(2):
            total = send.total(b, slice(0, 512))
            at = m * 1024 + b * 512
            for h in range(2):
                swap[h, :, at : at + 512] = total[h * 24 : h * 24 + 24]
    sibling = s + 1 - 2 * core
    swap_copy = remote(swap.at[1 - core], swapped, swap_sem.at[0], swap_sem.at[1], sibling, t)
    swap_copy.start()

    pltpu.make_async_copy(quarters, quarters, bsem.at[1]).wait()

    def collect(k, total):
        return total + quarters[k]

    sums_ref[share, :] = lax.fori_loop(0, CHIPS, collect, jnp.zeros((8, 128), F32))
    last_sum = [
        remote(sums_ref.at[share], sums_ref.at[share], csem.at[0, k], csem.at[1, k], *member)
        for k, member in enumerate(members)
    ]
    for cp in last_sum:
        cp.start()
    for send, spots in (
        (send_qo, ((0, 384, 0), (384, 384, 1152), (768, 128, 768))),
        (send_kv, ((0, 384, 384), (384, 256, 896))),
    ):
        send.wait()
        for first, width, at in spots:
            total = send.total(0, slice(first, first + width))
            for h in range(2):
                swap2[h, :, at : at + width] = total[h * 24 : h * 24 + 24]
    swap2_copy = remote(swap2.at[1 - core], swapped2, swap2_sem.at[0], swap2_sem.at[1], sibling, t)
    swap2_copy.start()
    swap_copy.wait()
    swap_out(swap, swapped, ((gate_ref, 0), (up_ref, 1024), (down_ref, 2048)), 1024, core)
    for cp in results[6:]:
        cp.start()

    for ring in (
        ring_dout, ring_mix, ring_hid, ring_gate, ring_up, ring_dres, ring_ffn, ring_q, ring_k, ring_vx,
        ring_vz,
    ):
        ring.drain()
    for send in (send_gate, send_up, send_down, send_qo, send_kv):
        send.drain()
    home_sends(dq_out, land, gsend, grecv, chip, core, t, False)
    tile_sends(dms, dmix, tsend, trecv, chip, core, t, False)
    for gather in (gather_f, gather_r):
        gather.drain()
    red3.drain()
    red4.drain()

    @pl.when(served)
    def _():
        for k in (SPANS - 2, SPANS - 1):
            for u in range(PER_SPAN):
                to_sibling(PER_SPAN * lax.rem(chip + k, SPANS) + u).wait_send()

    for count, case in ((CHIPS // 2 - 1, self_served), (CHIPS // 2, jnp.logical_not(self_served))):

        @pl.when(jnp.logical_and(served, case))
        def _():
            sent = both.at[pl.ds(0, count)]
            pltpu.make_async_copy(sent, sent, ksend.at[0]).wait()

    for cp in last_sum:
        cp.wait()
    for cp in first_sum:
        cp.wait_send()
    others = quarters.at[pl.ds(0, CHIPS - 1)]
    pltpu.make_async_copy(others, others, bsem.at[0]).wait()
    swap2_copy.wait()
    outs = ((gq_ref, 0), (gk_ref, 384), (gv_ref, 768), (go_ref, 1152))
    swap_out(swap2, swapped2, outs, 384, core)
    for cp in results[2:6]:
        cp.start()
    for cp in results:
        cp.wait()


def swap_out(swap, swapped, outs, width, core):
    mine = swap[core]
    for c in range(2):

        @pl.when(core == c)
        def _():
            for ref, at in outs:
                ref[:, c * width : (c + 1) * width] = mine[:, at : at + width]
                other = (1 - c) * width
                ref[:, other : other + width] = swapped[:, at : at + width]


def layer(x, cot, mask, attn, ffn, sub, lambdas, wq, wk, wv, wo, wg, wu, wd):
    half = (CHIPS // 2, BLOCK, 256)
    vm = pltpu.VMEM
    sem = pltpu.SemaphoreType.DMA
    return pl.pallas_call(
        layer_kernel,
        name="layer",
        out_shape=(
            shape((ROWS, D), F32),
            shape((ROWS, D), F32),
            *([shape((24, 768), F32)] * 4),
            *([shape((24, 2048), F32)] * 3),
            shape((32, 128), F32),
            shape(GATHERED_Q, BF),
            shape(GATHERED_Q, BF),
        ),
        in_specs=[VM] * 7 + [ANY] * 7,
        out_specs=(ANY,) * 9 + (VM,) + (ANY,) * 2,
        scratch_shapes=[
            vm((ROWS, D), F32),
            vm((ROWS, D), F32),
            *([vm((24, 768), F32)] * 4),
            *([vm((24, 2048), F32)] * 3),
            vm((ROWS, D), F32),
            vm((3, BLOCK, 384), BF),
            *([vm(GATHERED_Q, BF)] * 2),
            vm((4, BLOCK, 128), BF),
            vm((4, BLOCK, 256), BF),
            *([vm(GATHERED_Q, BF)] * 2),
            vm((384, 896), BF),
            vm((384, 640), BF),
            vm((8, CHUNK, 896), BF),
            vm((8, CHUNK, 640), BF),
            vm((2, 24, 1536), F32),
            vm((24, 1536), F32),
            vm((32, 128), F32),
            vm((3, 32, 128), F32),
            vm((8, 128), F32),
            vm((CHIPS, 8, 128), F32),
            vm((3, 2, TILE, 128), BF),
            vm((D, 384), BF),
            vm((D, 1024), BF),
            vm((D, 1024), BF),
            vm((D, 1024), BF),
            vm((BLOCK, D), BF),
            vm((BLOCK, D), BF),
            vm((3, 2, TILE, 128), BF),
            vm((BLOCK, D), BF),
            vm((2, BLOCK, 512), BF),
            vm((2, BLOCK, 512), BF),
            vm((2, BLOCK, 512), BF),
            vm((BLOCK, 384), BF),
            vm((SLOTS, TILE, 128), BF),
            vm(KV, BF),
            vm((SLOTS, 128, 2 * TILE), F32),
            vm((SLOTS, 1, 2 * TILE), F32),
            vm((SLOTS, TILE, 128), BF),
            vm(GATHERED, BF),
            *([vm((4, BLOCK, 512), BF)] * 3),
            vm(GATHERED, BF),
            *([vm((768, 512), BF)] * 3),
            *([vm((16, CHUNK, 512), BF)] * 3),
            vm((2, 24, 3072), F32),
            vm((24, 3072), F32),
            vm((128, CHIPS * BLOCK), BF),
            vm((SPAN, 256), F32),
            vm((SLOTS, 128, 2 * TILE), BF),
            vm((SLOTS, 2 * TILE, 128), BF),
            vm((SLOTS, 128, TILE), BF),
            vm((SLOTS, TILE, 128), BF),
            vm((SLOTS, 2, TILE), F32),
            vm((SLOTS, 128, 2 * TILE), F32),
            vm((SLOTS, TILE, 128), BF),
            vm((2 * PER_SPAN, BLOCK, 256), BF),
            vm(half, BF),
            vm(half, BF),
            vm((3 * PER_HEAD, BLOCK, 256), BF),
            vm((8, BLOCK), F32),
            pltpu.SMEM((2,), F32),
            vm((8, 2 * TILE), F32),
            *(REDUCE_SCRATCH * 2),
            *(GATHER_SEMS * 4),
            *(RING_SEMS * 12),
            *ONCE_SEMS,
            *(RING_SEMS * 5),
            sem((4,)),
            sem((SLOTS,)),
            sem((3, 2)),
            sem((6,)),
            sem((SLOTS,)),
            sem((2,)),
            sem((2 * PER_SPAN,)),
            sem((CHIPS // 2,)),
            sem((1,)),
            sem((1,)),
            sem((SLOTS,)),
            sem((3, 2)),
            sem((3,)),
            sem((2,)),
            sem((2,)),
            sem((2, 3)),
            sem((2,)),
            sem((2, 3)),
            sem((9,)),
            sem((1,)),
            sem((CHIPS,)),
            sem((1,)),
            sem((6,)),
            sem((SLOTS,)),
        ],
        compiler_params=pltpu.CompilerParams(
            collective_id=0, has_side_effects=True, vmem_limit_bytes=VMEM_LIMIT
        ),
    )(x, cot, mask, attn, ffn, sub, lambdas, wq, wk, wv, wo, wg, wu, wd)


def publish(lambdas, sums, arrays):
    count = len(arrays)

    def kernel(lambdas_ref, sums_ref, *refs):
        for k in range(count):
            refs[count + k][...] = refs[k][...]
        attn_ref, ffn_ref, sub_ref, grad_ref = refs[2 * count :]
        attn_ref[...] = sums_ref[0:12, :]
        ffn_ref[...] = sums_ref[12:24, :]
        sub_ref[...] = sums_ref[24:25, :]
        vectors, first, second = lambda_parts(lambdas_ref)
        d_lam = as_column(sums_ref[25:26, :])[:12, :1]
        factors = (d_lam * first, d_lam * first, -d_lam * second, -d_lam * second)
        for k, other in enumerate((1, 0, 3, 2)):
            grad_ref[:, k, :] = factors[k] * vectors[other]

    return pl.pallas_call(
        kernel,
        name="publish",
        out_shape=tuple(shape(a.shape, a.dtype) for a in arrays)
        + (shape((12, 128), F32), shape((12, 128), F32), shape((1, 128), F32), shape((12, 4, 64), F32)),
        in_specs=[VM] * (count + 2),
        out_specs=(VM,) * (count + 4),
    )(lambdas, sums, *arrays)


def on_device(
    hidden_in, cotangent, needle_mask, attn_gain, lambdas, subln_gain, ffn_gain,
    weight_query, weight_key, weight_value, weight_out, weight_gate, weight_up, weight_down,
):
    mask = needle_mask.reshape(1, ROWS)
    attn = attn_gain.reshape(12, 128)
    sub = subln_gain.reshape(1, 128)
    by_head = jnp.transpose(lambdas, (1, 0, 2))
    *results, sums, _, _ = layer(
        hidden_in, cotangent, mask, attn, ffn_gain.reshape(12, 128), sub, by_head,
        weight_query, weight_key, weight_value, weight_out, weight_gate, weight_up, weight_down,
    )
    *results, attn_grad, ffn_grad, sub_grad, lambda_grad = publish(by_head, sums, results)
    return (
        *results,
        attn_grad.reshape(D),
        jnp.transpose(lambda_grad, (1, 0, 2)),
        sub_grad.reshape(128),
        ffn_grad.reshape(D),
    )


def solution(mesh):
    split = P(None, "tp")
    rows = P(("seq", "tp"), None)
    both = P("seq", "tp")
    return jax.shard_map(
        on_device,
        mesh=mesh,
        in_specs=(rows, rows, P(("seq", "tp"))) + (P(),) * 4 + (split,) * 7,
        out_specs=(rows, rows) + (both,) * 7 + (P(),) * 4,
        check_vma=False,
    )
```

```python
import math

import jax
import jax.numpy as jnp
from jax import lax
from jax.experimental import pallas as pl
from jax.experimental.pallas import tpu as pltpu
from jax.sharding import PartitionSpec as P

MESH = pl.DeviceIdType.MESH
BF = jnp.bfloat16
F32 = jnp.float32
EPS = 1e-06
LAMBDA_INIT = 0.8 - 0.6 * math.exp(-3.6)
OUT_SCALE = 1.0 - LAMBDA_INIT
D = 1536
CHIPS = 32
PER_HEAD = 5
WORKERS = 15
ROWS = 64
BLOCK = 256
TILE = 128
SLOTS = 7
KB = 512
LOG2E = 1.4426950408889634
SCORE = 0.125 * LOG2E
VMEM_LIMIT = 63 * 2**20


def place():
    s = lax.axis_index("seq")
    return s // 2, s % 2, lax.axis_index("tp")


def worker(chip, core):
    x, y, z = chip % 4, chip // 4 % 2, chip // 8
    at = 4 * z + x
    return (x + y + z) % 2, at, at % PER_HEAD * 2 + core, at < WORKERS


def worker_chip(parity, at):
    x, z = at % 4, at // 4
    return (2 * z + (x + z + parity) % 2) * 4 + x


def owner_of(tile):
    step = (tile - 4) // 10
    pos = (tile - 4) % 10
    slot = jnp.where(step % 2 == 0, pos, 9 - pos)
    early = tile < 4
    return jnp.where(early, tile, slot), jnp.where(early, 0, step + 1)


def tile_of(slot, r):
    if r == 0:
        return slot
    return 4 + 10 * (r - 1) + (slot if (r - 1) % 2 == 0 else 9 - slot)


def matmul(a, b):
    return jnp.dot(a, b, preferred_element_type=F32)


def matmul_t(a, b):
    return lax.dot_general(a, b, (((1,), (1,)), ((), ())), preferred_element_type=F32)


def rms_scale(values, axis=-1):
    return lax.rsqrt(jnp.mean(values * values, axis=axis, keepdims=True) + EPS)


def norm_back(grad_normed, gain, rms, hat, axis=-1):
    scaled = grad_normed * gain
    return rms * (scaled - hat * jnp.mean(scaled * hat, axis=axis, keepdims=True))


def greet_all(chip, core, t):
    barrier = pltpu.get_barrier_semaphore()
    s = 2 * chip + core

    def greet(o, carry):
        pl.semaphore_signal(
            barrier, inc=1, device_id=(lax.rem(s + o, 2 * CHIPS), t), device_id_type=MESH
        )
        return carry

    lax.fori_loop(1, 2 * CHIPS, greet, 0)
    pl.semaphore_signal(barrier, inc=1, device_id=(s, 1 - t), device_id_type=MESH)
    pl.semaphore_wait(barrier, 2 * CHIPS)


def remote(src, dst, send_sem, recv_sem, s, t):
    return pltpu.make_async_remote_copy(
        src_ref=src,
        dst_ref=dst,
        send_sem=send_sem,
        recv_sem=recv_sem,
        device_id=(s, t),
        device_id_type=MESH,
    )


def rows_at(ref, start, count):
    return ref.at[pl.ds(pl.multiple_of(start, ROWS), count)]


class QuadGather:
    def __init__(self, buf, send, recv, chip, core, t):
        self.buf, self.send, self.recv = buf, send, recv
        self.chip, self.core, self.t = chip, core, t
        mine = core * 128 + t * ROWS
        self.mine = mine
        self.near = core * 128 + (1 - t) * ROWS
        sib = (2 * chip + 1 - core, t)
        self.to_near = self.copy(mine, 0, (2 * chip + core, 1 - t))
        self.to_sib = self.copy(mine, 1, sib)
        self.forward = self.copy(self.near, 2, sib)

    def copy(self, row, k, target):
        view = rows_at(self.buf, row, ROWS)
        return remote(view, view, self.send.at[k], self.recv.at[k], *target)

    def start(self):
        self.to_near.start()
        self.to_sib.start()

    def finish(self):
        self.to_near.wait_recv()
        self.forward.start()
        self.to_sib.wait_recv()
        self.forward.wait_recv()

    def drain(self):
        self.to_near.wait_send()
        self.to_sib.wait_send()
        self.forward.wait_send()


class RingGather:
    def __init__(self, pieces, land, send, recv, axis, chip, core, t):
        at = chip % 4 if axis == "x" else chip // 8
        self.local = pltpu.make_async_copy(pieces(at), land.at[at], recv.at[0])
        self.land, self.send, self.recv = land, send, recv
        self.copies = []
        for k in (1, 3, 2):
            if axis == "x":
                peer, chip_to = (at + k) % 4, chip - at + (at + k) % 4
            else:
                peer, chip_to = (at + k) % 4, (chip + 8 * k) % CHIPS
            self.copies.append(
                remote(pieces(peer), land.at[at], send.at[0], recv.at[0], 2 * chip_to + core, t)
            )

    def start(self):
        self.local.start()
        for cp in self.copies:
            cp.start()

    def finish(self):
        pltpu.make_async_copy(self.land, self.land, self.recv.at[0]).wait()

    def drain(self):
        three = self.land.at[pl.ds(0, 3)]
        pltpu.make_async_copy(three, three, self.send.at[0]).wait()


class RingGatherOnce:
    def __init__(self, pieces, land, send, recv, pass_send, pass_recv, axis, chip, core, t):
        at = chip % 4 if axis == "x" else chip // 8
        self.mine = pl.ds(pl.multiple_of(core * 128, 128), 128)
        self.local = pltpu.make_async_copy(pieces(at), land.at[at], recv.at[0])
        self.local_at = at
        self.copies, self.passes = [], []
        for k in (1, 3, 2):
            peer = (at + k) % 4
            chip_to = chip - at + peer if axis == "x" else (chip + 8 * k) % CHIPS
            self.copies.append(
                remote(
                    pieces(peer).at[self.mine], land.at[at, self.mine],
                    send.at[k - 1], recv.at[4 - k], 2 * chip_to + core, t,
                )
            )
            view = land.at[peer, self.mine]
            self.passes.append(
                (
                    pltpu.make_async_copy(pieces(at).at[self.mine], view, recv.at[k]),
                    remote(view, view, pass_send.at[k - 1], pass_recv.at[k - 1], 2 * chip + 1 - core, t),
                )
            )

    def start(self):
        self.local.start()
        for cp in self.copies:
            cp.start()

    def forward(self):
        for arrive, cp in self.passes:
            arrive.wait()
            cp.start()

    def finish(self):
        self.local.wait()
        for _, cp in self.passes:
            cp.wait_recv()

    def drain(self):
        for cp in self.copies:
            cp.wait_send()
        for _, cp in self.passes:
            cp.wait_send()


ONCE_SEMS = [
    pltpu.SemaphoreType.DMA((3,)),
    pltpu.SemaphoreType.DMA((4,)),
    pltpu.SemaphoreType.DMA((3,)),
    pltpu.SemaphoreType.DMA((3,)),
]
RING_SEMS = [pltpu.SemaphoreType.DMA((1,)), pltpu.SemaphoreType.DMA((1,))]


def block_grad(dst, start, left, right, step, at=0, total=768):
    width = right.shape[1]

    def one(m, carry):
        cols = pl.ds(pl.multiple_of(m * step, 128), step)
        part = left[:, :, pl.ds(pl.multiple_of(at + m * step, 128), step)].reshape(4 * BLOCK, step)
        dst[cols, start : start + width] = lax.dot_general(
            part, right, (((0,), (0,)), ((), ())), preferred_element_type=F32
        ).astype(BF)
        return carry

    lax.fori_loop(0, total // step, one, 0)


CHUNK = 48


class Scatter:
    def __init__(self, part, land, send, recv, count, first, spot, chip, core, t):
        self.part, self.land, self.send, self.recv = part, land, send, recv
        self.count, self.first, self.spot = count, first, spot
        self.chip, self.core, self.t = chip, core, t

    def source(self, i):
        return self.part.at[pl.ds(pl.multiple_of(i * CHUNK, 16), CHUNK)]

    def each(self):
        self.some(0, self.count)

    def some(self, first, end):
        def one(o, carry):
            i = lax.rem(self.chip + 1 + 3 * o, self.count)
            owner = self.first + i
            to = self.land.at[self.spot]

            @pl.when(owner == self.chip)
            def _():
                pltpu.make_async_copy(self.source(i), to, self.recv.at[0]).start()

            @pl.when(owner != self.chip)
            def _():
                remote(
                    self.source(i), to, self.send.at[0], self.recv.at[0], 2 * owner + self.core, self.t
                ).start()

            return carry

        lax.fori_loop(first, end, one, 0)

    def wait(self):
        pltpu.make_async_copy(self.land, self.land, self.recv.at[0]).wait()

    def drain(self):
        own = jnp.logical_and(self.chip >= self.first, self.chip < self.first + self.count)
        for count, case in ((self.count - 1, own), (self.count, jnp.logical_not(own))):

            @pl.when(case)
            def _():
                sent = self.part.at[pl.ds(0, count * CHUNK)]
                pltpu.make_async_copy(sent, sent, self.send.at[0]).wait()

    def total(self, b, cols):
        def one(k, carry):
            return carry + self.land[8 * b + k, :, cols].astype(F32)

        return lax.fori_loop(0, 8, one, jnp.zeros((CHUNK, cols.stop - cols.start), F32))


GATHER_SEMS = [pltpu.SemaphoreType.DMA((3,)), pltpu.SemaphoreType.DMA((3,))]
CW = 512
NC = D // CW


class QuadReduce:
    def __init__(self, part, dsend, drecv, ysend, yrecv, ds, dr, ys, yr, chip, core, t):
        self.part, self.dsend, self.drecv = part, dsend, drecv
        self.ysend, self.yrecv = ysend, yrecv
        self.core, self.t = core, t
        self.ds, self.ys = ds, ys
        self.d = [
            remote(dsend.at[k], drecv.at[k], ds.at[0], dr.at[k], 2 * chip + 1 - core, t)
            for k in range(NC)
        ]
        self.y = [
            remote(ysend.at[k], yrecv.at[k], ys.at[0], yr.at[k], 2 * chip + core, 1 - t)
            for k in range(NC)
        ]

    def rows(self, start, count, k):
        return self.part[pl.ds(pl.multiple_of(start, ROWS), count), k * CW : (k + 1) * CW]

    def put(self, k, value):
        self.part[:, k * CW : (k + 1) * CW] = value
        self.dsend[k] = self.rows((1 - self.core) * 128, 128, k).astype(BF)
        self.d[k].start()

    def middle(self, k):
        self.d[k].wait_recv()
        near = (1 - self.t) * ROWS
        far = self.rows(self.core * 128 + near, ROWS, k)
        got = self.drecv[k, pl.ds(pl.multiple_of(near, ROWS), ROWS), :]
        self.ysend[k] = (far + got.astype(F32)).astype(BF)
        self.y[k].start()

    def result(self, k):
        mine = self.t * ROWS
        own = self.rows(self.core * 128 + mine, ROWS, k)
        got = self.drecv[k, pl.ds(pl.multiple_of(mine, ROWS), ROWS), :].astype(F32)
        self.y[k].wait_recv()
        return own + got + self.yrecv[k].astype(F32)

    def run(self, term):
        for k in range(NC):
            self.put(k, term(k))
            if k:
                self.middle(k - 1)
        self.middle(NC - 1)

    def drain(self):
        pltpu.make_async_copy(self.dsend, self.dsend, self.ds.at[0]).wait()
        pltpu.make_async_copy(self.ysend, self.ysend, self.ys.at[0]).wait()


REDUCE_SCRATCH = [
    pltpu.VMEM((BLOCK, D), F32),
    pltpu.VMEM((NC, 128, CW), BF),
    pltpu.VMEM((NC, 128, CW), BF),
    pltpu.VMEM((NC, ROWS, CW), BF),
    pltpu.VMEM((NC, ROWS, CW), BF),
] + [pltpu.SemaphoreType.DMA((n,)) for n in (1, NC, 1, NC)]


def tile_sends(tiles, land, send, recv, chip, core, t, start):
    s = 2 * chip + core
    for j in range(3):
        for u in range(2):
            slot, index = owner_of(2 * chip + u)
            target = 2 * worker_chip(core, j * PER_HEAD + slot // 2) + slot % 2
            k = j * 2 + u

            if start:

                @pl.when(target == s)
                def _():
                    pltpu.make_async_copy(tiles.at[j, u], land.at[index], recv.at[index]).start()

            @pl.when(target != s)
            def _():
                cp = remote(tiles.at[j, u], land.at[index], send.at[k], recv.at[index], target, t)
                if start:
                    cp.start()
                else:
                    cp.wait_send()


def tile_waits(tiles, land, send, recv, chip, core, t):
    _, _, slot, served = worker(chip, core)
    for r in range(SLOTS):
        here = served
        if r == 0:
            here = jnp.logical_and(here, slot < 4)

        @pl.when(here)
        def _():
            pltpu.make_async_copy(tiles.at[0, 0], land.at[r], recv.at[r]).wait()


def home_sends(tiles, land, send, recv, chip, core, t, start):
    s = 2 * chip + core
    parity, at, slot, served = worker(chip, core)
    for r in range(SLOTS):
        here = served
        if r == 0:
            here = jnp.logical_and(here, slot < 4)
        tile = tile_of(slot, r)
        target = (tile // 2) * 2 + parity
        j, u = at // PER_HEAD, tile % 2

        if start:

            @pl.when(jnp.logical_and(here, target == s))
            def _():
                pltpu.make_async_copy(tiles.at[r], land.at[j, u], recv.at[j, u]).start()

        @pl.when(jnp.logical_and(here, target != s))
        def _():
            cp = remote(tiles.at[r], land.at[j, u], send.at[r], recv.at[j, u], target, t)
            if start:
                cp.start()
            else:
                cp.wait_send()


def home_waits(tiles, land, recv):
    for j in range(3):
        for u in range(2):
            pltpu.make_async_copy(tiles.at[0], land.at[j, u], recv.at[j, u]).wait()


def weight_load(ref, buf, sem, core, width):
    return pltpu.make_async_copy(
        ref.at[:, pl.ds(pl.multiple_of(core * width, 128), width)], buf, sem
    )


VM = pl.BlockSpec(memory_space=pltpu.VMEM)
ANY = pl.BlockSpec(memory_space=pl.ANY)


def shape(dims, dtype):
    return jax.ShapeDtypeStruct(dims, dtype)


HALVES = (2, BLOCK, 768)
QUARTERS = (4, BLOCK, 384)
GATHERED = (4, BLOCK, 768)
GATHERED_Q = (4, BLOCK, 384)
KV = (CHIPS, BLOCK, 256)
STEP = 2048


def eye(size):
    row = lax.broadcasted_iota(jnp.int32, (size, size), 0)
    col = lax.broadcasted_iota(jnp.int32, (size, size), 1)
    return jnp.where(row == col, 1.0, 0.0).astype(BF)


def both_maps(q_t):
    top = lax.broadcasted_iota(jnp.int32, q_t.shape, 0) < 64
    return jnp.concatenate([jnp.where(top, q_t, 0.0), jnp.where(top, 0.0, q_t)], axis=1)


def key_mask(start, count, tile, width):
    key = start + lax.broadcasted_iota(jnp.int32, (count, width), 0)
    query = tile * TILE + lax.broadcasted_iota(jnp.int32, (count, width), 1) % TILE
    return key <= query


def group_norm(parts, lam):
    first, second = parts[:, :TILE], parts[:, TILE:]
    differ = first - lam * second
    rms = rms_scale(differ, 0)
    return rms, differ * rms


def long_row(ref):
    return jnp.concatenate([ref[k : k + 1, :] for k in range(12)], axis=1)


def as_column(row):
    return jnp.broadcast_to(row, (128, 128)).T


def mask_column(mask_ref):
    mask = mask_ref[...].astype(F32)
    return as_column(jnp.concatenate([mask, mask], axis=1))[:ROWS, :1]


def lambda_parts(lambdas_ref):
    vectors = [lambdas_ref[:, k, :] for k in range(4)]
    first = jnp.exp(jnp.sum(vectors[0] * vectors[1], axis=-1, keepdims=True))
    second = jnp.exp(jnp.sum(vectors[2] * vectors[3], axis=-1, keepdims=True))
    return vectors, first, second


def lambda_of(lambdas_ref, head):
    _, first, second = lambda_parts(lambdas_ref)
    every = first - second + LAMBDA_INIT
    mine = lax.broadcasted_iota(jnp.int32, every.shape, 0) == head
    return jnp.sum(jnp.where(mine, every, 0.0), axis=0, keepdims=True)


SPAN = 1024
SPANS = CHIPS * BLOCK // SPAN
PER_SPAN = SPAN // BLOCK // 2
EARLY_SPANS = 5


def layer_kernel(
    x_ref, cot_ref, mask_ref, attn_ref, ffn_ref, sub_ref, lambdas_ref,
    wq_ref, wk_ref, wv_ref, wo_ref, wg_ref, wu_ref, wd_ref,
    out_to, grad_to, gq_to, gk_to, gv_to, go_to, gate_to, up_to, down_to, sums_ref,
    xnormed_ref, znormed_ref,
    out_ref, grad_ref, gq_ref, gk_ref, gv_ref, go_ref, gate_ref, up_ref, down_ref,
    dres, dqkv_ref, rq, rk, rvx, rvz, xmix, xdres, pqo, pkv, sqo, skv, swap2, swapped2,
    vec, vecs, quarter, quarters,
    land, wo, wg, wu, wd, fbuf, nbuf, dms, obuf, dgate, dup, hid, mix,
    q, kv, parts_all, logs, dmix,
    lffn, lgate, lup, lhid, ldout, pgate, pup, pdown, sgate, sup, sdown, swap, swapped,
    turned, acc, q_cols, q_rows, d_cols, d_rows, deltas, dq_acc, dq_out, given, sib, both, home,
    crest, kmax, weights, *rest,
):
    chip, core, t = place()
    s = 2 * chip + core
    parity, place_at, slot, served = worker(chip, core)
    head = 3 * parity + place_at // PER_HEAD
    x_at, z_at = chip % 4, chip // 8
    taken = iter(rest)

    def take(count):
        return [next(taken) for _ in range(count)]

    reduces = [take(9) for _ in range(2)]
    gather_sems = [take(2) for _ in range(4)]
    ring_sems = [take(2) for _ in range(12)]
    once_sems = take(4)
    scatter = [take(2) for _ in range(5)]
    wsem, hsend, hrecv, tsend, trecv, swap_sem = take(6)
    dsend, drecv, ksend, krecv, gsend, grecv = take(6)
    w2sem, lsem, swap2_sem, asem, bsem, csem = take(6)
    (osem,) = take(1)
    results = [
        pltpu.make_async_copy(src, dst, osem.at[k])
        for k, (src, dst) in enumerate(
            (
                (out_ref, out_to), (grad_ref, grad_to), (gq_ref, gq_to), (gk_ref, gk_to),
                (gv_ref, gv_to), (go_ref, go_to), (gate_ref, gate_to), (up_ref, up_to),
                (down_ref, down_to),
            )
        )
    ]
    kvsend, kvrecv, fsend, qsend, qrecv = take(5)
    rbuf = nbuf


    def halves(ref):
        return lambda p: ref.at[:, pl.ds(pl.multiple_of(p // 2 * 768, 128), 768)]

    def quarters_of(ref):
        return lambda p: ref.at[:, pl.ds(pl.multiple_of(p * 384, 128), 384)]

    gather_f = QuadGather(fbuf, *gather_sems[0], chip, core, t)
    gather_r = QuadGather(rbuf, *gather_sems[1], chip, core, t)
    ring_dout = RingGather(halves(obuf), ldout, *ring_sems[0], "x", chip, core, t)
    ring_mix = RingGather(lambda p: mix, xmix, *ring_sems[1], "x", chip, core, t)
    ring_hid = RingGather(lambda p: hid.at[p % 2], lhid, *ring_sems[2], "x", chip, core, t)
    ring_gate = RingGather(lambda p: dgate.at[p % 2], lgate, *ring_sems[3], "z", chip, core, t)
    ring_up = RingGather(lambda p: dup.at[p % 2], lup, *ring_sems[10], "z", chip, core, t)
    ring_dres = RingGather(
        quarters_of(rbuf), xdres, *ring_sems[4], "x", chip, core, t,
    )
    ring_xn = RingGather(quarters_of(nbuf), xnormed_ref, *ring_sems[5], "x", chip, core, t)
    ring_zn = RingGather(quarters_of(nbuf), znormed_ref, *ring_sems[6], "z", chip, core, t)
    ring_q = RingGather(lambda p: dqkv_ref.at[0], rq, *ring_sems[7], "x", chip, core, t)
    ring_k = RingGather(lambda p: dqkv_ref.at[1], rk, *ring_sems[8], "z", chip, core, t)
    ring_vx = RingGather(
        lambda p: dqkv_ref.at[2, :, :128], rvx, *ring_sems[9], "x", chip, core, t
    )
    ring_vz = RingGather(
        lambda p: dqkv_ref.at[2, :, 128:], rvz, *ring_sems[11], "z", chip, core, t
    )
    send_qo = Scatter(pqo, sqo, *scatter[2], 8, 8 * x_at, chip // 4, chip, core, t)
    send_kv = Scatter(pkv, skv, *scatter[3], 8, 8 * z_at, chip % 8, chip, core, t)
    members = ((s + 1 - 2 * core, t), (s, 1 - t), (s + 1 - 2 * core, 1 - t))
    ring_ffn = RingGatherOnce(
        halves(fbuf), lffn, *once_sems, "z", chip, core, t,
    )
    send_down = Scatter(
        pdown, sdown, *scatter[0], 16, 16 * (x_at // 2), 8 * (x_at % 2) + chip // 4, chip, core, t
    )
    send_gate, send_up = (
        Scatter(
            part, to, *sems, 16, 16 * (z_at // 2), 8 * (z_at % 2) + chip % 8, chip, core, t
        )
        for part, to, sems in ((pgate, sgate, scatter[1]), (pup, sup, scatter[4]))
    )
    first_loads = [
        weight_load(ref, buf.at[:, k * 384 : (k + 1) * 384], w2sem.at[i], core, 384)
        for i, (ref, buf, k) in enumerate(((wk_ref, wg, 0), (wv_ref, wg, 1), (wq_ref, wu, 0)))
    ]
    loads = [
        weight_load(wo_ref, wo, wsem.at[0], core, 384),
        weight_load(wg_ref, wg, wsem.at[1], core, 1024),
        weight_load(wu_ref, wu, wsem.at[2], core, 1024),
        weight_load(wd_ref, wd, wsem.at[3], core, 1024),
    ]
    for load in (first_loads[2], *first_loads[:2], loads[0]):
        load.start()
    quad = QuadGather(nbuf, *gather_sems[2], chip, core, t)
    quad_o = QuadGather(obuf, *gather_sems[3], chip, core, t)
    mine = pl.ds(pl.multiple_of(quad.mine, ROWS), ROWS)
    x = x_ref[...]
    normed = (x * rms_scale(x) * long_row(attn_ref)).astype(BF)
    nbuf[mine, :] = normed
    greet_all(chip, core, t)
    quad.start()
    dout = cot_ref[...] * mask_column(mask_ref)
    obuf[mine, :] = dout.astype(BF)
    lam = lambda_of(lambdas_ref, 6 * t + head)
    sub = as_column(sub_ref[...])
    ffn_gain = long_row(ffn_ref)
    vec[...] = jnp.zeros_like(vec)
    unit = eye(128)
    quad.finish()
    def kv_piece(j):
        return dqkv_ref.at[j, :, :256]

    self_served = jnp.logical_and(parity == core, chip % 2 == core)

    def kv_sends():
        def one(o, carry):
            w = lax.rem(chip + 7 * o, WORKERS)
            j = w // PER_HEAD
            target = 2 * worker_chip(core, w) + chip % 2

            @pl.when(target == s)
            def _():
                pltpu.make_async_copy(kv_piece(j), kv.at[chip], kvrecv.at[chip]).start()

            @pl.when(target != s)
            def _():
                remote(kv_piece(j), kv.at[chip], kvsend.at[0], kvrecv.at[chip], target, t).start()

            return carry

        lax.fori_loop(0, WORKERS, one, 0)

    first_loads[2].wait()
    value = matmul(nbuf[...], wu[:, :384]).astype(BF)
    for j in range(3):
        for u in range(2):
            dms[j, u] = value[u * 128 : (u + 1) * 128, j * 128 : (j + 1) * 128]
    tile_sends(dms, q, qsend, qrecv, chip, core, t, True)
    for k in range(2):
        first_loads[k].wait()
        value = matmul(nbuf[...], wg[:, k * 384 : (k + 1) * 384]).astype(BF)
        for j in range(3):
            dqkv_ref[j, :, k * 128 : (k + 1) * 128] = value[:, j * 128 : (j + 1) * 128]

    kv_sends()
    for load in loads[1:]:
        load.start()

    def tile_at(r):
        late = 4 + 10 * (r - 1) + jnp.where((r - 1) % 2 == 0, slot, 9 - slot)
        return jnp.where(r == 0, slot, late)

    def tiles_from(first, span):
        reach, past = 0, 0
        for r in range(SLOTS):
            last = tile_of(slot, r) * TILE // span
            counts = (slot < 4) if r == 0 else True
            reach += jnp.where(jnp.logical_and(counts, last >= first), 1, 0)
            past += jnp.where(jnp.logical_and(counts, last > first), 1, 0)
        return SLOTS - reach, SLOTS - past

    def each_tile(first, span, step):
        reach, past = tiles_from(first, span)

        def masked_step(r, carry):
            step(r, True)
            return carry

        def full_step(r, carry):
            step(r, False)
            return carry

        lax.fori_loop(reach, past, masked_step, 0)
        lax.fori_loop(past, SLOTS, full_step, 0)

    def source_of(o, half):
        return lax.rem((chip // 2 + o) * 2 + half, CHIPS)

    def arrive(source):
        pltpu.make_async_copy(kv_piece(0), kv.at[source], kvrecv.at[source]).wait()

    def turn(source):
        both_t = matmul_t(eye(256), kv[source])
        turned[:, pl.ds(pl.multiple_of(source * BLOCK, BLOCK), BLOCK)] = both_t[128:].astype(BF)
        square = both_t[:128] * both_t[:128]
        for m in range(2):
            largest = jnp.sum(square[64 * m : 64 * m + 64], axis=0, keepdims=True)
            crest[m : m + 1, :] = jnp.maximum(crest[m : m + 1, :], largest)

    @pl.when(served)
    def _():
        crest[...] = jnp.zeros_like(crest)

        def take(o, carry):
            source = source_of(o, core)
            arrive(source)
            view = kv.at[source]
            remote(view, view, fsend.at[0], kvrecv.at[source], s + 1 - 2 * core, t).start()
            turn(source)
            return carry

        lax.fori_loop(0, CHIPS // 2, take, 0)

        def take_passed(o, carry):
            source = source_of(o, 1 - core)
            arrive(source)
            turn(source)
            return carry

        lax.fori_loop(0, CHIPS // 2, take_passed, 0)
        for m in range(2):
            kmax[m] = jnp.max(crest[m : m + 1, :])

    quad_o.start()
    tile_waits(dms, q, qsend, qrecv, chip, core, t)
    ring_zn.start()
    front = dq_acc.at[0]

    for r in range(SLOTS):
        tile = tile_of(slot, r)
        if r == 4:
            quad_o.finish()
            ring_dout.start()

        @pl.when(served if r else jnp.logical_and(served, slot < 4))
        def _():
            q_t = q[r].astype(F32).T
            square = q_t * q_t
            bound = SCORE * jnp.concatenate(
                [
                    jnp.sqrt(jnp.sum(square[:64], axis=0, keepdims=True) * kmax[0]),
                    jnp.sqrt(jnp.sum(square[64:], axis=0, keepdims=True) * kmax[1]),
                ],
                axis=1,
            )
            q_both = both_maps(q_t).astype(BF)
            q_cols[r] = q_both
            front[...] = jnp.zeros((128, 2 * TILE), F32)
            weights[...] = jnp.zeros_like(weights)

            def step(b, masked):
                sums, out = None, None
                for u in range(STEP // KB):
                    start = pl.multiple_of(b * STEP + u * KB, KB)
                    pair = pl.ds(b * (STEP // BLOCK) + u * (KB // BLOCK), KB // BLOCK)
                    score = matmul(kv[pair, :, :128].reshape(KB, 128), q_both)
                    prob = jnp.exp2(score * SCORE - bound)
                    if masked:
                        prob = jnp.where(key_mask(start, KB, tile, 2 * TILE), prob, 0.0)
                    part = jnp.sum(prob.reshape(KB // 8, 8, 2 * TILE), axis=0)
                    term = matmul(turned[:, pl.ds(start, KB)], prob.astype(BF))
                    sums = part if sums is None else sums + part
                    out = term if out is None else out + term
                weights[...] += sums
                front[...] += out

            full = tile * TILE // STEP

            def body(b, carry):
                step(b, False)
                return carry

            lax.fori_loop(0, full, body, 0)
            step(full, True)
            whole = jnp.sum(weights[...], axis=0, keepdims=True)
            parts = front[...] / whole
            parts_all[r] = parts
            logs[r] = bound + jnp.log(whole) * LOG2E
            rms, hat = group_norm(parts, lam)
            dq_out[r] = (hat * sub * OUT_SCALE).T.astype(BF)

    @pl.when(served)
    def _():
        passed = kv.at[pl.ds(0, CHIPS // 2)]
        pltpu.make_async_copy(passed, passed, fsend.at[0]).wait()

    home_sends(dq_out, land, hsend, hrecv, chip, core, t, True)
    loads[0].wait()
    home_waits(dq_out, land, hrecv)
    for j in range(3):
        for u in range(2):
            mix[u * 128 : (u + 1) * 128, j * 128 : (j + 1) * 128] = land[j, u]
    red = QuadReduce(*reduces[0], chip, core, t)
    red.run(lambda k: matmul_t(mix[...], wo[k * CW : (k + 1) * CW, :]))
    ring_xn.start()
    ring_mix.start()
    home_sends(dq_out, land, hsend, hrecv, chip, core, t, False)
    own_kv = jnp.logical_and(self_served, served)
    for count, case in ((WORKERS - 1, own_kv), (WORKERS, jnp.logical_not(own_kv))):

        @pl.when(case)
        def _():
            sent = kv.at[pl.ds(0, count)]
            pltpu.make_async_copy(sent, sent, kvsend.at[0]).wait()

    tile_sends(dms, q, qsend, qrecv, chip, core, t, False)
    resid = x_ref[...] + jnp.concatenate([red.result(k) for k in range(NC)], axis=1)
    ffn_rms = rms_scale(resid)
    ffn_hat = resid * ffn_rms
    fbuf[mine, :] = (ffn_hat * ffn_gain).astype(BF)
    gather_f.start()

    @pl.when(served)
    def _():
        def flip(b, carry):
            rows = pl.ds(pl.multiple_of(b * KB, KB), KB)
            block = kv[pl.ds(2 * b, 2), :, :128].reshape(KB, 128)
            turned[:, rows] = matmul_t(unit, block).astype(BF)
            return carry

        lax.fori_loop(0, CHIPS * BLOCK // KB, flip, 0)

    for load in loads[1:]:
        load.wait()
    red.drain()
    gather_f.finish()
    ring_ffn.start()

    def hidden_step(n, carry):
        cols = pl.ds(pl.multiple_of(n * 256, 256), 256)
        b, at = n // 2, n % 2
        gate = matmul(fbuf[...], wg[:, cols])
        up = matmul(fbuf[...], wu[:, cols])
        d_hidden = matmul(obuf[...], wd[:, cols])
        sig = 1.0 / (1.0 + jnp.exp(-gate))
        silu = gate * sig
        to = pl.ds(pl.multiple_of(at * 256, 256), 256)
        hid[b, :, to] = (silu * up).astype(BF)
        dgate[b, :, to] = (d_hidden * up * sig * (1.0 + gate * (1.0 - sig))).astype(BF)
        dup[b, :, to] = (d_hidden * silu).astype(BF)
        return carry

    lax.fori_loop(0, 4, hidden_step, 0)
    ring_gate.start()
    ring_hid.start()
    red2 = QuadReduce(*reduces[0], chip, core, t)

    def ffn_term(k):
        rows = slice(k * CW, (k + 1) * CW)
        return (
            matmul_t(dgate[0], wg[rows, :512])
            + matmul_t(dgate[1], wg[rows, 512:])
            + matmul_t(dup[0], wu[rows, :512])
            + matmul_t(dup[1], wu[rows, 512:])
        )

    quad.drain()
    quad_o.drain()
    for ring in (ring_zn, ring_xn):
        ring.finish()
        ring.drain()
    red2.run(ffn_term)
    late_loads = [
        weight_load(ref, buf.at[:, k * 384 : (k + 1) * 384], w2sem.at[i], core, 384)
        for i, (ref, buf, k) in enumerate(((wq_ref, wg, 0), (wk_ref, wg, 1), (wv_ref, wu, 0)))
    ]
    for load in late_loads:
        load.start()
    red3 = QuadReduce(*reduces[1], chip, core, t)
    d_ffn = jnp.concatenate([red2.result(k) for k in range(NC)], axis=1)
    part = jnp.sum(d_ffn * ffn_hat, axis=0, keepdims=True)
    for k in range(12):
        vec[12 + k : 13 + k, :] = part[:, k * 128 : (k + 1) * 128]
    d_resid = dout + norm_back(d_ffn, ffn_gain, ffn_rms, ffn_hat)
    dres[...] = d_resid
    rbuf[mine, :] = d_resid.astype(BF)
    gather_r.start()
    ring_ffn.forward()
    red3.run(
        lambda k: matmul_t(hid[0], wd[k * CW : (k + 1) * CW, :512])
        + matmul_t(hid[1], wd[k * CW : (k + 1) * CW, 512:])
    )
    gather_r.finish()
    d_mixed = matmul(rbuf[...], wo[...]).astype(BF)
    for j in range(3):
        for u in range(2):
            dms[j, u] = d_mixed[u * 128 : (u + 1) * 128, j * 128 : (j + 1) * 128]
    tile_sends(dms, dmix, tsend, trecv, chip, core, t, True)
    out_ref[...] = resid + jnp.concatenate([red3.result(k) for k in range(NC)], axis=1)
    results[0].start()

    def to_sibling(o):
        at = o % (2 * PER_SPAN)
        return remote(given.at[at], sib.at[o], dsend.at[at], drecv.at[o], s + 1 - 2 * core, t)

    def to_home(o):
        target = 2 * (2 * o + core) + parity
        spot = home.at[place_at]

        @pl.when(target == s)
        def _():
            pltpu.make_async_copy(both.at[o], spot, krecv.at[0]).start()

        @pl.when(target != s)
        def _():
            remote(both.at[o], spot, ksend.at[0], krecv.at[0], target, t).start()

    ring_dout.finish()
    ring_hid.finish()
    block_grad(pdown, 0, ldout, lhid[...].reshape(4 * BLOCK, 512), 256)
    lefts = [
        pltpu.make_async_copy(src, ldout.at[:, :, k * 384 : (k + 1) * 384], lsem.at[k])
        for k, src in enumerate((xnormed_ref, znormed_ref))
    ]
    for left in lefts:
        left.start()
    tile_waits(dms, dmix, tsend, trecv, chip, core, t)
    ring_up.start()
    ring_dres.start()
    send_down.each()
    ring_ffn.finish()
    ring_gate.finish()
    block_grad(pgate, 0, lffn, lgate[...].reshape(4 * BLOCK, 512), 256)

    for r in range(SLOTS):

        @pl.when(served if r else jnp.logical_and(served, slot < 4))
        def _():
            q_wide = q[r].astype(F32)
            left = lax.broadcasted_iota(jnp.int32, q_wide.shape, 1) < 64
            q_rows[r] = jnp.concatenate(
                [jnp.where(left, q_wide, 0.0), jnp.where(left, 0.0, q_wide)], axis=0
            ).astype(BF)
            parts = parts_all[r]
            first, second = parts[:, :TILE], parts[:, TILE:]
            rms, hat = group_norm(parts, lam)
            e_t = dmix[r].astype(F32).T * OUT_SCALE
            column = jnp.sum(e_t * hat, axis=1, keepdims=True)
            d_differ = norm_back(e_t, sub, rms, hat, 0).astype(BF)
            d_wide = d_differ.astype(F32)
            d_cols[r] = d_differ
            d_rows[r] = d_wide.T.astype(BF)
            second_dot = jnp.sum(d_wide * second, axis=0, keepdims=True)
            row = lax.broadcasted_iota(jnp.int32, (128, 128), 0)
            lane = lax.broadcasted_iota(jnp.int32, (128, 128), 1)
            vec[24:25, :] += jnp.sum(jnp.where(row == lane, column, 0.0), axis=0, keepdims=True)
            here = lax.broadcasted_iota(jnp.int32, (1, 128), 1) == 6 * t + head
            vec[25:26, :] -= jnp.where(here, jnp.sum(second_dot, axis=1, keepdims=True), 0.0)
            deltas[r, 0:1, :] = jnp.sum(d_wide * first, axis=0, keepdims=True)
            deltas[r, 1:2, :] = -lam * second_dot
            dq_acc[r] = jnp.zeros((128, 2 * TILE), F32)

    def pass_on(k):
        for u in range(PER_SPAN):
            o = PER_SPAN * lax.rem(chip + k, SPANS) + u
            to_sibling(o).wait_recv()
            both[o] = (both[o].astype(F32) + sib[o].astype(F32)).astype(BF)
            to_home(o)

    def span(k, carry):
        b = lax.rem(chip + k, SPANS)
        start = pl.multiple_of(b * SPAN, SPAN)
        rows = pl.ds(start, SPAN)
        blocks = pl.ds(b * (SPAN // BLOCK), SPAN // BLOCK)
        acc[...] = jnp.zeros_like(acc)

        def step(r, masked):
            score = matmul(kv[blocks, :, :128].reshape(SPAN, 128), q_cols[r])
            prob = jnp.exp2(score * SCORE - logs[r])
            if masked:
                prob = jnp.where(key_mask(start, SPAN, tile_at(r), 2 * TILE), prob, 0.0)
            upper = matmul(kv[blocks, :, 128:].reshape(SPAN, 128), d_cols[r])
            p1, p2 = prob[:, :TILE], prob[:, TILE:]
            ds = jnp.concatenate(
                [p1 * (upper - deltas[r, 0:1, :]), p2 * (-lam * upper - deltas[r, 1:2, :])],
                axis=1,
            ).astype(BF)
            mixed = (p1 - lam * p2).astype(BF)
            acc[:, :128] += matmul(ds, q_rows[r])
            acc[:, 128:] += matmul(mixed, d_rows[r])
            dq_acc[r] += matmul(turned[:, rows], ds)

        each_tile(b, SPAN, step)

        @pl.when(k >= 2)
        def _():
            for u in range(PER_SPAN):
                to_sibling(PER_SPAN * lax.rem(chip + k - 2, SPANS) + u).wait_send()

        for u in range(PER_SPAN):
            o = PER_SPAN * b + u
            for ref, at, which in ((given, o % (2 * PER_SPAN), 1 - core), (both, o, core)):
                part = acc[pl.ds(pl.multiple_of((2 * u + which) * BLOCK, BLOCK), BLOCK), :]
                ref[at, :, :128] = (part[:, :128] * 0.125).astype(BF)
                ref[at, :, 128:] = part[:, 128:].astype(BF)
            to_sibling(o).start()

        @pl.when(k > 0)
        def _():
            pass_on(k - 1)

        return carry

    def early(k, carry):
        span(k, carry)

        @pl.when(k < 2)
        def _():
            send_gate.some(8 * k, 8 * k + 8)

        return carry

    def late(k, carry):
        span(k, carry)

        at = 6 * (k - EARLY_SPANS)
        send_up.some(at, jnp.minimum(at + 6, 16))
        return carry

    @pl.when(served)
    def _():
        lax.fori_loop(0, EARLY_SPANS, early, 0)

    @pl.when(jnp.logical_not(served))
    def _():
        send_gate.each()

    ring_up.finish()
    block_grad(pup, 0, lffn, lup[...].reshape(4 * BLOCK, 512), 256)

    @pl.when(jnp.logical_not(served))
    def _():
        send_up.each()

    @pl.when(served)
    def _():
        lax.fori_loop(EARLY_SPANS, SPANS, late, 0)
        pass_on(SPANS - 1)

    for r in range(SLOTS):

        @pl.when(served if r else jnp.logical_and(served, slot < 4))
        def _():
            dq_t = jnp.concatenate([dq_acc[r, :64, :TILE], dq_acc[r, 64:, TILE:]], axis=0)
            dq_out[r] = (dq_t * 0.125).T.astype(BF)

    home_sends(dq_out, land, gsend, grecv, chip, core, t, True)
    home_waits(dq_out, land, grecv)
    for j in range(3):
        for u in range(2):
            dqkv_ref[0, u * 128 : (u + 1) * 128, j * 128 : (j + 1) * 128] = land[j, u]
    ring_q.start()
    pltpu.make_async_copy(home, home, krecv.at[0]).wait()
    for j in range(3):
        total = jnp.zeros((BLOCK, 256), F32)
        for p in range(PER_HEAD):
            spot = j * PER_HEAD + p
            total = total + home[spot].astype(F32)
        dqkv_ref[1, :, j * 128 : (j + 1) * 128] = total[:, :128].astype(BF)
        dqkv_ref[2, :, j * 128 : (j + 1) * 128] = total[:, 128:].astype(BF)
    ring_k.start()
    ring_vx.start()
    ring_vz.start()

    for load in late_loads:
        load.wait()
    red2.drain()
    red4 = QuadReduce(*reduces[0], chip, core, t)

    def normed_term(k):
        rows = slice(k * CW, (k + 1) * CW)
        return (
            matmul_t(dqkv_ref[0], wg[rows, :384])
            + matmul_t(dqkv_ref[1], wg[rows, 384:768])
            + matmul_t(dqkv_ref[2], wu[rows, :384])
        )

    red4.run(normed_term)
    ring_mix.finish()
    ring_dres.finish()
    block_grad(pqo, 384, xdres, xmix[...].reshape(4 * BLOCK, 384), 384, 0, 384)
    x = x_ref[...]
    rms = rms_scale(x)
    hat = x * rms
    d_normed = jnp.concatenate([red4.result(k) for k in range(NC)], axis=1)
    part = jnp.sum(d_normed * hat, axis=0, keepdims=True)
    for k in range(12):
        vec[k : k + 1, :] = part[:, k * 128 : (k + 1) * 128]
    first_sum = [
        remote(vec, vecs.at[k], asem.at[0, k], asem.at[1, k], *member)
        for k, member in enumerate(members)
    ]
    for cp in first_sum:
        cp.start()
    grad_ref[...] = dres[...] + norm_back(d_normed, long_row(attn_ref), rms, hat)
    results[1].start()
    for cp in first_sum:
        cp.wait_recv()
    share = pl.ds(pl.multiple_of((2 * core + t) * 8, 8), 8)
    quarter[...] = (vec[share, :] + vecs[0, share, :]) + (vecs[1, share, :] + vecs[2, share, :])

    def spread(k, carry):
        to = 2 * lax.rem(chip + k, CHIPS) + core
        remote(quarter, quarters.at[chip], bsem.at[0], bsem.at[1], to, t).start()
        return carry

    own = pltpu.make_async_copy(quarter, quarters.at[chip], bsem.at[1])
    own.start()
    lax.fori_loop(1, CHIPS, spread, 0)
    for left in lefts:
        left.wait()
    ring_q.finish()
    block_grad(pqo, 0, ldout, rq[...].reshape(4 * BLOCK, 384), 384, 0, 384)
    ring_vx.finish()
    block_grad(pqo, 768, ldout, rvx[...].reshape(4 * BLOCK, 128), 384, 0, 384)
    send_qo.each()
    ring_k.finish()
    block_grad(pkv, 0, ldout, rk[...].reshape(4 * BLOCK, 384), 384, 384, 384)
    ring_vz.finish()
    block_grad(pkv, 384, ldout, rvz[...].reshape(4 * BLOCK, 256), 384, 384, 384)
    send_kv.each()

    send_down.wait()
    for b in range(2):
        total = send_down.total(b, slice(0, 512))
        for h in range(2):
            swap[h, :, 2048 + b * 512 : 2560 + b * 512] = total[h * 24 : h * 24 + 24]
    for m, send in enumerate((send_gate, send_up)):
        send.wait()
        for b in range(2):
            total = send.total(b, slice(0, 512))
            at = m * 1024 + b * 512
            for h in range(2):
                swap[h, :, at : at + 512] = total[h * 24 : h * 24 + 24]
    sibling = s + 1 - 2 * core
    swap_copy = remote(swap.at[1 - core], swapped, swap_sem.at[0], swap_sem.at[1], sibling, t)
    swap_copy.start()

    pltpu.make_async_copy(quarters, quarters, bsem.at[1]).wait()

    def collect(k, total):
        return total + quarters[k]

    sums_ref[share, :] = lax.fori_loop(0, CHIPS, collect, jnp.zeros((8, 128), F32))
    last_sum = [
        remote(sums_ref.at[share], sums_ref.at[share], csem.at[0, k], csem.at[1, k], *member)
        for k, member in enumerate(members)
    ]
    for cp in last_sum:
        cp.start()
    for send, spots in (
        (send_qo, ((0, 384, 0), (384, 384, 1152), (768, 128, 768))),
        (send_kv, ((0, 384, 384), (384, 256, 896))),
    ):
        send.wait()
        for first, width, at in spots:
            total = send.total(0, slice(first, first + width))
            for h in range(2):
                swap2[h, :, at : at + width] = total[h * 24 : h * 24 + 24]
    swap2_copy = remote(swap2.at[1 - core], swapped2, swap2_sem.at[0], swap2_sem.at[1], sibling, t)
    swap2_copy.start()
    swap_copy.wait()
    swap_out(swap, swapped, ((gate_ref, 0), (up_ref, 1024), (down_ref, 2048)), 1024, core)
    for cp in results[6:]:
        cp.start()

    for ring in (
        ring_dout, ring_mix, ring_hid, ring_gate, ring_up, ring_dres, ring_ffn, ring_q, ring_k, ring_vx,
        ring_vz,
    ):
        ring.drain()
    for send in (send_gate, send_up, send_down, send_qo, send_kv):
        send.drain()
    home_sends(dq_out, land, gsend, grecv, chip, core, t, False)
    tile_sends(dms, dmix, tsend, trecv, chip, core, t, False)
    for gather in (gather_f, gather_r):
        gather.drain()
    red3.drain()
    red4.drain()

    @pl.when(served)
    def _():
        for k in (SPANS - 2, SPANS - 1):
            for u in range(PER_SPAN):
                to_sibling(PER_SPAN * lax.rem(chip + k, SPANS) + u).wait_send()

    for count, case in ((CHIPS // 2 - 1, self_served), (CHIPS // 2, jnp.logical_not(self_served))):

        @pl.when(jnp.logical_and(served, case))
        def _():
            sent = both.at[pl.ds(0, count)]
            pltpu.make_async_copy(sent, sent, ksend.at[0]).wait()

    for cp in last_sum:
        cp.wait()
    for cp in first_sum:
        cp.wait_send()
    others = quarters.at[pl.ds(0, CHIPS - 1)]
    pltpu.make_async_copy(others, others, bsem.at[0]).wait()
    swap2_copy.wait()
    outs = ((gq_ref, 0), (gk_ref, 384), (gv_ref, 768), (go_ref, 1152))
    swap_out(swap2, swapped2, outs, 384, core)
    for cp in results[2:6]:
        cp.start()
    for cp in results:
        cp.wait()


def swap_out(swap, swapped, outs, width, core):
    mine = swap[core]
    for c in range(2):

        @pl.when(core == c)
        def _():
            for ref, at in outs:
                ref[:, c * width : (c + 1) * width] = mine[:, at : at + width]
                other = (1 - c) * width
                ref[:, other : other + width] = swapped[:, at : at + width]


def layer(x, cot, mask, attn, ffn, sub, lambdas, wq, wk, wv, wo, wg, wu, wd):
    half = (CHIPS // 2, BLOCK, 256)
    vm = pltpu.VMEM
    sem = pltpu.SemaphoreType.DMA
    return pl.pallas_call(
        layer_kernel,
        name="layer",
        out_shape=(
            shape((ROWS, D), F32),
            shape((ROWS, D), F32),
            *([shape((24, 768), F32)] * 4),
            *([shape((24, 2048), F32)] * 3),
            shape((32, 128), F32),
            shape(GATHERED_Q, BF),
            shape(GATHERED_Q, BF),
        ),
        in_specs=[VM] * 7 + [ANY] * 7,
        out_specs=(ANY,) * 9 + (VM,) + (ANY,) * 2,
        scratch_shapes=[
            vm((ROWS, D), F32),
            vm((ROWS, D), F32),
            *([vm((24, 768), F32)] * 4),
            *([vm((24, 2048), F32)] * 3),
            vm((ROWS, D), F32),
            vm((3, BLOCK, 384), BF),
            *([vm(GATHERED_Q, BF)] * 2),
            vm((4, BLOCK, 128), BF),
            vm((4, BLOCK, 256), BF),
            *([vm(GATHERED_Q, BF)] * 2),
            vm((384, 896), BF),
            vm((384, 640), BF),
            vm((8, CHUNK, 896), BF),
            vm((8, CHUNK, 640), BF),
            vm((2, 24, 1536), F32),
            vm((24, 1536), F32),
            vm((32, 128), F32),
            vm((3, 32, 128), F32),
            vm((8, 128), F32),
            vm((CHIPS, 8, 128), F32),
            vm((3, 2, TILE, 128), BF),
            vm((D, 384), BF),
            vm((D, 1024), BF),
            vm((D, 1024), BF),
            vm((D, 1024), BF),
            vm((BLOCK, D), BF),
            vm((BLOCK, D), BF),
            vm((3, 2, TILE, 128), BF),
            vm((BLOCK, D), BF),
            vm((2, BLOCK, 512), BF),
            vm((2, BLOCK, 512), BF),
            vm((2, BLOCK, 512), BF),
            vm((BLOCK, 384), BF),
            vm((SLOTS, TILE, 128), BF),
            vm(KV, BF),
            vm((SLOTS, 128, 2 * TILE), F32),
            vm((SLOTS, 1, 2 * TILE), F32),
            vm((SLOTS, TILE, 128), BF),
            vm(GATHERED, BF),
            *([vm((4, BLOCK, 512), BF)] * 3),
            vm(GATHERED, BF),
            *([vm((768, 512), BF)] * 3),
            *([vm((16, CHUNK, 512), BF)] * 3),
            vm((2, 24, 3072), F32),
            vm((24, 3072), F32),
            vm((128, CHIPS * BLOCK), BF),
            vm((SPAN, 256), F32),
            vm((SLOTS, 128, 2 * TILE), BF),
            vm((SLOTS, 2 * TILE, 128), BF),
            vm((SLOTS, 128, TILE), BF),
            vm((SLOTS, TILE, 128), BF),
            vm((SLOTS, 2, TILE), F32),
            vm((SLOTS, 128, 2 * TILE), F32),
            vm((SLOTS, TILE, 128), BF),
            vm((2 * PER_SPAN, BLOCK, 256), BF),
            vm(half, BF),
            vm(half, BF),
            vm((3 * PER_HEAD, BLOCK, 256), BF),
            vm((8, BLOCK), F32),
            pltpu.SMEM((2,), F32),
            vm((8, 2 * TILE), F32),
            *(REDUCE_SCRATCH * 2),
            *(GATHER_SEMS * 4),
            *(RING_SEMS * 12),
            *ONCE_SEMS,
            *(RING_SEMS * 5),
            sem((4,)),
            sem((SLOTS,)),
            sem((3, 2)),
            sem((6,)),
            sem((SLOTS,)),
            sem((2,)),
            sem((2 * PER_SPAN,)),
            sem((CHIPS // 2,)),
            sem((1,)),
            sem((1,)),
            sem((SLOTS,)),
            sem((3, 2)),
            sem((3,)),
            sem((2,)),
            sem((2,)),
            sem((2, 3)),
            sem((2,)),
            sem((2, 3)),
            sem((9,)),
            sem((1,)),
            sem((CHIPS,)),
            sem((1,)),
            sem((6,)),
            sem((SLOTS,)),
        ],
        compiler_params=pltpu.CompilerParams(
            collective_id=0, has_side_effects=True, vmem_limit_bytes=VMEM_LIMIT
        ),
    )(x, cot, mask, attn, ffn, sub, lambdas, wq, wk, wv, wo, wg, wu, wd)


def publish(lambdas, sums, arrays):
    count = len(arrays)

    def kernel(lambdas_ref, sums_ref, *refs):
        for k in range(count):
            refs[count + k][...] = refs[k][...]
        attn_ref, ffn_ref, sub_ref, grad_ref = refs[2 * count :]
        attn_ref[...] = sums_ref[0:12, :]
        ffn_ref[...] = sums_ref[12:24, :]
        sub_ref[...] = sums_ref[24:25, :]
        vectors, first, second = lambda_parts(lambdas_ref)
        d_lam = as_column(sums_ref[25:26, :])[:12, :1]
        factors = (d_lam * first, d_lam * first, -d_lam * second, -d_lam * second)
        for k, other in enumerate((1, 0, 3, 2)):
            grad_ref[:, k, :] = factors[k] * vectors[other]

    return pl.pallas_call(
        kernel,
        name="publish",
        out_shape=tuple(shape(a.shape, a.dtype) for a in arrays)
        + (shape((12, 128), F32), shape((12, 128), F32), shape((1, 128), F32), shape((12, 4, 64), F32)),
        in_specs=[VM] * (count + 2),
        out_specs=(VM,) * (count + 4),
    )(lambdas, sums, *arrays)


def on_device(
    hidden_in, cotangent, needle_mask, attn_gain, lambdas, subln_gain, ffn_gain,
    weight_query, weight_key, weight_value, weight_out, weight_gate, weight_up, weight_down,
):
    mask = needle_mask.reshape(1, ROWS)
    attn = attn_gain.reshape(12, 128)
    sub = subln_gain.reshape(1, 128)
    by_head = jnp.transpose(lambdas, (1, 0, 2))
    *results, sums, _, _ = layer(
        hidden_in, cotangent, mask, attn, ffn_gain.reshape(12, 128), sub, by_head,
        weight_query, weight_key, weight_value, weight_out, weight_gate, weight_up, weight_down,
    )
    *results, attn_grad, ffn_grad, sub_grad, lambda_grad = publish(by_head, sums, results)
    return (
        *results,
        attn_grad.reshape(D),
        jnp.transpose(lambda_grad, (1, 0, 2)),
        sub_grad.reshape(128),
        ffn_grad.reshape(D),
    )


def solution(mesh):
    split = P(None, "tp")
    rows = P(("seq", "tp"), None)
    both = P("seq", "tp")
    return jax.shard_map(
        on_device,
        mesh=mesh,
        in_specs=(rows, rows, P(("seq", "tp"))) + (P(),) * 4 + (split,) * 7,
        out_specs=(rows, rows) + (both,) * 7 + (P(),) * 4,
        check_vma=False,
    )
```
